32 devices in a mesh: dp: 16 (over z, x, core), seq: 2 (over y).
Axes of the slice: x: 2, y: 2, z: 4, core: 2. Of those that a mesh axis runs over, the one named last changes fastest.
Arguments:
- targets: bfloat16 [4, 16, 1024, 768], P(None, 'dp', 'seq'), may hold values from -6 to 6
- memory: bfloat16 [4, 16, 1024, 768], P(None, 'dp', 'seq'), may hold values from -6 to 6
- row_kind: int32 [4, 16], P(None, 'dp'), may hold values from 0 to 1
- loss_mask: int32 [4, 16, 1024], P(None, 'dp', 'seq'), may hold values 0 or 1
- cotangent: bfloat16 [4, 16, 1024, 768], P(None, 'dp', 'seq'), may hold values from -6 to 6
- norm_self_gain: float32 [768], replicated, may hold values from 0.5 to 1.5
- norm_self_bias: float32 [768], replicated, may hold values from -1.75 to 1.75
- self_input: bfloat16 [768, 2304], replicated, may hold values from -0.21875 to 0.21875
- self_query_bias: float32 [768], replicated, may hold values from -3 to 3
- self_value_bias: float32 [768], replicated, may hold values from -0.1875 to 0.1875
- self_output: bfloat16 [768, 768], replicated, may hold values from -3.5 to 3.5
- self_output_bias: float32 [768], replicated, may hold values from -1.75 to 1.75
- norm_cross_gain: float32 [768], replicated, may hold values from 0.5 to 1.5
- norm_cross_bias: float32 [768], replicated, may hold values from -1.75 to 1.75
- cross_query: bfloat16 [768, 768], replicated, may hold values from -0.21875 to 0.21875
- cross_query_bias: float32 [768], replicated, may hold values from -3 to 3
- cross_input: bfloat16 [768, 1536], replicated, may hold values from -0.21875 to 0.21875
- cross_value_bias: float32 [768], replicated, may hold values from -0.1875 to 0.1875
- cross_output: bfloat16 [768, 768], replicated, may hold values from -3.5 to 3.5
- cross_output_bias: float32 [768], replicated, may hold values from -1.75 to 1.75
- norm_feed_gain: float32 [768], replicated, may hold values from 0.5 to 1.5
- norm_feed_bias: float32 [768], replicated, may hold values from -1.75 to 1.75
- feed_in: bfloat16 [768, 3072], replicated, may hold values from -0.21875 to 0.21875
- feed_in_bias: float32 [3072], replicated, may hold values from -3 to 3
- feed_out: bfloat16 [3072, 768], replicated, may hold values from -0.109375 to 0.109375
- feed_out_bias: float32 [768], replicated, may hold values from -1.75 to 1.75
Outputs:
- layer_output: bfloat16 [4, 16, 1024, 768], P(None, 'dp', 'seq')
- targets_gradient: float32 [4, 16, 1024, 768], P(None, 'dp', 'seq')
- memory_gradient: float32 [4, 16, 1024, 768], P(None, 'dp', 'seq')
- norm_self_gain_gradient: float32 [768], P('dp')
- norm_self_bias_gradient: float32 [768], P('dp')
- self_input_gradient: float32 [768, 2304], P('dp')
- self_query_bias_gradient: float32 [768], P('dp')
- self_value_bias_gradient: float32 [768], P('dp')
- self_output_gradient: float32 [768, 768], P('dp')
- self_output_bias_gradient: float32 [768], P('dp')
- norm_cross_gain_gradient: float32 [768], P('dp')
- norm_cross_bias_gradient: float32 [768], P('dp')
- cross_query_gradient: float32 [768, 768], P('dp')
- cross_query_bias_gradient: float32 [768], P('dp')
- cross_input_gradient: float32 [768, 1536], P('dp')
- cross_value_bias_gradient: float32 [768], P('dp')
- cross_output_gradient: float32 [768, 768], P('dp')
- cross_output_bias_gradient: float32 [768], P('dp')
- norm_feed_gain_gradient: float32 [768], P('dp')
- norm_feed_bias_gradient: float32 [768], P('dp')
- feed_in_gradient: float32 [768, 3072], P('dp')
- feed_in_bias_gradient: float32 [3072], P('dp')
- feed_out_gradient: float32 [3072, 768], P('dp')
- feed_out_bias_gradient: float32 [768], P('dp')
The draws below stay inside these ranges and needn't reach their ends.
Inputs may be any that keep to these rules, and one draw needn't show every extreme that they name: `row_kind`: 0 marks a gap-sentence row, whose self-attention is causal; 1 a masked-token row, which attends to all its positions.
All inputs are finite; a program needn't handle non-finite values. No bound on the sum of `loss_mask` on one device may be relied on, other than what follows from the above.
Results may differ from the reference program's by a relative error of at most 0.038.
Values may be sent and summed in bfloat16 or wider, within the bound.
A program may use at most 576 MiB of HBM per device.

```python
import jax
import jax.numpy as jnp
from jax import lax

D = 768
HEADS = 12
HEAD = 64
FF = 3072
LEN = 1024
MICRO = 4
BATCH = 16


def plant(drawn, key, least, high):
    dims = drawn.shape
    place = [jax.random.randint(jax.random.fold_in(key, axis), (), 0, dims[axis]) for axis in range(len(dims))]
    drawn = drawn.at[tuple(place)].set(least)
    longest = dims.index(max(dims))
    place[longest] = (place[longest] + 1) % dims[longest]
    return drawn.at[tuple(place)].set(high)


def shard_levels(rng, shape, pieces, low, high):
    factor_of, own = 1.0, jax.random.fold_in(rng, 6)
    for position, parts in pieces:
        steps = jnp.exp(jax.random.uniform(jax.random.fold_in(own, position), (parts,), jnp.float32, low / len(pieces), high / len(pieces)))
        factor_of = factor_of * jnp.repeat(steps, shape[position] // parts).reshape([-1 if axis == position else 1 for axis in range(len(shape))])
    return factor_of


def bell_draw(own_key, dims, deviation, bound, pieces=(), held_as=jnp.bfloat16):
    entries = deviation * jax.random.normal(own_key, dims, jnp.float32)
    if pieces:
        entries = entries * shard_levels(own_key, dims, pieces, -0.22, 0.18)
    return jnp.clip(entries, -bound, bound).astype(held_as)


def setup_inputs(seed: int = 0) -> dict:
    seeds = jax.random.split(jax.random.key(seed), 27)
    targets = bell_draw(seeds[0], (MICRO, BATCH, LEN, D), 1.0, 6.0, ((1, 16), (2, 2)))
    memory = bell_draw(seeds[1], (MICRO, BATCH, LEN, D), 1.0, 6.0, ((1, 16), (2, 2)))
    row_kind = plant(jax.random.randint(seeds[2], (MICRO, BATCH), 0, 2), jax.random.fold_in(seeds[2], 1), 0, 1).astype(jnp.int32)
    loss_mask = plant((jax.random.randint(seeds[3], (MICRO, BATCH, LEN), 0, 4) < 3).astype(jnp.int32), jax.random.fold_in(seeds[3], 1), 0, 1)
    cotangent = bell_draw(seeds[4], (MICRO, BATCH, LEN, D), 1.0, 6.0, ((1, 16), (2, 2)))
    norm_self_gain = jnp.clip(1.0 + 0.1 * jax.random.normal(seeds[5], (D,), jnp.float32), 0.5, 1.5)
    norm_self_bias = bell_draw(seeds[6], (D,), 0.3, 1.75, (), jnp.float32)
    self_input = bell_draw(seeds[7], (D, 3 * D), D ** -0.5, 0.21875)
    self_query_bias = bell_draw(seeds[8], (D,), 0.5, 3.0, (), jnp.float32)
    self_value_bias = bell_draw(seeds[9], (D,), 0.03, 0.1875, (), jnp.float32)
    self_output = bell_draw(seeds[10], (D, D), (max(1, 4 * D // LEN)) ** -0.5, 3.5)
    self_output_bias = bell_draw(seeds[11], (D,), 0.3, 1.75, (), jnp.float32)
    norm_cross_gain = jnp.clip(1.0 + 0.1 * jax.random.normal(seeds[12], (D,), jnp.float32), 0.5, 1.5)
    norm_cross_bias = bell_draw(seeds[13], (D,), 0.3, 1.75, (), jnp.float32)
    cross_query = bell_draw(seeds[14], (D, D), D ** -0.5, 0.21875)
    cross_query_bias = bell_draw(seeds[15], (D,), 0.5, 3.0, (), jnp.float32)
    cross_input = bell_draw(seeds[16], (D, 2 * D), D ** -0.5, 0.21875)
    cross_value_bias = bell_draw(seeds[17], (D,), 0.03, 0.1875, (), jnp.float32)
    cross_output = bell_draw(seeds[18], (D, D), (max(1, 4 * D // LEN)) ** -0.5, 3.5)
    cross_output_bias = bell_draw(seeds[19], (D,), 0.3, 1.75, (), jnp.float32)
    norm_feed_gain = jnp.clip(1.0 + 0.1 * jax.random.normal(seeds[20], (D,), jnp.float32), 0.5, 1.5)
    norm_feed_bias = bell_draw(seeds[21], (D,), 0.3, 1.75, (), jnp.float32)
    feed_in = bell_draw(seeds[22], (D, FF), D ** -0.5, 0.21875)
    feed_in_bias = bell_draw(seeds[23], (FF,), 0.5, 3.0, (), jnp.float32)
    feed_out = bell_draw(seeds[24], (FF, D), FF ** -0.5, 0.109375)
    feed_out_bias = bell_draw(seeds[25], (D,), 0.3, 1.75, (), jnp.float32)
    return {"targets": targets, "memory": memory, "row_kind": row_kind, "loss_mask": loss_mask, "cotangent": cotangent, "norm_self_gain": norm_self_gain, "norm_self_bias": norm_self_bias, "self_input": self_input, "self_query_bias": self_query_bias, "self_value_bias": self_value_bias, "self_output": self_output, "self_output_bias": self_output_bias, "norm_cross_gain": norm_cross_gain, "norm_cross_bias": norm_cross_bias, "cross_query": cross_query, "cross_query_bias": cross_query_bias, "cross_input": cross_input, "cross_value_bias": cross_value_bias, "cross_output": cross_output, "cross_output_bias": cross_output_bias, "norm_feed_gain": norm_feed_gain, "norm_feed_bias": norm_feed_bias, "feed_in": feed_in, "feed_in_bias": feed_in_bias, "feed_out": feed_out, "feed_out_bias": feed_out_bias}


epsilon = 1e-05
blocked_score = -1e+30
highest = lax.Precision.HIGHEST

@jax.custom_vjp
def low(v):
    return lax.optimization_barrier(v.astype(jnp.bfloat16)).astype(jnp.float32)

@jax.custom_vjp
def low_back(v):
    return v

def low_keep(v):
    return (low(v), None)

def low_pass(kept, grad):
    return (grad,)

def back_keep(v):
    return (v, None)

def back_low(kept, grad):
    return (low(grad),)
low.defvjp(low_keep, low_pass)
low_back.defvjp(back_keep, back_low)

def normed(values, norm_gain, norm_shift):
    center = values - lax.optimization_barrier(jnp.mean(values, axis=-1, keepdims=True))
    spread = lax.optimization_barrier(jnp.mean(center * center, axis=-1, keepdims=True))
    return center * lax.rsqrt(spread + epsilon) * norm_gain + norm_shift

def matmul(first_rows, second_rows):
    return jnp.dot(first_rows, second_rows, precision=highest)

def attend(queries, key_rows, values, allowed):
    query_count = queries.shape[0]
    key_count = key_rows.shape[0]
    query_heads = queries.reshape(query_count, HEADS, HEAD)
    key_heads = key_rows.reshape(key_count, HEADS, HEAD)
    value_heads = values.reshape(key_count, HEADS, HEAD)
    scores = low_back(jnp.einsum('qhe,khe->hqk', query_heads, key_heads, precision=highest))
    scores = jnp.where(allowed[None], scores, blocked_score)
    weights = low(jax.nn.softmax(scores, axis=-1))
    mixed = jnp.einsum('hqk,khe->qhe', weights, value_heads, precision=highest)
    return low(low_back(mixed.reshape(query_count, HEADS * HEAD)))

def decoder_layer(params, inputs, memory_rows, row_flag):
    self_gain, self_shift, self_input, self_query_bias, self_value_bias, self_output, self_output_bias, cross_gain, cross_shift, cross_query, cross_query_bias, cross_input, cross_value_bias, cross_output, cross_output_bias, feed_gain, feed_shift, feed_in, feed_in_bias, feed_out, feed_out_bias = params
    query_scale = HEAD ** (-0.5)
    first_normed = low(normed(inputs, self_gain, self_shift))
    self_joint = low_back(matmul(first_normed, self_input))
    queries = low((self_joint[:, :D] + self_query_bias) * query_scale)
    key_rows = low(self_joint[:, D:2 * D])
    values = low(self_joint[:, 2 * D:] + self_value_bias)
    positions = jnp.arange(LEN)
    allowed = (positions[None, :] <= positions[:, None]) | (row_flag == 1)
    self_mixed = attend(queries, key_rows, values, allowed)
    after_self = inputs + low_back(matmul(self_mixed, self_output)) + self_output_bias
    second_normed = low(normed(after_self, cross_gain, cross_shift))
    cross_queries = low((low_back(matmul(second_normed, cross_query)) + cross_query_bias) * query_scale)
    cross_joint = low_back(matmul(memory_rows, cross_input))
    cross_keys = low(cross_joint[:, :D])
    cross_values = low(cross_joint[:, D:] + cross_value_bias)
    everywhere = jnp.ones((LEN, LEN), dtype=bool)
    cross_mixed = attend(cross_queries, cross_keys, cross_values, everywhere)
    after_cross = after_self + low_back(matmul(cross_mixed, cross_output)) + cross_output_bias
    third_normed = low(normed(after_cross, feed_gain, feed_shift))
    hidden = low(jax.nn.gelu(low_back(matmul(third_normed, feed_in)) + feed_in_bias, approximate=False))
    return after_cross + low_back(matmul(hidden, feed_out)) + feed_out_bias

def reference(targets, memory, row_kind, loss_mask, cotangent, norm_self_gain, norm_self_bias, self_input, self_query_bias, self_value_bias, self_output, self_output_bias, norm_cross_gain, norm_cross_bias, cross_query, cross_query_bias, cross_input, cross_value_bias, cross_output, cross_output_bias, norm_feed_gain, norm_feed_bias, feed_in, feed_in_bias, feed_out, feed_out_bias):
    weights = tuple((argument_value.astype(jnp.float32) for argument_value in (norm_self_gain, norm_self_bias, self_input, self_query_bias, self_value_bias, self_output, self_output_bias, norm_cross_gain, norm_cross_bias, cross_query, cross_query_bias, cross_input, cross_value_bias, cross_output, cross_output_bias, norm_feed_gain, norm_feed_bias, feed_in, feed_in_bias, feed_out, feed_out_bias)))
    row_total = MICRO * BATCH
    inputs = targets.astype(jnp.float32).reshape(row_total, LEN, D)
    sources = memory.astype(jnp.float32).reshape(row_total, LEN, D)
    row_flags = row_kind.reshape(row_total)
    upstream = (cotangent.astype(jnp.float32) * loss_mask.astype(jnp.float32)[..., None]).reshape(row_total, LEN, D)

    def one_row(totals, row_entry):
        row_input, row_source, row_flag, row_upstream = row_entry

        def forward(params, layer_input, layer_source):
            return decoder_layer(params, layer_input, layer_source, row_flag)
        result, pullback = jax.vjp(forward, weights, row_input, row_source)
        param_grads, input_grad, source_grad = pullback(row_upstream)
        totals = tuple((running + added for running, added in zip(totals, param_grads)))
        return (totals, (result.astype(jnp.bfloat16), input_grad, source_grad))
    initial = tuple((jnp.zeros_like(argument_value) for argument_value in weights))
    totals, (results, input_grads, source_grads) = lax.scan(one_row, initial, (inputs, sources, row_flags, upstream))
    full_shape = (MICRO, BATCH, LEN, D)
    return (results.reshape(full_shape), input_grads.reshape(full_shape), source_grads.reshape(full_shape), totals[0], totals[1], totals[2], totals[3], totals[4], totals[5], totals[6], totals[7], totals[8], totals[9], totals[10], totals[11], totals[12], totals[13], totals[14], totals[15], totals[16], totals[17], totals[18], totals[19], totals[20])
```

```python
import functools

import jax
import jax.numpy as jnp
from jax import lax
from jax.experimental import pallas as pl
from jax.experimental.pallas import tpu as pltpu
from jax.sharding import PartitionSpec as P

HEADS = 12
HEAD = 64


epsilon = 1e-05
blocked_score = -1e30


def normed(values, norm_gain, norm_shift):
    center = values - jnp.mean(values, axis=-1, keepdims=True)
    spread = jnp.mean(center * center, axis=-1, keepdims=True)
    return center * lax.rsqrt(spread + epsilon) * norm_gain + norm_shift


def normed_back(values, norm_gain, norm_shift, upstream):
    unused, pullback = jax.vjp(normed, values, norm_gain, norm_shift)
    return pullback(upstream)


def gelu_exact(values):
    return jax.nn.gelu(values, approximate=False)


def project_rows(row_block, weight):
    return jnp.einsum("bpd,de->bpe", row_block, weight, preferred_element_type=jnp.float32)


def project_back(row_block, weight):
    return jnp.einsum("bpe,de->bpd", row_block, weight, preferred_element_type=jnp.float32)


def outer_sum(first_rows, second_rows):
    return jnp.einsum("bpd,bpe->de", first_rows, second_rows, preferred_element_type=jnp.float32)


def split_heads(row_block):
    return row_block.reshape(row_block.shape[0], row_block.shape[1], HEADS, HEAD)


def masked_scores(queries, key_rows, allowed):
    scores = jnp.einsum(
        "bphe,bshe->bhps",
        split_heads(queries),
        split_heads(key_rows),
        preferred_element_type=jnp.float32,
    )
    if allowed is None:
        return scores
    return jnp.where(allowed[:, None], scores, blocked_score)


def attend_forward(queries, key_rows, values, allowed):
    scores = masked_scores(queries, key_rows, allowed)
    highest_score = jnp.max(scores, axis=-1, keepdims=True)
    raised = jnp.exp(scores - highest_score)
    totals = jnp.sum(raised, axis=-1, keepdims=True)
    weights = (raised / totals).astype(jnp.bfloat16)
    mixed = jnp.einsum(
        "bhps,bshe->bphe", weights, split_heads(values), preferred_element_type=jnp.float32
    )
    return (mixed.reshape(queries.shape).astype(jnp.bfloat16), highest_score + jnp.log(totals))


def attend_backward(queries, key_rows, values, allowed, log_totals, upstream):
    weights = jnp.exp(masked_scores(queries, key_rows, allowed) - log_totals)
    upstream_heads = split_heads(upstream)
    value_grads = jnp.einsum(
        "bhps,bphe->bshe",
        weights.astype(jnp.bfloat16),
        upstream_heads,
        preferred_element_type=jnp.float32,
    )
    weight_grads = jnp.einsum(
        "bphe,bshe->bhps", upstream_heads, split_heads(values), preferred_element_type=jnp.float32
    )
    score_grads = weights * (weight_grads - jnp.sum(weight_grads * weights, axis=-1, keepdims=True))
    score_low = score_grads.astype(jnp.bfloat16)
    query_grads = jnp.einsum(
        "bhps,bshe->bphe", score_low, split_heads(key_rows), preferred_element_type=jnp.float32
    ).reshape(queries.shape)
    key_grads = jnp.einsum(
        "bhps,bphe->bshe", score_low, split_heads(queries), preferred_element_type=jnp.float32
    ).reshape(key_rows.shape)
    return (query_grads, jnp.concatenate([key_grads, value_grads.reshape(key_rows.shape)], axis=-1))


def split_sequences(
    targets,
    memory,
    row_kind,
    loss_mask,
    cotangent,
    norm_self_gain,
    norm_self_bias,
    self_input,
    self_query_bias,
    self_value_bias,
    self_output,
    self_output_bias,
    norm_cross_gain,
    norm_cross_bias,
    cross_query,
    cross_query_bias,
    cross_input,
    cross_value_bias,
    cross_output,
    cross_output_bias,
    norm_feed_gain,
    norm_feed_bias,
    feed_in,
    feed_in_bias,
    feed_out,
    feed_out_bias,
):
    model_width = targets.shape[3]
    part_rows = targets.shape[2]
    key_span = part_rows * lax.axis_size("seq")
    query_scale = HEAD ** (-0.5)
    places = lax.axis_index("seq") * part_rows + jnp.arange(part_rows)
    causal = jnp.arange(key_span)[None, :] <= places[:, None]
    results, input_grads, source_grads = ([], [], [])
    totals = None
    for micro_index in range(targets.shape[0]):
        inputs = targets[micro_index].astype(jnp.float32)
        memory_local = memory[micro_index]
        allowed = causal[None] | (row_kind[micro_index] == 1)[:, None, None]
        first_normed = normed(inputs, norm_self_gain, norm_self_bias).astype(jnp.bfloat16)
        self_joint = project_rows(first_normed, self_input)
        queries = ((self_joint[..., :model_width] + self_query_bias) * query_scale).astype(
            jnp.bfloat16
        )
        own_pairs = jnp.concatenate(
            [
                self_joint[..., model_width : 2 * model_width],
                self_joint[..., 2 * model_width :] + self_value_bias,
            ],
            axis=-1,
        ).astype(jnp.bfloat16)
        gathered_self = lax.all_gather(own_pairs, "seq", axis=1, tiled=True)
        key_rows = gathered_self[..., :model_width]
        value_rows = gathered_self[..., model_width:]
        self_mixed, self_totals = attend_forward(queries, key_rows, value_rows, allowed)
        after_self = inputs + project_rows(self_mixed, self_output) + self_output_bias
        second_normed = normed(after_self, norm_cross_gain, norm_cross_bias).astype(jnp.bfloat16)
        cross_queries = (
            (project_rows(second_normed, cross_query) + cross_query_bias) * query_scale
        ).astype(jnp.bfloat16)
        joined = project_rows(lax.all_gather(memory_local, "seq", axis=1, tiled=True), cross_input)
        gathered_cross = jnp.concatenate(
            [joined[..., :model_width], joined[..., model_width:] + cross_value_bias], axis=-1
        ).astype(jnp.bfloat16)
        cross_keys = gathered_cross[..., :model_width]
        cross_values = gathered_cross[..., model_width:]
        cross_mixed, cross_totals = attend_forward(cross_queries, cross_keys, cross_values, None)
        after_cross = after_self + project_rows(cross_mixed, cross_output) + cross_output_bias
        third_normed = normed(after_cross, norm_feed_gain, norm_feed_bias).astype(jnp.bfloat16)
        activated, gelu_pullback = jax.vjp(
            gelu_exact, project_rows(third_normed, feed_in) + feed_in_bias
        )
        activated_low = activated.astype(jnp.bfloat16)
        results.append(
            (after_cross + project_rows(activated_low, feed_out) + feed_out_bias).astype(
                jnp.bfloat16
            )
        )
        pieces = [None] * 21
        grad_output = (
            cotangent[micro_index].astype(jnp.float32)
            * loss_mask[micro_index].astype(jnp.float32)[..., None]
        )
        output_low = grad_output.astype(jnp.bfloat16)
        pieces[19] = outer_sum(activated_low, output_low)
        pieces[20] = jnp.sum(grad_output, axis=(0, 1))
        grad_hidden = gelu_pullback(project_back(output_low, feed_out))[0]
        hidden_low = grad_hidden.astype(jnp.bfloat16)
        pieces[17] = outer_sum(third_normed, hidden_low)
        pieces[18] = jnp.sum(grad_hidden, axis=(0, 1))
        through_feed, pieces[15], pieces[16] = normed_back(
            after_cross, norm_feed_gain, norm_feed_bias, project_back(hidden_low, feed_in)
        )
        grad_cross = grad_output + through_feed
        cross_low = grad_cross.astype(jnp.bfloat16)
        pieces[13] = outer_sum(cross_mixed, cross_low)
        pieces[14] = jnp.sum(grad_cross, axis=(0, 1))
        cross_upstream = project_back(cross_low, cross_output).astype(jnp.bfloat16)
        cross_query_grads, cross_pair_grads = attend_backward(
            cross_queries, cross_keys, cross_values, None, cross_totals, cross_upstream
        )
        own_cross = lax.psum_scatter(
            cross_pair_grads.astype(jnp.bfloat16), "seq", scatter_dimension=1, tiled=True
        ).astype(jnp.float32)
        pieces[12] = jnp.sum(own_cross[..., model_width:], axis=(0, 1))
        own_cross_low = own_cross.astype(jnp.bfloat16)
        pieces[11] = outer_sum(memory_local, own_cross_low)
        source_grads.append(project_back(own_cross_low, cross_input))
        scaled_cross = cross_query_grads * query_scale
        pieces[10] = jnp.sum(scaled_cross, axis=(0, 1))
        scaled_cross_low = scaled_cross.astype(jnp.bfloat16)
        pieces[9] = outer_sum(second_normed, scaled_cross_low)
        through_cross, pieces[7], pieces[8] = normed_back(
            after_self,
            norm_cross_gain,
            norm_cross_bias,
            project_back(scaled_cross_low, cross_query),
        )
        grad_self = grad_cross + through_cross
        self_low = grad_self.astype(jnp.bfloat16)
        pieces[5] = outer_sum(self_mixed, self_low)
        pieces[6] = jnp.sum(grad_self, axis=(0, 1))
        self_upstream = project_back(self_low, self_output).astype(jnp.bfloat16)
        self_query_grads, self_pair_grads = attend_backward(
            queries, key_rows, value_rows, allowed, self_totals, self_upstream
        )
        own_self = lax.psum_scatter(
            self_pair_grads.astype(jnp.bfloat16), "seq", scatter_dimension=1, tiled=True
        ).astype(jnp.float32)
        scaled_self = self_query_grads * query_scale
        pieces[3] = jnp.sum(scaled_self, axis=(0, 1))
        pieces[4] = jnp.sum(own_self[..., model_width:], axis=(0, 1))
        joint_low = jnp.concatenate([scaled_self, own_self], axis=-1).astype(jnp.bfloat16)
        pieces[2] = outer_sum(first_normed, joint_low)
        through_first, pieces[0], pieces[1] = normed_back(
            inputs, norm_self_gain, norm_self_bias, project_back(joint_low, self_input)
        )
        input_grads.append(grad_self + through_first)
        totals = (
            pieces
            if totals is None
            else [running + added for running, added in zip(totals, pieces)]
        )
    def reduced(total):
        block = lax.psum_scatter(
            total.astype(jnp.bfloat16), "dp", scatter_dimension=0, tiled=True
        )
        return lax.psum(block, "seq").astype(jnp.float32)

    final = [reduced(total) for total in totals]
    return (jnp.stack(results), jnp.stack(input_grads), jnp.stack(source_grads)) + tuple(final)


def contract(first, second, first_dim, second_dim):
    return lax.dot_general(
        first, second, (((first_dim,), (second_dim,)), ((), ())), preferred_element_type=jnp.float32
    )


def head_masks(pair):
    lane = lax.broadcasted_iota(jnp.int32, (1, pair.shape[1]), 1)
    zero = jnp.zeros((), pair.dtype)
    return (jnp.where(lane < HEAD, pair, zero), jnp.where(lane < HEAD, zero, pair))


def attend_kernel(info_ref, q_ref, k_ref, v_ref, o_ref, e_ref, r_ref, *, block, use_mask):
    length = k_ref.shape[1]
    values_turned = v_ref[0].T
    ones = jnp.ones((16, length), jnp.bfloat16)
    own = length // 2
    causal = info_ref[1 + pl.program_id(0)] == 0 if use_mask else None

    def allowed(start):
        offset = info_ref[0] * own
        key_place = lax.broadcasted_iota(jnp.int32, (length, 1), 0) + offset
        key_place = jnp.where(key_place >= length, key_place - length, key_place)
        query_place = lax.broadcasted_iota(jnp.int32, (1, block), 1) + start + offset
        query_place = jnp.where(query_place >= length, query_place - length, query_place)
        return key_place <= query_place

    def run(masked, shifted):
        lowest, highest = None, None
        for start in range(0, length, block):
            mixed = []
            for head, queries in enumerate(head_masks(q_ref[0, start : start + block, :])):
                scores = contract(k_ref[0], queries, 1, 1)
                if masked and shifted:
                    scores = jnp.where(allowed(start), scores, blocked_score)
                if shifted:
                    scores = scores - jnp.max(scores, axis=0, keepdims=True)
                raised = jnp.exp(scores)
                if masked:
                    raised = jnp.where(allowed(start), raised, 0.0)
                low = raised.astype(jnp.bfloat16)
                e_ref[0, head, :, start : start + block] = low
                turned = jnp.concatenate(
                    [values_turned[head * HEAD : (head + 1) * HEAD], ones], axis=0
                )
                sums = contract(turned, low, 1, 0)
                total = sums[HEAD : HEAD + 1]
                if not shifted:
                    lowest = total if lowest is None else jnp.minimum(lowest, total)
                    highest = total if highest is None else jnp.maximum(highest, total)
                inverse = 1.0 / total
                r_ref[0, 0, head : head + 1, start : start + block] = inverse
                mixed.append(sums[:HEAD] * inverse)
            o_ref[0, start : start + block, :] = (
                jnp.concatenate(mixed, axis=0).T.astype(jnp.bfloat16)
            )
        if not shifted:
            in_range = (jnp.min(lowest) > 1e-20) & (jnp.max(highest) < 1e30)

            @pl.when(jnp.logical_not(in_range))
            def _():
                run(masked, True)

    if use_mask:

        @pl.when(causal)
        def _():
            run(True, False)

        @pl.when(jnp.logical_not(causal))
        def _():
            run(False, False)

    else:
        run(False, False)


def attend(info, queries, keys, values, use_mask, offsets):
    count, length = queries.shape[:2]
    pairs = HEADS * HEAD // 128
    width = HEADS * HEAD

    def spec(offset):
        return pl.BlockSpec((1, length, 128), lambda s, p, info: (s, 0, offset * pairs + p))

    return pl.pallas_call(
        functools.partial(attend_kernel, block=length // 2, use_mask=use_mask),
        grid_spec=pltpu.PrefetchScalarGridSpec(
            num_scalar_prefetch=1,
            grid=(count, pairs),
            in_specs=[spec(offset) for offset in offsets],
            out_specs=[
                spec(0),
                pl.BlockSpec((1, 2, length, length), lambda s, p, info: (s, p, 0, 0)),
                pl.BlockSpec((1, 1, 2, length), lambda s, p, info: (s, p, 0, 0)),
            ],
        ),
        out_shape=[
            jax.ShapeDtypeStruct((count, length, width), jnp.bfloat16),
            jax.ShapeDtypeStruct((count, HEADS, length, length), jnp.bfloat16),
            jax.ShapeDtypeStruct((count, pairs, 2, length), jnp.float32),
        ],
        compiler_params=pltpu.CompilerParams(vmem_limit_bytes=56 * 2**20),
        cost_estimate=pl.CostEstimate(
            flops=4 * count * HEADS * length * length * 256,
            bytes_accessed=count * HEADS * length * length * 2,
            transcendentals=count * HEADS * length * length,
        ),
        name="attend",
    )(info, queries, keys, values)


def attend_back_kernel(q_ref, k_ref, v_ref, o_ref, g_ref, e_ref, r_ref, dq_ref, dk_ref, dv_ref):
    length = k_ref.shape[1]
    keys_turned = k_ref[0].T
    upstream = g_ref[0].astype(jnp.float32)
    products = (o_ref[0].astype(jnp.float32) * upstream).T
    upstream = upstream.T
    parts, deltas = [], []
    for head in range(2):
        rows = slice(head * HEAD, (head + 1) * HEAD)
        inverse = r_ref[0, 0, head : head + 1, :]
        parts.append(upstream[rows] * inverse)
        deltas.append(jnp.sum(products[rows], axis=0, keepdims=True) * inverse)
    scaled = head_masks(jnp.concatenate(parts, axis=0).T.astype(jnp.bfloat16))
    queries = head_masks(q_ref[0])
    key_sum, value_sum, query_parts = 0.0, 0.0, []
    for head in range(2):
        rows = slice(head * HEAD, (head + 1) * HEAD)
        low = e_ref[0, head]
        grads = contract(v_ref[0], scaled[head], 1, 1)
        score_low = (low.astype(jnp.float32) * (grads - deltas[head])).astype(jnp.bfloat16)
        value_sum += contract(low, scaled[head], 1, 0)
        key_sum += contract(score_low, queries[head], 1, 0)
        query_parts.append(contract(keys_turned[rows], score_low, 1, 0))
    turned = jnp.concatenate(query_parts, axis=0) * (HEAD**-0.5)
    dq_ref[0] = turned.T.astype(jnp.bfloat16)
    dk_ref[0] = key_sum.astype(jnp.bfloat16)
    dv_ref[0] = value_sum.astype(jnp.bfloat16)


def attend_back(queries, keys, values, offsets, mixed, upstream, raised, inverse):
    count, length = queries.shape[:2]
    pairs = HEADS * HEAD // 128
    width = HEADS * HEAD

    def spec(offset):
        return pl.BlockSpec((1, length, 128), lambda s, p: (s, 0, offset * pairs + p))

    return pl.pallas_call(
        attend_back_kernel,
        grid=(count, pairs),
        in_specs=[spec(offset) for offset in offsets]
        + [
            spec(0),
            spec(0),
            pl.BlockSpec((1, 2, length, length), lambda s, p: (s, p, 0, 0)),
            pl.BlockSpec((1, 1, 2, length), lambda s, p: (s, p, 0, 0)),
        ],
        out_specs=[spec(0)] * 3,
        out_shape=[jax.ShapeDtypeStruct((count, length, width), jnp.bfloat16)] * 3,
        compiler_params=pltpu.CompilerParams(vmem_limit_bytes=56 * 2**20),
        cost_estimate=pl.CostEstimate(
            flops=8 * count * HEADS * length * length * 256,
            bytes_accessed=count * HEADS * length * length * 2,
            transcendentals=0,
        ),
        name="attend_back",
    )(queries, keys, values, mixed, upstream, raised, inverse)


SWAP = ((0, 1), (1, 0))


def tree_sum(blocks):
    place = lax.axis_index("dp")
    count = lax.axis_size("dp")
    steps = count.bit_length() - 1
    blocks = blocks.reshape((2,) * steps + blocks.shape[1:])
    for step in range(steps):
        bit = 1 << step
        mine = (place // bit) % 2
        axis = steps - 1 - step
        kept = lax.dynamic_index_in_dim(blocks, mine, axis, keepdims=False)
        sent = lax.dynamic_index_in_dim(blocks, 1 - mine, axis, keepdims=False)
        got = lax.ppermute(sent, "dp", [(i, i ^ bit) for i in range(count)])
        blocks = (kept.astype(jnp.float32) + got.astype(jnp.float32)).astype(jnp.bfloat16)
    got = lax.ppermute(blocks, "seq", SWAP)
    return blocks.astype(jnp.float32) + got.astype(jnp.float32)


def whole_sequences(
    targets,
    memory,
    row_kind,
    loss_mask,
    cotangent,
    norm_self_gain,
    norm_self_bias,
    self_input,
    self_query_bias,
    self_value_bias,
    self_output,
    self_output_bias,
    norm_cross_gain,
    norm_cross_bias,
    cross_query,
    cross_query_bias,
    cross_input,
    cross_value_bias,
    cross_output,
    cross_output_bias,
    norm_feed_gain,
    norm_feed_bias,
    feed_in,
    feed_in_bias,
    feed_out,
    feed_out_bias,
):
    micros, _, own, width = targets.shape
    held = micros // 2
    side = lax.axis_index("seq")
    query_scale = HEAD ** (-0.5)

    def take(rows):
        kept = lax.dynamic_slice_in_dim(rows, side * held, held, axis=0)
        sent = lax.dynamic_slice_in_dim(rows, (1 - side) * held, held, axis=0)
        got = lax.ppermute(sent, "seq", SWAP)
        return jnp.concatenate([kept[:, 0], got[:, 0]], axis=1)

    def give(rows, dtype):
        got = lax.ppermute(rows[:, own:].astype(jnp.bfloat16), "seq", SWAP).astype(dtype)
        kept = rows[:, :own].astype(dtype)
        first = jnp.where(side == 0, kept, got)
        second = jnp.where(side == 0, got, kept)
        return jnp.concatenate([first, second], axis=0)[:, None]

    inputs = take(targets).astype(jnp.float32)
    sources = take(memory)
    output_low = take(
        (cotangent.astype(jnp.float32) * loss_mask.astype(jnp.float32)[..., None]).astype(
            jnp.bfloat16
        )
    )
    kinds = lax.dynamic_slice_in_dim(row_kind[:, 0], side * held, held, axis=0)
    info = jnp.concatenate([side[None].astype(jnp.int32), kinds])

    first_normed = normed(inputs, norm_self_gain, norm_self_bias).astype(jnp.bfloat16)
    joint_bias = jnp.concatenate(
        [self_query_bias, jnp.zeros_like(self_query_bias), self_value_bias]
    )
    joint_scale = jnp.where(jnp.arange(3 * width) < width, query_scale, 1.0)
    joint = ((project_rows(first_normed, self_input) + joint_bias) * joint_scale).astype(
        jnp.bfloat16
    )
    self_mixed, self_raised, self_inverse = attend(info, joint, joint, joint, True, (0, 1, 2))
    after_self = inputs + project_rows(self_mixed, self_output) + self_output_bias
    second_normed = normed(after_self, norm_cross_gain, norm_cross_bias).astype(jnp.bfloat16)
    cross_queries = (
        (project_rows(second_normed, cross_query) + cross_query_bias) * query_scale
    ).astype(jnp.bfloat16)
    pair_bias = jnp.concatenate([jnp.zeros_like(cross_value_bias), cross_value_bias])
    cross_pairs = (project_rows(sources, cross_input) + pair_bias).astype(jnp.bfloat16)
    cross_mixed, cross_raised, cross_inverse = attend(
        info, cross_queries, cross_pairs, cross_pairs, False, (0, 0, 1)
    )
    after_cross = after_self + project_rows(cross_mixed, cross_output) + cross_output_bias
    third_normed = normed(after_cross, norm_feed_gain, norm_feed_bias).astype(jnp.bfloat16)
    activated, gelu_pullback = jax.vjp(
        gelu_exact, project_rows(third_normed, feed_in) + feed_in_bias
    )
    activated_low = activated.astype(jnp.bfloat16)
    result = (after_cross + project_rows(activated_low, feed_out) + feed_out_bias).astype(
        jnp.bfloat16
    )
    pieces = [None] * 21
    grad_output = output_low.astype(jnp.float32)
    pieces[19] = outer_sum(activated_low, output_low)
    pieces[20] = jnp.sum(grad_output, axis=(0, 1))
    grad_hidden = gelu_pullback(project_back(output_low, feed_out))[0]
    hidden_low = grad_hidden.astype(jnp.bfloat16)
    pieces[17] = outer_sum(third_normed, hidden_low)
    pieces[18] = jnp.sum(grad_hidden, axis=(0, 1))
    through_feed, pieces[15], pieces[16] = normed_back(
        after_cross, norm_feed_gain, norm_feed_bias, project_back(hidden_low, feed_in)
    )
    grad_cross = grad_output + through_feed
    cross_low = grad_cross.astype(jnp.bfloat16)
    pieces[13] = outer_sum(cross_mixed, cross_low)
    pieces[14] = jnp.sum(grad_cross, axis=(0, 1))
    cross_upstream = project_back(cross_low, cross_output).astype(jnp.bfloat16)
    scaled_cross, cross_key_grads, cross_value_grads = attend_back(
        cross_queries, cross_pairs, cross_pairs, (0, 0, 1), cross_mixed, cross_upstream,
        cross_raised, cross_inverse,
    )
    pair_grads = jnp.concatenate([cross_key_grads, cross_value_grads], axis=-1)
    pieces[12] = jnp.sum(cross_value_grads.astype(jnp.float32), axis=(0, 1))
    pieces[11] = outer_sum(sources, pair_grads)
    source_grad = project_back(pair_grads, cross_input)
    pieces[10] = jnp.sum(scaled_cross.astype(jnp.float32), axis=(0, 1))
    pieces[9] = outer_sum(second_normed, scaled_cross)
    through_cross, pieces[7], pieces[8] = normed_back(
        after_self, norm_cross_gain, norm_cross_bias, project_back(scaled_cross, cross_query)
    )
    grad_self = grad_cross + through_cross
    self_low = grad_self.astype(jnp.bfloat16)
    pieces[5] = outer_sum(self_mixed, self_low)
    pieces[6] = jnp.sum(grad_self, axis=(0, 1))
    self_upstream = project_back(self_low, self_output).astype(jnp.bfloat16)
    joint_grads = attend_back(
        joint, joint, joint, (0, 1, 2), self_mixed, self_upstream, self_raised, self_inverse
    )
    pieces[3] = jnp.sum(joint_grads[0].astype(jnp.float32), axis=(0, 1))
    pieces[4] = jnp.sum(joint_grads[2].astype(jnp.float32), axis=(0, 1))
    joint_low = jnp.concatenate(joint_grads, axis=-1)
    pieces[2] = outer_sum(first_normed, joint_low)
    through_first, pieces[0], pieces[1] = normed_back(
        inputs, norm_self_gain, norm_self_bias, project_back(joint_low, self_input)
    )
    input_grad = grad_self + through_first

    count = lax.axis_size("dp")
    final = [None] * 21
    small = []
    for index, piece in enumerate(pieces):
        if piece.ndim == 2:
            blocks = piece.astype(jnp.bfloat16).reshape(count, piece.shape[0] // count, -1)
            final[index] = tree_sum(blocks)
        else:
            small.append((index, piece.reshape(count, -1)))
    joined = tree_sum(jnp.concatenate([part for _, part in small], axis=1).astype(jnp.bfloat16))
    place = 0
    for index, part in small:
        final[index] = joined[place : place + part.shape[1]]
        place += part.shape[1]
    return (
        give(result, jnp.bfloat16),
        give(input_grad, jnp.float32),
        give(source_grad, jnp.float32),
    ) + tuple(final)


def solution(mesh):
    in_specs = (
        P(None, "dp", "seq", None),
        P(None, "dp", "seq", None),
        P(None, "dp"),
        P(None, "dp", "seq"),
        P(None, "dp", "seq", None),
        P(),
        P(),
        P(),
        P(),
        P(),
        P(),
        P(),
        P(),
        P(),
        P(),
        P(),
        P(),
        P(),
        P(),
        P(),
        P(),
        P(),
        P(),
        P(),
        P(),
        P(),
    )
    out_specs = (
        P(None, "dp", "seq", None),
        P(None, "dp", "seq", None),
        P(None, "dp", "seq", None),
        P("dp"),
        P("dp"),
        P("dp", None),
        P("dp"),
        P("dp"),
        P("dp", None),
        P("dp"),
        P("dp"),
        P("dp"),
        P("dp", None),
        P("dp"),
        P("dp", None),
        P("dp"),
        P("dp", None),
        P("dp"),
        P("dp"),
        P("dp"),
        P("dp", None),
        P("dp"),
        P("dp", None),
        P("dp"),
    )

    def on_device(*arguments):
        micros = arguments[0].shape[0]
        rows = lax.axis_size("dp")
        pairs = lax.axis_size("seq") == 2 and micros % 2 == 0
        whole = pairs and rows & (rows - 1) == 0
        return (whole_sequences if whole else split_sequences)(*arguments)

    return jax.shard_map(
        on_device, mesh=mesh, in_specs=in_specs, out_specs=out_specs, check_vma=False
    )
```

```python
import functools

import jax
import jax.numpy as jnp
from jax import lax
from jax.experimental import pallas as pl
from jax.experimental.pallas import tpu as pltpu
from jax.sharding import PartitionSpec as P

HEADS = 12
HEAD = 64


epsilon = 1e-05
blocked_score = -1e30


def normed(values, norm_gain, norm_shift):
    center = values - jnp.mean(values, axis=-1, keepdims=True)
    spread = jnp.mean(center * center, axis=-1, keepdims=True)
    return center * lax.rsqrt(spread + epsilon) * norm_gain + norm_shift


def normed_back(values, norm_gain, norm_shift, upstream):
    unused, pullback = jax.vjp(normed, values, norm_gain, norm_shift)
    return pullback(upstream)


def gelu_exact(values):
    return jax.nn.gelu(values, approximate=False)


def project_rows(row_block, weight):
    return jnp.einsum("bpd,de->bpe", row_block, weight, preferred_element_type=jnp.float32)


def project_back(row_block, weight):
    return jnp.einsum("bpe,de->bpd", row_block, weight, preferred_element_type=jnp.float32)


def outer_sum(first_rows, second_rows):
    return jnp.einsum("bpd,bpe->de", first_rows, second_rows, preferred_element_type=jnp.float32)


def split_heads(row_block):
    return row_block.reshape(row_block.shape[0], row_block.shape[1], HEADS, HEAD)


def masked_scores(queries, key_rows, allowed):
    scores = jnp.einsum(
        "bphe,bshe->bhps",
        split_heads(queries),
        split_heads(key_rows),
        preferred_element_type=jnp.float32,
    )
    if allowed is None:
        return scores
    return jnp.where(allowed[:, None], scores, blocked_score)


def attend_forward(queries, key_rows, values, allowed):
    scores = masked_scores(queries, key_rows, allowed)
    highest_score = jnp.max(scores, axis=-1, keepdims=True)
    raised = jnp.exp(scores - highest_score)
    totals = jnp.sum(raised, axis=-1, keepdims=True)
    weights = (raised / totals).astype(jnp.bfloat16)
    mixed = jnp.einsum(
        "bhps,bshe->bphe", weights, split_heads(values), preferred_element_type=jnp.float32
    )
    return (mixed.reshape(queries.shape).astype(jnp.bfloat16), highest_score + jnp.log(totals))


def attend_backward(queries, key_rows, values, allowed, log_totals, upstream):
    weights = jnp.exp(masked_scores(queries, key_rows, allowed) - log_totals)
    upstream_heads = split_heads(upstream)
    value_grads = jnp.einsum(
        "bhps,bphe->bshe",
        weights.astype(jnp.bfloat16),
        upstream_heads,
        preferred_element_type=jnp.float32,
    )
    weight_grads = jnp.einsum(
        "bphe,bshe->bhps", upstream_heads, split_heads(values), preferred_element_type=jnp.float32
    )
    score_grads = weights * (weight_grads - jnp.sum(weight_grads * weights, axis=-1, keepdims=True))
    score_low = score_grads.astype(jnp.bfloat16)
    query_grads = jnp.einsum(
        "bhps,bshe->bphe", score_low, split_heads(key_rows), preferred_element_type=jnp.float32
    ).reshape(queries.shape)
    key_grads = jnp.einsum(
        "bhps,bphe->bshe", score_low, split_heads(queries), preferred_element_type=jnp.float32
    ).reshape(key_rows.shape)
    return (query_grads, jnp.concatenate([key_grads, value_grads.reshape(key_rows.shape)], axis=-1))


def split_sequences(
    targets,
    memory,
    row_kind,
    loss_mask,
    cotangent,
    norm_self_gain,
    norm_self_bias,
    self_input,
    self_query_bias,
    self_value_bias,
    self_output,
    self_output_bias,
    norm_cross_gain,
    norm_cross_bias,
    cross_query,
    cross_query_bias,
    cross_input,
    cross_value_bias,
    cross_output,
    cross_output_bias,
    norm_feed_gain,
    norm_feed_bias,
    feed_in,
    feed_in_bias,
    feed_out,
    feed_out_bias,
):
    model_width = targets.shape[3]
    part_rows = targets.shape[2]
    key_span = part_rows * lax.axis_size("seq")
    query_scale = HEAD ** (-0.5)
    places = lax.axis_index("seq") * part_rows + jnp.arange(part_rows)
    causal = jnp.arange(key_span)[None, :] <= places[:, None]
    results, input_grads, source_grads = ([], [], [])
    totals = None
    for micro_index in range(targets.shape[0]):
        inputs = targets[micro_index].astype(jnp.float32)
        memory_local = memory[micro_index]
        allowed = causal[None] | (row_kind[micro_index] == 1)[:, None, None]
        first_normed = normed(inputs, norm_self_gain, norm_self_bias).astype(jnp.bfloat16)
        self_joint = project_rows(first_normed, self_input)
        queries = ((self_joint[..., :model_width] + self_query_bias) * query_scale).astype(
            jnp.bfloat16
        )
        own_pairs = jnp.concatenate(
            [
                self_joint[..., model_width : 2 * model_width],
                self_joint[..., 2 * model_width :] + self_value_bias,
            ],
            axis=-1,
        ).astype(jnp.bfloat16)
        gathered_self = lax.all_gather(own_pairs, "seq", axis=1, tiled=True)
        key_rows = gathered_self[..., :model_width]
        value_rows = gathered_self[..., model_width:]
        self_mixed, self_totals = attend_forward(queries, key_rows, value_rows, allowed)
        after_self = inputs + project_rows(self_mixed, self_output) + self_output_bias
        second_normed = normed(after_self, norm_cross_gain, norm_cross_bias).astype(jnp.bfloat16)
        cross_queries = (
            (project_rows(second_normed, cross_query) + cross_query_bias) * query_scale
        ).astype(jnp.bfloat16)
        joined = project_rows(lax.all_gather(memory_local, "seq", axis=1, tiled=True), cross_input)
        gathered_cross = jnp.concatenate(
            [joined[..., :model_width], joined[..., model_width:] + cross_value_bias], axis=-1
        ).astype(jnp.bfloat16)
        cross_keys = gathered_cross[..., :model_width]
        cross_values = gathered_cross[..., model_width:]
        cross_mixed, cross_totals = attend_forward(cross_queries, cross_keys, cross_values, None)
        after_cross = after_self + project_rows(cross_mixed, cross_output) + cross_output_bias
        third_normed = normed(after_cross, norm_feed_gain, norm_feed_bias).astype(jnp.bfloat16)
        activated, gelu_pullback = jax.vjp(
            gelu_exact, project_rows(third_normed, feed_in) + feed_in_bias
        )
        activated_low = activated.astype(jnp.bfloat16)
        results.append(
            (after_cross + project_rows(activated_low, feed_out) + feed_out_bias).astype(
                jnp.bfloat16
            )
        )
        pieces = [None] * 21
        grad_output = (
            cotangent[micro_index].astype(jnp.float32)
            * loss_mask[micro_index].astype(jnp.float32)[..., None]
        )
        output_low = grad_output.astype(jnp.bfloat16)
        pieces[19] = outer_sum(activated_low, output_low)
        pieces[20] = jnp.sum(grad_output, axis=(0, 1))
        grad_hidden = gelu_pullback(project_back(output_low, feed_out))[0]
        hidden_low = grad_hidden.astype(jnp.bfloat16)
        pieces[17] = outer_sum(third_normed, hidden_low)
        pieces[18] = jnp.sum(grad_hidden, axis=(0, 1))
        through_feed, pieces[15], pieces[16] = normed_back(
            after_cross, norm_feed_gain, norm_feed_bias, project_back(hidden_low, feed_in)
        )
        grad_cross = grad_output + through_feed
        cross_low = grad_cross.astype(jnp.bfloat16)
        pieces[13] = outer_sum(cross_mixed, cross_low)
        pieces[14] = jnp.sum(grad_cross, axis=(0, 1))
        cross_upstream = project_back(cross_low, cross_output).astype(jnp.bfloat16)
        cross_query_grads, cross_pair_grads = attend_backward(
            cross_queries, cross_keys, cross_values, None, cross_totals, cross_upstream
        )
        own_cross = lax.psum_scatter(
            cross_pair_grads.astype(jnp.bfloat16), "seq", scatter_dimension=1, tiled=True
        ).astype(jnp.float32)
        pieces[12] = jnp.sum(own_cross[..., model_width:], axis=(0, 1))
        own_cross_low = own_cross.astype(jnp.bfloat16)
        pieces[11] = outer_sum(memory_local, own_cross_low)
        source_grads.append(project_back(own_cross_low, cross_input))
        scaled_cross = cross_query_grads * query_scale
        pieces[10] = jnp.sum(scaled_cross, axis=(0, 1))
        scaled_cross_low = scaled_cross.astype(jnp.bfloat16)
        pieces[9] = outer_sum(second_normed, scaled_cross_low)
        through_cross, pieces[7], pieces[8] = normed_back(
            after_self,
            norm_cross_gain,
            norm_cross_bias,
            project_back(scaled_cross_low, cross_query),
        )
        grad_self = grad_cross + through_cross
        self_low = grad_self.astype(jnp.bfloat16)
        pieces[5] = outer_sum(self_mixed, self_low)
        pieces[6] = jnp.sum(grad_self, axis=(0, 1))
        self_upstream = project_back(self_low, self_output).astype(jnp.bfloat16)
        self_query_grads, self_pair_grads = attend_backward(
            queries, key_rows, value_rows, allowed, self_totals, self_upstream
        )
        own_self = lax.psum_scatter(
            self_pair_grads.astype(jnp.bfloat16), "seq", scatter_dimension=1, tiled=True
        ).astype(jnp.float32)
        scaled_self = self_query_grads * query_scale
        pieces[3] = jnp.sum(scaled_self, axis=(0, 1))
        pieces[4] = jnp.sum(own_self[..., model_width:], axis=(0, 1))
        joint_low = jnp.concatenate([scaled_self, own_self], axis=-1).astype(jnp.bfloat16)
        pieces[2] = outer_sum(first_normed, joint_low)
        through_first, pieces[0], pieces[1] = normed_back(
            inputs, norm_self_gain, norm_self_bias, project_back(joint_low, self_input)
        )
        input_grads.append(grad_self + through_first)
        totals = (
            pieces
            if totals is None
            else [running + added for running, added in zip(totals, pieces)]
        )
    def reduced(total):
        block = lax.psum_scatter(
            total.astype(jnp.bfloat16), "dp", scatter_dimension=0, tiled=True
        )
        return lax.psum(block, "seq").astype(jnp.float32)

    final = [reduced(total) for total in totals]
    return (jnp.stack(results), jnp.stack(input_grads), jnp.stack(source_grads)) + tuple(final)


def contract(first, second, first_dim, second_dim):
    return lax.dot_general(
        first, second, (((first_dim,), (second_dim,)), ((), ())), preferred_element_type=jnp.float32
    )


def head_masks(pair):
    lane = lax.broadcasted_iota(jnp.int32, (1, pair.shape[1]), 1)
    zero = jnp.zeros((), pair.dtype)
    return (jnp.where(lane < HEAD, pair, zero), jnp.where(lane < HEAD, zero, pair))


def attend_kernel(info_ref, q_ref, k_ref, v_ref, o_ref, e_ref, r_ref, *, block, use_mask):
    length = k_ref.shape[1]
    values_turned = v_ref[0].T
    ones = jnp.ones((16, length), jnp.bfloat16)
    own = length // 2
    causal = info_ref[1 + pl.program_id(0)] == 0 if use_mask else None

    def allowed(start):
        offset = info_ref[0] * own
        key_place = lax.broadcasted_iota(jnp.int32, (length, 1), 0) + offset
        key_place = jnp.where(key_place >= length, key_place - length, key_place)
        query_place = lax.broadcasted_iota(jnp.int32, (1, block), 1) + start + offset
        query_place = jnp.where(query_place >= length, query_place - length, query_place)
        return key_place <= query_place

    def run(masked, shifted):
        lowest, highest = None, None
        for start in range(0, length, block):
            mixed = []
            for head, queries in enumerate(head_masks(q_ref[0, start : start + block, :])):
                scores = contract(k_ref[0], queries, 1, 1)
                if masked and shifted:
                    scores = jnp.where(allowed(start), scores, blocked_score)
                if shifted:
                    scores = scores - jnp.max(scores, axis=0, keepdims=True)
                raised = jnp.exp(scores)
                if masked:
                    raised = jnp.where(allowed(start), raised, 0.0)
                low = raised.astype(jnp.bfloat16)
                e_ref[0, head, :, start : start + block] = low
                turned = jnp.concatenate(
                    [values_turned[head * HEAD : (head + 1) * HEAD], ones], axis=0
                )
                sums = contract(turned, low, 1, 0)
                total = sums[HEAD : HEAD + 1]
                if not shifted:
                    lowest = total if lowest is None else jnp.minimum(lowest, total)
                    highest = total if highest is None else jnp.maximum(highest, total)
                inverse = 1.0 / total
                r_ref[0, 0, head : head + 1, start : start + block] = inverse
                mixed.append(sums[:HEAD] * inverse)
            o_ref[0, start : start + block, :] = (
                jnp.concatenate(mixed, axis=0).T.astype(jnp.bfloat16)
            )
        if not shifted:
            in_range = (jnp.min(lowest) > 1e-20) & (jnp.max(highest) < 1e30)

            @pl.when(jnp.logical_not(in_range))
            def _():
                run(masked, True)

    if use_mask:

        @pl.when(causal)
        def _():
            run(True, False)

        @pl.when(jnp.logical_not(causal))
        def _():
            run(False, False)

    else:
        run(False, False)


def attend(info, queries, keys, values, use_mask, offsets):
    count, length = queries.shape[:2]
    pairs = HEADS * HEAD // 128
    width = HEADS * HEAD

    def spec(offset):
        return pl.BlockSpec((1, length, 128), lambda s, p, info: (s, 0, offset * pairs + p))

    return pl.pallas_call(
        functools.partial(attend_kernel, block=length // 2, use_mask=use_mask),
        grid_spec=pltpu.PrefetchScalarGridSpec(
            num_scalar_prefetch=1,
            grid=(count, pairs),
            in_specs=[spec(offset) for offset in offsets],
            out_specs=[
                spec(0),
                pl.BlockSpec((1, 2, length, length), lambda s, p, info: (s, p, 0, 0)),
                pl.BlockSpec((1, 1, 2, length), lambda s, p, info: (s, p, 0, 0)),
            ],
        ),
        out_shape=[
            jax.ShapeDtypeStruct((count, length, width), jnp.bfloat16),
            jax.ShapeDtypeStruct((count, HEADS, length, length), jnp.bfloat16),
            jax.ShapeDtypeStruct((count, pairs, 2, length), jnp.float32),
        ],
        compiler_params=pltpu.CompilerParams(vmem_limit_bytes=56 * 2**20),
        cost_estimate=pl.CostEstimate(
            flops=4 * count * HEADS * length * length * 256,
            bytes_accessed=count * HEADS * length * length * 2,
            transcendentals=count * HEADS * length * length,
        ),
        name="attend",
    )(info, queries, keys, values)


def attend_back_kernel(q_ref, k_ref, v_ref, o_ref, g_ref, e_ref, r_ref, dq_ref, dk_ref, dv_ref):
    length = k_ref.shape[1]
    keys_turned = k_ref[0].T
    upstream = g_ref[0].astype(jnp.float32)
    products = (o_ref[0].astype(jnp.float32) * upstream).T
    upstream = upstream.T
    parts, deltas = [], []
    for head in range(2):
        rows = slice(head * HEAD, (head + 1) * HEAD)
        inverse = r_ref[0, 0, head : head + 1, :]
        parts.append(upstream[rows] * inverse)
        deltas.append(jnp.sum(products[rows], axis=0, keepdims=True) * inverse)
    scaled = head_masks(jnp.concatenate(parts, axis=0).T.astype(jnp.bfloat16))
    queries = head_masks(q_ref[0])
    key_sum, value_sum, query_parts = 0.0, 0.0, []
    for head in range(2):
        rows = slice(head * HEAD, (head + 1) * HEAD)
        low = e_ref[0, head]
        grads = contract(v_ref[0], scaled[head], 1, 1)
        score_low = (low.astype(jnp.float32) * (grads - deltas[head])).astype(jnp.bfloat16)
        value_sum += contract(low, scaled[head], 1, 0)
        key_sum += contract(score_low, queries[head], 1, 0)
        query_parts.append(contract(keys_turned[rows], score_low, 1, 0))
    turned = jnp.concatenate(query_parts, axis=0) * (HEAD**-0.5)
    dq_ref[0] = turned.T.astype(jnp.bfloat16)
    dk_ref[0] = key_sum.astype(jnp.bfloat16)
    dv_ref[0] = value_sum.astype(jnp.bfloat16)


def attend_back(first, pairs_now, previous, queries, keys, values, offsets, *rest):
    count, length = queries.shape[:2]
    pairs = HEADS * HEAD // 128
    width = HEADS * HEAD

    def spec(offset):
        return pl.BlockSpec((1, length, 128), lambda s, p: (s, 0, offset * pairs + first + p))

    kernel = attend_back_kernel
    aliases = {}
    if previous:
        kernel = lambda *refs: attend_back_kernel(*refs[3:])
        aliases = {0: 0, 1: 1, 2: 2}
    return pl.pallas_call(
        kernel,
        grid=(count, pairs_now),
        in_specs=[pl.BlockSpec(memory_space=pl.ANY)] * len(previous)
        + [spec(offset) for offset in offsets]
        + [
            spec(0),
            spec(0),
            pl.BlockSpec((1, 2, length, length), lambda s, p: (s, first + p, 0, 0)),
            pl.BlockSpec((1, 1, 2, length), lambda s, p: (s, first + p, 0, 0)),
        ],
        out_specs=[spec(0)] * 3,
        out_shape=[jax.ShapeDtypeStruct((count, length, width), jnp.bfloat16)] * 3,
        input_output_aliases=aliases,
        compiler_params=pltpu.CompilerParams(vmem_limit_bytes=56 * 2**20),
        cost_estimate=pl.CostEstimate(
            flops=16 * count * pairs_now * length * length * 256,
            bytes_accessed=4 * count * pairs_now * length * length,
            transcendentals=0,
        ),
        name="attend_back",
    )(*previous, queries, keys, values, *rest)


def normal_parts(values):
    center = values - jnp.mean(values, axis=-1, keepdims=True)
    inverse = lax.rsqrt(jnp.mean(center * center, axis=-1, keepdims=True) + epsilon)
    return center * inverse, inverse


def normal_back(unit, inverse, norm_gain, upstream):
    inner = upstream * norm_gain
    shift = jnp.mean(inner, axis=-1, keepdims=True)
    tilt = jnp.mean(inner * unit, axis=-1, keepdims=True)
    return inverse * (inner - shift - unit * tilt)


def gelu_parts(values):
    size = jnp.abs(values)
    ratio = 1.0 / (1.0 + 0.2316418882663604 * size)
    series = 0.5307027145
    for weight in (-0.7265760135, 0.7107068705, -0.142248368, 0.127414796):
        series = series * ratio + weight
    bell = jnp.exp(-0.5 * values * values)
    upper = series * ratio * bell
    chance = jnp.where(values < 0, upper, 1.0 - upper)
    return values * chance, chance + values * (0.3989422804014327 * bell)


def column_sum(values):
    return jnp.sum(values, axis=0, keepdims=True)


def split_rows(core, rows, kept_ref, sent_ref):
    half = rows.shape[0] // 2
    low = rows.astype(jnp.bfloat16)

    @pl.when(core == 0)
    def _():
        kept_ref[0], sent_ref[0] = low[:half], low[half:]

    @pl.when(core != 0)
    def _():
        kept_ref[0], sent_ref[0] = low[half:], low[:half]


def feed_kernel(
    info_ref, x_ref, mixed_ref, dy_ref, wc_ref, wi_ref, wo_ref, vec_ref, bi_ref,
    out_ref, dx_ref, do_ref, vsum_ref, bsum_ref, ki_ref, si_ref, ko_ref, so_ref, kc_ref, sc_ref,
    ai_ref, ao_ref, ac_ref, *, steps, chunk,
):
    step = pl.program_id(0)

    @pl.when(step == 0)
    def _():
        for ref in (vsum_ref, bsum_ref, ai_ref, ao_ref, ac_ref):
            ref[...] = jnp.zeros_like(ref)

    @pl.when(step < steps)
    def _():
        cross_bias, gain, shift, out_bias = (vec_ref[i : i + 1, :] for i in range(4))
        mixed = mixed_ref[...]
        x2 = x_ref[...] + contract(mixed, wc_ref[...], 1, 0) + cross_bias
        unit, inverse = normal_parts(x2)
        normal = (unit * gain + shift).astype(jnp.bfloat16)
        normal_turned = normal.T
        dy = dy_ref[...]
        dy_turned = dy.T
        result, upstream = None, None
        for start in range(0, wi_ref.shape[1], chunk):
            part = slice(start, start + chunk)
            hidden = contract(normal, wi_ref[:, part], 1, 0) + bi_ref[:, part]
            active, slope = gelu_parts(hidden)
            active = active.astype(jnp.bfloat16)
            down = contract(active, wo_ref[part, :], 1, 0)
            result = down if result is None else result + down
            grads = contract(dy, wo_ref[part, :], 1, 1) * slope
            bsum_ref[:, part] += column_sum(grads)
            low = grads.astype(jnp.bfloat16)
            up = contract(low, wi_ref[:, part], 1, 1)
            upstream = up if upstream is None else upstream + up
            ao_ref[:, part] += contract(dy_turned, active, 1, 0)
            ai_ref[:, part] += contract(normal_turned, low, 1, 0)
        out_ref[...] = (x2 + result + out_bias).astype(jnp.bfloat16)
        wide = dy.astype(jnp.float32)
        dx = wide + normal_back(unit, inverse, gain, upstream)
        dx_ref[...] = dx
        dx_low = dx.astype(jnp.bfloat16)
        do_ref[...] = contract(dx_low, wc_ref[...], 1, 1).astype(jnp.bfloat16)
        ac_ref[...] += contract(mixed.T, dx_low, 1, 0)
        vsum_ref[0:1, :] += column_sum(dx)
        vsum_ref[1:2, :] += column_sum(upstream * unit)
        vsum_ref[2:3, :] += column_sum(upstream)
        vsum_ref[3:4, :] += column_sum(wide)

    @pl.when(step >= steps)
    def _():
        at = step - steps
        core = info_ref[0]
        rows = 2 * ki_ref.shape[1]
        split_rows(core, ai_ref[pl.ds(pl.multiple_of(at * rows, 16), rows), :], ki_ref, si_ref)
        split_rows(core, ac_ref[pl.ds(pl.multiple_of(at * rows, 16), rows), :], kc_ref, sc_ref)
        rows = 2 * ko_ref.shape[1]
        columns = ao_ref[:, pl.ds(pl.multiple_of(at * rows, 128), rows)]
        split_rows(core, columns.astype(jnp.bfloat16).T, ko_ref, so_ref)


def resident(array):
    return pl.BlockSpec(array.shape, lambda *_: (0,) * array.ndim, pipeline_mode=pl.Buffered(1))


def feed(info, x1, mixed, dy, wc, wi, wo, vectors, bi, parts, block=512, chunk=768):
    rows, width = x1.shape
    inner = wi.shape[1]
    steps = rows // block
    pairs = parts // 2
    row = lambda g, info: (jnp.minimum(g, steps - 1), 0)
    late = lambda g, info: (jnp.maximum(g - steps, 0), 0, 0)
    row_spec = pl.BlockSpec((block, width), row)
    fixed = lambda *_: (0, 0)

    def piece(high, wide):
        return (
            [pl.BlockSpec((1, high // parts, wide), late)] * 2,
            [jax.ShapeDtypeStruct((pairs, high // parts, wide), jnp.bfloat16)] * 2,
        )

    pieces = [piece(width, inner), piece(inner, width), piece(width, width)]
    return pl.pallas_call(
        functools.partial(feed_kernel, steps=steps, chunk=chunk),
        grid_spec=pltpu.PrefetchScalarGridSpec(
            num_scalar_prefetch=1,
            grid=(steps + pairs,),
            in_specs=[row_spec] * 3 + [resident(a) for a in (wc, wi, wo, vectors, bi)],
            out_specs=[row_spec] * 3
            + [pl.BlockSpec((8, width), fixed), pl.BlockSpec((1, inner), fixed)]
            + sum([p[0] for p in pieces], []),
            scratch_shapes=[
                pltpu.VMEM((width, inner), jnp.float32),
                pltpu.VMEM((width, inner), jnp.float32),
                pltpu.VMEM((width, width), jnp.float32),
            ],
        ),
        out_shape=[
            jax.ShapeDtypeStruct((rows, width), jnp.bfloat16),
            jax.ShapeDtypeStruct((rows, width), jnp.float32),
            jax.ShapeDtypeStruct((rows, width), jnp.bfloat16),
            jax.ShapeDtypeStruct((8, width), jnp.float32),
            jax.ShapeDtypeStruct((1, inner), jnp.float32),
        ]
        + sum([p[1] for p in pieces], []),
        compiler_params=pltpu.CompilerParams(vmem_limit_bytes=60 * 2**20),
        cost_estimate=pl.CostEstimate(
            flops=2 * rows * width * (6 * inner + 3 * width),
            bytes_accessed=60 * 2**20,
            transcendentals=rows * inner,
        ),
        name="feed",
    )(info, x1, mixed, dy, wc, wi, wo, vectors, bi)

SWAP = ((0, 1), (1, 0))


class Tree:
    def __init__(self, kept, sent, order):
        self.count = lax.axis_size("dp")
        self.bits = [1 << i for i in reversed(range(1, self.count.bit_length() - 1))]
        self.order = [bit for bit in order(self.bits)]
        shape = (2,) * len(self.bits) + kept.shape[1:]
        self.kept, self.sent, self.bit = kept.reshape(shape), sent.reshape(shape), 1
        self.got, self.total = None, None

    def exchange(self):
        if self.total is not None or self.got is not None:
            return
        if self.bit:
            pairs = [(i, i ^ self.bit) for i in range(self.count)]
            self.got = lax.ppermute(self.sent, "dp", pairs)
        else:
            self.got = lax.ppermute(self.kept, "seq", SWAP)

    def add(self):
        if self.got is None:
            return
        total = self.kept.astype(jnp.float32) + self.got.astype(jnp.float32)
        self.got = None
        if not self.bit:
            self.total = total
            return
        self.kept = total.astype(jnp.bfloat16)
        if not self.order:
            self.bit = 0
            return
        self.bit = self.order.pop(0)
        axis = self.bits.index(self.bit)
        self.bits.remove(self.bit)
        mine = (lax.axis_index("dp") // self.bit) % 2
        whole = self.kept
        self.kept = lax.dynamic_index_in_dim(whole, mine, axis, keepdims=False)
        self.sent = lax.dynamic_index_in_dim(whole, 1 - mine, axis, keepdims=False)


def low_first(bits):
    return bits[::-1]


def second_first(bits):
    turned = bits[::-1]
    return turned[1:2] + turned[:1] + turned[2:]


def tree_of(total, order):
    count = lax.axis_size("dp")
    blocks = total.astype(jnp.bfloat16).reshape((count // 2, 2, total.shape[0] // count, -1))
    core = lax.axis_index("dp") % 2
    return Tree(
        lax.dynamic_index_in_dim(blocks, core, 1, keepdims=False),
        lax.dynamic_index_in_dim(blocks, 1 - core, 1, keepdims=False),
        order,
    )


def exchange(trees):
    for tree in trees:
        tree.exchange()


def settle(trees, values):
    trees = [tree for tree in trees if tree.got is not None]
    gots, values = lax.optimization_barrier(([tree.got for tree in trees], values))
    for tree, got in zip(trees, gots):
        tree.got = got
        tree.add()
    return values


def finish(trees):
    while any(tree.total is None for tree in trees):
        exchange(trees)
        settle(trees, ())


def whole_sequences(
    targets,
    memory,
    row_kind,
    loss_mask,
    cotangent,
    norm_self_gain,
    norm_self_bias,
    self_input,
    self_query_bias,
    self_value_bias,
    self_output,
    self_output_bias,
    norm_cross_gain,
    norm_cross_bias,
    cross_query,
    cross_query_bias,
    cross_input,
    cross_value_bias,
    cross_output,
    cross_output_bias,
    norm_feed_gain,
    norm_feed_bias,
    feed_in,
    feed_in_bias,
    feed_out,
    feed_out_bias,
):
    micros, _, own, width = targets.shape
    held = micros // 2
    side = lax.axis_index("seq")
    query_scale = HEAD ** (-0.5)

    def take(rows):
        kept = lax.dynamic_slice_in_dim(rows, side * held, held, axis=0)
        sent = lax.dynamic_slice_in_dim(rows, (1 - side) * held, held, axis=0)
        got = lax.ppermute(sent, "seq", SWAP)
        return jnp.concatenate([kept[:, 0], got[:, 0]], axis=1)

    def give(rows, dtype):
        got = lax.ppermute(rows[:, own:].astype(jnp.bfloat16), "seq", SWAP).astype(dtype)
        kept = rows[:, :own].astype(dtype)
        first = jnp.where(side == 0, kept, got)
        second = jnp.where(side == 0, got, kept)
        return jnp.concatenate([first, second], axis=0)[:, None]

    inputs = take(targets).astype(jnp.float32)
    sources = take(memory)
    output_low = take(
        (cotangent.astype(jnp.float32) * loss_mask.astype(jnp.float32)[..., None]).astype(
            jnp.bfloat16
        )
    )
    kinds = lax.dynamic_slice_in_dim(row_kind[:, 0], side * held, held, axis=0)
    info = jnp.concatenate([side[None].astype(jnp.int32), kinds])

    first_normed = normed(inputs, norm_self_gain, norm_self_bias).astype(jnp.bfloat16)
    joint_bias = jnp.concatenate(
        [self_query_bias, jnp.zeros_like(self_query_bias), self_value_bias]
    )
    joint_scale = jnp.where(jnp.arange(3 * width) < width, query_scale, 1.0)
    joint = ((project_rows(first_normed, self_input) + joint_bias) * joint_scale).astype(
        jnp.bfloat16
    )
    self_mixed, self_raised, self_inverse = attend(info, joint, joint, joint, True, (0, 1, 2))
    after_self = inputs + project_rows(self_mixed, self_output) + self_output_bias
    second_normed = normed(after_self, norm_cross_gain, norm_cross_bias).astype(jnp.bfloat16)
    cross_queries = (
        (project_rows(second_normed, cross_query) + cross_query_bias) * query_scale
    ).astype(jnp.bfloat16)
    pair_bias = jnp.concatenate([jnp.zeros_like(cross_value_bias), cross_value_bias])
    cross_pairs = (project_rows(sources, cross_input) + pair_bias).astype(jnp.bfloat16)
    cross_mixed, cross_raised, cross_inverse = attend(
        info, cross_queries, cross_pairs, cross_pairs, False, (0, 0, 1)
    )
    vectors = jnp.concatenate(
        [
            jnp.stack([cross_output_bias, norm_feed_gain, norm_feed_bias, feed_out_bias]),
            jnp.zeros((4, width), jnp.float32),
        ]
    )
    flat = lambda rows: rows.reshape(-1, width)
    result, grad_cross, cross_upstream, vector_sums, hidden_sums, *feed_parts = feed(
        (lax.axis_index("dp") % 2)[None].astype(jnp.int32),
        flat(after_self),
        flat(cross_mixed),
        flat(output_low),
        cross_output,
        feed_in,
        feed_out,
        vectors,
        feed_in_bias[None],
        lax.axis_size("dp"),
    )
    result, grad_cross, cross_upstream = (
        rows.reshape(inputs.shape) for rows in (result, grad_cross, cross_upstream)
    )
    pieces = [None] * 21
    pieces[14], pieces[15], pieces[16], pieces[20] = vector_sums[:4]
    pieces[18] = hidden_sums[0]
    feed_trees = [
        Tree(*feed_parts[0:2], low_first),
        Tree(*feed_parts[2:4], second_first),
        Tree(*feed_parts[4:6], low_first),
    ]
    pairs = HEADS * HEAD // 128
    first = pairs // 2
    cross_inputs = (
        cross_queries, cross_pairs, cross_pairs, (0, 0, 1), cross_mixed, cross_upstream,
        cross_raised, cross_inverse,
    )
    exchange(feed_trees)
    half_grads = attend_back(0, first, (), *cross_inputs)
    half_grads = settle(feed_trees, half_grads)
    exchange(feed_trees)
    scaled_cross, cross_key_grads, cross_value_grads = settle(
        feed_trees, attend_back(first, pairs - first, half_grads, *cross_inputs)
    )
    exchange(feed_trees)
    pair_grads = jnp.concatenate([cross_key_grads, cross_value_grads], axis=-1)
    pieces[12] = jnp.sum(cross_value_grads.astype(jnp.float32), axis=(0, 1))
    pieces[11] = outer_sum(sources, pair_grads)
    source_grad = project_back(pair_grads, cross_input)
    pieces[10] = jnp.sum(scaled_cross.astype(jnp.float32), axis=(0, 1))
    pieces[9] = outer_sum(second_normed, scaled_cross)
    through_cross, pieces[7], pieces[8] = normed_back(
        after_self, norm_cross_gain, norm_cross_bias, project_back(scaled_cross, cross_query)
    )
    grad_self = grad_cross + through_cross
    self_low = grad_self.astype(jnp.bfloat16)
    pieces[5] = outer_sum(self_mixed, self_low)
    pieces[6] = jnp.sum(grad_self, axis=(0, 1))
    self_upstream = project_back(self_low, self_output).astype(jnp.bfloat16)
    pieces[5], pieces[9], pieces[11], self_upstream, source_grad = settle(
        feed_trees, (pieces[5], pieces[9], pieces[11], self_upstream, source_grad)
    )
    exchange(feed_trees)
    mid_trees = [
        tree_of(pieces[11], low_first),
        tree_of(pieces[9], second_first),
        tree_of(pieces[5], second_first),
    ]
    exchange(mid_trees)
    self_inputs = (
        joint, joint, joint, (0, 1, 2), self_mixed, self_upstream, self_raised, self_inverse
    )
    half_grads = settle(feed_trees + mid_trees, attend_back(0, first, (), *self_inputs))
    exchange(feed_trees + mid_trees)
    joint_grads = settle(
        feed_trees + mid_trees, attend_back(first, pairs - first, half_grads, *self_inputs)
    )
    exchange(mid_trees)
    pieces[3] = jnp.sum(joint_grads[0].astype(jnp.float32), axis=(0, 1))
    pieces[4] = jnp.sum(joint_grads[2].astype(jnp.float32), axis=(0, 1))
    joint_low = jnp.concatenate(joint_grads, axis=-1)
    pieces[2] = outer_sum(first_normed, joint_low)
    late_trees = [
        tree_of(pieces[2][:, : 3 * width // 2], low_first),
        tree_of(pieces[2][:, 3 * width // 2 :], second_first),
    ]
    exchange(late_trees)
    through_first, pieces[0], pieces[1] = normed_back(
        inputs, norm_self_gain, norm_self_bias, project_back(joint_low, self_input)
    )
    input_grad = grad_self + through_first
    count = lax.axis_size("dp")
    small = []
    for index, piece in enumerate(pieces):
        if piece is not None and piece.ndim == 1:
            small.append((index, piece.reshape(count, -1)))
    joined = jnp.concatenate([part for _, part in small], axis=1)
    late_trees.append(tree_of(joined, low_first))
    finish(feed_trees + mid_trees + late_trees[:2])
    finish(late_trees[2:])
    final = [None] * 21
    for index, tree in zip((17, 19, 13, 11, 9, 5), feed_trees + mid_trees):
        final[index] = tree.total
    final[2] = jnp.concatenate([late_trees[0].total, late_trees[1].total], axis=1)
    joined = late_trees[2].total
    place = 0
    for index, part in small:
        final[index] = joined[0, place : place + part.shape[1]]
        place += part.shape[1]
    return (
        give(result, jnp.bfloat16),
        give(input_grad, jnp.float32),
        give(source_grad, jnp.float32),
    ) + tuple(final)


def solution(mesh):
    in_specs = (
        P(None, "dp", "seq", None),
        P(None, "dp", "seq", None),
        P(None, "dp"),
        P(None, "dp", "seq"),
        P(None, "dp", "seq", None),
        P(),
        P(),
        P(),
        P(),
        P(),
        P(),
        P(),
        P(),
        P(),
        P(),
        P(),
        P(),
        P(),
        P(),
        P(),
        P(),
        P(),
        P(),
        P(),
        P(),
        P(),
    )
    out_specs = (
        P(None, "dp", "seq", None),
        P(None, "dp", "seq", None),
        P(None, "dp", "seq", None),
        P("dp"),
        P("dp"),
        P("dp", None),
        P("dp"),
        P("dp"),
        P("dp", None),
        P("dp"),
        P("dp"),
        P("dp"),
        P("dp", None),
        P("dp"),
        P("dp", None),
        P("dp"),
        P("dp", None),
        P("dp"),
        P("dp"),
        P("dp"),
        P("dp", None),
        P("dp"),
        P("dp", None),
        P("dp"),
    )

    def on_device(*arguments):
        micros = arguments[0].shape[0]
        rows = lax.axis_size("dp")
        pairs = lax.axis_size("seq") == 2 and micros % 2 == 0
        whole = pairs and rows & (rows - 1) == 0
        return (whole_sequences if whole else split_sequences)(*arguments)

    return jax.shard_map(
        on_device, mesh=mesh, in_specs=in_specs, out_specs=out_specs, check_vma=False
    )
```

```python
import functools

import jax
import jax.numpy as jnp
from jax import lax
from jax.experimental import pallas as pl
from jax.experimental.pallas import tpu as pltpu
from jax.sharding import PartitionSpec as P

HEADS = 12
HEAD = 64


epsilon = 1e-05
blocked_score = -1e30


def normed(values, norm_gain, norm_shift):
    center = values - jnp.mean(values, axis=-1, keepdims=True)
    spread = jnp.mean(center * center, axis=-1, keepdims=True)
    return center * lax.rsqrt(spread + epsilon) * norm_gain + norm_shift


def normed_back(values, norm_gain, norm_shift, upstream):
    unused, pullback = jax.vjp(normed, values, norm_gain, norm_shift)
    return pullback(upstream)


def gelu_exact(values):
    return jax.nn.gelu(values, approximate=False)


def project_rows(row_block, weight):
    return jnp.einsum("bpd,de->bpe", row_block, weight, preferred_element_type=jnp.float32)


def project_back(row_block, weight):
    return jnp.einsum("bpe,de->bpd", row_block, weight, preferred_element_type=jnp.float32)


def outer_sum(first_rows, second_rows):
    return jnp.einsum("bpd,bpe->de", first_rows, second_rows, preferred_element_type=jnp.float32)


def split_heads(row_block):
    return row_block.reshape(row_block.shape[0], row_block.shape[1], HEADS, HEAD)


def masked_scores(queries, key_rows, allowed):
    scores = jnp.einsum(
        "bphe,bshe->bhps",
        split_heads(queries),
        split_heads(key_rows),
        preferred_element_type=jnp.float32,
    )
    if allowed is None:
        return scores
    return jnp.where(allowed[:, None], scores, blocked_score)


def attend_forward(queries, key_rows, values, allowed):
    scores = masked_scores(queries, key_rows, allowed)
    highest_score = jnp.max(scores, axis=-1, keepdims=True)
    raised = jnp.exp(scores - highest_score)
    totals = jnp.sum(raised, axis=-1, keepdims=True)
    weights = (raised / totals).astype(jnp.bfloat16)
    mixed = jnp.einsum(
        "bhps,bshe->bphe", weights, split_heads(values), preferred_element_type=jnp.float32
    )
    return (mixed.reshape(queries.shape).astype(jnp.bfloat16), highest_score + jnp.log(totals))


def attend_backward(queries, key_rows, values, allowed, log_totals, upstream):
    weights = jnp.exp(masked_scores(queries, key_rows, allowed) - log_totals)
    upstream_heads = split_heads(upstream)
    value_grads = jnp.einsum(
        "bhps,bphe->bshe",
        weights.astype(jnp.bfloat16),
        upstream_heads,
        preferred_element_type=jnp.float32,
    )
    weight_grads = jnp.einsum(
        "bphe,bshe->bhps", upstream_heads, split_heads(values), preferred_element_type=jnp.float32
    )
    score_grads = weights * (weight_grads - jnp.sum(weight_grads * weights, axis=-1, keepdims=True))
    score_low = score_grads.astype(jnp.bfloat16)
    query_grads = jnp.einsum(
        "bhps,bshe->bphe", score_low, split_heads(key_rows), preferred_element_type=jnp.float32
    ).reshape(queries.shape)
    key_grads = jnp.einsum(
        "bhps,bphe->bshe", score_low, split_heads(queries), preferred_element_type=jnp.float32
    ).reshape(key_rows.shape)
    return (query_grads, jnp.concatenate([key_grads, value_grads.reshape(key_rows.shape)], axis=-1))


def split_sequences(
    targets,
    memory,
    row_kind,
    loss_mask,
    cotangent,
    norm_self_gain,
    norm_self_bias,
    self_input,
    self_query_bias,
    self_value_bias,
    self_output,
    self_output_bias,
    norm_cross_gain,
    norm_cross_bias,
    cross_query,
    cross_query_bias,
    cross_input,
    cross_value_bias,
    cross_output,
    cross_output_bias,
    norm_feed_gain,
    norm_feed_bias,
    feed_in,
    feed_in_bias,
    feed_out,
    feed_out_bias,
):
    model_width = targets.shape[3]
    part_rows = targets.shape[2]
    key_span = part_rows * lax.axis_size("seq")
    query_scale = HEAD ** (-0.5)
    places = lax.axis_index("seq") * part_rows + jnp.arange(part_rows)
    causal = jnp.arange(key_span)[None, :] <= places[:, None]
    results, input_grads, source_grads = ([], [], [])
    totals = None
    for micro_index in range(targets.shape[0]):
        inputs = targets[micro_index].astype(jnp.float32)
        memory_local = memory[micro_index]
        allowed = causal[None] | (row_kind[micro_index] == 1)[:, None, None]
        first_normed = normed(inputs, norm_self_gain, norm_self_bias).astype(jnp.bfloat16)
        self_joint = project_rows(first_normed, self_input)
        queries = ((self_joint[..., :model_width] + self_query_bias) * query_scale).astype(
            jnp.bfloat16
        )
        own_pairs = jnp.concatenate(
            [
                self_joint[..., model_width : 2 * model_width],
                self_joint[..., 2 * model_width :] + self_value_bias,
            ],
            axis=-1,
        ).astype(jnp.bfloat16)
        gathered_self = lax.all_gather(own_pairs, "seq", axis=1, tiled=True)
        key_rows = gathered_self[..., :model_width]
        value_rows = gathered_self[..., model_width:]
        self_mixed, self_totals = attend_forward(queries, key_rows, value_rows, allowed)
        after_self = inputs + project_rows(self_mixed, self_output) + self_output_bias
        second_normed = normed(after_self, norm_cross_gain, norm_cross_bias).astype(jnp.bfloat16)
        cross_queries = (
            (project_rows(second_normed, cross_query) + cross_query_bias) * query_scale
        ).astype(jnp.bfloat16)
        joined = project_rows(lax.all_gather(memory_local, "seq", axis=1, tiled=True), cross_input)
        gathered_cross = jnp.concatenate(
            [joined[..., :model_width], joined[..., model_width:] + cross_value_bias], axis=-1
        ).astype(jnp.bfloat16)
        cross_keys = gathered_cross[..., :model_width]
        cross_values = gathered_cross[..., model_width:]
        cross_mixed, cross_totals = attend_forward(cross_queries, cross_keys, cross_values, None)
        after_cross = after_self + project_rows(cross_mixed, cross_output) + cross_output_bias
        third_normed = normed(after_cross, norm_feed_gain, norm_feed_bias).astype(jnp.bfloat16)
        activated, gelu_pullback = jax.vjp(
            gelu_exact, project_rows(third_normed, feed_in) + feed_in_bias
        )
        activated_low = activated.astype(jnp.bfloat16)
        results.append(
            (after_cross + project_rows(activated_low, feed_out) + feed_out_bias).astype(
                jnp.bfloat16
            )
        )
        pieces = [None] * 21
        grad_output = (
            cotangent[micro_index].astype(jnp.float32)
            * loss_mask[micro_index].astype(jnp.float32)[..., None]
        )
        output_low = grad_output.astype(jnp.bfloat16)
        pieces[19] = outer_sum(activated_low, output_low)
        pieces[20] = jnp.sum(grad_output, axis=(0, 1))
        grad_hidden = gelu_pullback(project_back(output_low, feed_out))[0]
        hidden_low = grad_hidden.astype(jnp.bfloat16)
        pieces[17] = outer_sum(third_normed, hidden_low)
        pieces[18] = jnp.sum(grad_hidden, axis=(0, 1))
        through_feed, pieces[15], pieces[16] = normed_back(
            after_cross, norm_feed_gain, norm_feed_bias, project_back(hidden_low, feed_in)
        )
        grad_cross = grad_output + through_feed
        cross_low = grad_cross.astype(jnp.bfloat16)
        pieces[13] = outer_sum(cross_mixed, cross_low)
        pieces[14] = jnp.sum(grad_cross, axis=(0, 1))
        cross_upstream = project_back(cross_low, cross_output).astype(jnp.bfloat16)
        cross_query_grads, cross_pair_grads = attend_backward(
            cross_queries, cross_keys, cross_values, None, cross_totals, cross_upstream
        )
        own_cross = lax.psum_scatter(
            cross_pair_grads.astype(jnp.bfloat16), "seq", scatter_dimension=1, tiled=True
        ).astype(jnp.float32)
        pieces[12] = jnp.sum(own_cross[..., model_width:], axis=(0, 1))
        own_cross_low = own_cross.astype(jnp.bfloat16)
        pieces[11] = outer_sum(memory_local, own_cross_low)
        source_grads.append(project_back(own_cross_low, cross_input))
        scaled_cross = cross_query_grads * query_scale
        pieces[10] = jnp.sum(scaled_cross, axis=(0, 1))
        scaled_cross_low = scaled_cross.astype(jnp.bfloat16)
        pieces[9] = outer_sum(second_normed, scaled_cross_low)
        through_cross, pieces[7], pieces[8] = normed_back(
            after_self,
            norm_cross_gain,
            norm_cross_bias,
            project_back(scaled_cross_low, cross_query),
        )
        grad_self = grad_cross + through_cross
        self_low = grad_self.astype(jnp.bfloat16)
        pieces[5] = outer_sum(self_mixed, self_low)
        pieces[6] = jnp.sum(grad_self, axis=(0, 1))
        self_upstream = project_back(self_low, self_output).astype(jnp.bfloat16)
        self_query_grads, self_pair_grads = attend_backward(
            queries, key_rows, value_rows, allowed, self_totals, self_upstream
        )
        own_self = lax.psum_scatter(
            self_pair_grads.astype(jnp.bfloat16), "seq", scatter_dimension=1, tiled=True
        ).astype(jnp.float32)
        scaled_self = self_query_grads * query_scale
        pieces[3] = jnp.sum(scaled_self, axis=(0, 1))
        pieces[4] = jnp.sum(own_self[..., model_width:], axis=(0, 1))
        joint_low = jnp.concatenate([scaled_self, own_self], axis=-1).astype(jnp.bfloat16)
        pieces[2] = outer_sum(first_normed, joint_low)
        through_first, pieces[0], pieces[1] = normed_back(
            inputs, norm_self_gain, norm_self_bias, project_back(joint_low, self_input)
        )
        input_grads.append(grad_self + through_first)
        totals = (
            pieces
            if totals is None
            else [running + added for running, added in zip(totals, pieces)]
        )
    def reduced(total):
        block = lax.psum_scatter(
            total.astype(jnp.bfloat16), "dp", scatter_dimension=0, tiled=True
        )
        return lax.psum(block, "seq").astype(jnp.float32)

    final = [reduced(total) for total in totals]
    return (jnp.stack(results), jnp.stack(input_grads), jnp.stack(source_grads)) + tuple(final)


def contract(first, second, first_dim, second_dim):
    return lax.dot_general(
        first, second, (((first_dim,), (second_dim,)), ((), ())), preferred_element_type=jnp.float32
    )


def head_masks(pair):
    lane = lax.broadcasted_iota(jnp.int32, (1, pair.shape[1]), 1)
    zero = jnp.zeros((), pair.dtype)
    return (jnp.where(lane < HEAD, pair, zero), jnp.where(lane < HEAD, zero, pair))


ATTEND_LIMIT = 40 * 2**20


def attend_kernel(info_ref, q_ref, k_ref, v_ref, o_ref, e_ref, r_ref, *, use_mask):
    length = k_ref.shape[1]
    half = length // 2
    values_turned = v_ref[0].T
    ones = jnp.ones((16, length), jnp.bfloat16)
    side = info_ref[0]

    def run(masked, shifted, side_now=None):
        lowest, highest = None, None
        below = (
            lax.broadcasted_iota(jnp.int32, (half, 1), 0)
            <= lax.broadcasted_iota(jnp.int32, (1, half), 1)
            if masked
            else None
        )
        for at in range(2):
            queries_at = slice(at * half, (at + 1) * half)
            if masked:
                seen = [at] if at == side_now else [0, 1]
            else:
                seen = [None]
            mixed = []
            for head, queries in enumerate(head_masks(q_ref[0, queries_at, :])):
                tiles = []
                for key_at in seen:
                    rows = slice(0, length)
                    if key_at is not None:
                        rows = slice(key_at * half, (key_at + 1) * half)
                    scores = contract(k_ref[0, rows, :], queries, 1, 1)
                    if key_at == at:
                        scores = jnp.where(below, scores, blocked_score)
                    tiles.append((rows, scores))
                if shifted:
                    highest_score = functools.reduce(
                        jnp.maximum,
                        [jnp.max(scores, axis=0, keepdims=True) for _, scores in tiles],
                    )
                    tiles = [(rows, scores - highest_score) for rows, scores in tiles]
                sums = None
                for rows, scores in tiles:
                    low = jnp.exp(scores).astype(jnp.bfloat16)
                    e_ref[0, head, rows, queries_at] = low
                    turned = jnp.concatenate(
                        [values_turned[head * HEAD : (head + 1) * HEAD, rows], ones[:, rows]], axis=0
                    )
                    part = contract(turned, low, 1, 0)
                    sums = part if sums is None else sums + part
                if masked and len(seen) == 1:
                    other = slice((1 - at) * half, (2 - at) * half)
                    e_ref[0, head, other, queries_at] = jnp.zeros((half, half), jnp.bfloat16)
                total = sums[HEAD : HEAD + 1]
                if not shifted:
                    lowest = total if lowest is None else jnp.minimum(lowest, total)
                    highest = total if highest is None else jnp.maximum(highest, total)
                inverse = 1.0 / total
                r_ref[0, 0, head : head + 1, queries_at] = inverse
                mixed.append(sums[:HEAD] * inverse)
            o_ref[0, queries_at, :] = jnp.concatenate(mixed, axis=0).T.astype(jnp.bfloat16)
        if not shifted:
            in_range = (jnp.min(lowest) > 1e-20) & (jnp.max(highest) < 1e30)

            @pl.when(jnp.logical_not(in_range))
            def _():
                run(masked, True, side_now)

    if not use_mask:
        run(False, False)
        return
    causal = info_ref[2 + pl.program_id(0)] == 0
    for side_now in range(2):

        @pl.when(causal & (side == side_now))
        def _():
            run(True, False, side_now)

    @pl.when(jnp.logical_not(causal))
    def _():
        run(False, False)


def attend(info, queries, keys, values, use_mask, offsets):
    count, length = queries.shape[:2]
    pairs = HEADS * HEAD // 128
    width = HEADS * HEAD

    def spec(offset):
        return pl.BlockSpec((1, length, 128), lambda s, p, info: (s, 0, offset * pairs + p))

    return pl.pallas_call(
        functools.partial(attend_kernel, use_mask=use_mask),
        grid_spec=pltpu.PrefetchScalarGridSpec(
            num_scalar_prefetch=1,
            grid=(count, pairs),
            in_specs=[spec(offset) for offset in offsets],
            out_specs=[
                spec(0),
                pl.BlockSpec((1, 2, length, length), lambda s, p, info: (s, p, 0, 0)),
                pl.BlockSpec((1, 1, 2, length), lambda s, p, info: (s, p, 0, 0)),
            ],
        ),
        out_shape=[
            jax.ShapeDtypeStruct((count, length, width), jnp.bfloat16),
            jax.ShapeDtypeStruct((count, HEADS, length, length), jnp.bfloat16),
            jax.ShapeDtypeStruct((count, pairs, 2, length), jnp.float32),
        ],
        compiler_params=pltpu.CompilerParams(vmem_limit_bytes=ATTEND_LIMIT),
        cost_estimate=pl.CostEstimate(
            flops=4 * count * HEADS * length * length * 256,
            bytes_accessed=count * HEADS * length * length * 2,
            transcendentals=count * HEADS * length * length,
        ),
        name="attend",
    )(info, queries, keys, values)


def attend_back_kernel(q_ref, k_ref, v_ref, o_ref, g_ref, e_ref, r_ref, dq_ref, dk_ref, dv_ref):
    length = k_ref.shape[1]
    keys_turned = k_ref[0].T
    upstream = g_ref[0].astype(jnp.float32)
    products = (o_ref[0].astype(jnp.float32) * upstream).T
    upstream = upstream.T
    parts, deltas = [], []
    for head in range(2):
        rows = slice(head * HEAD, (head + 1) * HEAD)
        inverse = r_ref[0, 0, head : head + 1, :]
        parts.append(upstream[rows] * inverse)
        deltas.append(jnp.sum(products[rows], axis=0, keepdims=True) * inverse)
    scaled = head_masks(jnp.concatenate(parts, axis=0).T.astype(jnp.bfloat16))
    queries = head_masks(q_ref[0])
    key_sum, value_sum, query_parts = 0.0, 0.0, []
    for head in range(2):
        rows = slice(head * HEAD, (head + 1) * HEAD)
        low = e_ref[0, head]
        grads = contract(v_ref[0], scaled[head], 1, 1)
        score_low = (low.astype(jnp.float32) * (grads - deltas[head])).astype(jnp.bfloat16)
        value_sum += contract(low, scaled[head], 1, 0)
        key_sum += contract(score_low, queries[head], 1, 0)
        query_parts.append(contract(keys_turned[rows], score_low, 1, 0))
    turned = jnp.concatenate(query_parts, axis=0) * (HEAD**-0.5)
    dq_ref[0] = turned.T.astype(jnp.bfloat16)
    dk_ref[0] = key_sum.astype(jnp.bfloat16)
    dv_ref[0] = value_sum.astype(jnp.bfloat16)


def attend_back(place, size, previous, queries, keys, values, offsets, *rest):
    count, length = queries.shape[:2]
    pairs = HEADS * HEAD // 128
    width = HEADS * HEAD

    start, first = place

    def spec(offset):
        return pl.BlockSpec(
            (1, length, 128), lambda s, p: (start + s, 0, offset * pairs + first + p)
        )

    kernel = attend_back_kernel
    aliases = {}
    if previous:
        kernel = lambda *refs: attend_back_kernel(*refs[3:])
        aliases = {0: 0, 1: 1, 2: 2}
    return pl.pallas_call(
        kernel,
        grid=size,
        in_specs=[pl.BlockSpec(memory_space=pl.ANY)] * len(previous)
        + [spec(offset) for offset in offsets]
        + [
            spec(0),
            spec(0),
            pl.BlockSpec((1, 2, length, length), lambda s, p: (start + s, first + p, 0, 0)),
            pl.BlockSpec((1, 1, 2, length), lambda s, p: (start + s, first + p, 0, 0)),
        ],
        out_specs=[spec(0)] * 3,
        out_shape=[jax.ShapeDtypeStruct((count, length, width), jnp.bfloat16)] * 3,
        input_output_aliases=aliases,
        compiler_params=pltpu.CompilerParams(vmem_limit_bytes=ATTEND_LIMIT),
        cost_estimate=pl.CostEstimate(
            flops=16 * size[0] * size[1] * length * length * 256,
            bytes_accessed=4 * size[0] * size[1] * length * length,
            transcendentals=0,
        ),
        name="attend_back",
    )(*previous, queries, keys, values, *rest)


def normal_parts(values):
    center = values - jnp.mean(values, axis=-1, keepdims=True)
    inverse = lax.rsqrt(jnp.mean(center * center, axis=-1, keepdims=True) + epsilon)
    return center * inverse, inverse


def normal_back(unit, inverse, norm_gain, upstream):
    inner = upstream * norm_gain
    shift = jnp.mean(inner, axis=-1, keepdims=True)
    tilt = jnp.mean(inner * unit, axis=-1, keepdims=True)
    return inverse * (inner - shift - unit * tilt)


def gelu_parts(values):
    size = jnp.abs(values)
    ratio = 1.0 / (1.0 + 0.2316418882663604 * size)
    series = 0.5307027145
    for weight in (-0.7265760135, 0.7107068705, -0.142248368, 0.127414796):
        series = series * ratio + weight
    bell = jnp.exp(-0.5 * values * values)
    upper = series * ratio * bell
    chance = jnp.where(values < 0, upper, 1.0 - upper)
    return values * chance, chance + values * (0.3989422804014327 * bell)


def column_sum(values):
    return jnp.sum(values, axis=0, keepdims=True)


def resident(array):
    return pl.BlockSpec(array.shape, lambda *_: (0,) * array.ndim, pipeline_mode=pl.Buffered(1))


def whole_block(array):
    return pl.BlockSpec(array.shape, lambda *_: (0,) * len(array.shape))


def like(shape, dtype=jnp.float32):
    return jax.ShapeDtypeStruct(tuple(shape), dtype)


def pick(take_first, first_ref, second_ref):
    return lax.cond(take_first, lambda: first_ref[...], lambda: second_ref[...])


ONCE = {"pipeline_mode": pl.Buffered(1)}


def own_spec(own, width, held, last, **more):
    def place(step, info):
        return (info[0] * held + jnp.minimum(step, last) // 2, 0, 0)

    return pl.BlockSpec((None, own, width), place, **more)


def got_spec(own, width, last, **more):
    return pl.BlockSpec(
        (None, own, width), lambda step, info: (jnp.minimum(step, last) // 2, 0, 0), **more
    )


def row_spec(own, width, last, **more):
    return pl.BlockSpec((own, width), lambda step, info: (jnp.minimum(step, last), 0), **more)


def kernel_call(kernel, name, info, arrays, in_specs, outs, out_specs, grid, flops, moved, **more):
    scratch = more.pop("scratch", [])
    return pl.pallas_call(
        kernel,
        grid_spec=pltpu.PrefetchScalarGridSpec(
            num_scalar_prefetch=1,
            grid=(grid,),
            in_specs=in_specs,
            out_specs=out_specs,
            scratch_shapes=scratch,
        ),
        out_shape=outs,
        compiler_params=pltpu.CompilerParams(
            vmem_limit_bytes=more.pop("limit", 48) * 2**20
        ),
        cost_estimate=pl.CostEstimate(flops=flops, bytes_accessed=moved, transcendentals=0),
        name=name,
        **more,
    )(info, *arrays)


def enter_kernel(info_ref, own_ref, got_ref, w_ref, vec_ref, bias_ref, x_ref, out_ref, *, norm):
    x = pick(pl.program_id(0) % 2 == 0, own_ref, got_ref)
    x_ref[...] = x
    if norm:
        unit, _ = normal_parts(x.astype(jnp.float32))
        x = (unit * vec_ref[0:1, :] + vec_ref[1:2, :]).astype(jnp.bfloat16)
    width = x.shape[1]
    for start in range(0, w_ref.shape[1], width):
        part = slice(start, start + width)
        total = contract(x, w_ref[:, part], 1, 0) + bias_ref[:, part]
        if norm and start == 0:
            total = total * (HEAD**-0.5)
        out_ref[:, part] = total.astype(jnp.bfloat16)


def enter(info, owns, gots, weight, vectors, bias, norm):
    held, own, width = gots.shape
    rows = 2 * held * own
    last = 2 * held - 1
    wide = weight.shape[1]
    return kernel_call(
        functools.partial(enter_kernel, norm=norm),
        "enter",
        info,
        (owns, gots, weight, vectors, bias),
        [own_spec(own, width, held, last), got_spec(own, width, last)]
        + [resident(a) for a in (weight, vectors, bias)],
        [like((rows, width), jnp.bfloat16), like((rows, wide), jnp.bfloat16)],
        [row_spec(own, width, last), row_spec(own, wide, last)],
        2 * held,
        2 * rows * width * wide,
        2 * rows * (2 * width + wide),
    )


def middle_kernel(info_ref, x_ref, mixed_ref, wo_ref, wq_ref, vec_ref, after_ref, q_ref):
    out_bias, gain, shift, query_bias = (vec_ref[i : i + 1, :] for i in range(4))
    after = (
        x_ref[...].astype(jnp.float32) + contract(mixed_ref[...], wo_ref[...], 1, 0) + out_bias
    )
    after_ref[...] = after
    unit, _ = normal_parts(after)
    normal = (unit * gain + shift).astype(jnp.bfloat16)
    queries = (contract(normal, wq_ref[...], 1, 0) + query_bias) * (HEAD**-0.5)
    q_ref[...] = queries.astype(jnp.bfloat16)


def middle(info, x, mixed, wo, wq, vectors, own):
    rows, width = x.shape
    last = rows // own - 1
    spec = row_spec(own, width, last)
    return kernel_call(
        middle_kernel,
        "middle",
        info,
        (x, mixed, wo, wq, vectors),
        [spec, spec] + [resident(a) for a in (wo, wq, vectors)],
        [like((rows, width)), like((rows, width), jnp.bfloat16)],
        [spec, spec],
        rows // own,
        4 * rows * width * width,
        10 * rows * width,
    )


def write_split(core, rows, kept_ref, sent_ref, start):
    half = rows.shape[0] // 2
    low = rows.astype(jnp.bfloat16)
    place = slice(start, start + half)

    @pl.when(core == 0)
    def _():
        kept_ref[0, place, :] = low[:half]
        sent_ref[0, place, :] = low[half:]

    @pl.when(core != 0)
    def _():
        kept_ref[0, place, :] = low[half:]
        sent_ref[0, place, :] = low[:half]


def acc_rows(ref, at, rows):
    return ref[pl.ds(pl.multiple_of(at * rows, 16), rows), :]


def piece(parts, high, wide, steps):
    late = lambda g, info: (jnp.maximum(g - steps, 0), 0, 0)
    return (
        [pl.BlockSpec((1, high, wide), late)] * 2,
        [like((parts // 2, high, wide), jnp.bfloat16)] * 2,
    )


def put_rows(step, value, own_ref, got_ref):
    @pl.when(step % 2 == 0)
    def _():
        own_ref[...] = value.astype(own_ref.dtype)

    @pl.when(step % 2 != 0)
    def _():
        got_ref[...] = value.astype(got_ref.dtype)


def feed_kernel(
    info_ref, x_ref, mixed_ref, dyo_ref, dyg_ref, wc_ref, wi_ref, wo_ref, vec_ref, bi_ref,
    own_ref, got_ref, dx_ref, do_ref, vsum_ref, bsum_ref, ki_ref, si_ref, ko_ref, so_ref,
    ai_ref, ao_ref, ac_ref, *, steps, chunk, parts,
):
    step = pl.program_id(0)

    @pl.when(step == 0)
    def _():
        for ref in (vsum_ref, bsum_ref, ai_ref, ao_ref, ac_ref):
            ref[...] = jnp.zeros_like(ref)

    @pl.when(step < steps)
    def _():
        cross_bias, gain, shift, out_bias = (vec_ref[i : i + 1, :] for i in range(4))
        mixed = mixed_ref[...]
        x2 = x_ref[...] + contract(mixed, wc_ref[...], 1, 0) + cross_bias
        unit, inverse = normal_parts(x2)
        normal = (unit * gain + shift).astype(jnp.bfloat16)
        normal_turned = normal.T
        dy = pick(step % 2 == 0, dyo_ref, dyg_ref)
        dy_turned = dy.T
        result, upstream = None, None
        for start in range(0, wi_ref.shape[1], chunk):
            part = slice(start, start + chunk)
            hidden = contract(normal, wi_ref[:, part], 1, 0) + bi_ref[:, part]
            active, slope = gelu_parts(hidden)
            active = active.astype(jnp.bfloat16)
            down = contract(active, wo_ref[part, :], 1, 0)
            result = down if result is None else result + down
            grads = contract(dy, wo_ref[part, :], 1, 1) * slope
            bsum_ref[:, part] += column_sum(grads)
            low = grads.astype(jnp.bfloat16)
            up = contract(low, wi_ref[:, part], 1, 1)
            upstream = up if upstream is None else upstream + up
            ao_ref[:, part] += contract(dy_turned, active, 1, 0)
            ai_ref[:, part] += contract(normal_turned, low, 1, 0)
        put_rows(step, x2 + result + out_bias, own_ref, got_ref)
        wide = dy.astype(jnp.float32)
        dx = wide + normal_back(unit, inverse, gain, upstream)
        dx_ref[...] = dx
        dx_low = dx.astype(jnp.bfloat16)
        do_ref[...] = contract(dx_low, wc_ref[...], 1, 1).astype(jnp.bfloat16)
        ac_ref[...] += contract(mixed.T, dx_low, 1, 0)
        vsum_ref[0:1, :] += column_sum(dx)
        vsum_ref[1:2, :] += column_sum(upstream * unit)
        vsum_ref[2:3, :] += column_sum(upstream)
        vsum_ref[3:4, :] += column_sum(wide)

    @pl.when(step >= steps)
    def _():
        at = step - steps
        core = info_ref[1]
        rows = 2 * ki_ref.shape[1]
        inner = 2 * ai_ref.shape[1] // parts
        write_split(core, acc_rows(ai_ref, at, rows), ki_ref, si_ref, 0)
        columns = ao_ref[:, pl.ds(pl.multiple_of(at * inner, 128), inner)]
        write_split(core, columns.astype(jnp.bfloat16).T, ko_ref, so_ref, 0)
        write_split(core, acc_rows(ac_ref, at, rows), ko_ref, so_ref, inner // 2)


def feed(info, x1, mixed, dys, dy_gots, wc, wi, wo, vectors, bi, parts, chunk=768):
    rows, width = x1.shape
    held, own = dy_gots.shape[:2]
    micros = dys.shape[0]
    inner = wi.shape[1]
    steps = 2 * held
    last = steps - 1
    row = row_spec(own, width, last)
    pieces = [
        piece(parts, width // parts, inner, steps),
        piece(parts, (inner + width) // parts, width, steps),
    ]
    sums = [like((8, width)), like((1, inner))]
    return kernel_call(
        functools.partial(feed_kernel, steps=steps, chunk=chunk, parts=parts),
        "feed",
        info,
        (x1, mixed, dys, dy_gots, wc, wi, wo, vectors, bi),
        [row_spec(own, width, last, **ONCE)] * 2
        + [own_spec(own, width, held, last, **ONCE), got_spec(own, width, last, **ONCE)]
        + [resident(a) for a in (wc, wi, wo, vectors, bi)],
        [
            like((micros, own, width), jnp.bfloat16),
            like((held, own, width), jnp.bfloat16),
            like((rows, width)),
            like((rows, width), jnp.bfloat16),
        ]
        + sums
        + sum([p[1] for p in pieces], []),
        [own_spec(own, width, held, last), got_spec(own, width, last), row, row]
        + [whole_block(a) for a in sums]
        + sum([p[0] for p in pieces], []),
        steps + parts // 2,
        2 * rows * width * (6 * inner + 3 * width),
        60 * 2**20,
        scratch=[
            pltpu.VMEM((width, inner), jnp.float32),
            pltpu.VMEM((width, inner), jnp.float32),
            pltpu.VMEM((width, width), jnp.float32),
        ],
        limit=62,
    )


def return_kernel(
    info_ref, dq_ref, dk_ref, dv_ref, x_ref, dx_ref, mixed_ref, src_ref, wq_ref, wi_ref, wo_ref,
    vec_ref, own_ref, got_ref, dxo_ref, do_ref, vsum_ref, ka_ref, sa_ref, kb_ref, sb_ref,
    aq_ref, ao_ref, ai_ref, *, steps,
):
    step = pl.program_id(0)

    @pl.when(step == 0)
    def _():
        for ref in (vsum_ref, aq_ref, ao_ref, ai_ref):
            ref[...] = jnp.zeros_like(ref)

    @pl.when(step < steps)
    def _():
        width = x_ref.shape[1]
        gain, shift = vec_ref[0:1, :], vec_ref[1:2, :]
        dq, dk, dv = dq_ref[...], dk_ref[...], dv_ref[...]
        upstream = contract(dq, wq_ref[...], 1, 1)
        unit, inverse = normal_parts(x_ref[...])
        normal = (unit * gain + shift).astype(jnp.bfloat16)
        dx = dx_ref[...] + normal_back(unit, inverse, gain, upstream)
        dxo_ref[...] = dx
        low = dx.astype(jnp.bfloat16)
        do_ref[...] = contract(low, wo_ref[...], 1, 1).astype(jnp.bfloat16)
        source = contract(dk, wi_ref[:, :width], 1, 1) + contract(dv, wi_ref[:, width:], 1, 1)
        put_rows(step, source, own_ref, got_ref)
        aq_ref[...] += contract(normal.T, dq, 1, 0)
        ao_ref[...] += contract(mixed_ref[...].T, low, 1, 0)
        turned = src_ref[...].T
        ai_ref[:, :width] += contract(turned, dk, 1, 0)
        ai_ref[:, width:] += contract(turned, dv, 1, 0)
        vsum_ref[0:1, :] += column_sum(upstream * unit)
        vsum_ref[1:2, :] += column_sum(upstream)
        vsum_ref[2:3, :] += column_sum(dx)
        vsum_ref[3:4, :] += column_sum(dq.astype(jnp.float32))
        vsum_ref[4:5, :] += column_sum(dv.astype(jnp.float32))

    @pl.when(step >= steps)
    def _():
        at = step - steps
        core = info_ref[1]
        rows = 2 * ka_ref.shape[1]
        write_split(core, acc_rows(ai_ref, at, rows), ka_ref, sa_ref, 0)
        write_split(core, acc_rows(aq_ref, at, rows), kb_ref, sb_ref, 0)
        write_split(core, acc_rows(ao_ref, at, rows), kb_ref, sb_ref, rows // 2)


def return_rows(info, grads, x1, dx2, mixed, sources, wq, wi, wo, vectors, own, micros, parts):
    rows, width = x1.shape
    held = rows // own // 2
    steps = 2 * held
    last = steps - 1
    row = row_spec(own, width, last)
    pieces = [
        piece(parts, width // parts, 2 * width, steps),
        piece(parts, 2 * width // parts, width, steps),
    ]
    sums = like((8, width))
    return kernel_call(
        functools.partial(return_kernel, steps=steps),
        "return_rows",
        info,
        (*grads, x1, dx2, mixed, sources, wq, wi, wo, vectors),
        [row] * 7 + [resident(a) for a in (wq, wi, wo, vectors)],
        [
            like((micros, own, width)),
            like((held, own, width), jnp.bfloat16),
            like((rows, width)),
            like((rows, width), jnp.bfloat16),
            sums,
        ]
        + sum([p[1] for p in pieces], []),
        [own_spec(own, width, held, last), got_spec(own, width, last), row, row, whole_block(sums)]
        + sum([p[0] for p in pieces], []),
        steps + parts // 2,
        16 * rows * width * width,
        40 * 2**20,
        scratch=[
            pltpu.VMEM((width, width), jnp.float32),
            pltpu.VMEM((width, width), jnp.float32),
            pltpu.VMEM((width, 2 * width), jnp.float32),
        ],
        limit=56,
    )


def last_weight_kernel(
    info_ref, dq_ref, dk_ref, dv_ref, x_ref, vec_ref, ka_ref, sa_ref, kb_ref, sb_ref, acc_ref,
    *, steps,
):
    step = pl.program_id(0)

    @pl.when(step == 0)
    def _():
        acc_ref[...] = jnp.zeros_like(acc_ref)

    @pl.when(step < steps)
    def _():
        unit, _ = normal_parts(x_ref[...].astype(jnp.float32))
        turned = (unit * vec_ref[0:1, :] + vec_ref[1:2, :]).astype(jnp.bfloat16).T
        width = x_ref.shape[1]
        for at, ref in enumerate((dq_ref, dk_ref, dv_ref)):
            acc_ref[:, at * width : (at + 1) * width] += contract(turned, ref[...], 1, 0)

    @pl.when(step >= steps)
    def _():
        rows = acc_rows(acc_ref, step - steps, 2 * ka_ref.shape[1])
        half = ka_ref.shape[2]
        write_split(info_ref[1], rows[:, :half], ka_ref, sa_ref, 0)
        write_split(info_ref[1], rows[:, half:], kb_ref, sb_ref, 0)


def last_weight(info, grads, x, vectors, own, parts):
    rows, width = x.shape
    steps = rows // own
    row = row_spec(own, width, steps - 1)
    pieces = [piece(parts, width // parts, 3 * width // 2, steps)] * 2
    return kernel_call(
        functools.partial(last_weight_kernel, steps=steps),
        "last_weight",
        info,
        (*grads, x, vectors),
        [row] * 4 + [resident(vectors)],
        sum([p[1] for p in pieces], []),
        sum([p[0] for p in pieces], []),
        steps + parts // 2,
        6 * rows * width * width,
        20 * 2**20,
        scratch=[pltpu.VMEM((width, 3 * width), jnp.float32)],
    )


def leave_kernel(
    info_ref, dq_ref, dk_ref, dv_ref, x_ref, dx_ref, w_ref, vec_ref, *refs
):
    own_ref, got_ref, vsum_ref = refs[-3:]
    step = pl.program_id(0)

    @pl.when(step == 0)
    def _():
        vsum_ref[...] = jnp.zeros_like(vsum_ref)

    width = x_ref.shape[1]
    dq, dk, dv = dq_ref[...], dk_ref[...], dv_ref[...]
    upstream = (
        contract(dq, w_ref[:, :width], 1, 1)
        + contract(dk, w_ref[:, width : 2 * width], 1, 1)
        + contract(dv, w_ref[:, 2 * width :], 1, 1)
    )
    unit, inverse = normal_parts(x_ref[...].astype(jnp.float32))
    dx = dx_ref[...] + normal_back(unit, inverse, vec_ref[0:1, :], upstream)
    put_rows(step, dx, own_ref, got_ref)
    vsum_ref[0:1, :] += column_sum(upstream * unit)
    vsum_ref[1:2, :] += column_sum(upstream)
    vsum_ref[2:3, :] += column_sum(dq.astype(jnp.float32))
    vsum_ref[3:4, :] += column_sum(dv.astype(jnp.float32))


def leave(info, at, previous, grads, x, dx1, weight, vectors, own, micros):
    rows, width = x.shape
    held = rows // own // 2
    row = pl.BlockSpec((own, width), lambda step, info: (2 * at + step, 0))
    more = {"input_output_aliases": {8: 0}} if previous else {}
    sums = like((8, width))
    return kernel_call(
        leave_kernel,
        "leave",
        info,
        (*grads, x, dx1, weight, vectors, *previous),
        [row] * 5
        + [resident(a) for a in (weight, vectors)]
        + [pl.BlockSpec(memory_space=pl.ANY)] * len(previous),
        [like((micros, own, width)), like((own, width), jnp.bfloat16), sums],
        [
            pl.BlockSpec((None, own, width), lambda step, info: (info[0] * held + at, 0, 0)),
            pl.BlockSpec((own, width), lambda step, info: (0, 0)),
            whole_block(sums),
        ],
        2,
        12 * own * width * width,
        16 * 2**20,
        **more,
    )


SWAP = ((0, 1), (1, 0))


class Tree:
    def __init__(self, kept, sent, order):
        self.count = lax.axis_size("dp")
        self.bits = [1 << i for i in reversed(range(1, self.count.bit_length() - 1))]
        self.order = [bit for bit in order(self.bits)]
        shape = (2,) * len(self.bits) + kept.shape[1:]
        self.kept, self.sent, self.bit = kept.reshape(shape), sent.reshape(shape), 1
        self.got, self.total = None, None

    def exchange(self):
        if self.total is not None or self.got is not None:
            return
        if self.bit:
            pairs = [(i, i ^ self.bit) for i in range(self.count)]
            self.got = lax.ppermute(self.sent, "dp", pairs)
        else:
            self.got = lax.ppermute(self.kept, "seq", SWAP)

    def add(self):
        if self.got is None:
            return
        total = self.kept.astype(jnp.float32) + self.got.astype(jnp.float32)
        self.got = None
        if not self.bit:
            self.total = total
            return
        self.kept = total.astype(jnp.bfloat16)
        if not self.order:
            self.bit = 0
            return
        self.bit = self.order.pop(0)
        axis = self.bits.index(self.bit)
        self.bits.remove(self.bit)
        mine = (lax.axis_index("dp") // self.bit) % 2
        whole = self.kept
        self.kept = lax.dynamic_index_in_dim(whole, mine, axis, keepdims=False)
        self.sent = lax.dynamic_index_in_dim(whole, 1 - mine, axis, keepdims=False)


def low_first(bits):
    return bits[::-1]


def second_first(bits):
    turned = bits[::-1]
    return turned[1:2] + turned[:1] + turned[2:]


def exchange(trees):
    for tree in trees:
        tree.exchange()


def settle(trees, values):
    trees = [tree for tree in trees if tree.got is not None]
    gots, values = lax.optimization_barrier(([tree.got for tree in trees], values))
    for tree, got in zip(trees, gots):
        tree.got = got
        tree.add()
    return values


def finish(trees):
    while any(tree.total is None for tree in trees):
        exchange(trees)
        settle(trees, ())


def whole_sequences(
    targets,
    memory,
    row_kind,
    loss_mask,
    cotangent,
    norm_self_gain,
    norm_self_bias,
    self_input,
    self_query_bias,
    self_value_bias,
    self_output,
    self_output_bias,
    norm_cross_gain,
    norm_cross_bias,
    cross_query,
    cross_query_bias,
    cross_input,
    cross_value_bias,
    cross_output,
    cross_output_bias,
    norm_feed_gain,
    norm_feed_bias,
    feed_in,
    feed_in_bias,
    feed_out,
    feed_out_bias,
):
    micros, _, own, width = targets.shape
    held = micros // 2
    side = lax.axis_index("seq")
    parts = lax.axis_size("dp")
    place = lax.axis_index("dp")
    length = 2 * own
    pairs = HEADS * HEAD // 128

    def swap(rows):
        sent = lax.dynamic_slice_in_dim(rows, (1 - side) * held, held, axis=0)
        return lax.ppermute(sent, "seq", SWAP)

    def give(owns, got, at):
        got = lax.ppermute(got, "seq", SWAP).astype(owns.dtype)
        return lax.dynamic_update_slice_in_dim(owns, got, (1 - side) * held + at, axis=0)

    def pack(*rows):
        zero = jnp.zeros((8 - len(rows), width), jnp.float32)
        return jnp.concatenate([jnp.stack(rows), zero])

    def batch(rows):
        return rows.reshape(held, length, -1)

    def flat(rows):
        return rows.reshape(held * length, -1)

    targets, memory = targets[:, 0], memory[:, 0]
    target_gots = swap(targets)
    memory_gots = swap(memory)
    upstreams = (
        cotangent[:, 0].astype(jnp.float32) * loss_mask[:, 0].astype(jnp.float32)[..., None]
    ).astype(jnp.bfloat16)
    upstream_gots = swap(upstreams)
    kinds = lax.dynamic_slice_in_dim(row_kind[:, 0], side * held, held, axis=0)
    info = jnp.concatenate([jnp.stack([side, place % 2]).astype(jnp.int32), kinds])

    self_vectors = pack(norm_self_gain, norm_self_bias)
    zero = jnp.zeros_like(self_query_bias)
    joint_bias = jnp.concatenate([self_query_bias, zero, self_value_bias])[None]
    inputs, joint = enter(
        info, targets, target_gots, self_input, self_vectors, joint_bias, True
    )
    joint = batch(joint)
    self_mixed, self_raised, self_inverse = attend(info, joint, joint, joint, True, (0, 1, 2))
    after_self, cross_queries = middle(
        info,
        inputs,
        flat(self_mixed),
        self_output,
        cross_query,
        pack(self_output_bias, norm_cross_gain, norm_cross_bias, cross_query_bias),
        own,
    )
    pair_bias = jnp.concatenate([zero, cross_value_bias])[None]
    sources, cross_pairs = enter(
        info, memory, memory_gots, cross_input, self_vectors, pair_bias, False
    )
    cross_queries, cross_pairs = batch(cross_queries), batch(cross_pairs)
    cross_mixed, cross_raised, cross_inverse = attend(
        info, cross_queries, cross_pairs, cross_pairs, False, (0, 0, 1)
    )
    results, result_gots, grad_cross, cross_upstream, feed_sums, hidden_sums, *feed_parts = feed(
        info,
        after_self,
        flat(cross_mixed),
        upstreams,
        upstream_gots,
        cross_output,
        feed_in,
        feed_out,
        pack(cross_output_bias, norm_feed_gain, norm_feed_bias, feed_out_bias),
        feed_in_bias[None],
        parts,
    )
    feed_trees = [Tree(*feed_parts[0:2], low_first), Tree(*feed_parts[2:4], second_first)]
    first = pairs // 2
    cross_inputs = (
        cross_queries, cross_pairs, cross_pairs, (0, 0, 1), cross_mixed, batch(cross_upstream),
        cross_raised, cross_inverse,
    )
    exchange(feed_trees)
    half_grads = settle(feed_trees, attend_back((0, 0), (held, first), (), *cross_inputs))
    exchange(feed_trees)
    cross_grads = settle(
        feed_trees, attend_back((0, first), (held, pairs - first), half_grads, *cross_inputs)
    )
    exchange(feed_trees)
    source_grads, source_gots, grad_self, self_upstream, return_sums, *mid_parts = settle(
        feed_trees,
        return_rows(
            info,
            [flat(rows) for rows in cross_grads],
            after_self,
            grad_cross,
            flat(self_mixed),
            sources,
            cross_query,
            cross_input,
            self_output,
            pack(norm_cross_gain, norm_cross_bias),
            own,
            micros,
            parts,
        ),
    )
    mid_trees = [Tree(*mid_parts[0:2], low_first), Tree(*mid_parts[2:4], second_first)]
    exchange(feed_trees + mid_trees)
    self_inputs = (
        joint, joint, joint, (0, 1, 2), self_mixed, batch(self_upstream), self_raised, self_inverse
    )
    grads = settle(feed_trees + mid_trees, attend_back((0, 0), (1, pairs), (), *self_inputs))
    exchange(feed_trees + mid_trees)
    input_grads, leave_sums, leave_gots = (), [], []

    def leave_one(at, grads, input_grads):
        input_grads, got, sums = leave(
            info, at, input_grads, [flat(rows) for rows in grads], inputs, grad_self,
            self_input, self_vectors, own, micros,
        )
        leave_sums.append(sums)
        leave_gots.append(got[None])
        return (input_grads,)

    for at in range(held - 1):
        input_grads = leave_one(at, grads, input_grads)
        grads, input_grads = lax.optimization_barrier((grads, input_grads))
        grads = settle(
            feed_trees + mid_trees, attend_back((at + 1, 0), (1, pairs), grads, *self_inputs)
        )
        exchange(feed_trees + mid_trees)
    late_parts = last_weight(
        info, [flat(rows) for rows in grads], inputs, self_vectors, own, parts
    )
    late_trees = [Tree(*late_parts[0:2], low_first), Tree(*late_parts[2:4], second_first)]
    exchange(late_trees)
    grads, _ = lax.optimization_barrier((grads, late_parts[0]))
    (input_grads,) = leave_one(held - 1, grads, input_grads)
    leave_sums = sum(leave_sums)
    small = [
        (0, leave_sums[0]), (1, leave_sums[1]), (3, leave_sums[2]), (4, leave_sums[3]),
        (6, return_sums[2]), (7, return_sums[0]), (8, return_sums[1]), (10, return_sums[3]),
        (12, return_sums[4]), (14, feed_sums[0]), (15, feed_sums[1]), (16, feed_sums[2]),
        (20, feed_sums[3]), (18, hidden_sums[0]),
    ]
    joined = jnp.concatenate([row.reshape(parts, -1) for _, row in small], axis=1)
    halves = joined.astype(jnp.bfloat16).reshape(parts // 2, 2, 1, -1)
    small_tree = Tree(
        lax.dynamic_index_in_dim(halves, place % 2, 1, keepdims=False),
        lax.dynamic_index_in_dim(halves, 1 - place % 2, 1, keepdims=False),
        low_first,
    )
    finish(feed_trees + mid_trees + late_trees)
    finish([small_tree])
    rows = width // parts
    final = [None] * 21
    for index, row in small:
        size = row.shape[0] // parts
        final[index] = small_tree.total[0, :size]
        small_tree.total = small_tree.total[:, size:]
    inner_rows = feed_in.shape[1] // parts
    final[17] = feed_trees[0].total
    final[19] = feed_trees[1].total[:inner_rows]
    final[13] = feed_trees[1].total[inner_rows:]
    final[11] = mid_trees[0].total
    final[9] = mid_trees[1].total[:rows]
    final[5] = mid_trees[1].total[rows:]
    final[2] = jnp.concatenate([tree.total for tree in late_trees], axis=1)
    results = give(results, result_gots, 0)
    source_grads = give(source_grads, source_gots, 0)
    for at in range(held):
        input_grads = give(input_grads, leave_gots[at], at)
    return (results[:, None], input_grads[:, None], source_grads[:, None]) + tuple(final)


def solution(mesh):
    in_specs = (
        P(None, "dp", "seq", None),
        P(None, "dp", "seq", None),
        P(None, "dp"),
        P(None, "dp", "seq"),
        P(None, "dp", "seq", None),
        P(),
        P(),
        P(),
        P(),
        P(),
        P(),
        P(),
        P(),
        P(),
        P(),
        P(),
        P(),
        P(),
        P(),
        P(),
        P(),
        P(),
        P(),
        P(),
        P(),
        P(),
    )
    out_specs = (
        P(None, "dp", "seq", None),
        P(None, "dp", "seq", None),
        P(None, "dp", "seq", None),
        P("dp"),
        P("dp"),
        P("dp", None),
        P("dp"),
        P("dp"),
        P("dp", None),
        P("dp"),
        P("dp"),
        P("dp"),
        P("dp", None),
        P("dp"),
        P("dp", None),
        P("dp"),
        P("dp", None),
        P("dp"),
        P("dp"),
        P("dp"),
        P("dp", None),
        P("dp"),
        P("dp", None),
        P("dp"),
    )

    def on_device(*arguments):
        micros = arguments[0].shape[0]
        rows = lax.axis_size("dp")
        pairs = lax.axis_size("seq") == 2 and micros % 2 == 0
        whole = pairs and rows & (rows - 1) == 0
        return (whole_sequences if whole else split_sequences)(*arguments)

    return jax.shard_map(
        on_device, mesh=mesh, in_specs=in_specs, out_specs=out_specs, check_vma=False
    )
```

```python
import functools

import jax
import jax.numpy as jnp
from jax import lax
from jax.experimental import pallas as pl
from jax.experimental.pallas import tpu as pltpu
from jax.sharding import PartitionSpec as P

HEADS = 12
HEAD = 64


epsilon = 1e-05
blocked_score = -1e30


def normed(values, norm_gain, norm_shift):
    center = values - jnp.mean(values, axis=-1, keepdims=True)
    spread = jnp.mean(center * center, axis=-1, keepdims=True)
    return center * lax.rsqrt(spread + epsilon) * norm_gain + norm_shift


def normed_back(values, norm_gain, norm_shift, upstream):
    unused, pullback = jax.vjp(normed, values, norm_gain, norm_shift)
    return pullback(upstream)


def gelu_exact(values):
    return jax.nn.gelu(values, approximate=False)


def project_rows(row_block, weight):
    return jnp.einsum("bpd,de->bpe", row_block, weight, preferred_element_type=jnp.float32)


def project_back(row_block, weight):
    return jnp.einsum("bpe,de->bpd", row_block, weight, preferred_element_type=jnp.float32)


def outer_sum(first_rows, second_rows):
    return jnp.einsum("bpd,bpe->de", first_rows, second_rows, preferred_element_type=jnp.float32)


def split_heads(row_block):
    return row_block.reshape(row_block.shape[0], row_block.shape[1], HEADS, HEAD)


def masked_scores(queries, key_rows, allowed):
    scores = jnp.einsum(
        "bphe,bshe->bhps",
        split_heads(queries),
        split_heads(key_rows),
        preferred_element_type=jnp.float32,
    )
    if allowed is None:
        return scores
    return jnp.where(allowed[:, None], scores, blocked_score)


def attend_forward(queries, key_rows, values, allowed):
    scores = masked_scores(queries, key_rows, allowed)
    highest_score = jnp.max(scores, axis=-1, keepdims=True)
    raised = jnp.exp(scores - highest_score)
    totals = jnp.sum(raised, axis=-1, keepdims=True)
    weights = (raised / totals).astype(jnp.bfloat16)
    mixed = jnp.einsum(
        "bhps,bshe->bphe", weights, split_heads(values), preferred_element_type=jnp.float32
    )
    return (mixed.reshape(queries.shape).astype(jnp.bfloat16), highest_score + jnp.log(totals))


def attend_backward(queries, key_rows, values, allowed, log_totals, upstream):
    weights = jnp.exp(masked_scores(queries, key_rows, allowed) - log_totals)
    upstream_heads = split_heads(upstream)
    value_grads = jnp.einsum(
        "bhps,bphe->bshe",
        weights.astype(jnp.bfloat16),
        upstream_heads,
        preferred_element_type=jnp.float32,
    )
    weight_grads = jnp.einsum(
        "bphe,bshe->bhps", upstream_heads, split_heads(values), preferred_element_type=jnp.float32
    )
    score_grads = weights * (weight_grads - jnp.sum(weight_grads * weights, axis=-1, keepdims=True))
    score_low = score_grads.astype(jnp.bfloat16)
    query_grads = jnp.einsum(
        "bhps,bshe->bphe", score_low, split_heads(key_rows), preferred_element_type=jnp.float32
    ).reshape(queries.shape)
    key_grads = jnp.einsum(
        "bhps,bphe->bshe", score_low, split_heads(queries), preferred_element_type=jnp.float32
    ).reshape(key_rows.shape)
    return (query_grads, jnp.concatenate([key_grads, value_grads.reshape(key_rows.shape)], axis=-1))


def split_sequences(
    targets,
    memory,
    row_kind,
    loss_mask,
    cotangent,
    norm_self_gain,
    norm_self_bias,
    self_input,
    self_query_bias,
    self_value_bias,
    self_output,
    self_output_bias,
    norm_cross_gain,
    norm_cross_bias,
    cross_query,
    cross_query_bias,
    cross_input,
    cross_value_bias,
    cross_output,
    cross_output_bias,
    norm_feed_gain,
    norm_feed_bias,
    feed_in,
    feed_in_bias,
    feed_out,
    feed_out_bias,
):
    model_width = targets.shape[3]
    part_rows = targets.shape[2]
    key_span = part_rows * lax.axis_size("seq")
    query_scale = HEAD ** (-0.5)
    places = lax.axis_index("seq") * part_rows + jnp.arange(part_rows)
    causal = jnp.arange(key_span)[None, :] <= places[:, None]
    results, input_grads, source_grads = ([], [], [])
    totals = None
    for micro_index in range(targets.shape[0]):
        inputs = targets[micro_index].astype(jnp.float32)
        memory_local = memory[micro_index]
        allowed = causal[None] | (row_kind[micro_index] == 1)[:, None, None]
        first_normed = normed(inputs, norm_self_gain, norm_self_bias).astype(jnp.bfloat16)
        self_joint = project_rows(first_normed, self_input)
        queries = ((self_joint[..., :model_width] + self_query_bias) * query_scale).astype(
            jnp.bfloat16
        )
        own_pairs = jnp.concatenate(
            [
                self_joint[..., model_width : 2 * model_width],
                self_joint[..., 2 * model_width :] + self_value_bias,
            ],
            axis=-1,
        ).astype(jnp.bfloat16)
        gathered_self = lax.all_gather(own_pairs, "seq", axis=1, tiled=True)
        key_rows = gathered_self[..., :model_width]
        value_rows = gathered_self[..., model_width:]
        self_mixed, self_totals = attend_forward(queries, key_rows, value_rows, allowed)
        after_self = inputs + project_rows(self_mixed, self_output) + self_output_bias
        second_normed = normed(after_self, norm_cross_gain, norm_cross_bias).astype(jnp.bfloat16)
        cross_queries = (
            (project_rows(second_normed, cross_query) + cross_query_bias) * query_scale
        ).astype(jnp.bfloat16)
        joined = project_rows(lax.all_gather(memory_local, "seq", axis=1, tiled=True), cross_input)
        gathered_cross = jnp.concatenate(
            [joined[..., :model_width], joined[..., model_width:] + cross_value_bias], axis=-1
        ).astype(jnp.bfloat16)
        cross_keys = gathered_cross[..., :model_width]
        cross_values = gathered_cross[..., model_width:]
        cross_mixed, cross_totals = attend_forward(cross_queries, cross_keys, cross_values, None)
        after_cross = after_self + project_rows(cross_mixed, cross_output) + cross_output_bias
        third_normed = normed(after_cross, norm_feed_gain, norm_feed_bias).astype(jnp.bfloat16)
        activated, gelu_pullback = jax.vjp(
            gelu_exact, project_rows(third_normed, feed_in) + feed_in_bias
        )
        activated_low = activated.astype(jnp.bfloat16)
        results.append(
            (after_cross + project_rows(activated_low, feed_out) + feed_out_bias).astype(
                jnp.bfloat16
            )
        )
        pieces = [None] * 21
        grad_output = (
            cotangent[micro_index].astype(jnp.float32)
            * loss_mask[micro_index].astype(jnp.float32)[..., None]
        )
        output_low = grad_output.astype(jnp.bfloat16)
        pieces[19] = outer_sum(activated_low, output_low)
        pieces[20] = jnp.sum(grad_output, axis=(0, 1))
        grad_hidden = gelu_pullback(project_back(output_low, feed_out))[0]
        hidden_low = grad_hidden.astype(jnp.bfloat16)
        pieces[17] = outer_sum(third_normed, hidden_low)
        pieces[18] = jnp.sum(grad_hidden, axis=(0, 1))
        through_feed, pieces[15], pieces[16] = normed_back(
            after_cross, norm_feed_gain, norm_feed_bias, project_back(hidden_low, feed_in)
        )
        grad_cross = grad_output + through_feed
        cross_low = grad_cross.astype(jnp.bfloat16)
        pieces[13] = outer_sum(cross_mixed, cross_low)
        pieces[14] = jnp.sum(grad_cross, axis=(0, 1))
        cross_upstream = project_back(cross_low, cross_output).astype(jnp.bfloat16)
        cross_query_grads, cross_pair_grads = attend_backward(
            cross_queries, cross_keys, cross_values, None, cross_totals, cross_upstream
        )
        own_cross = lax.psum_scatter(
            cross_pair_grads.astype(jnp.bfloat16), "seq", scatter_dimension=1, tiled=True
        ).astype(jnp.float32)
        pieces[12] = jnp.sum(own_cross[..., model_width:], axis=(0, 1))
        own_cross_low = own_cross.astype(jnp.bfloat16)
        pieces[11] = outer_sum(memory_local, own_cross_low)
        source_grads.append(project_back(own_cross_low, cross_input))
        scaled_cross = cross_query_grads * query_scale
        pieces[10] = jnp.sum(scaled_cross, axis=(0, 1))
        scaled_cross_low = scaled_cross.astype(jnp.bfloat16)
        pieces[9] = outer_sum(second_normed, scaled_cross_low)
        through_cross, pieces[7], pieces[8] = normed_back(
            after_self,
            norm_cross_gain,
            norm_cross_bias,
            project_back(scaled_cross_low, cross_query),
        )
        grad_self = grad_cross + through_cross
        self_low = grad_self.astype(jnp.bfloat16)
        pieces[5] = outer_sum(self_mixed, self_low)
        pieces[6] = jnp.sum(grad_self, axis=(0, 1))
        self_upstream = project_back(self_low, self_output).astype(jnp.bfloat16)
        self_query_grads, self_pair_grads = attend_backward(
            queries, key_rows, value_rows, allowed, self_totals, self_upstream
        )
        own_self = lax.psum_scatter(
            self_pair_grads.astype(jnp.bfloat16), "seq", scatter_dimension=1, tiled=True
        ).astype(jnp.float32)
        scaled_self = self_query_grads * query_scale
        pieces[3] = jnp.sum(scaled_self, axis=(0, 1))
        pieces[4] = jnp.sum(own_self[..., model_width:], axis=(0, 1))
        joint_low = jnp.concatenate([scaled_self, own_self], axis=-1).astype(jnp.bfloat16)
        pieces[2] = outer_sum(first_normed, joint_low)
        through_first, pieces[0], pieces[1] = normed_back(
            inputs, norm_self_gain, norm_self_bias, project_back(joint_low, self_input)
        )
        input_grads.append(grad_self + through_first)
        totals = (
            pieces
            if totals is None
            else [running + added for running, added in zip(totals, pieces)]
        )
    def reduced(total):
        block = lax.psum_scatter(
            total.astype(jnp.bfloat16), "dp", scatter_dimension=0, tiled=True
        )
        return lax.psum(block, "seq").astype(jnp.float32)

    final = [reduced(total) for total in totals]
    return (jnp.stack(results), jnp.stack(input_grads), jnp.stack(source_grads)) + tuple(final)


def contract(first, second, first_dim, second_dim):
    return lax.dot_general(
        first, second, (((first_dim,), (second_dim,)), ((), ())), preferred_element_type=jnp.float32
    )


def head_masks(pair):
    lane = lax.broadcasted_iota(jnp.int32, (1, pair.shape[1]), 1)
    zero = jnp.zeros((), pair.dtype)
    return (jnp.where(lane < HEAD, pair, zero), jnp.where(lane < HEAD, zero, pair))


LIMIT = 62 * 2**20


def attend_kernel(info_ref, q_ref, k_ref, v_ref, *refs, use_mask, start):
    o_ref, e_ref, r_ref = refs[-3:]
    length = k_ref.shape[1]
    half = length // 2
    values_turned = v_ref[0].T
    ones = jnp.ones((16, length), jnp.bfloat16)
    side = info_ref[0]

    def run(masked, shifted, side_now=None):
        lowest, highest = None, None
        below = (
            lax.broadcasted_iota(jnp.int32, (half, 1), 0)
            <= lax.broadcasted_iota(jnp.int32, (1, half), 1)
            if masked
            else None
        )
        for at in range(2):
            queries_at = slice(at * half, (at + 1) * half)
            if masked:
                seen = [at] if at == side_now else [0, 1]
            else:
                seen = [None]
            mixed = []
            for head, queries in enumerate(head_masks(q_ref[0, queries_at, :])):
                tiles = []
                for key_at in seen:
                    rows = slice(0, length)
                    if key_at is not None:
                        rows = slice(key_at * half, (key_at + 1) * half)
                    scores = contract(k_ref[0, rows, :], queries, 1, 1)
                    if key_at == at:
                        scores = jnp.where(below, scores, blocked_score)
                    tiles.append((rows, scores))
                if shifted:
                    highest_score = functools.reduce(
                        jnp.maximum,
                        [jnp.max(scores, axis=0, keepdims=True) for _, scores in tiles],
                    )
                    tiles = [(rows, scores - highest_score) for rows, scores in tiles]
                sums = None
                for rows, scores in tiles:
                    low = jnp.exp(scores).astype(jnp.bfloat16)
                    e_ref[0, head, rows, queries_at] = low
                    turned = jnp.concatenate(
                        [values_turned[head * HEAD : (head + 1) * HEAD, rows], ones[:, rows]], axis=0
                    )
                    part = contract(turned, low, 1, 0)
                    sums = part if sums is None else sums + part
                if masked and len(seen) == 1:
                    other = slice((1 - at) * half, (2 - at) * half)
                    e_ref[0, head, other, queries_at] = jnp.zeros((half, half), jnp.bfloat16)
                total = sums[HEAD : HEAD + 1]
                if not shifted:
                    lowest = total if lowest is None else jnp.minimum(lowest, total)
                    highest = total if highest is None else jnp.maximum(highest, total)
                inverse = 1.0 / total
                r_ref[0, 0, head : head + 1, queries_at] = inverse
                mixed.append(sums[:HEAD] * inverse)
            o_ref[0, queries_at, :] = jnp.concatenate(mixed, axis=0).T.astype(jnp.bfloat16)
        if not shifted:
            in_range = (jnp.min(lowest) > 1e-20) & (jnp.max(highest) < 1e30)

            @pl.when(jnp.logical_not(in_range))
            def _():
                run(masked, True, side_now)

    if not use_mask:
        run(False, False)
        return
    causal = info_ref[2 + start + pl.program_id(0)] == 0
    for side_now in range(2):

        @pl.when(causal & (side == side_now))
        def _():
            run(True, False, side_now)

    @pl.when(jnp.logical_not(causal))
    def _():
        run(False, False)


def attend(info, start, count_now, previous, queries, keys, values, use_mask, offsets):
    count, length = queries.shape[:2]
    pairs = HEADS * HEAD // 128
    width = HEADS * HEAD

    def spec(offset):
        return pl.BlockSpec((1, length, 128), lambda s, p, info: (start + s, 0, offset * pairs + p))

    place = lambda s, p, info: (start + s, p, 0, 0)
    return pl.pallas_call(
        functools.partial(attend_kernel, use_mask=use_mask, start=start),
        grid_spec=pltpu.PrefetchScalarGridSpec(
            num_scalar_prefetch=1,
            grid=(count_now, pairs),
            in_specs=[spec(offset) for offset in offsets]
            + [pl.BlockSpec(memory_space=pl.ANY)] * len(previous),
            out_specs=[
                spec(0),
                pl.BlockSpec((1, 2, length, length), place),
                pl.BlockSpec((1, 1, 2, length), place),
            ],
        ),
        out_shape=[
            jax.ShapeDtypeStruct((count, length, width), jnp.bfloat16),
            jax.ShapeDtypeStruct((count, HEADS, length, length), jnp.bfloat16),
            jax.ShapeDtypeStruct((count, pairs, 2, length), jnp.float32),
        ],
        input_output_aliases={4: 0, 5: 1, 6: 2} if previous else {},
        compiler_params=pltpu.CompilerParams(vmem_limit_bytes=LIMIT),
        cost_estimate=pl.CostEstimate(
            flops=4 * count_now * HEADS * length * length * 256,
            bytes_accessed=count_now * HEADS * length * length * 2,
            transcendentals=count_now * HEADS * length * length,
        ),
        name="attend",
    )(info, queries, keys, values, *previous)


def attend_back_kernel(q_ref, k_ref, v_ref, o_ref, g_ref, e_ref, r_ref, dq_ref, dk_ref, dv_ref):
    length = k_ref.shape[1]
    keys_turned = k_ref[0].T
    upstream = g_ref[0].astype(jnp.float32)
    products = (o_ref[0].astype(jnp.float32) * upstream).T
    upstream = upstream.T
    parts, deltas = [], []
    for head in range(2):
        rows = slice(head * HEAD, (head + 1) * HEAD)
        inverse = r_ref[0, 0, head : head + 1, :]
        parts.append(upstream[rows] * inverse)
        deltas.append(jnp.sum(products[rows], axis=0, keepdims=True) * inverse)
    scaled = head_masks(jnp.concatenate(parts, axis=0).T.astype(jnp.bfloat16))
    queries = head_masks(q_ref[0])
    key_sum, value_sum, query_parts = 0.0, 0.0, []
    for head in range(2):
        rows = slice(head * HEAD, (head + 1) * HEAD)
        low = e_ref[0, head]
        grads = contract(v_ref[0], scaled[head], 1, 1)
        score_low = (low.astype(jnp.float32) * (grads - deltas[head])).astype(jnp.bfloat16)
        value_sum += contract(low, scaled[head], 1, 0)
        key_sum += contract(score_low, queries[head], 1, 0)
        query_parts.append(contract(keys_turned[rows], score_low, 1, 0))
    turned = jnp.concatenate(query_parts, axis=0) * (HEAD**-0.5)
    dq_ref[0] = turned.T.astype(jnp.bfloat16)
    dk_ref[0] = key_sum.astype(jnp.bfloat16)
    dv_ref[0] = value_sum.astype(jnp.bfloat16)


def attend_back(place, size, previous, queries, keys, values, offsets, *rest):
    count, length = queries.shape[:2]
    pairs = HEADS * HEAD // 128
    width = HEADS * HEAD

    start, first = place

    def spec(offset):
        return pl.BlockSpec(
            (1, length, 128), lambda s, p: (start + s, 0, offset * pairs + first + p)
        )

    kernel = attend_back_kernel
    aliases = {}
    if previous:
        kernel = lambda *refs: attend_back_kernel(*refs[3:])
        aliases = {0: 0, 1: 1, 2: 2}
    return pl.pallas_call(
        kernel,
        grid=size,
        in_specs=[pl.BlockSpec(memory_space=pl.ANY)] * len(previous)
        + [spec(offset) for offset in offsets]
        + [
            spec(0),
            spec(0),
            pl.BlockSpec((1, 2, length, length), lambda s, p: (start + s, first + p, 0, 0)),
            pl.BlockSpec((1, 1, 2, length), lambda s, p: (start + s, first + p, 0, 0)),
        ],
        out_specs=[spec(0)] * 3,
        out_shape=[jax.ShapeDtypeStruct((count, length, width), jnp.bfloat16)] * 3,
        input_output_aliases=aliases,
        compiler_params=pltpu.CompilerParams(vmem_limit_bytes=LIMIT),
        cost_estimate=pl.CostEstimate(
            flops=16 * size[0] * size[1] * length * length * 256,
            bytes_accessed=4 * size[0] * size[1] * length * length,
            transcendentals=0,
        ),
        name="attend_back",
    )(*previous, queries, keys, values, *rest)


def normal_parts(values):
    center = values - jnp.mean(values, axis=-1, keepdims=True)
    inverse = lax.rsqrt(jnp.mean(center * center, axis=-1, keepdims=True) + epsilon)
    return center * inverse, inverse


def normal_back(unit, inverse, norm_gain, upstream):
    inner = upstream * norm_gain
    shift = jnp.mean(inner, axis=-1, keepdims=True)
    tilt = jnp.mean(inner * unit, axis=-1, keepdims=True)
    return inverse * (inner - shift - unit * tilt)


def gelu_parts(values):
    size = jnp.abs(values)
    ratio = 1.0 / (1.0 + 0.2316418882663604 * size)
    series = 0.5307027145
    for weight in (-0.7265760135, 0.7107068705, -0.142248368, 0.127414796):
        series = series * ratio + weight
    bell = jnp.exp(-0.5 * values * values)
    upper = series * ratio * bell
    chance = jnp.where(values < 0, upper, 1.0 - upper)
    return values * chance, chance + values * (0.3989422804014327 * bell)


def column_sum(values):
    return jnp.sum(values, axis=0, keepdims=True)


def resident(array):
    return pl.BlockSpec(array.shape, lambda *_: (0,) * array.ndim, pipeline_mode=pl.Buffered(1))


def whole_block(array):
    return pl.BlockSpec(array.shape, lambda *_: (0,) * len(array.shape))


def like(shape, dtype=jnp.float32):
    return jax.ShapeDtypeStruct(tuple(shape), dtype)


def pick(take_first, first_ref, second_ref):
    return jnp.where(take_first, first_ref[...], second_ref[...])


ONCE = {"pipeline_mode": pl.Buffered(1)}


def own_spec(own, width, held, last, **more):
    def place(step, info):
        return (info[0] * held + jnp.minimum(step, last) // 2, 0, 0)

    return pl.BlockSpec((None, own, width), place, **more)


def got_spec(own, width, last, **more):
    return pl.BlockSpec(
        (None, own, width), lambda step, info: (jnp.minimum(step, last) // 2, 0, 0), **more
    )


def row_spec(own, width, last, **more):
    return pl.BlockSpec((own, width), lambda step, info: (jnp.minimum(step, last), 0), **more)


def kernel_call(kernel, name, info, arrays, in_specs, outs, out_specs, grid, flops, moved, **more):
    scratch = more.pop("scratch", [])
    return pl.pallas_call(
        kernel,
        grid_spec=pltpu.PrefetchScalarGridSpec(
            num_scalar_prefetch=1,
            grid=(grid,),
            in_specs=in_specs,
            out_specs=out_specs,
            scratch_shapes=scratch,
        ),
        out_shape=outs,
        compiler_params=pltpu.CompilerParams(
            vmem_limit_bytes=more.pop("limit", LIMIT)
        ),
        cost_estimate=pl.CostEstimate(flops=flops, bytes_accessed=moved, transcendentals=0),
        name=name,
        **more,
    )(info, *arrays)


def enter_kernel(info_ref, own_ref, got_ref, w_ref, vec_ref, bias_ref, *refs, norm):
    x_ref, out_ref = refs[-2:]
    x = pick(pl.program_id(0) % 2 == 0, own_ref, got_ref)
    x_ref[...] = x
    if norm:
        unit, _ = normal_parts(x.astype(jnp.float32))
        x = (unit * vec_ref[0:1, :] + vec_ref[1:2, :]).astype(jnp.bfloat16)
    width = x.shape[1]
    for start in range(0, w_ref.shape[1], width):
        part = slice(start, start + width)
        total = contract(x, w_ref[:, part], 1, 0) + bias_ref[:, part]
        if norm and start == 0:
            total = total * (HEAD**-0.5)
        out_ref[:, part] = total.astype(jnp.bfloat16)


def enter(info, at, previous, held, owns, gots, weight, vectors, bias, norm):
    count, own, width = gots.shape
    rows = 2 * held * own
    wide = weight.shape[1]
    own_rows = pl.BlockSpec(
        (None, own, width), lambda step, info: (info[0] * held + at + step // 2, 0, 0)
    )
    row = lambda step, info: (2 * at + step, 0)
    return kernel_call(
        functools.partial(enter_kernel, norm=norm),
        "enter",
        info,
        (owns, gots, weight, vectors, bias, *previous),
        [own_rows, got_spec(own, width, 2 * count - 1)]
        + [resident(a) for a in (weight, vectors, bias)]
        + [pl.BlockSpec(memory_space=pl.ANY)] * len(previous),
        [like((rows, width), jnp.bfloat16), like((rows, wide), jnp.bfloat16)],
        [pl.BlockSpec((own, width), row), pl.BlockSpec((own, wide), row)],
        2 * count,
        4 * count * own * width * wide,
        4 * count * own * (2 * width + wide),
        input_output_aliases={6: 0, 7: 1} if previous else {},
    )


def middle_kernel(info_ref, x_ref, mixed_ref, wo_ref, wq_ref, vec_ref, after_ref, q_ref):
    out_bias, gain, shift, query_bias = (vec_ref[i : i + 1, :] for i in range(4))
    after = (
        x_ref[...].astype(jnp.float32) + contract(mixed_ref[...], wo_ref[...], 1, 0) + out_bias
    )
    after_ref[...] = after
    unit, _ = normal_parts(after)
    normal = (unit * gain + shift).astype(jnp.bfloat16)
    queries = (contract(normal, wq_ref[...], 1, 0) + query_bias) * (HEAD**-0.5)
    q_ref[...] = queries.astype(jnp.bfloat16)


def middle(info, x, mixed, wo, wq, vectors, own):
    rows, width = x.shape
    last = rows // own - 1
    spec = row_spec(own, width, last)
    return kernel_call(
        middle_kernel,
        "middle",
        info,
        (x, mixed, wo, wq, vectors),
        [spec, spec] + [resident(a) for a in (wo, wq, vectors)],
        [like((rows, width)), like((rows, width), jnp.bfloat16)],
        [spec, spec],
        rows // own,
        4 * rows * width * width,
        10 * rows * width,
    )


def write_split(core, rows, kept_ref, sent_ref, start):
    half = rows.shape[0] // 2
    low = rows.astype(jnp.bfloat16)
    place = slice(start, start + half)

    @pl.when(core == 0)
    def _():
        kept_ref[0, place, :] = low[:half]
        sent_ref[0, place, :] = low[half:]

    @pl.when(core != 0)
    def _():
        kept_ref[0, place, :] = low[half:]
        sent_ref[0, place, :] = low[:half]


def write_wide(core, rows, kept_ref, sent_ref, start):
    half, width = rows.shape[0] // 2, kept_ref.shape[2]
    for at in range(rows.shape[1] // width):
        part = rows[:, at * width : (at + 1) * width]
        write_split(core, part, kept_ref, sent_ref, start + at * half)


def acc_rows(ref, at, rows):
    return ref[pl.ds(pl.multiple_of(at * rows, 16), rows), :]


def piece(parts, high, wide, steps, order):
    bits = parts.bit_length() - 2

    def late(step, info):
        at = jnp.maximum(step - steps, 0)
        place = 0
        for bit in order(bits):
            place = 2 * place + (at // 2**bit) % 2
        return (place, 0, 0)

    return (
        [pl.BlockSpec((1, high, wide), late)] * 2,
        [like((parts // 2, high, wide), jnp.bfloat16)] * 2,
    )


def low_first(bits):
    return list(range(bits))


def second_first(bits):
    return list(range(bits))[1:2] + [0] + list(range(2, bits))


def put_rows(step, value, own_ref, got_ref):
    @pl.when(step % 2 == 0)
    def _():
        own_ref[...] = value.astype(own_ref.dtype)

    @pl.when(step % 2 != 0)
    def _():
        got_ref[...] = value.astype(got_ref.dtype)


def feed_kernel(
    info_ref, x_ref, mixed_ref, dyo_ref, dyg_ref, wc_ref, wi_ref, wo_ref, vec_ref, bi_ref,
    own_ref, got_ref, dx_ref, do_ref, vsum_ref, bsum_ref, kept_ref, sent_ref, ai_ref, ao_ref,
    ac_ref, *, steps, chunk, parts,
):
    step = pl.program_id(0)

    @pl.when(step == 0)
    def _():
        for ref in (vsum_ref, bsum_ref, ai_ref, ao_ref, ac_ref):
            ref[...] = jnp.zeros_like(ref)

    @pl.when(step < steps)
    def _():
        cross_bias, gain, shift, out_bias = (vec_ref[i : i + 1, :] for i in range(4))
        mixed = mixed_ref[...]
        x2 = x_ref[...] + contract(mixed, wc_ref[...], 1, 0) + cross_bias
        unit, inverse = normal_parts(x2)
        normal = (unit * gain + shift).astype(jnp.bfloat16)
        normal_turned = normal.T
        dy = pick(step % 2 == 0, dyo_ref, dyg_ref)
        dy_turned = dy.T
        result, upstream = None, None
        for start in range(0, wi_ref.shape[1], chunk):
            part = slice(start, start + chunk)
            hidden = contract(normal, wi_ref[:, part], 1, 0) + bi_ref[:, part]
            active, slope = gelu_parts(hidden)
            active = active.astype(jnp.bfloat16)
            down = contract(active, wo_ref[part, :], 1, 0)
            result = down if result is None else result + down
            grads = contract(dy, wo_ref[part, :], 1, 1) * slope
            bsum_ref[:, part] += column_sum(grads)
            low = grads.astype(jnp.bfloat16)
            up = contract(low, wi_ref[:, part], 1, 1)
            upstream = up if upstream is None else upstream + up
            ao_ref[:, part] += contract(dy_turned, active, 1, 0)
            ai_ref[:, part] += contract(normal_turned, low, 1, 0)
        put_rows(step, x2 + result + out_bias, own_ref, got_ref)
        wide = dy.astype(jnp.float32)
        dx = wide + normal_back(unit, inverse, gain, upstream)
        dx_ref[...] = dx
        dx_low = dx.astype(jnp.bfloat16)
        do_ref[...] = contract(dx_low, wc_ref[...], 1, 1).astype(jnp.bfloat16)
        ac_ref[...] += contract(mixed.T, dx_low, 1, 0)
        vsum_ref[0:1, :] += column_sum(dx)
        vsum_ref[1:2, :] += column_sum(upstream * unit)
        vsum_ref[2:3, :] += column_sum(upstream)
        vsum_ref[3:4, :] += column_sum(wide)

    @pl.when(step >= steps)
    def _():
        at = step - steps
        core = info_ref[1]
        width, wide = ai_ref.shape
        rows = 2 * width // parts
        inner = 2 * wide // parts
        columns = ao_ref[:, pl.ds(pl.multiple_of(at * inner, 128), inner)]
        write_split(core, columns.astype(jnp.bfloat16).T, kept_ref, sent_ref, 0)
        write_split(core, acc_rows(ac_ref, at, rows), kept_ref, sent_ref, inner // 2)
        write_wide(core, acc_rows(ai_ref, at, rows), kept_ref, sent_ref, (inner + rows) // 2)


def feed(info, x1, mixed, dys, dy_gots, wc, wi, wo, vectors, bi, parts, chunk=768):
    rows, width = x1.shape
    held, own = dy_gots.shape[:2]
    micros = dys.shape[0]
    inner = wi.shape[1]
    steps = 2 * held
    last = steps - 1
    row = row_spec(own, width, last)
    pieces = [piece(parts, (2 * inner + width) // parts, width, steps, low_first)]
    sums = [like((8, width)), like((1, inner))]
    return kernel_call(
        functools.partial(feed_kernel, steps=steps, chunk=chunk, parts=parts),
        "feed",
        info,
        (x1, mixed, dys, dy_gots, wc, wi, wo, vectors, bi),
        [row_spec(own, width, last, **ONCE)] * 2
        + [own_spec(own, width, held, last, **ONCE), got_spec(own, width, last, **ONCE)]
        + [resident(a) for a in (wc, wi, wo, vectors, bi)],
        [
            like((micros, own, width), jnp.bfloat16),
            like((held, own, width), jnp.bfloat16),
            like((rows, width)),
            like((rows, width), jnp.bfloat16),
        ]
        + sums
        + sum([p[1] for p in pieces], []),
        [own_spec(own, width, held, last), got_spec(own, width, last), row, row]
        + [whole_block(a) for a in sums]
        + sum([p[0] for p in pieces], []),
        steps + parts // 2,
        2 * rows * width * (6 * inner + 3 * width),
        60 * 2**20,
        scratch=[
            pltpu.VMEM((width, inner), jnp.float32),
            pltpu.VMEM((width, inner), jnp.float32),
            pltpu.VMEM((width, width), jnp.float32),
        ],
        limit=LIMIT,
    )


def return_kernel(
    info_ref, dq_ref, dk_ref, dv_ref, x_ref, dx_ref, mixed_ref, src_ref, wq_ref, wi_ref, wo_ref,
    vec_ref, own_ref, got_ref, dxo_ref, do_ref, vsum_ref, kept_ref, sent_ref, aq_ref, ao_ref,
    ai_ref, *, steps, parts,
):
    step = pl.program_id(0)

    @pl.when(step == 0)
    def _():
        for ref in (vsum_ref, aq_ref, ao_ref, ai_ref):
            ref[...] = jnp.zeros_like(ref)

    @pl.when(step < steps)
    def _():
        width = x_ref.shape[1]
        gain, shift = vec_ref[0:1, :], vec_ref[1:2, :]
        dq, dk, dv = dq_ref[...], dk_ref[...], dv_ref[...]
        upstream = contract(dq, wq_ref[...], 1, 1)
        unit, inverse = normal_parts(x_ref[...])
        normal = (unit * gain + shift).astype(jnp.bfloat16)
        dx = dx_ref[...] + normal_back(unit, inverse, gain, upstream)
        dxo_ref[...] = dx
        low = dx.astype(jnp.bfloat16)
        do_ref[...] = contract(low, wo_ref[...], 1, 1).astype(jnp.bfloat16)
        source = contract(dk, wi_ref[:, :width], 1, 1) + contract(dv, wi_ref[:, width:], 1, 1)
        put_rows(step, source, own_ref, got_ref)
        aq_ref[...] += contract(normal.T, dq, 1, 0)
        ao_ref[...] += contract(mixed_ref[...].T, low, 1, 0)
        turned = src_ref[...].T
        ai_ref[:, :width] += contract(turned, dk, 1, 0)
        ai_ref[:, width:] += contract(turned, dv, 1, 0)
        vsum_ref[0:1, :] += column_sum(upstream * unit)
        vsum_ref[1:2, :] += column_sum(upstream)
        vsum_ref[2:3, :] += column_sum(dx)
        vsum_ref[3:4, :] += column_sum(dq.astype(jnp.float32))
        vsum_ref[4:5, :] += column_sum(dv.astype(jnp.float32))

    @pl.when(step >= steps)
    def _():
        at = step - steps
        core = info_ref[1]
        rows = 2 * aq_ref.shape[0] // parts
        write_split(core, acc_rows(aq_ref, at, rows), kept_ref, sent_ref, 0)
        write_split(core, acc_rows(ao_ref, at, rows), kept_ref, sent_ref, rows // 2)
        write_wide(core, acc_rows(ai_ref, at, rows), kept_ref, sent_ref, rows)


def return_rows(info, grads, x1, dx2, mixed, sources, wq, wi, wo, vectors, own, micros, parts):
    rows, width = x1.shape
    held = rows // own // 2
    steps = 2 * held
    last = steps - 1
    row = row_spec(own, width, last)
    pieces = [piece(parts, 4 * width // parts, width, steps, low_first)]
    sums = like((8, width))
    return kernel_call(
        functools.partial(return_kernel, steps=steps, parts=parts),
        "return_rows",
        info,
        (*grads, x1, dx2, mixed, sources, wq, wi, wo, vectors),
        [row] * 7 + [resident(a) for a in (wq, wi, wo, vectors)],
        [
            like((micros, own, width)),
            like((held, own, width), jnp.bfloat16),
            like((rows, width)),
            like((rows, width), jnp.bfloat16),
            sums,
        ]
        + sum([p[1] for p in pieces], []),
        [own_spec(own, width, held, last), got_spec(own, width, last), row, row, whole_block(sums)]
        + sum([p[0] for p in pieces], []),
        steps + parts // 2,
        16 * rows * width * width,
        40 * 2**20,
        scratch=[
            pltpu.VMEM((width, width), jnp.float32),
            pltpu.VMEM((width, width), jnp.float32),
            pltpu.VMEM((width, 2 * width), jnp.float32),
        ],
    )


def last_weight_kernel(
    info_ref, dq_ref, dk_ref, dv_ref, x_ref, vec_ref, ka_ref, sa_ref, kb_ref, sb_ref, acc_ref,
    *, steps,
):
    step = pl.program_id(0)

    @pl.when(step == 0)
    def _():
        acc_ref[...] = jnp.zeros_like(acc_ref)

    @pl.when(step < steps)
    def _():
        unit, _ = normal_parts(x_ref[...].astype(jnp.float32))
        turned = (unit * vec_ref[0:1, :] + vec_ref[1:2, :]).astype(jnp.bfloat16).T
        width = x_ref.shape[1]
        for at, ref in enumerate((dq_ref, dk_ref, dv_ref)):
            acc_ref[:, at * width : (at + 1) * width] += contract(turned, ref[...], 1, 0)

    @pl.when(step >= steps)
    def _():
        rows = acc_rows(acc_ref, step - steps, 2 * ka_ref.shape[1])
        half = ka_ref.shape[2]
        write_split(info_ref[1], rows[:, :half], ka_ref, sa_ref, 0)
        write_split(info_ref[1], rows[:, half:], kb_ref, sb_ref, 0)


def last_weight(info, grads, x, vectors, own, parts):
    rows, width = x.shape
    steps = rows // own
    row = row_spec(own, width, steps - 1)
    pieces = [
        piece(parts, width // parts, 3 * width // 2, steps, order)
        for order in (low_first, second_first)
    ]
    return kernel_call(
        functools.partial(last_weight_kernel, steps=steps),
        "last_weight",
        info,
        (*grads, x, vectors),
        [row] * 4 + [resident(vectors)],
        sum([p[1] for p in pieces], []),
        sum([p[0] for p in pieces], []),
        steps + parts // 2,
        6 * rows * width * width,
        20 * 2**20,
        scratch=[pltpu.VMEM((width, 3 * width), jnp.float32)],
    )


def leave_kernel(
    info_ref, dq_ref, dk_ref, dv_ref, x_ref, dx_ref, w_ref, vec_ref, *refs
):
    own_ref, got_ref, vsum_ref = refs[-3:]
    step = pl.program_id(0)

    @pl.when(step == 0)
    def _():
        vsum_ref[...] = jnp.zeros_like(vsum_ref)

    width = x_ref.shape[1]
    dq, dk, dv = dq_ref[...], dk_ref[...], dv_ref[...]
    upstream = (
        contract(dq, w_ref[:, :width], 1, 1)
        + contract(dk, w_ref[:, width : 2 * width], 1, 1)
        + contract(dv, w_ref[:, 2 * width :], 1, 1)
    )
    unit, inverse = normal_parts(x_ref[...].astype(jnp.float32))
    dx = dx_ref[...] + normal_back(unit, inverse, vec_ref[0:1, :], upstream)
    put_rows(step, dx, own_ref, got_ref)
    vsum_ref[0:1, :] += column_sum(upstream * unit)
    vsum_ref[1:2, :] += column_sum(upstream)
    vsum_ref[2:3, :] += column_sum(dq.astype(jnp.float32))
    vsum_ref[3:4, :] += column_sum(dv.astype(jnp.float32))


def leave(info, at, previous, grads, x, dx1, weight, vectors, own, micros):
    rows, width = x.shape
    held = rows // own // 2
    row = pl.BlockSpec((own, width), lambda step, info: (2 * at + step, 0))
    more = {"input_output_aliases": {8: 0}} if previous else {}
    sums = like((8, width))
    return kernel_call(
        leave_kernel,
        "leave",
        info,
        (*grads, x, dx1, weight, vectors, *previous),
        [row] * 5
        + [resident(a) for a in (weight, vectors)]
        + [pl.BlockSpec(memory_space=pl.ANY)] * len(previous),
        [like((micros, own, width)), like((own, width), jnp.bfloat16), sums],
        [
            pl.BlockSpec((None, own, width), lambda step, info: (info[0] * held + at, 0, 0)),
            pl.BlockSpec((own, width), lambda step, info: (0, 0)),
            whole_block(sums),
        ],
        2,
        12 * own * width * width,
        16 * 2**20,
        **more,
    )


SWAP = ((0, 1), (1, 0))


class Tree:
    def __init__(self, kept, sent, order):
        self.count = lax.axis_size("dp")
        bits = self.count.bit_length() - 2
        shape = (2,) * bits + kept.shape[1:]
        self.order = [2 << bit for bit in order(bits)]
        self.kept, self.sent, self.bit = kept.reshape(shape), sent.reshape(shape), 1
        self.got, self.total = None, None

    def exchange(self):
        if self.total is not None or self.got is not None:
            return
        if self.bit:
            pairs = [(i, i ^ self.bit) for i in range(self.count)]
            self.got = lax.ppermute(self.sent, "dp", pairs)
        else:
            self.got = lax.ppermute(self.kept, "seq", SWAP)

    def add(self):
        if self.got is None:
            return
        total = self.kept.astype(jnp.float32) + self.got.astype(jnp.float32)
        self.got = None
        if not self.bit:
            self.total = total
            return
        total = total.astype(jnp.bfloat16)
        if not self.order:
            self.bit, self.kept = 0, total
            return
        self.bit = self.order.pop(0)
        mine = (lax.axis_index("dp") // self.bit) % 2
        self.kept = lax.dynamic_index_in_dim(total, mine, 0, keepdims=False)
        self.sent = lax.dynamic_index_in_dim(total, 1 - mine, 0, keepdims=False)


class Whole:
    def __init__(self, rows):
        self.count = lax.axis_size("dp")
        self.rows, self.bit, self.got, self.total = rows, 1, None, None

    def exchange(self):
        if self.total is not None or self.got is not None:
            return
        if self.bit < self.count:
            pairs = [(i, i ^ self.bit) for i in range(self.count)]
            self.got = lax.ppermute(self.rows, "dp", pairs)
        else:
            self.got = lax.ppermute(self.rows, "seq", SWAP)

    def add(self):
        if self.got is None:
            return
        self.rows = self.rows + self.got
        self.got = None
        if self.bit == self.count:
            self.total = self.rows
        self.bit *= 2


def exchange(trees):
    for tree in trees:
        tree.exchange()


def settle(trees, values):
    trees = [tree for tree in trees if tree.got is not None]
    gots, values = lax.optimization_barrier(([tree.got for tree in trees], values))
    for tree, got in zip(trees, gots):
        tree.got = got
        tree.add()
    return values


def finish(trees):
    while any(tree.total is None for tree in trees):
        exchange(trees)
        settle(trees, ())


def whole_sequences(
    targets,
    memory,
    row_kind,
    loss_mask,
    cotangent,
    norm_self_gain,
    norm_self_bias,
    self_input,
    self_query_bias,
    self_value_bias,
    self_output,
    self_output_bias,
    norm_cross_gain,
    norm_cross_bias,
    cross_query,
    cross_query_bias,
    cross_input,
    cross_value_bias,
    cross_output,
    cross_output_bias,
    norm_feed_gain,
    norm_feed_bias,
    feed_in,
    feed_in_bias,
    feed_out,
    feed_out_bias,
):
    micros, _, own, width = targets.shape
    held = micros // 2
    side = lax.axis_index("seq")
    parts = lax.axis_size("dp")
    place = lax.axis_index("dp")
    length = 2 * own
    pairs = HEADS * HEAD // 128

    def swap(rows, at, count):
        sent = lax.dynamic_slice_in_dim(rows, (1 - side) * held + at, count, axis=0)
        return lax.ppermute(sent, "seq", SWAP)

    def give(owns, got, at):
        got = got.astype(owns.dtype)
        return lax.dynamic_update_slice_in_dim(owns, got, (1 - side) * held + at, axis=0)

    def pack(*rows):
        zero = jnp.zeros((8 - len(rows), width), jnp.float32)
        return jnp.concatenate([jnp.stack(rows), zero])

    def batch(rows):
        return rows.reshape(held, length, -1)

    def flat(rows):
        return rows.reshape(held * length, -1)

    targets, memory = targets[:, 0], memory[:, 0]
    target_gots = [swap(targets, at, 1) for at in range(held)]
    memory_gots = swap(memory, 0, held)
    upstreams = (
        cotangent[:, 0].astype(jnp.float32) * loss_mask[:, 0].astype(jnp.float32)[..., None]
    ).astype(jnp.bfloat16)
    upstream_gots = swap(upstreams, 0, held)
    kinds = lax.dynamic_slice_in_dim(row_kind[:, 0], side * held, held, axis=0)
    info = jnp.concatenate([jnp.stack([side, place % 2]).astype(jnp.int32), kinds])

    self_vectors = pack(norm_self_gain, norm_self_bias)
    zero = jnp.zeros_like(self_query_bias)
    joint_bias = jnp.concatenate([self_query_bias, zero, self_value_bias])[None]
    entered, attended = (), ()
    for at in range(held):
        entered = enter(
            info, at, entered, held, targets, target_gots[at], self_input, self_vectors,
            joint_bias, True,
        )
        joint = batch(entered[1])
        attended = attend(info, at, 1, attended, joint, joint, joint, True, (0, 1, 2))
        entered, attended = lax.optimization_barrier((entered, attended))
    inputs, joint = entered[0], batch(entered[1])
    self_mixed, self_raised, self_inverse = attended
    after_self, cross_queries = middle(
        info,
        inputs,
        flat(self_mixed),
        self_output,
        cross_query,
        pack(self_output_bias, norm_cross_gain, norm_cross_bias, cross_query_bias),
        own,
    )
    pair_bias = jnp.concatenate([zero, cross_value_bias])[None]
    sources, cross_pairs = enter(
        info, 0, (), held, memory, memory_gots, cross_input, self_vectors, pair_bias, False
    )
    cross_queries, cross_pairs = batch(cross_queries), batch(cross_pairs)
    cross_mixed, cross_raised, cross_inverse = attend(
        info, 0, held, (), cross_queries, cross_pairs, cross_pairs, False, (0, 0, 1)
    )
    results, result_gots, grad_cross, cross_upstream, feed_sums, hidden_sums, *feed_parts = feed(
        info,
        after_self,
        flat(cross_mixed),
        upstreams,
        upstream_gots,
        cross_output,
        feed_in,
        feed_out,
        pack(cross_output_bias, norm_feed_gain, norm_feed_bias, feed_out_bias),
        feed_in_bias[None],
        parts,
    )
    feed_trees = [Tree(*feed_parts, low_first)]
    first = pairs // 2
    cross_inputs = (
        cross_queries, cross_pairs, cross_pairs, (0, 0, 1), cross_mixed, batch(cross_upstream),
        cross_raised, cross_inverse,
    )
    exchange(feed_trees)
    result_gots = lax.ppermute(result_gots, "seq", SWAP)
    half_grads, result_gots = settle(
        feed_trees, (attend_back((0, 0), (held, first), (), *cross_inputs), result_gots)
    )
    exchange(feed_trees)
    cross_grads = attend_back((0, first), (held, pairs - first), half_grads, *cross_inputs)
    source_grads, source_gots, grad_self, self_upstream, return_sums, *mid_parts = settle(
        feed_trees,
        return_rows(
            info,
            [flat(rows) for rows in cross_grads],
            after_self,
            grad_cross,
            flat(self_mixed),
            sources,
            cross_query,
            cross_input,
            self_output,
            pack(norm_cross_gain, norm_cross_bias),
            own,
            micros,
            parts,
        ),
    )
    early_sums = Whole(
        jnp.concatenate([feed_sums, return_sums, hidden_sums.reshape(-1, width)], axis=0)
    )
    mid_trees = [Tree(*mid_parts, low_first), early_sums]
    exchange(feed_trees + mid_trees)
    self_inputs = (
        joint, joint, joint, (0, 1, 2), self_mixed, batch(self_upstream), self_raised, self_inverse
    )
    source_gots = lax.ppermute(source_gots, "seq", SWAP)
    grads, source_gots = settle(
        feed_trees + mid_trees,
        (attend_back((0, 0), (1, pairs), (), *self_inputs), source_gots),
    )
    exchange(feed_trees + mid_trees)
    kept, leave_sums = (), []
    trees = feed_trees + mid_trees
    for at in range(held):
        if at == held - 1:
            late_parts = last_weight(
                info, [flat(rows) for rows in grads], inputs, self_vectors, own, parts
            )
            late_trees = [
                Tree(*late_parts[0:2], low_first),
                Tree(*late_parts[2:4], second_first),
            ]
            trees = trees + late_trees
            exchange(trees)
            grads, _ = lax.optimization_barrier((grads, late_parts[0]))
        kept, got, sums = leave(
            info, at, kept, [flat(rows) for rows in grads], inputs, grad_self,
            self_input, self_vectors, own, micros,
        )
        leave_sums.append(sums)
        if at < held - 1:
            grads, kept = lax.optimization_barrier((grads, kept))
            back = lax.ppermute(got, "seq", SWAP)
            grads, back = settle(
                trees,
                (attend_back((at + 1, 0), (1, pairs), grads, *self_inputs), back),
            )
            exchange(trees)
            back = back.astype(kept.dtype)[None]
            kept = (
                lax.dynamic_update_slice_in_dim(kept, back, (1 - side) * held + at, axis=0),
            )
    input_grads, got, sums = settle(trees, (kept, got, sum(leave_sums)))
    late_sums = Whole(sums)
    trees = trees + [late_sums]
    exchange(trees)
    back = lax.ppermute(got, "seq", SWAP)
    settle(trees, ())
    exchange(trees)
    back = settle(trees, back)
    exchange(trees)
    input_grads = give(input_grads, back[None], held - 1)
    finish(trees)
    rows = width // parts
    inner_rows = feed_in.shape[1] // parts
    final = [None] * 21

    def mine(row):
        return lax.dynamic_slice_in_dim(row, place * (row.shape[0] // parts), row.shape[0] // parts)

    def widen(block):
        return jnp.concatenate([block[i : i + rows] for i in range(0, len(block), rows)], axis=1)

    for index, at in ((14, 0), (15, 1), (16, 2), (20, 3), (7, 8), (8, 9), (6, 10), (10, 11), (12, 12)):
        final[index] = mine(early_sums.total[at])
    final[18] = mine(early_sums.total[16:].reshape(-1))
    for index, at in ((0, 0), (1, 1), (3, 2), (4, 3)):
        final[index] = mine(late_sums.total[at])
    feed_total, mid_total = feed_trees[0].total, mid_trees[0].total
    final[19] = feed_total[:inner_rows]
    final[13] = feed_total[inner_rows : inner_rows + rows]
    final[17] = widen(feed_total[inner_rows + rows :])
    final[9] = mid_total[:rows]
    final[5] = mid_total[rows : 2 * rows]
    final[11] = widen(mid_total[2 * rows :])
    final[2] = jnp.concatenate([tree.total for tree in late_trees], axis=1)
    results = give(results, result_gots, 0)
    source_grads = give(source_grads, source_gots, 0)
    return (results[:, None], input_grads[:, None], source_grads[:, None]) + tuple(final)


def solution(mesh):
    in_specs = (
        P(None, "dp", "seq", None),
        P(None, "dp", "seq", None),
        P(None, "dp"),
        P(None, "dp", "seq"),
        P(None, "dp", "seq", None),
        P(),
        P(),
        P(),
        P(),
        P(),
        P(),
        P(),
        P(),
        P(),
        P(),
        P(),
        P(),
        P(),
        P(),
        P(),
        P(),
        P(),
        P(),
        P(),
        P(),
        P(),
    )
    out_specs = (
        P(None, "dp", "seq", None),
        P(None, "dp", "seq", None),
        P(None, "dp", "seq", None),
        P("dp"),
        P("dp"),
        P("dp", None),
        P("dp"),
        P("dp"),
        P("dp", None),
        P("dp"),
        P("dp"),
        P("dp"),
        P("dp", None),
        P("dp"),
        P("dp", None),
        P("dp"),
        P("dp", None),
        P("dp"),
        P("dp"),
        P("dp"),
        P("dp", None),
        P("dp"),
        P("dp", None),
        P("dp"),
    )

    def on_device(*arguments):
        micros = arguments[0].shape[0]
        rows = lax.axis_size("dp")
        pairs = lax.axis_size("seq") == 2 and micros % 2 == 0
        whole = pairs and rows & (rows - 1) == 0
        return (whole_sequences if whole else split_sequences)(*arguments)

    return jax.shard_map(
        on_device, mesh=mesh, in_specs=in_specs, out_specs=out_specs, check_vma=False
    )
```

```python
import functools

import jax
import jax.numpy as jnp
from jax import lax
from jax.experimental import pallas as pl
from jax.experimental.pallas import tpu as pltpu
from jax.sharding import PartitionSpec as P

HEADS = 12
HEAD = 64


epsilon = 1e-05
blocked_score = -1e30


def normed(values, norm_gain, norm_shift):
    center = values - jnp.mean(values, axis=-1, keepdims=True)
    spread = jnp.mean(center * center, axis=-1, keepdims=True)
    return center * lax.rsqrt(spread + epsilon) * norm_gain + norm_shift


def normed_back(values, norm_gain, norm_shift, upstream):
    unused, pullback = jax.vjp(normed, values, norm_gain, norm_shift)
    return pullback(upstream)


def gelu_exact(values):
    return jax.nn.gelu(values, approximate=False)


def project_rows(row_block, weight):
    return jnp.einsum("bpd,de->bpe", row_block, weight, preferred_element_type=jnp.float32)


def project_back(row_block, weight):
    return jnp.einsum("bpe,de->bpd", row_block, weight, preferred_element_type=jnp.float32)


def outer_sum(first_rows, second_rows):
    return jnp.einsum("bpd,bpe->de", first_rows, second_rows, preferred_element_type=jnp.float32)


def split_heads(row_block):
    return row_block.reshape(row_block.shape[0], row_block.shape[1], HEADS, HEAD)


def masked_scores(queries, key_rows, allowed):
    scores = jnp.einsum(
        "bphe,bshe->bhps",
        split_heads(queries),
        split_heads(key_rows),
        preferred_element_type=jnp.float32,
    )
    if allowed is None:
        return scores
    return jnp.where(allowed[:, None], scores, blocked_score)


def attend_forward(queries, key_rows, values, allowed):
    scores = masked_scores(queries, key_rows, allowed)
    highest_score = jnp.max(scores, axis=-1, keepdims=True)
    raised = jnp.exp(scores - highest_score)
    totals = jnp.sum(raised, axis=-1, keepdims=True)
    weights = (raised / totals).astype(jnp.bfloat16)
    mixed = jnp.einsum(
        "bhps,bshe->bphe", weights, split_heads(values), preferred_element_type=jnp.float32
    )
    return (mixed.reshape(queries.shape).astype(jnp.bfloat16), highest_score + jnp.log(totals))


def attend_backward(queries, key_rows, values, allowed, log_totals, upstream):
    weights = jnp.exp(masked_scores(queries, key_rows, allowed) - log_totals)
    upstream_heads = split_heads(upstream)
    value_grads = jnp.einsum(
        "bhps,bphe->bshe",
        weights.astype(jnp.bfloat16),
        upstream_heads,
        preferred_element_type=jnp.float32,
    )
    weight_grads = jnp.einsum(
        "bphe,bshe->bhps", upstream_heads, split_heads(values), preferred_element_type=jnp.float32
    )
    score_grads = weights * (weight_grads - jnp.sum(weight_grads * weights, axis=-1, keepdims=True))
    score_low = score_grads.astype(jnp.bfloat16)
    query_grads = jnp.einsum(
        "bhps,bshe->bphe", score_low, split_heads(key_rows), preferred_element_type=jnp.float32
    ).reshape(queries.shape)
    key_grads = jnp.einsum(
        "bhps,bphe->bshe", score_low, split_heads(queries), preferred_element_type=jnp.float32
    ).reshape(key_rows.shape)
    return (query_grads, jnp.concatenate([key_grads, value_grads.reshape(key_rows.shape)], axis=-1))


def split_sequences(
    targets,
    memory,
    row_kind,
    loss_mask,
    cotangent,
    norm_self_gain,
    norm_self_bias,
    self_input,
    self_query_bias,
    self_value_bias,
    self_output,
    self_output_bias,
    norm_cross_gain,
    norm_cross_bias,
    cross_query,
    cross_query_bias,
    cross_input,
    cross_value_bias,
    cross_output,
    cross_output_bias,
    norm_feed_gain,
    norm_feed_bias,
    feed_in,
    feed_in_bias,
    feed_out,
    feed_out_bias,
):
    model_width = targets.shape[3]
    part_rows = targets.shape[2]
    key_span = part_rows * lax.axis_size("seq")
    query_scale = HEAD ** (-0.5)
    places = lax.axis_index("seq") * part_rows + jnp.arange(part_rows)
    causal = jnp.arange(key_span)[None, :] <= places[:, None]
    results, input_grads, source_grads = ([], [], [])
    totals = None
    for micro_index in range(targets.shape[0]):
        inputs = targets[micro_index].astype(jnp.float32)
        memory_local = memory[micro_index]
        allowed = causal[None] | (row_kind[micro_index] == 1)[:, None, None]
        first_normed = normed(inputs, norm_self_gain, norm_self_bias).astype(jnp.bfloat16)
        self_joint = project_rows(first_normed, self_input)
        queries = ((self_joint[..., :model_width] + self_query_bias) * query_scale).astype(
            jnp.bfloat16
        )
        own_pairs = jnp.concatenate(
            [
                self_joint[..., model_width : 2 * model_width],
                self_joint[..., 2 * model_width :] + self_value_bias,
            ],
            axis=-1,
        ).astype(jnp.bfloat16)
        gathered_self = lax.all_gather(own_pairs, "seq", axis=1, tiled=True)
        key_rows = gathered_self[..., :model_width]
        value_rows = gathered_self[..., model_width:]
        self_mixed, self_totals = attend_forward(queries, key_rows, value_rows, allowed)
        after_self = inputs + project_rows(self_mixed, self_output) + self_output_bias
        second_normed = normed(after_self, norm_cross_gain, norm_cross_bias).astype(jnp.bfloat16)
        cross_queries = (
            (project_rows(second_normed, cross_query) + cross_query_bias) * query_scale
        ).astype(jnp.bfloat16)
        joined = project_rows(lax.all_gather(memory_local, "seq", axis=1, tiled=True), cross_input)
        gathered_cross = jnp.concatenate(
            [joined[..., :model_width], joined[..., model_width:] + cross_value_bias], axis=-1
        ).astype(jnp.bfloat16)
        cross_keys = gathered_cross[..., :model_width]
        cross_values = gathered_cross[..., model_width:]
        cross_mixed, cross_totals = attend_forward(cross_queries, cross_keys, cross_values, None)
        after_cross = after_self + project_rows(cross_mixed, cross_output) + cross_output_bias
        third_normed = normed(after_cross, norm_feed_gain, norm_feed_bias).astype(jnp.bfloat16)
        activated, gelu_pullback = jax.vjp(
            gelu_exact, project_rows(third_normed, feed_in) + feed_in_bias
        )
        activated_low = activated.astype(jnp.bfloat16)
        results.append(
            (after_cross + project_rows(activated_low, feed_out) + feed_out_bias).astype(
                jnp.bfloat16
            )
        )
        pieces = [None] * 21
        grad_output = (
            cotangent[micro_index].astype(jnp.float32)
            * loss_mask[micro_index].astype(jnp.float32)[..., None]
        )
        output_low = grad_output.astype(jnp.bfloat16)
        pieces[19] = outer_sum(activated_low, output_low)
        pieces[20] = jnp.sum(grad_output, axis=(0, 1))
        grad_hidden = gelu_pullback(project_back(output_low, feed_out))[0]
        hidden_low = grad_hidden.astype(jnp.bfloat16)
        pieces[17] = outer_sum(third_normed, hidden_low)
        pieces[18] = jnp.sum(grad_hidden, axis=(0, 1))
        through_feed, pieces[15], pieces[16] = normed_back(
            after_cross, norm_feed_gain, norm_feed_bias, project_back(hidden_low, feed_in)
        )
        grad_cross = grad_output + through_feed
        cross_low = grad_cross.astype(jnp.bfloat16)
        pieces[13] = outer_sum(cross_mixed, cross_low)
        pieces[14] = jnp.sum(grad_cross, axis=(0, 1))
        cross_upstream = project_back(cross_low, cross_output).astype(jnp.bfloat16)
        cross_query_grads, cross_pair_grads = attend_backward(
            cross_queries, cross_keys, cross_values, None, cross_totals, cross_upstream
        )
        own_cross = lax.psum_scatter(
            cross_pair_grads.astype(jnp.bfloat16), "seq", scatter_dimension=1, tiled=True
        ).astype(jnp.float32)
        pieces[12] = jnp.sum(own_cross[..., model_width:], axis=(0, 1))
        own_cross_low = own_cross.astype(jnp.bfloat16)
        pieces[11] = outer_sum(memory_local, own_cross_low)
        source_grads.append(project_back(own_cross_low, cross_input))
        scaled_cross = cross_query_grads * query_scale
        pieces[10] = jnp.sum(scaled_cross, axis=(0, 1))
        scaled_cross_low = scaled_cross.astype(jnp.bfloat16)
        pieces[9] = outer_sum(second_normed, scaled_cross_low)
        through_cross, pieces[7], pieces[8] = normed_back(
            after_self,
            norm_cross_gain,
            norm_cross_bias,
            project_back(scaled_cross_low, cross_query),
        )
        grad_self = grad_cross + through_cross
        self_low = grad_self.astype(jnp.bfloat16)
        pieces[5] = outer_sum(self_mixed, self_low)
        pieces[6] = jnp.sum(grad_self, axis=(0, 1))
        self_upstream = project_back(self_low, self_output).astype(jnp.bfloat16)
        self_query_grads, self_pair_grads = attend_backward(
            queries, key_rows, value_rows, allowed, self_totals, self_upstream
        )
        own_self = lax.psum_scatter(
            self_pair_grads.astype(jnp.bfloat16), "seq", scatter_dimension=1, tiled=True
        ).astype(jnp.float32)
        scaled_self = self_query_grads * query_scale
        pieces[3] = jnp.sum(scaled_self, axis=(0, 1))
        pieces[4] = jnp.sum(own_self[..., model_width:], axis=(0, 1))
        joint_low = jnp.concatenate([scaled_self, own_self], axis=-1).astype(jnp.bfloat16)
        pieces[2] = outer_sum(first_normed, joint_low)
        through_first, pieces[0], pieces[1] = normed_back(
            inputs, norm_self_gain, norm_self_bias, project_back(joint_low, self_input)
        )
        input_grads.append(grad_self + through_first)
        totals = (
            pieces
            if totals is None
            else [running + added for running, added in zip(totals, pieces)]
        )
    def reduced(total):
        block = lax.psum_scatter(
            total.astype(jnp.bfloat16), "dp", scatter_dimension=0, tiled=True
        )
        return lax.psum(block, "seq").astype(jnp.float32)

    final = [reduced(total) for total in totals]
    return (jnp.stack(results), jnp.stack(input_grads), jnp.stack(source_grads)) + tuple(final)


def contract(first, second, first_dim, second_dim):
    return lax.dot_general(
        first, second, (((first_dim,), (second_dim,)), ((), ())), preferred_element_type=jnp.float32
    )


def head_masks(pair):
    lane = lax.broadcasted_iota(jnp.int32, (1, pair.shape[1]), 1)
    zero = jnp.zeros((), pair.dtype)
    return (jnp.where(lane < HEAD, pair, zero), jnp.where(lane < HEAD, zero, pair))


LIMIT = 62 * 2**20


def attend_kernel(info_ref, q_ref, k_ref, v_ref, *refs, use_mask, start):
    o_ref, e_ref, r_ref, mask_ref = refs[-4:]
    length = k_ref.shape[1]
    half = length // 2
    values_turned = v_ref[0].T
    ones = jnp.ones((16, length), jnp.bfloat16)

    def run(masked, shifted):
        lowest, highest = None, None
        for at in range(2):
            queries_at = slice(at * half, (at + 1) * half)
            mixed = []
            for head, queries in enumerate(head_masks(q_ref[0, queries_at, :])):
                scores = contract(k_ref[0], queries, 1, 1)
                if shifted:
                    if masked:
                        seen = mask_ref[:, queries_at].astype(jnp.float32) > 0
                        scores = jnp.where(seen, scores, blocked_score)
                    scores = scores - jnp.max(scores, axis=0, keepdims=True)
                low = jnp.exp(scores).astype(jnp.bfloat16)
                if masked:
                    low = low * mask_ref[:, queries_at]
                e_ref[0, head, :, queries_at] = low
                turned = jnp.concatenate(
                    [values_turned[head * HEAD : (head + 1) * HEAD], ones], axis=0
                )
                sums = contract(turned, low, 1, 0)
                total = sums[HEAD : HEAD + 1]
                if not shifted:
                    lowest = total if lowest is None else jnp.minimum(lowest, total)
                    highest = total if highest is None else jnp.maximum(highest, total)
                inverse = 1.0 / total
                r_ref[0, 0, head : head + 1, queries_at] = inverse
                mixed.append(sums[:HEAD] * inverse)
            o_ref[0, queries_at, :] = jnp.concatenate(mixed, axis=0).T.astype(jnp.bfloat16)
        if not shifted:
            in_range = (jnp.min(lowest) > 1e-20) & (jnp.max(highest) < 1e30)

            @pl.when(jnp.logical_not(in_range))
            def _():
                run(masked, True)

    if not use_mask:
        run(False, False)
        return
    causal = info_ref[2 + start + pl.program_id(0)] == 0

    @pl.when(causal & (pl.program_id(1) == 0))
    def _():
        later = info_ref[0] * half
        query = lax.broadcasted_iota(jnp.int32, (1, length), 1)
        query = jnp.where(query < half, query + later, query - later)

        @pl.loop(0, length, step=64)
        def _(row):
            key = lax.broadcasted_iota(jnp.int32, (64, 1), 0) + row
            key = jnp.where(key < half, key + later, key - later)
            seen = jnp.where(key <= query, 1.0, 0.0)
            mask_ref[pl.ds(pl.multiple_of(row, 64), 64), :] = seen.astype(jnp.bfloat16)

    @pl.when(causal)
    def _():
        run(True, False)

    @pl.when(jnp.logical_not(causal))
    def _():
        run(False, False)


def attend(info, start, count_now, previous, queries, keys, values, use_mask, offsets):
    count, length = queries.shape[:2]
    pairs = HEADS * HEAD // 128
    width = HEADS * HEAD

    def spec(offset):
        return pl.BlockSpec((1, length, 128), lambda s, p, info: (start + s, 0, offset * pairs + p))

    place = lambda s, p, info: (start + s, p, 0, 0)
    return pl.pallas_call(
        functools.partial(attend_kernel, use_mask=use_mask, start=start),
        grid_spec=pltpu.PrefetchScalarGridSpec(
            num_scalar_prefetch=1,
            grid=(count_now, pairs),
            in_specs=[spec(offset) for offset in offsets]
            + [pl.BlockSpec(memory_space=pl.ANY)] * len(previous),
            out_specs=[
                spec(0),
                pl.BlockSpec((1, 2, length, length), place),
                pl.BlockSpec((1, 1, 2, length), place),
            ],
            scratch_shapes=[pltpu.VMEM((length, length), jnp.bfloat16)],
        ),
        out_shape=[
            jax.ShapeDtypeStruct((count, length, width), jnp.bfloat16),
            jax.ShapeDtypeStruct((count, HEADS, length, length), jnp.bfloat16),
            jax.ShapeDtypeStruct((count, pairs, 2, length), jnp.float32),
        ],
        input_output_aliases={4: 0, 5: 1, 6: 2} if previous else {},
        compiler_params=pltpu.CompilerParams(vmem_limit_bytes=LIMIT),
        cost_estimate=pl.CostEstimate(
            flops=4 * count_now * HEADS * length * length * 256,
            bytes_accessed=count_now * HEADS * length * length * 2,
            transcendentals=count_now * HEADS * length * length,
        ),
        name="attend",
    )(info, queries, keys, values, *previous)


def attend_back_kernel(q_ref, k_ref, v_ref, o_ref, g_ref, e_ref, r_ref, dq_ref, dk_ref, dv_ref):
    length = k_ref.shape[1]
    keys_turned = k_ref[0].T
    upstream = g_ref[0].astype(jnp.float32)
    products = (o_ref[0].astype(jnp.float32) * upstream).T
    upstream = upstream.T
    parts, deltas = [], []
    for head in range(2):
        rows = slice(head * HEAD, (head + 1) * HEAD)
        inverse = r_ref[0, 0, head : head + 1, :]
        parts.append(upstream[rows] * inverse)
        deltas.append(jnp.sum(products[rows], axis=0, keepdims=True) * inverse)
    scaled = head_masks(jnp.concatenate(parts, axis=0).T.astype(jnp.bfloat16))
    queries = head_masks(q_ref[0])
    key_sum, value_sum, query_parts = 0.0, 0.0, []
    for head in range(2):
        rows = slice(head * HEAD, (head + 1) * HEAD)
        low = e_ref[0, head]
        grads = contract(v_ref[0], scaled[head], 1, 1)
        score_low = (low.astype(jnp.float32) * (grads - deltas[head])).astype(jnp.bfloat16)
        value_sum += contract(low, scaled[head], 1, 0)
        key_sum += contract(score_low, queries[head], 1, 0)
        query_parts.append(contract(keys_turned[rows], score_low, 1, 0))
    turned = jnp.concatenate(query_parts, axis=0) * (HEAD**-0.5)
    dq_ref[0] = turned.T.astype(jnp.bfloat16)
    dk_ref[0] = key_sum.astype(jnp.bfloat16)
    dv_ref[0] = value_sum.astype(jnp.bfloat16)


def attend_back(place, size, previous, queries, keys, values, offsets, *rest):
    count, length = queries.shape[:2]
    pairs = HEADS * HEAD // 128
    width = HEADS * HEAD

    start, first = place

    def spec(offset):
        return pl.BlockSpec(
            (1, length, 128), lambda s, p: (start + s, 0, offset * pairs + first + p)
        )

    kernel = attend_back_kernel
    aliases = {}
    if previous:
        kernel = lambda *refs: attend_back_kernel(*refs[3:])
        aliases = {0: 0, 1: 1, 2: 2}
    return pl.pallas_call(
        kernel,
        grid=size,
        in_specs=[pl.BlockSpec(memory_space=pl.ANY)] * len(previous)
        + [spec(offset) for offset in offsets]
        + [
            spec(0),
            spec(0),
            pl.BlockSpec((1, 2, length, length), lambda s, p: (start + s, first + p, 0, 0)),
            pl.BlockSpec((1, 1, 2, length), lambda s, p: (start + s, first + p, 0, 0)),
        ],
        out_specs=[spec(0)] * 3,
        out_shape=[jax.ShapeDtypeStruct((count, length, width), jnp.bfloat16)] * 3,
        input_output_aliases=aliases,
        compiler_params=pltpu.CompilerParams(vmem_limit_bytes=LIMIT),
        cost_estimate=pl.CostEstimate(
            flops=16 * size[0] * size[1] * length * length * 256,
            bytes_accessed=4 * size[0] * size[1] * length * length,
            transcendentals=0,
        ),
        name="attend_back",
    )(*previous, queries, keys, values, *rest)


def normal_parts(values):
    center = values - jnp.mean(values, axis=-1, keepdims=True)
    inverse = lax.rsqrt(jnp.mean(center * center, axis=-1, keepdims=True) + epsilon)
    return center * inverse, inverse


def normal_back(unit, inverse, norm_gain, upstream):
    inner = upstream * norm_gain
    shift = jnp.mean(inner, axis=-1, keepdims=True)
    tilt = jnp.mean(inner * unit, axis=-1, keepdims=True)
    return inverse * (inner - shift - unit * tilt)


def gelu_parts(values):
    size = jnp.abs(values)
    ratio = 1.0 / (1.0 + 0.2316418882663604 * size)
    series = 0.5307027145
    for weight in (-0.7265760135, 0.7107068705, -0.142248368, 0.127414796):
        series = series * ratio + weight
    bell = jnp.exp(-0.5 * values * values)
    upper = series * ratio * bell
    chance = jnp.where(values < 0, upper, 1.0 - upper)
    return values * chance, chance + values * (0.3989422804014327 * bell)


def column_sum(values):
    return jnp.sum(values, axis=0, keepdims=True)


def resident(array):
    return pl.BlockSpec(array.shape, lambda *_: (0,) * array.ndim, pipeline_mode=pl.Buffered(1))


def whole_block(array):
    return pl.BlockSpec(array.shape, lambda *_: (0,) * len(array.shape))


def like(shape, dtype=jnp.float32):
    return jax.ShapeDtypeStruct(tuple(shape), dtype)


def pick(take_first, first_ref, second_ref):
    return jnp.where(take_first, first_ref[...], second_ref[...])


ONCE = {"pipeline_mode": pl.Buffered(1)}


def own_spec(own, width, held, last, **more):
    def place(step, info):
        return (info[0] * held + jnp.minimum(step, last) // 2, 0, 0)

    return pl.BlockSpec((None, own, width), place, **more)


def got_spec(own, width, last, **more):
    return pl.BlockSpec(
        (None, own, width), lambda step, info: (jnp.minimum(step, last) // 2, 0, 0), **more
    )


def row_spec(own, width, last, **more):
    return pl.BlockSpec((own, width), lambda step, info: (jnp.minimum(step, last), 0), **more)


def kernel_call(kernel, name, info, arrays, in_specs, outs, out_specs, grid, flops, moved, **more):
    scratch = more.pop("scratch", [])
    return pl.pallas_call(
        kernel,
        grid_spec=pltpu.PrefetchScalarGridSpec(
            num_scalar_prefetch=1,
            grid=(grid,),
            in_specs=in_specs,
            out_specs=out_specs,
            scratch_shapes=scratch,
        ),
        out_shape=outs,
        compiler_params=pltpu.CompilerParams(
            vmem_limit_bytes=more.pop("limit", LIMIT)
        ),
        cost_estimate=pl.CostEstimate(flops=flops, bytes_accessed=moved, transcendentals=0),
        name=name,
        **more,
    )(info, *arrays)


GROUP = 32


def sweep(rows, width, sums, body):
    def step(index, totals):
        parts = body(pl.ds(pl.multiple_of(index * GROUP, GROUP), GROUP))
        return tuple(
            total + jnp.sum(part.reshape(GROUP // 8, 8, width), axis=0)
            for total, part in zip(totals, parts or ())
        )

    zeros = tuple(jnp.zeros((8, width), jnp.float32) for _ in range(sums))
    totals = lax.fori_loop(0, rows // GROUP, step, zeros)
    return [column_sum(total) for total in totals]


def add_sums(ref, sums):
    for at, row in enumerate(sums):
        ref[at : at + 1, :] += row


def enter_kernel(info_ref, own_ref, got_ref, w_ref, vec_ref, bias_ref, *refs, norm):
    x_ref, out_ref, normal_ref = refs[-3:]
    first = pl.program_id(0) % 2 == 0
    rows, width = x_ref.shape

    def normalise(place):
        x = jnp.where(first, own_ref[place, :], got_ref[place, :])
        x_ref[place, :] = x
        unit, _ = normal_parts(x.astype(jnp.float32))
        normal_ref[place, :] = (unit * vec_ref[0:1, :] + vec_ref[1:2, :]).astype(jnp.bfloat16)

    if norm:
        sweep(rows, width, 0, normalise)
        x = normal_ref[...]
    else:
        x = pick(first, own_ref, got_ref)
        x_ref[...] = x
    for start in range(0, w_ref.shape[1], width):
        part = slice(start, start + width)
        total = contract(x, w_ref[:, part], 1, 0) + bias_ref[:, part]
        if norm and start == 0:
            total = total * (HEAD**-0.5)
        out_ref[:, part] = total.astype(jnp.bfloat16)


def enter(info, at, previous, held, owns, gots, weight, vectors, bias, norm):
    count, own, width = gots.shape
    rows = 2 * held * own
    wide = weight.shape[1]
    own_rows = pl.BlockSpec(
        (None, own, width), lambda step, info: (info[0] * held + at + step // 2, 0, 0)
    )
    row = lambda step, info: (2 * at + step, 0)
    return kernel_call(
        functools.partial(enter_kernel, norm=norm),
        "enter",
        info,
        (owns, gots, weight, vectors, bias, *previous),
        [own_rows, got_spec(own, width, 2 * count - 1)]
        + [resident(a) for a in (weight, vectors, bias)]
        + [pl.BlockSpec(memory_space=pl.ANY)] * len(previous),
        [like((rows, width), jnp.bfloat16), like((rows, wide), jnp.bfloat16)],
        [pl.BlockSpec((own, width), row), pl.BlockSpec((own, wide), row)],
        2 * count,
        4 * count * own * width * wide,
        4 * count * own * (2 * width + wide),
        scratch=[pltpu.VMEM((own, width), jnp.bfloat16)],
        input_output_aliases={6: 0, 7: 1} if previous else {},
    )


def middle_kernel(info_ref, x_ref, mixed_ref, wo_ref, wq_ref, vec_ref, after_ref, q_ref, normal_ref):
    out_bias, gain, shift, query_bias = (vec_ref[i : i + 1, :] for i in range(4))
    after_ref[...] = contract(mixed_ref[...], wo_ref[...], 1, 0)

    def normalise(place):
        after = after_ref[place, :] + x_ref[place, :].astype(jnp.float32) + out_bias
        after_ref[place, :] = after
        unit, _ = normal_parts(after)
        normal_ref[place, :] = (unit * gain + shift).astype(jnp.bfloat16)

    sweep(*x_ref.shape, 0, normalise)
    queries = (contract(normal_ref[...], wq_ref[...], 1, 0) + query_bias) * (HEAD**-0.5)
    q_ref[...] = queries.astype(jnp.bfloat16)


def middle(info, x, mixed, wo, wq, vectors, own):
    rows, width = x.shape
    last = rows // own - 1
    spec = row_spec(own, width, last)
    return kernel_call(
        middle_kernel,
        "middle",
        info,
        (x, mixed, wo, wq, vectors),
        [spec, spec] + [resident(a) for a in (wo, wq, vectors)],
        [like((rows, width)), like((rows, width), jnp.bfloat16)],
        [spec, spec],
        rows // own,
        4 * rows * width * width,
        10 * rows * width,
        scratch=[pltpu.VMEM((own, width), jnp.bfloat16)],
    )


def write_split(core, rows, kept_ref, sent_ref, start):
    half = rows.shape[0] // 2
    low = rows.astype(jnp.bfloat16)
    place = slice(start, start + half)

    @pl.when(core == 0)
    def _():
        kept_ref[0, place, :] = low[:half]
        sent_ref[0, place, :] = low[half:]

    @pl.when(core != 0)
    def _():
        kept_ref[0, place, :] = low[half:]
        sent_ref[0, place, :] = low[:half]


def write_wide(core, rows, kept_ref, sent_ref, start):
    half, width = rows.shape[0] // 2, kept_ref.shape[2]
    for at in range(rows.shape[1] // width):
        part = rows[:, at * width : (at + 1) * width]
        write_split(core, part, kept_ref, sent_ref, start + at * half)


def acc_rows(ref, at, rows):
    return ref[pl.ds(pl.multiple_of(at * rows, 16), rows), :]


def piece(parts, high, wide, steps, order):
    bits = parts.bit_length() - 2

    def late(step, info):
        at = jnp.maximum(step - steps, 0)
        place = 0
        for bit in order(bits):
            place = 2 * place + (at // 2**bit) % 2
        return (place, 0, 0)

    return (
        [pl.BlockSpec((1, high, wide), late)] * 2,
        [like((parts // 2, high, wide), jnp.bfloat16)] * 2,
    )


def low_first(bits):
    return list(range(bits))


def second_first(bits):
    return list(range(bits))[1:2] + [0] + list(range(2, bits))


def put_rows(step, value, own_ref, got_ref):
    @pl.when(step % 2 == 0)
    def _():
        own_ref[...] = value.astype(own_ref.dtype)

    @pl.when(step % 2 != 0)
    def _():
        got_ref[...] = value.astype(got_ref.dtype)


def feed_kernel(
    info_ref, x_ref, mixed_ref, dyo_ref, dyg_ref, wc_ref, wi_ref, wo_ref, vec_ref, bi_ref,
    own_ref, got_ref, dx_ref, do_ref, vsum_ref, bsum_ref, kept_ref, sent_ref, ai_ref, ao_ref,
    ac_ref, normal_ref, x2_ref, up_ref, *, steps, chunk, parts,
):
    step = pl.program_id(0)

    @pl.when(step == 0)
    def _():
        for ref in (vsum_ref, bsum_ref, ai_ref, ao_ref, ac_ref):
            ref[...] = jnp.zeros_like(ref)

    @pl.when(step < steps)
    def _():
        cross_bias, gain, shift, out_bias = (vec_ref[i : i + 1, :] for i in range(4))
        mixed = mixed_ref[...]
        rows, width = x_ref.shape
        up_ref[...] = contract(mixed, wc_ref[...], 1, 0)

        def normalise(place):
            x2 = up_ref[place, :] + x_ref[place, :] + cross_bias
            x2_ref[place, :] = x2
            unit, _ = normal_parts(x2)
            normal_ref[place, :] = (unit * gain + shift).astype(jnp.bfloat16)

        sweep(rows, width, 0, normalise)
        normal = normal_ref[...]
        normal_turned = normal.T
        dy = pick(step % 2 == 0, dyo_ref, dyg_ref)
        dy_turned = dy.T
        result, upstream = None, None
        for start in range(0, wi_ref.shape[1], chunk):
            part = slice(start, start + chunk)
            hidden = contract(normal, wi_ref[:, part], 1, 0) + bi_ref[:, part]
            active, slope = gelu_parts(hidden)
            active = active.astype(jnp.bfloat16)
            down = contract(active, wo_ref[part, :], 1, 0)
            result = down if result is None else result + down
            grads = contract(dy, wo_ref[part, :], 1, 1) * slope
            bsum_ref[:, part] += column_sum(grads)
            low = grads.astype(jnp.bfloat16)
            up = contract(low, wi_ref[:, part], 1, 1)
            upstream = up if upstream is None else upstream + up
            ao_ref[:, part] += contract(dy_turned, active, 1, 0)
            ai_ref[:, part] += contract(normal_turned, low, 1, 0)
        put_rows(step, x2_ref[...] + result + out_bias, own_ref, got_ref)
        up_ref[...] = upstream

        def back(place):
            unit, inverse = normal_parts(x2_ref[place, :])
            upstream = up_ref[place, :]
            wide = jnp.where(step % 2 == 0, dyo_ref[place, :], dyg_ref[place, :])
            wide = wide.astype(jnp.float32)
            dx = wide + normal_back(unit, inverse, gain, upstream)
            dx_ref[place, :] = dx
            normal_ref[place, :] = dx.astype(jnp.bfloat16)
            return dx, upstream * unit, upstream, wide

        add_sums(vsum_ref, sweep(rows, width, 4, back))
        dx_low = normal_ref[...]
        do_ref[...] = contract(dx_low, wc_ref[...], 1, 1).astype(jnp.bfloat16)
        ac_ref[...] += contract(mixed.T, dx_low, 1, 0)

    @pl.when(step >= steps)
    def _():
        at = step - steps
        core = info_ref[1]
        width, wide = ai_ref.shape
        rows = 2 * width // parts
        inner = 2 * wide // parts
        columns = ao_ref[:, pl.ds(pl.multiple_of(at * inner, 128), inner)]
        write_split(core, columns.astype(jnp.bfloat16).T, kept_ref, sent_ref, 0)
        write_split(core, acc_rows(ac_ref, at, rows), kept_ref, sent_ref, inner // 2)
        write_wide(core, acc_rows(ai_ref, at, rows), kept_ref, sent_ref, (inner + rows) // 2)


def feed(info, x1, mixed, dys, dy_gots, wc, wi, wo, vectors, bi, parts, chunk=768):
    rows, width = x1.shape
    held, own = dy_gots.shape[:2]
    micros = dys.shape[0]
    inner = wi.shape[1]
    steps = 2 * held
    last = steps - 1
    row = row_spec(own, width, last)
    pieces = [piece(parts, (2 * inner + width) // parts, width, steps, low_first)]
    sums = [like((8, width)), like((1, inner))]
    return kernel_call(
        functools.partial(feed_kernel, steps=steps, chunk=chunk, parts=parts),
        "feed",
        info,
        (x1, mixed, dys, dy_gots, wc, wi, wo, vectors, bi),
        [row_spec(own, width, last, **ONCE)] * 2
        + [own_spec(own, width, held, last, **ONCE), got_spec(own, width, last, **ONCE)]
        + [resident(a) for a in (wc, wi, wo, vectors, bi)],
        [
            like((micros, own, width), jnp.bfloat16),
            like((held, own, width), jnp.bfloat16),
            like((rows, width)),
            like((rows, width), jnp.bfloat16),
        ]
        + sums
        + sum([p[1] for p in pieces], []),
        [own_spec(own, width, held, last), got_spec(own, width, last), row, row]
        + [whole_block(a) for a in sums]
        + sum([p[0] for p in pieces], []),
        steps + parts // 2,
        2 * rows * width * (6 * inner + 3 * width),
        60 * 2**20,
        scratch=[
            pltpu.VMEM((width, inner), jnp.float32),
            pltpu.VMEM((width, inner), jnp.float32),
            pltpu.VMEM((width, width), jnp.float32),
            pltpu.VMEM((own, width), jnp.bfloat16),
            pltpu.VMEM((own, width), jnp.float32),
            pltpu.VMEM((own, width), jnp.float32),
        ],
    )


def return_kernel(
    info_ref, dq_ref, dk_ref, dv_ref, x_ref, dx_ref, mixed_ref, src_ref, wq_ref, wi_ref, wo_ref,
    vec_ref, own_ref, got_ref, dxo_ref, do_ref, vsum_ref, kept_ref, sent_ref, aq_ref, ao_ref,
    ai_ref, normal_ref, low_ref, up_ref, *, steps, parts,
):
    step = pl.program_id(0)

    @pl.when(step == 0)
    def _():
        for ref in (vsum_ref, aq_ref, ao_ref, ai_ref):
            ref[...] = jnp.zeros_like(ref)

    @pl.when(step < steps)
    def _():
        rows, width = x_ref.shape
        gain, shift = vec_ref[0:1, :], vec_ref[1:2, :]
        up_ref[...] = contract(dq_ref[...], wq_ref[...], 1, 1)

        def back(place):
            unit, inverse = normal_parts(x_ref[place, :])
            upstream = up_ref[place, :]
            normal_ref[place, :] = (unit * gain + shift).astype(jnp.bfloat16)
            dx = dx_ref[place, :] + normal_back(unit, inverse, gain, upstream)
            dxo_ref[place, :] = dx
            low_ref[place, :] = dx.astype(jnp.bfloat16)
            dq, dv = dq_ref[place, :], dv_ref[place, :]
            return (
                upstream * unit, upstream, dx, dq.astype(jnp.float32), dv.astype(jnp.float32)
            )

        add_sums(vsum_ref, sweep(rows, width, 5, back))
        dk, dv = dk_ref[...], dv_ref[...]
        source = contract(dk, wi_ref[:, :width], 1, 1) + contract(dv, wi_ref[:, width:], 1, 1)
        put_rows(step, source, own_ref, got_ref)
        turned = src_ref[...].T
        ai_ref[:, :width] += contract(turned, dk, 1, 0)
        ai_ref[:, width:] += contract(turned, dv, 1, 0)
        low = low_ref[...]
        do_ref[...] = contract(low, wo_ref[...], 1, 1).astype(jnp.bfloat16)
        aq_ref[...] += contract(normal_ref[...].T, dq_ref[...], 1, 0)
        ao_ref[...] += contract(mixed_ref[...].T, low, 1, 0)

    @pl.when(step >= steps)
    def _():
        at = step - steps
        core = info_ref[1]
        rows = 2 * aq_ref.shape[0] // parts
        write_split(core, acc_rows(aq_ref, at, rows), kept_ref, sent_ref, 0)
        write_split(core, acc_rows(ao_ref, at, rows), kept_ref, sent_ref, rows // 2)
        write_wide(core, acc_rows(ai_ref, at, rows), kept_ref, sent_ref, rows)


def return_rows(info, grads, x1, dx2, mixed, sources, wq, wi, wo, vectors, own, micros, parts):
    rows, width = x1.shape
    held = rows // own // 2
    steps = 2 * held
    last = steps - 1
    row = row_spec(own, width, last)
    pieces = [piece(parts, 4 * width // parts, width, steps, low_first)]
    sums = like((8, width))
    return kernel_call(
        functools.partial(return_kernel, steps=steps, parts=parts),
        "return_rows",
        info,
        (*grads, x1, dx2, mixed, sources, wq, wi, wo, vectors),
        [row] * 7 + [resident(a) for a in (wq, wi, wo, vectors)],
        [
            like((micros, own, width)),
            like((held, own, width), jnp.bfloat16),
            like((rows, width)),
            like((rows, width), jnp.bfloat16),
            sums,
        ]
        + sum([p[1] for p in pieces], []),
        [own_spec(own, width, held, last), got_spec(own, width, last), row, row, whole_block(sums)]
        + sum([p[0] for p in pieces], []),
        steps + parts // 2,
        16 * rows * width * width,
        40 * 2**20,
        scratch=[
            pltpu.VMEM((width, width), jnp.float32),
            pltpu.VMEM((width, width), jnp.float32),
            pltpu.VMEM((width, 2 * width), jnp.float32),
            pltpu.VMEM((own, width), jnp.bfloat16),
            pltpu.VMEM((own, width), jnp.bfloat16),
            pltpu.VMEM((own, width), jnp.float32),
        ],
    )


def last_weight_kernel(
    info_ref, dq_ref, dk_ref, dv_ref, x_ref, vec_ref, ka_ref, sa_ref, kb_ref, sb_ref, acc_ref,
    normal_ref, *, steps,
):
    step = pl.program_id(0)

    @pl.when(step == 0)
    def _():
        acc_ref[...] = jnp.zeros_like(acc_ref)

    @pl.when(step < steps)
    def _():
        rows, width = x_ref.shape

        def normalise(place):
            unit, _ = normal_parts(x_ref[place, :].astype(jnp.float32))
            normal = unit * vec_ref[0:1, :] + vec_ref[1:2, :]
            normal_ref[place, :] = normal.astype(jnp.bfloat16)

        sweep(rows, width, 0, normalise)
        turned = normal_ref[...].T
        for at, ref in enumerate((dq_ref, dk_ref, dv_ref)):
            acc_ref[:, at * width : (at + 1) * width] += contract(turned, ref[...], 1, 0)

    @pl.when(step >= steps)
    def _():
        rows = acc_rows(acc_ref, step - steps, 2 * ka_ref.shape[1])
        half = ka_ref.shape[2]
        write_split(info_ref[1], rows[:, :half], ka_ref, sa_ref, 0)
        write_split(info_ref[1], rows[:, half:], kb_ref, sb_ref, 0)


def last_weight(info, grads, x, vectors, own, parts):
    rows, width = x.shape
    steps = rows // own
    row = row_spec(own, width, steps - 1)
    pieces = [
        piece(parts, width // parts, 3 * width // 2, steps, order)
        for order in (low_first, second_first)
    ]
    return kernel_call(
        functools.partial(last_weight_kernel, steps=steps),
        "last_weight",
        info,
        (*grads, x, vectors),
        [row] * 4 + [resident(vectors)],
        sum([p[1] for p in pieces], []),
        sum([p[0] for p in pieces], []),
        steps + parts // 2,
        6 * rows * width * width,
        20 * 2**20,
        scratch=[
            pltpu.VMEM((width, 3 * width), jnp.float32),
            pltpu.VMEM((own, width), jnp.bfloat16),
        ],
    )


def leave_kernel(
    info_ref, dq_ref, dk_ref, dv_ref, x_ref, dx_ref, w_ref, vec_ref, *refs
):
    own_ref, got_ref, vsum_ref, up_ref = refs[-4:]
    step = pl.program_id(0)

    @pl.when(step == 0)
    def _():
        vsum_ref[...] = jnp.zeros_like(vsum_ref)

    rows, width = x_ref.shape
    up_ref[...] = (
        contract(dq_ref[...], w_ref[:, :width], 1, 1)
        + contract(dk_ref[...], w_ref[:, width : 2 * width], 1, 1)
        + contract(dv_ref[...], w_ref[:, 2 * width :], 1, 1)
    )

    def finish_rows(out_ref):
        def back(place):
            unit, inverse = normal_parts(x_ref[place, :].astype(jnp.float32))
            upstream = up_ref[place, :]
            dx = dx_ref[place, :] + normal_back(unit, inverse, vec_ref[0:1, :], upstream)
            out_ref[place, :] = dx.astype(out_ref.dtype)
            dq, dv = dq_ref[place, :], dv_ref[place, :]
            return upstream * unit, upstream, dq.astype(jnp.float32), dv.astype(jnp.float32)

        add_sums(vsum_ref, sweep(rows, width, 4, back))

    @pl.when(step == 0)
    def _():
        finish_rows(own_ref)

    @pl.when(step != 0)
    def _():
        finish_rows(got_ref)


def leave(info, at, previous, grads, x, dx1, weight, vectors, own, micros):
    rows, width = x.shape
    held = rows // own // 2
    row = pl.BlockSpec((own, width), lambda step, info: (2 * at + step, 0))
    more = {"input_output_aliases": {8: 0}} if previous else {}
    sums = like((8, width))
    return kernel_call(
        leave_kernel,
        "leave",
        info,
        (*grads, x, dx1, weight, vectors, *previous),
        [row] * 5
        + [resident(a) for a in (weight, vectors)]
        + [pl.BlockSpec(memory_space=pl.ANY)] * len(previous),
        [like((micros, own, width)), like((own, width), jnp.bfloat16), sums],
        [
            pl.BlockSpec((None, own, width), lambda step, info: (info[0] * held + at, 0, 0)),
            pl.BlockSpec((own, width), lambda step, info: (0, 0)),
            whole_block(sums),
        ],
        2,
        12 * own * width * width,
        16 * 2**20,
        scratch=[pltpu.VMEM((own, width), jnp.float32)],
        **more,
    )


SWAP = ((0, 1), (1, 0))


class Tree:
    def __init__(self, kept, sent, order):
        self.count = lax.axis_size("dp")
        bits = self.count.bit_length() - 2
        shape = (2,) * bits + kept.shape[1:]
        self.order = [2 << bit for bit in order(bits)]
        self.kept, self.sent, self.bit = kept.reshape(shape), sent.reshape(shape), 1
        self.got, self.total = None, None

    def exchange(self):
        if self.total is not None or self.got is not None:
            return
        if self.bit:
            pairs = [(i, i ^ self.bit) for i in range(self.count)]
            self.got = lax.ppermute(self.sent, "dp", pairs)
        else:
            self.got = lax.ppermute(self.kept, "seq", SWAP)

    def add(self):
        if self.got is None:
            return
        total = self.kept.astype(jnp.float32) + self.got.astype(jnp.float32)
        self.got = None
        if not self.bit:
            self.total = total
            return
        total = total.astype(jnp.bfloat16)
        if not self.order:
            self.bit, self.kept = 0, total
            return
        self.bit = self.order.pop(0)
        mine = (lax.axis_index("dp") // self.bit) % 2
        self.kept = lax.dynamic_index_in_dim(total, mine, 0, keepdims=False)
        self.sent = lax.dynamic_index_in_dim(total, 1 - mine, 0, keepdims=False)


class Whole:
    def __init__(self, rows):
        self.count = lax.axis_size("dp")
        self.rows, self.bit, self.got, self.total = rows, 1, None, None

    def exchange(self):
        if self.total is not None or self.got is not None:
            return
        if self.bit < self.count:
            pairs = [(i, i ^ self.bit) for i in range(self.count)]
            self.got = lax.ppermute(self.rows, "dp", pairs)
        else:
            self.got = lax.ppermute(self.rows, "seq", SWAP)

    def add(self):
        if self.got is None:
            return
        self.rows = self.rows + self.got
        self.got = None
        if self.bit == self.count:
            self.total = self.rows
        self.bit *= 2


def exchange(trees):
    for tree in trees:
        tree.exchange()


def settle(trees, values):
    trees = [tree for tree in trees if tree.got is not None]
    gots, values = lax.optimization_barrier(([tree.got for tree in trees], values))
    for tree, got in zip(trees, gots):
        tree.got = got
        tree.add()
    return values


def finish(trees):
    while any(tree.total is None for tree in trees):
        exchange(trees)
        settle(trees, ())


def whole_sequences(
    targets,
    memory,
    row_kind,
    loss_mask,
    cotangent,
    norm_self_gain,
    norm_self_bias,
    self_input,
    self_query_bias,
    self_value_bias,
    self_output,
    self_output_bias,
    norm_cross_gain,
    norm_cross_bias,
    cross_query,
    cross_query_bias,
    cross_input,
    cross_value_bias,
    cross_output,
    cross_output_bias,
    norm_feed_gain,
    norm_feed_bias,
    feed_in,
    feed_in_bias,
    feed_out,
    feed_out_bias,
):
    micros, _, own, width = targets.shape
    held = micros // 2
    side = lax.axis_index("seq")
    parts = lax.axis_size("dp")
    place = lax.axis_index("dp")
    length = 2 * own
    pairs = HEADS * HEAD // 128

    def swap(rows, at, count, after=()):
        sent = lax.dynamic_slice_in_dim(rows, (1 - side) * held + at, count, axis=0)
        sent, after = lax.optimization_barrier((sent, after))
        return lax.ppermute(sent, "seq", SWAP), after

    def give(owns, got, at):
        got = got.astype(owns.dtype)
        return lax.dynamic_update_slice_in_dim(owns, got, (1 - side) * held + at, axis=0)

    def pack(*rows):
        zero = jnp.zeros((8 - len(rows), width), jnp.float32)
        return jnp.concatenate([jnp.stack(rows), zero])

    def batch(rows):
        return rows.reshape(held, length, -1)

    def flat(rows):
        return rows.reshape(held * length, -1)

    targets, memory = targets[:, 0], memory[:, 0]
    upstreams = (
        cotangent[:, 0].astype(jnp.float32) * loss_mask[:, 0].astype(jnp.float32)[..., None]
    ).astype(jnp.bfloat16)
    target_gots, last_got = [], ()
    for at in range(held):
        got, last_got = swap(targets, at, 1, last_got)
        target_gots.append(got)
        if at:
            target_gots[at - 1] = last_got
        last_got = got
    memory_gots, target_gots[-1] = swap(memory, 0, held, last_got)
    upstream_gots, memory_gots = swap(upstreams, 0, held, memory_gots)
    kinds = lax.dynamic_slice_in_dim(row_kind[:, 0], side * held, held, axis=0)
    info = jnp.concatenate([jnp.stack([side, place % 2]).astype(jnp.int32), kinds])

    self_vectors = pack(norm_self_gain, norm_self_bias)
    zero = jnp.zeros_like(self_query_bias)
    joint_bias = jnp.concatenate([self_query_bias, zero, self_value_bias])[None]
    entered, attended = (), ()
    for at in range(held):
        entered = enter(
            info, at, entered, held, targets, target_gots[at], self_input, self_vectors,
            joint_bias, True,
        )
        joint = batch(entered[1])
        attended = attend(info, at, 1, attended, joint, joint, joint, True, (0, 1, 2))
        entered, attended = lax.optimization_barrier((entered, attended))
    inputs, joint = entered[0], batch(entered[1])
    self_mixed, self_raised, self_inverse = attended
    after_self, cross_queries = middle(
        info,
        inputs,
        flat(self_mixed),
        self_output,
        cross_query,
        pack(self_output_bias, norm_cross_gain, norm_cross_bias, cross_query_bias),
        own,
    )
    pair_bias = jnp.concatenate([zero, cross_value_bias])[None]
    sources, cross_pairs = enter(
        info, 0, (), held, memory, memory_gots, cross_input, self_vectors, pair_bias, False
    )
    cross_queries, cross_pairs = batch(cross_queries), batch(cross_pairs)
    cross_mixed, cross_raised, cross_inverse = attend(
        info, 0, held, (), cross_queries, cross_pairs, cross_pairs, False, (0, 0, 1)
    )
    results, result_gots, grad_cross, cross_upstream, feed_sums, hidden_sums, *feed_parts = feed(
        info,
        after_self,
        flat(cross_mixed),
        upstreams,
        upstream_gots,
        cross_output,
        feed_in,
        feed_out,
        pack(cross_output_bias, norm_feed_gain, norm_feed_bias, feed_out_bias),
        feed_in_bias[None],
        parts,
    )
    feed_trees = [Tree(*feed_parts, low_first)]
    first = pairs // 2
    cross_inputs = (
        cross_queries, cross_pairs, cross_pairs, (0, 0, 1), cross_mixed, batch(cross_upstream),
        cross_raised, cross_inverse,
    )
    exchange(feed_trees)
    result_gots = lax.ppermute(result_gots, "seq", SWAP)
    half_grads, result_gots = settle(
        feed_trees, (attend_back((0, 0), (held, first), (), *cross_inputs), result_gots)
    )
    exchange(feed_trees)
    cross_grads = attend_back((0, first), (held, pairs - first), half_grads, *cross_inputs)
    source_grads, source_gots, grad_self, self_upstream, return_sums, *mid_parts = settle(
        feed_trees,
        return_rows(
            info,
            [flat(rows) for rows in cross_grads],
            after_self,
            grad_cross,
            flat(self_mixed),
            sources,
            cross_query,
            cross_input,
            self_output,
            pack(norm_cross_gain, norm_cross_bias),
            own,
            micros,
            parts,
        ),
    )
    early_sums = Whole(
        jnp.concatenate([feed_sums, return_sums, hidden_sums.reshape(-1, width)], axis=0)
    )
    mid_trees = [Tree(*mid_parts, low_first), early_sums]
    exchange(feed_trees + mid_trees)
    self_inputs = (
        joint, joint, joint, (0, 1, 2), self_mixed, batch(self_upstream), self_raised, self_inverse
    )
    source_gots = lax.ppermute(source_gots, "seq", SWAP)
    grads, source_gots = settle(
        feed_trees + mid_trees,
        (attend_back((0, 0), (1, pairs), (), *self_inputs), source_gots),
    )
    exchange(feed_trees + mid_trees)
    kept, leave_sums = (), []
    trees = feed_trees + mid_trees
    for at in range(held):
        if at == held - 1:
            late_parts = last_weight(
                info, [flat(rows) for rows in grads], inputs, self_vectors, own, parts
            )
            late_trees = [
                Tree(*late_parts[0:2], low_first),
                Tree(*late_parts[2:4], second_first),
            ]
            trees = trees + late_trees
            exchange(trees)
            grads, _ = lax.optimization_barrier((grads, late_parts[0]))
        kept, got, sums = leave(
            info, at, kept, [flat(rows) for rows in grads], inputs, grad_self,
            self_input, self_vectors, own, micros,
        )
        leave_sums.append(sums)
        if at < held - 1:
            grads, kept = lax.optimization_barrier((grads, kept))
            back = lax.ppermute(got, "seq", SWAP)
            grads, back = settle(
                trees,
                (attend_back((at + 1, 0), (1, pairs), grads, *self_inputs), back),
            )
            exchange(trees)
            back = back.astype(kept.dtype)[None]
            kept = (
                lax.dynamic_update_slice_in_dim(kept, back, (1 - side) * held + at, axis=0),
            )
    input_grads, got, sums = settle(trees, (kept, got, sum(leave_sums)))
    late_sums = Whole(sums)
    trees = trees + [late_sums]
    exchange(trees)
    back = lax.ppermute(got, "seq", SWAP)
    settle(trees, ())
    exchange(trees)
    back = settle(trees, back)
    exchange(trees)
    input_grads = give(input_grads, back[None], held - 1)
    finish(trees)
    rows = width // parts
    inner_rows = feed_in.shape[1] // parts
    final = [None] * 21

    def mine(row):
        return lax.dynamic_slice_in_dim(row, place * (row.shape[0] // parts), row.shape[0] // parts)

    def widen(block):
        return jnp.concatenate([block[i : i + rows] for i in range(0, len(block), rows)], axis=1)

    for index, at in ((14, 0), (15, 1), (16, 2), (20, 3), (7, 8), (8, 9), (6, 10), (10, 11), (12, 12)):
        final[index] = mine(early_sums.total[at])
    final[18] = mine(early_sums.total[16:].reshape(-1))
    for index, at in ((0, 0), (1, 1), (3, 2), (4, 3)):
        final[index] = mine(late_sums.total[at])
    feed_total, mid_total = feed_trees[0].total, mid_trees[0].total
    final[19] = feed_total[:inner_rows]
    final[13] = feed_total[inner_rows : inner_rows + rows]
    final[17] = widen(feed_total[inner_rows + rows :])
    final[9] = mid_total[:rows]
    final[5] = mid_total[rows : 2 * rows]
    final[11] = widen(mid_total[2 * rows :])
    final[2] = jnp.concatenate([tree.total for tree in late_trees], axis=1)
    results = give(results, result_gots, 0)
    source_grads = give(source_grads, source_gots, 0)
    return (results[:, None], input_grads[:, None], source_grads[:, None]) + tuple(final)


def solution(mesh):
    in_specs = (
        P(None, "dp", "seq", None),
        P(None, "dp", "seq", None),
        P(None, "dp"),
        P(None, "dp", "seq"),
        P(None, "dp", "seq", None),
        P(),
        P(),
        P(),
        P(),
        P(),
        P(),
        P(),
        P(),
        P(),
        P(),
        P(),
        P(),
        P(),
        P(),
        P(),
        P(),
        P(),
        P(),
        P(),
        P(),
        P(),
    )
    out_specs = (
        P(None, "dp", "seq", None),
        P(None, "dp", "seq", None),
        P(None, "dp", "seq", None),
        P("dp"),
        P("dp"),
        P("dp", None),
        P("dp"),
        P("dp"),
        P("dp", None),
        P("dp"),
        P("dp"),
        P("dp"),
        P("dp", None),
        P("dp"),
        P("dp", None),
        P("dp"),
        P("dp", None),
        P("dp"),
        P("dp"),
        P("dp"),
        P("dp", None),
        P("dp"),
        P("dp", None),
        P("dp"),
    )

    def on_device(*arguments):
        micros = arguments[0].shape[0]
        rows = lax.axis_size("dp")
        pairs = lax.axis_size("seq") == 2 and micros % 2 == 0
        whole = pairs and rows & (rows - 1) == 0
        return (whole_sequences if whole else split_sequences)(*arguments)

    return jax.shard_map(
        on_device, mesh=mesh, in_specs=in_specs, out_specs=out_specs, check_vma=False
    )
```

```python
import functools

import jax
import jax.numpy as jnp
from jax import lax
from jax.experimental import pallas as pl
from jax.experimental.pallas import tpu as pltpu
from jax.sharding import PartitionSpec as P

HEADS = 12
HEAD = 64


epsilon = 1e-05
blocked_score = -1e30


def normed(values, norm_gain, norm_shift):
    center = values - jnp.mean(values, axis=-1, keepdims=True)
    spread = jnp.mean(center * center, axis=-1, keepdims=True)
    return center * lax.rsqrt(spread + epsilon) * norm_gain + norm_shift


def normed_back(values, norm_gain, norm_shift, upstream):
    unused, pullback = jax.vjp(normed, values, norm_gain, norm_shift)
    return pullback(upstream)


def gelu_exact(values):
    return jax.nn.gelu(values, approximate=False)


def project_rows(row_block, weight):
    return jnp.einsum("bpd,de->bpe", row_block, weight, preferred_element_type=jnp.float32)


def project_back(row_block, weight):
    return jnp.einsum("bpe,de->bpd", row_block, weight, preferred_element_type=jnp.float32)


def outer_sum(first_rows, second_rows):
    return jnp.einsum("bpd,bpe->de", first_rows, second_rows, preferred_element_type=jnp.float32)


def split_heads(row_block):
    return row_block.reshape(row_block.shape[0], row_block.shape[1], HEADS, HEAD)


def masked_scores(queries, key_rows, allowed):
    scores = jnp.einsum(
        "bphe,bshe->bhps",
        split_heads(queries),
        split_heads(key_rows),
        preferred_element_type=jnp.float32,
    )
    if allowed is None:
        return scores
    return jnp.where(allowed[:, None], scores, blocked_score)


def attend_forward(queries, key_rows, values, allowed):
    scores = masked_scores(queries, key_rows, allowed)
    highest_score = jnp.max(scores, axis=-1, keepdims=True)
    raised = jnp.exp(scores - highest_score)
    totals = jnp.sum(raised, axis=-1, keepdims=True)
    weights = (raised / totals).astype(jnp.bfloat16)
    mixed = jnp.einsum(
        "bhps,bshe->bphe", weights, split_heads(values), preferred_element_type=jnp.float32
    )
    return (mixed.reshape(queries.shape).astype(jnp.bfloat16), highest_score + jnp.log(totals))


def attend_backward(queries, key_rows, values, allowed, log_totals, upstream):
    weights = jnp.exp(masked_scores(queries, key_rows, allowed) - log_totals)
    upstream_heads = split_heads(upstream)
    value_grads = jnp.einsum(
        "bhps,bphe->bshe",
        weights.astype(jnp.bfloat16),
        upstream_heads,
        preferred_element_type=jnp.float32,
    )
    weight_grads = jnp.einsum(
        "bphe,bshe->bhps", upstream_heads, split_heads(values), preferred_element_type=jnp.float32
    )
    score_grads = weights * (weight_grads - jnp.sum(weight_grads * weights, axis=-1, keepdims=True))
    score_low = score_grads.astype(jnp.bfloat16)
    query_grads = jnp.einsum(
        "bhps,bshe->bphe", score_low, split_heads(key_rows), preferred_element_type=jnp.float32
    ).reshape(queries.shape)
    key_grads = jnp.einsum(
        "bhps,bphe->bshe", score_low, split_heads(queries), preferred_element_type=jnp.float32
    ).reshape(key_rows.shape)
    return (query_grads, jnp.concatenate([key_grads, value_grads.reshape(key_rows.shape)], axis=-1))


def split_sequences(
    targets,
    memory,
    row_kind,
    loss_mask,
    cotangent,
    norm_self_gain,
    norm_self_bias,
    self_input,
    self_query_bias,
    self_value_bias,
    self_output,
    self_output_bias,
    norm_cross_gain,
    norm_cross_bias,
    cross_query,
    cross_query_bias,
    cross_input,
    cross_value_bias,
    cross_output,
    cross_output_bias,
    norm_feed_gain,
    norm_feed_bias,
    feed_in,
    feed_in_bias,
    feed_out,
    feed_out_bias,
):
    model_width = targets.shape[3]
    part_rows = targets.shape[2]
    key_span = part_rows * lax.axis_size("seq")
    query_scale = HEAD ** (-0.5)
    places = lax.axis_index("seq") * part_rows + jnp.arange(part_rows)
    causal = jnp.arange(key_span)[None, :] <= places[:, None]
    results, input_grads, source_grads = ([], [], [])
    totals = None
    for micro_index in range(targets.shape[0]):
        inputs = targets[micro_index].astype(jnp.float32)
        memory_local = memory[micro_index]
        allowed = causal[None] | (row_kind[micro_index] == 1)[:, None, None]
        first_normed = normed(inputs, norm_self_gain, norm_self_bias).astype(jnp.bfloat16)
        self_joint = project_rows(first_normed, self_input)
        queries = ((self_joint[..., :model_width] + self_query_bias) * query_scale).astype(
            jnp.bfloat16
        )
        own_pairs = jnp.concatenate(
            [
                self_joint[..., model_width : 2 * model_width],
                self_joint[..., 2 * model_width :] + self_value_bias,
            ],
            axis=-1,
        ).astype(jnp.bfloat16)
        gathered_self = lax.all_gather(own_pairs, "seq", axis=1, tiled=True)
        key_rows = gathered_self[..., :model_width]
        value_rows = gathered_self[..., model_width:]
        self_mixed, self_totals = attend_forward(queries, key_rows, value_rows, allowed)
        after_self = inputs + project_rows(self_mixed, self_output) + self_output_bias
        second_normed = normed(after_self, norm_cross_gain, norm_cross_bias).astype(jnp.bfloat16)
        cross_queries = (
            (project_rows(second_normed, cross_query) + cross_query_bias) * query_scale
        ).astype(jnp.bfloat16)
        joined = project_rows(lax.all_gather(memory_local, "seq", axis=1, tiled=True), cross_input)
        gathered_cross = jnp.concatenate(
            [joined[..., :model_width], joined[..., model_width:] + cross_value_bias], axis=-1
        ).astype(jnp.bfloat16)
        cross_keys = gathered_cross[..., :model_width]
        cross_values = gathered_cross[..., model_width:]
        cross_mixed, cross_totals = attend_forward(cross_queries, cross_keys, cross_values, None)
        after_cross = after_self + project_rows(cross_mixed, cross_output) + cross_output_bias
        third_normed = normed(after_cross, norm_feed_gain, norm_feed_bias).astype(jnp.bfloat16)
        activated, gelu_pullback = jax.vjp(
            gelu_exact, project_rows(third_normed, feed_in) + feed_in_bias
        )
        activated_low = activated.astype(jnp.bfloat16)
        results.append(
            (after_cross + project_rows(activated_low, feed_out) + feed_out_bias).astype(
                jnp.bfloat16
            )
        )
        pieces = [None] * 21
        grad_output = (
            cotangent[micro_index].astype(jnp.float32)
            * loss_mask[micro_index].astype(jnp.float32)[..., None]
        )
        output_low = grad_output.astype(jnp.bfloat16)
        pieces[19] = outer_sum(activated_low, output_low)
        pieces[20] = jnp.sum(grad_output, axis=(0, 1))
        grad_hidden = gelu_pullback(project_back(output_low, feed_out))[0]
        hidden_low = grad_hidden.astype(jnp.bfloat16)
        pieces[17] = outer_sum(third_normed, hidden_low)
        pieces[18] = jnp.sum(grad_hidden, axis=(0, 1))
        through_feed, pieces[15], pieces[16] = normed_back(
            after_cross, norm_feed_gain, norm_feed_bias, project_back(hidden_low, feed_in)
        )
        grad_cross = grad_output + through_feed
        cross_low = grad_cross.astype(jnp.bfloat16)
        pieces[13] = outer_sum(cross_mixed, cross_low)
        pieces[14] = jnp.sum(grad_cross, axis=(0, 1))
        cross_upstream = project_back(cross_low, cross_output).astype(jnp.bfloat16)
        cross_query_grads, cross_pair_grads = attend_backward(
            cross_queries, cross_keys, cross_values, None, cross_totals, cross_upstream
        )
        own_cross = lax.psum_scatter(
            cross_pair_grads.astype(jnp.bfloat16), "seq", scatter_dimension=1, tiled=True
        ).astype(jnp.float32)
        pieces[12] = jnp.sum(own_cross[..., model_width:], axis=(0, 1))
        own_cross_low = own_cross.astype(jnp.bfloat16)
        pieces[11] = outer_sum(memory_local, own_cross_low)
        source_grads.append(project_back(own_cross_low, cross_input))
        scaled_cross = cross_query_grads * query_scale
        pieces[10] = jnp.sum(scaled_cross, axis=(0, 1))
        scaled_cross_low = scaled_cross.astype(jnp.bfloat16)
        pieces[9] = outer_sum(second_normed, scaled_cross_low)
        through_cross, pieces[7], pieces[8] = normed_back(
            after_self,
            norm_cross_gain,
            norm_cross_bias,
            project_back(scaled_cross_low, cross_query),
        )
        grad_self = grad_cross + through_cross
        self_low = grad_self.astype(jnp.bfloat16)
        pieces[5] = outer_sum(self_mixed, self_low)
        pieces[6] = jnp.sum(grad_self, axis=(0, 1))
        self_upstream = project_back(self_low, self_output).astype(jnp.bfloat16)
        self_query_grads, self_pair_grads = attend_backward(
            queries, key_rows, value_rows, allowed, self_totals, self_upstream
        )
        own_self = lax.psum_scatter(
            self_pair_grads.astype(jnp.bfloat16), "seq", scatter_dimension=1, tiled=True
        ).astype(jnp.float32)
        scaled_self = self_query_grads * query_scale
        pieces[3] = jnp.sum(scaled_self, axis=(0, 1))
        pieces[4] = jnp.sum(own_self[..., model_width:], axis=(0, 1))
        joint_low = jnp.concatenate([scaled_self, own_self], axis=-1).astype(jnp.bfloat16)
        pieces[2] = outer_sum(first_normed, joint_low)
        through_first, pieces[0], pieces[1] = normed_back(
            inputs, norm_self_gain, norm_self_bias, project_back(joint_low, self_input)
        )
        input_grads.append(grad_self + through_first)
        totals = (
            pieces
            if totals is None
            else [running + added for running, added in zip(totals, pieces)]
        )
    def reduced(total):
        block = lax.psum_scatter(
            total.astype(jnp.bfloat16), "dp", scatter_dimension=0, tiled=True
        )
        return lax.psum(block, "seq").astype(jnp.float32)

    final = [reduced(total) for total in totals]
    return (jnp.stack(results), jnp.stack(input_grads), jnp.stack(source_grads)) + tuple(final)


def contract(first, second, first_dim, second_dim):
    return lax.dot_general(
        first, second, (((first_dim,), (second_dim,)), ((), ())), preferred_element_type=jnp.float32
    )


def head_masks(pair):
    lane = lax.broadcasted_iota(jnp.int32, (1, pair.shape[1]), 1)
    zero = jnp.zeros((), pair.dtype)
    return (jnp.where(lane < HEAD, pair, zero), jnp.where(lane < HEAD, zero, pair))


LIMIT = 62 * 2**20


def attend_kernel(info_ref, q_ref, k_ref, v_ref, *refs, use_mask, start):
    o_ref, e_ref, r_ref, mask_ref = refs[-4:]
    length = k_ref.shape[1]
    half = length // 2
    values_turned = v_ref[0].T
    ones = jnp.ones((16, length), jnp.bfloat16)

    def run(masked, shifted):
        lowest, highest = None, None
        for at in range(2):
            queries_at = slice(at * half, (at + 1) * half)
            mixed = []
            for head, queries in enumerate(head_masks(q_ref[0, queries_at, :])):
                scores = contract(k_ref[0], queries, 1, 1)
                if shifted:
                    if masked:
                        seen = mask_ref[:, queries_at].astype(jnp.float32) > 0
                        scores = jnp.where(seen, scores, blocked_score)
                    scores = scores - jnp.max(scores, axis=0, keepdims=True)
                low = jnp.exp(scores).astype(jnp.bfloat16)
                if masked:
                    low = low * mask_ref[:, queries_at]
                e_ref[0, head, :, queries_at] = low
                turned = jnp.concatenate(
                    [values_turned[head * HEAD : (head + 1) * HEAD], ones], axis=0
                )
                sums = contract(turned, low, 1, 0)
                total = sums[HEAD : HEAD + 1]
                if not shifted:
                    lowest = total if lowest is None else jnp.minimum(lowest, total)
                    highest = total if highest is None else jnp.maximum(highest, total)
                inverse = 1.0 / total
                r_ref[0, 0, head : head + 1, queries_at] = inverse
                mixed.append(sums[:HEAD] * inverse)
            o_ref[0, queries_at, :] = jnp.concatenate(mixed, axis=0).T.astype(jnp.bfloat16)
        if not shifted:
            in_range = (jnp.min(lowest) > 1e-20) & (jnp.max(highest) < 1e30)

            @pl.when(jnp.logical_not(in_range))
            def _():
                run(masked, True)

    if not use_mask:
        run(False, False)
        return
    causal = info_ref[2 + start + pl.program_id(0)] == 0

    @pl.when(causal & (pl.program_id(1) == 0))
    def _():
        later = info_ref[0] * half
        query = lax.broadcasted_iota(jnp.int32, (1, length), 1)
        query = jnp.where(query < half, query + later, query - later)

        @pl.loop(0, length, step=64)
        def _(row):
            key = lax.broadcasted_iota(jnp.int32, (64, 1), 0) + row
            key = jnp.where(key < half, key + later, key - later)
            seen = jnp.where(key <= query, 1.0, 0.0)
            mask_ref[pl.ds(pl.multiple_of(row, 64), 64), :] = seen.astype(jnp.bfloat16)

    @pl.when(causal)
    def _():
        run(True, False)

    @pl.when(jnp.logical_not(causal))
    def _():
        run(False, False)


def attend(info, start, count_now, previous, queries, keys, values, use_mask, offsets):
    count, length = queries.shape[:2]
    pairs = HEADS * HEAD // 128
    width = HEADS * HEAD

    def spec(offset):
        return pl.BlockSpec((1, length, 128), lambda s, p, info: (start + s, 0, offset * pairs + p))

    place = lambda s, p, info: (start + s, p, 0, 0)
    return pl.pallas_call(
        functools.partial(attend_kernel, use_mask=use_mask, start=start),
        grid_spec=pltpu.PrefetchScalarGridSpec(
            num_scalar_prefetch=1,
            grid=(count_now, pairs),
            in_specs=[spec(offset) for offset in offsets]
            + [pl.BlockSpec(memory_space=pl.ANY)] * len(previous),
            out_specs=[
                spec(0),
                pl.BlockSpec((1, 2, length, length), place),
                pl.BlockSpec((1, 1, 2, length), place),
            ],
            scratch_shapes=[pltpu.VMEM((length, length), jnp.bfloat16)],
        ),
        out_shape=[
            jax.ShapeDtypeStruct((count, length, width), jnp.bfloat16),
            jax.ShapeDtypeStruct((count, HEADS, length, length), jnp.bfloat16),
            jax.ShapeDtypeStruct((count, pairs, 2, length), jnp.float32),
        ],
        input_output_aliases={4: 0, 5: 1, 6: 2} if previous else {},
        compiler_params=pltpu.CompilerParams(vmem_limit_bytes=LIMIT),
        cost_estimate=pl.CostEstimate(
            flops=4 * count_now * HEADS * length * length * 256,
            bytes_accessed=count_now * HEADS * length * length * 2,
            transcendentals=count_now * HEADS * length * length,
        ),
        name="attend",
    )(info, queries, keys, values, *previous)


def attend_back_kernel(q_ref, k_ref, v_ref, o_ref, g_ref, e_ref, r_ref, dq_ref, dk_ref, dv_ref):
    length = k_ref.shape[1]
    keys_turned = k_ref[0].T
    upstream = g_ref[0].astype(jnp.float32)
    products = (o_ref[0].astype(jnp.float32) * upstream).T
    upstream = upstream.T
    parts, deltas = [], []
    for head in range(2):
        rows = slice(head * HEAD, (head + 1) * HEAD)
        inverse = r_ref[0, 0, head : head + 1, :]
        parts.append(upstream[rows] * inverse)
        deltas.append(jnp.sum(products[rows], axis=0, keepdims=True) * inverse)
    scaled = head_masks(jnp.concatenate(parts, axis=0).T.astype(jnp.bfloat16))
    queries = head_masks(q_ref[0])
    key_sum, value_sum, query_parts = 0.0, 0.0, []
    for head in range(2):
        rows = slice(head * HEAD, (head + 1) * HEAD)
        low = e_ref[0, head]
        grads = contract(v_ref[0], scaled[head], 1, 1)
        score_low = (low.astype(jnp.float32) * (grads - deltas[head])).astype(jnp.bfloat16)
        value_sum += contract(low, scaled[head], 1, 0)
        key_sum += contract(score_low, queries[head], 1, 0)
        query_parts.append(contract(keys_turned[rows], score_low, 1, 0))
    turned = jnp.concatenate(query_parts, axis=0) * (HEAD**-0.5)
    dq_ref[0] = turned.T.astype(jnp.bfloat16)
    dk_ref[0] = key_sum.astype(jnp.bfloat16)
    dv_ref[0] = value_sum.astype(jnp.bfloat16)


def attend_back(place, size, previous, queries, keys, values, offsets, *rest):
    count, length = queries.shape[:2]
    pairs = HEADS * HEAD // 128
    width = HEADS * HEAD

    start, first = place

    def spec(offset):
        return pl.BlockSpec(
            (1, length, 128), lambda s, p: (start + s, 0, offset * pairs + first + p)
        )

    kernel = attend_back_kernel
    aliases = {}
    if previous:
        kernel = lambda *refs: attend_back_kernel(*refs[3:])
        aliases = {0: 0, 1: 1, 2: 2}
    return pl.pallas_call(
        kernel,
        grid=size,
        in_specs=[pl.BlockSpec(memory_space=pl.ANY)] * len(previous)
        + [spec(offset) for offset in offsets]
        + [
            spec(0),
            spec(0),
            pl.BlockSpec((1, 2, length, length), lambda s, p: (start + s, first + p, 0, 0)),
            pl.BlockSpec((1, 1, 2, length), lambda s, p: (start + s, first + p, 0, 0)),
        ],
        out_specs=[spec(0)] * 3,
        out_shape=[jax.ShapeDtypeStruct((count, length, width), jnp.bfloat16)] * 3,
        input_output_aliases=aliases,
        compiler_params=pltpu.CompilerParams(vmem_limit_bytes=LIMIT),
        cost_estimate=pl.CostEstimate(
            flops=16 * size[0] * size[1] * length * length * 256,
            bytes_accessed=4 * size[0] * size[1] * length * length,
            transcendentals=0,
        ),
        name="attend_back",
    )(*previous, queries, keys, values, *rest)


def normal_parts(values):
    center = values - jnp.mean(values, axis=-1, keepdims=True)
    inverse = lax.rsqrt(jnp.mean(center * center, axis=-1, keepdims=True) + epsilon)
    return center * inverse, inverse


def normal_back(unit, inverse, norm_gain, upstream):
    inner = upstream * norm_gain
    shift = jnp.mean(inner, axis=-1, keepdims=True)
    tilt = jnp.mean(inner * unit, axis=-1, keepdims=True)
    return inverse * (inner - shift - unit * tilt)


def gelu_parts(values):
    size = jnp.abs(values)
    ratio = 1.0 / (1.0 + 0.2316418882663604 * size)
    series = 0.5307027145
    for weight in (-0.7265760135, 0.7107068705, -0.142248368, 0.127414796):
        series = series * ratio + weight
    bell = jnp.exp(-0.5 * values * values)
    upper = series * ratio * bell
    chance = jnp.where(values < 0, upper, 1.0 - upper)
    return values * chance, chance + values * (0.3989422804014327 * bell)


def column_sum(values):
    return jnp.sum(values, axis=0, keepdims=True)


def resident(array):
    return pl.BlockSpec(array.shape, lambda *_: (0,) * array.ndim, pipeline_mode=pl.Buffered(1))


def whole_block(array):
    return pl.BlockSpec(array.shape, lambda *_: (0,) * len(array.shape))


def like(shape, dtype=jnp.float32):
    return jax.ShapeDtypeStruct(tuple(shape), dtype)


def pick(take_first, first_ref, second_ref):
    return jnp.where(take_first, first_ref[...], second_ref[...])


ONCE = {"pipeline_mode": pl.Buffered(1)}


def own_spec(own, width, held, last, **more):
    def place(step, info):
        return (info[0] * held + jnp.minimum(step, last) // 2, 0, 0)

    return pl.BlockSpec((None, own, width), place, **more)


def got_spec(own, width, last, **more):
    return pl.BlockSpec(
        (None, own, width), lambda step, info: (jnp.minimum(step, last) // 2, 0, 0), **more
    )


def row_spec(own, width, last, **more):
    return pl.BlockSpec((own, width), lambda step, info: (jnp.minimum(step, last), 0), **more)


def kernel_call(kernel, name, info, arrays, in_specs, outs, out_specs, grid, flops, moved, **more):
    scratch = more.pop("scratch", [])
    return pl.pallas_call(
        kernel,
        grid_spec=pltpu.PrefetchScalarGridSpec(
            num_scalar_prefetch=1,
            grid=(grid,),
            in_specs=in_specs,
            out_specs=out_specs,
            scratch_shapes=scratch,
        ),
        out_shape=outs,
        compiler_params=pltpu.CompilerParams(
            vmem_limit_bytes=more.pop("limit", LIMIT)
        ),
        cost_estimate=pl.CostEstimate(flops=flops, bytes_accessed=moved, transcendentals=0),
        name=name,
        **more,
    )(info, *arrays)


def enter_kernel(info_ref, own_ref, got_ref, w_ref, vec_ref, bias_ref, *refs, norm):
    x_ref, out_ref = refs[-2:]
    x = pick(pl.program_id(0) % 2 == 0, own_ref, got_ref)
    x_ref[...] = x
    if norm:
        unit, _ = normal_parts(x.astype(jnp.float32))
        x = (unit * vec_ref[0:1, :] + vec_ref[1:2, :]).astype(jnp.bfloat16)
    width = x.shape[1]
    for start in range(0, w_ref.shape[1], width):
        part = slice(start, start + width)
        total = contract(x, w_ref[:, part], 1, 0) + bias_ref[:, part]
        if norm and start == 0:
            total = total * (HEAD**-0.5)
        out_ref[:, part] = total.astype(jnp.bfloat16)


def enter(info, at, previous, held, owns, gots, weight, vectors, bias, norm):
    count, own, width = gots.shape
    rows = 2 * held * own
    wide = weight.shape[1]
    own_rows = pl.BlockSpec(
        (None, own, width), lambda step, info: (info[0] * held + at + step // 2, 0, 0)
    )
    row = lambda step, info: (2 * at + step, 0)
    return kernel_call(
        functools.partial(enter_kernel, norm=norm),
        "enter",
        info,
        (owns, gots, weight, vectors, bias, *previous),
        [own_rows, got_spec(own, width, 2 * count - 1)]
        + [resident(a) for a in (weight, vectors, bias)]
        + [pl.BlockSpec(memory_space=pl.ANY)] * len(previous),
        [like((rows, width), jnp.bfloat16), like((rows, wide), jnp.bfloat16)],
        [pl.BlockSpec((own, width), row), pl.BlockSpec((own, wide), row)],
        2 * count,
        4 * count * own * width * wide,
        4 * count * own * (2 * width + wide),
        input_output_aliases={6: 0, 7: 1} if previous else {},
    )


def middle_kernel(info_ref, x_ref, mixed_ref, wo_ref, wq_ref, vec_ref, after_ref, q_ref):
    out_bias, gain, shift, query_bias = (vec_ref[i : i + 1, :] for i in range(4))
    after = (
        x_ref[...].astype(jnp.float32) + contract(mixed_ref[...], wo_ref[...], 1, 0) + out_bias
    )
    after_ref[...] = after
    unit, _ = normal_parts(after)
    normal = (unit * gain + shift).astype(jnp.bfloat16)
    queries = (contract(normal, wq_ref[...], 1, 0) + query_bias) * (HEAD**-0.5)
    q_ref[...] = queries.astype(jnp.bfloat16)


def middle(info, x, mixed, wo, wq, vectors, own):
    rows, width = x.shape
    last = rows // own - 1
    spec = row_spec(own, width, last)
    return kernel_call(
        middle_kernel,
        "middle",
        info,
        (x, mixed, wo, wq, vectors),
        [spec, spec] + [resident(a) for a in (wo, wq, vectors)],
        [like((rows, width)), like((rows, width), jnp.bfloat16)],
        [spec, spec],
        rows // own,
        4 * rows * width * width,
        10 * rows * width,
    )


def write_split(core, rows, kept_ref, sent_ref, start):
    half = rows.shape[0] // 2
    low = rows.astype(jnp.bfloat16)
    place = slice(start, start + half)

    @pl.when(core == 0)
    def _():
        kept_ref[0, place, :] = low[:half]
        sent_ref[0, place, :] = low[half:]

    @pl.when(core != 0)
    def _():
        kept_ref[0, place, :] = low[half:]
        sent_ref[0, place, :] = low[:half]


def write_wide(core, rows, kept_ref, sent_ref, start):
    half, width = rows.shape[0] // 2, kept_ref.shape[2]
    for at in range(rows.shape[1] // width):
        part = rows[:, at * width : (at + 1) * width]
        write_split(core, part, kept_ref, sent_ref, start + at * half)


def acc_rows(ref, at, rows):
    return ref[pl.ds(pl.multiple_of(at * rows, 16), rows), :]


def piece(parts, high, wide, steps, order):
    bits = parts.bit_length() - 2

    def late(step, info):
        at = jnp.maximum(step - steps, 0)
        place = 0
        for bit in order(bits):
            place = 2 * place + (at // 2**bit) % 2
        return (place, 0, 0)

    return (
        [pl.BlockSpec((1, high, wide), late)] * 2,
        [like((parts // 2, high, wide), jnp.bfloat16)] * 2,
    )


def low_first(bits):
    return list(range(bits))


def second_first(bits):
    return list(range(bits))[1:2] + [0] + list(range(2, bits))


def put_rows(step, value, own_ref, got_ref):
    @pl.when(step % 2 == 0)
    def _():
        own_ref[...] = value.astype(own_ref.dtype)

    @pl.when(step % 2 != 0)
    def _():
        got_ref[...] = value.astype(got_ref.dtype)


def feed_kernel(
    info_ref, x_ref, mixed_ref, dyo_ref, dyg_ref, wc_ref, wi_ref, wo_ref, vec_ref, bi_ref,
    own_ref, got_ref, dx_ref, do_ref, vsum_ref, bsum_ref, kept_ref, sent_ref, ai_ref, ao_ref,
    ac_ref, *, steps, chunk, parts,
):
    step = pl.program_id(0)

    @pl.when(step == 0)
    def _():
        for ref in (vsum_ref, bsum_ref, ai_ref, ao_ref, ac_ref):
            ref[...] = jnp.zeros_like(ref)

    @pl.when(step < steps)
    def _():
        cross_bias, gain, shift, out_bias = (vec_ref[i : i + 1, :] for i in range(4))
        mixed = mixed_ref[...]
        x2 = x_ref[...] + contract(mixed, wc_ref[...], 1, 0) + cross_bias
        unit, inverse = normal_parts(x2)
        normal = (unit * gain + shift).astype(jnp.bfloat16)
        normal_turned = normal.T
        dy = pick(step % 2 == 0, dyo_ref, dyg_ref)
        dy_turned = dy.T
        result, upstream = None, None
        for start in range(0, wi_ref.shape[1], chunk):
            part = slice(start, start + chunk)
            hidden = contract(normal, wi_ref[:, part], 1, 0) + bi_ref[:, part]
            active, slope = gelu_parts(hidden)
            active = active.astype(jnp.bfloat16)
            down = contract(active, wo_ref[part, :], 1, 0)
            result = down if result is None else result + down
            grads = contract(dy, wo_ref[part, :], 1, 1) * slope
            bsum_ref[:, part] += column_sum(grads)
            low = grads.astype(jnp.bfloat16)
            up = contract(low, wi_ref[:, part], 1, 1)
            upstream = up if upstream is None else upstream + up
            ao_ref[:, part] += contract(dy_turned, active, 1, 0)
            ai_ref[:, part] += contract(normal_turned, low, 1, 0)
        put_rows(step, x2 + result + out_bias, own_ref, got_ref)
        wide = dy.astype(jnp.float32)
        dx = wide + normal_back(unit, inverse, gain, upstream)
        dx_ref[...] = dx
        dx_low = dx.astype(jnp.bfloat16)
        do_ref[...] = contract(dx_low, wc_ref[...], 1, 1).astype(jnp.bfloat16)
        ac_ref[...] += contract(mixed.T, dx_low, 1, 0)
        vsum_ref[0:1, :] += column_sum(dx)
        vsum_ref[1:2, :] += column_sum(upstream * unit)
        vsum_ref[2:3, :] += column_sum(upstream)
        vsum_ref[3:4, :] += column_sum(wide)

    @pl.when(step >= steps)
    def _():
        at = step - steps
        core = info_ref[1]
        width, wide = ai_ref.shape
        rows = 2 * width // parts
        inner = 2 * wide // parts
        columns = ao_ref[:, pl.ds(pl.multiple_of(at * inner, 128), inner)]
        write_split(core, columns.astype(jnp.bfloat16).T, kept_ref, sent_ref, 0)
        write_split(core, acc_rows(ac_ref, at, rows), kept_ref, sent_ref, inner // 2)
        write_wide(core, acc_rows(ai_ref, at, rows), kept_ref, sent_ref, (inner + rows) // 2)


def feed(info, x1, mixed, dys, dy_gots, wc, wi, wo, vectors, bi, parts, chunk=768):
    rows, width = x1.shape
    held, own = dy_gots.shape[:2]
    micros = dys.shape[0]
    inner = wi.shape[1]
    steps = 2 * held
    last = steps - 1
    row = row_spec(own, width, last)
    pieces = [piece(parts, (2 * inner + width) // parts, width, steps, low_first)]
    sums = [like((8, width)), like((1, inner))]
    return kernel_call(
        functools.partial(feed_kernel, steps=steps, chunk=chunk, parts=parts),
        "feed",
        info,
        (x1, mixed, dys, dy_gots, wc, wi, wo, vectors, bi),
        [row_spec(own, width, last, **ONCE)] * 2
        + [own_spec(own, width, held, last, **ONCE), got_spec(own, width, last, **ONCE)]
        + [resident(a) for a in (wc, wi, wo, vectors, bi)],
        [
            like((micros, own, width), jnp.bfloat16),
            like((held, own, width), jnp.bfloat16),
            like((rows, width)),
            like((rows, width), jnp.bfloat16),
        ]
        + sums
        + sum([p[1] for p in pieces], []),
        [own_spec(own, width, held, last), got_spec(own, width, last), row, row]
        + [whole_block(a) for a in sums]
        + sum([p[0] for p in pieces], []),
        steps + parts // 2,
        2 * rows * width * (6 * inner + 3 * width),
        60 * 2**20,
        scratch=[
            pltpu.VMEM((width, inner), jnp.float32),
            pltpu.VMEM((width, inner), jnp.float32),
            pltpu.VMEM((width, width), jnp.float32),
        ],
        limit=LIMIT,
    )


def return_kernel(
    info_ref, dq_ref, dk_ref, dv_ref, x_ref, dx_ref, mixed_ref, src_ref, wq_ref, wi_ref, wo_ref,
    vec_ref, own_ref, got_ref, dxo_ref, do_ref, vsum_ref, kept_ref, sent_ref, aq_ref, ao_ref,
    ai_ref, *, steps, parts,
):
    step = pl.program_id(0)

    @pl.when(step == 0)
    def _():
        for ref in (vsum_ref, aq_ref, ao_ref, ai_ref):
            ref[...] = jnp.zeros_like(ref)

    @pl.when(step < steps)
    def _():
        width = x_ref.shape[1]
        gain, shift = vec_ref[0:1, :], vec_ref[1:2, :]
        dq, dk, dv = dq_ref[...], dk_ref[...], dv_ref[...]
        upstream = contract(dq, wq_ref[...], 1, 1)
        unit, inverse = normal_parts(x_ref[...])
        normal = (unit * gain + shift).astype(jnp.bfloat16)
        dx = dx_ref[...] + normal_back(unit, inverse, gain, upstream)
        dxo_ref[...] = dx
        low = dx.astype(jnp.bfloat16)
        do_ref[...] = contract(low, wo_ref[...], 1, 1).astype(jnp.bfloat16)
        source = contract(dk, wi_ref[:, :width], 1, 1) + contract(dv, wi_ref[:, width:], 1, 1)
        put_rows(step, source, own_ref, got_ref)
        aq_ref[...] += contract(normal.T, dq, 1, 0)
        ao_ref[...] += contract(mixed_ref[...].T, low, 1, 0)
        turned = src_ref[...].T
        ai_ref[:, :width] += contract(turned, dk, 1, 0)
        ai_ref[:, width:] += contract(turned, dv, 1, 0)
        vsum_ref[0:1, :] += column_sum(upstream * unit)
        vsum_ref[1:2, :] += column_sum(upstream)
        vsum_ref[2:3, :] += column_sum(dx)
        vsum_ref[3:4, :] += column_sum(dq.astype(jnp.float32))
        vsum_ref[4:5, :] += column_sum(dv.astype(jnp.float32))

    @pl.when(step >= steps)
    def _():
        at = step - steps
        core = info_ref[1]
        rows = 2 * aq_ref.shape[0] // parts
        write_split(core, acc_rows(aq_ref, at, rows), kept_ref, sent_ref, 0)
        write_split(core, acc_rows(ao_ref, at, rows), kept_ref, sent_ref, rows // 2)
        write_wide(core, acc_rows(ai_ref, at, rows), kept_ref, sent_ref, rows)


def return_rows(info, grads, x1, dx2, mixed, sources, wq, wi, wo, vectors, own, micros, parts):
    rows, width = x1.shape
    held = rows // own // 2
    steps = 2 * held
    last = steps - 1
    row = row_spec(own, width, last)
    pieces = [piece(parts, 4 * width // parts, width, steps, low_first)]
    sums = like((8, width))
    return kernel_call(
        functools.partial(return_kernel, steps=steps, parts=parts),
        "return_rows",
        info,
        (*grads, x1, dx2, mixed, sources, wq, wi, wo, vectors),
        [row] * 7 + [resident(a) for a in (wq, wi, wo, vectors)],
        [
            like((micros, own, width)),
            like((held, own, width), jnp.bfloat16),
            like((rows, width)),
            like((rows, width), jnp.bfloat16),
            sums,
        ]
        + sum([p[1] for p in pieces], []),
        [own_spec(own, width, held, last), got_spec(own, width, last), row, row, whole_block(sums)]
        + sum([p[0] for p in pieces], []),
        steps + parts // 2,
        16 * rows * width * width,
        40 * 2**20,
        scratch=[
            pltpu.VMEM((width, width), jnp.float32),
            pltpu.VMEM((width, width), jnp.float32),
            pltpu.VMEM((width, 2 * width), jnp.float32),
        ],
    )


def last_weight_kernel(
    info_ref, dq_ref, dk_ref, dv_ref, x_ref, vec_ref, ka_ref, sa_ref, kb_ref, sb_ref, acc_ref,
    *, steps,
):
    step = pl.program_id(0)

    @pl.when(step == 0)
    def _():
        acc_ref[...] = jnp.zeros_like(acc_ref)

    @pl.when(step < steps)
    def _():
        unit, _ = normal_parts(x_ref[...].astype(jnp.float32))
        turned = (unit * vec_ref[0:1, :] + vec_ref[1:2, :]).astype(jnp.bfloat16).T
        width = x_ref.shape[1]
        for at, ref in enumerate((dq_ref, dk_ref, dv_ref)):
            acc_ref[:, at * width : (at + 1) * width] += contract(turned, ref[...], 1, 0)

    @pl.when(step >= steps)
    def _():
        rows = acc_rows(acc_ref, step - steps, 2 * ka_ref.shape[1])
        half = ka_ref.shape[2]
        write_split(info_ref[1], rows[:, :half], ka_ref, sa_ref, 0)
        write_split(info_ref[1], rows[:, half:], kb_ref, sb_ref, 0)


def last_weight(info, grads, x, vectors, own, parts):
    rows, width = x.shape
    steps = rows // own
    row = row_spec(own, width, steps - 1)
    pieces = [
        piece(parts, width // parts, 3 * width // 2, steps, order)
        for order in (low_first, second_first)
    ]
    return kernel_call(
        functools.partial(last_weight_kernel, steps=steps),
        "last_weight",
        info,
        (*grads, x, vectors),
        [row] * 4 + [resident(vectors)],
        sum([p[1] for p in pieces], []),
        sum([p[0] for p in pieces], []),
        steps + parts // 2,
        6 * rows * width * width,
        20 * 2**20,
        scratch=[pltpu.VMEM((width, 3 * width), jnp.float32)],
    )


def leave_kernel(
    info_ref, dq_ref, dk_ref, dv_ref, x_ref, dx_ref, w_ref, vec_ref, *refs
):
    own_ref, got_ref, vsum_ref = refs[-3:]
    step = pl.program_id(0)

    @pl.when(step == 0)
    def _():
        vsum_ref[...] = jnp.zeros_like(vsum_ref)

    width = x_ref.shape[1]
    dq, dk, dv = dq_ref[...], dk_ref[...], dv_ref[...]
    upstream = (
        contract(dq, w_ref[:, :width], 1, 1)
        + contract(dk, w_ref[:, width : 2 * width], 1, 1)
        + contract(dv, w_ref[:, 2 * width :], 1, 1)
    )
    unit, inverse = normal_parts(x_ref[...].astype(jnp.float32))
    dx = dx_ref[...] + normal_back(unit, inverse, vec_ref[0:1, :], upstream)
    put_rows(step, dx, own_ref, got_ref)
    vsum_ref[0:1, :] += column_sum(upstream * unit)
    vsum_ref[1:2, :] += column_sum(upstream)
    vsum_ref[2:3, :] += column_sum(dq.astype(jnp.float32))
    vsum_ref[3:4, :] += column_sum(dv.astype(jnp.float32))


def leave(info, at, previous, grads, x, dx1, weight, vectors, own, micros):
    rows, width = x.shape
    held = rows // own // 2
    row = pl.BlockSpec((own, width), lambda step, info: (2 * at + step, 0))
    more = {"input_output_aliases": {8: 0}} if previous else {}
    sums = like((8, width))
    return kernel_call(
        leave_kernel,
        "leave",
        info,
        (*grads, x, dx1, weight, vectors, *previous),
        [row] * 5
        + [resident(a) for a in (weight, vectors)]
        + [pl.BlockSpec(memory_space=pl.ANY)] * len(previous),
        [like((micros, own, width)), like((own, width), jnp.bfloat16), sums],
        [
            pl.BlockSpec((None, own, width), lambda step, info: (info[0] * held + at, 0, 0)),
            pl.BlockSpec((own, width), lambda step, info: (0, 0)),
            whole_block(sums),
        ],
        2,
        12 * own * width * width,
        16 * 2**20,
        **more,
    )


SWAP = ((0, 1), (1, 0))


class Tree:
    def __init__(self, kept, sent, order):
        self.count = lax.axis_size("dp")
        bits = self.count.bit_length() - 2
        shape = (2,) * bits + kept.shape[1:]
        self.order = [2 << bit for bit in order(bits)]
        self.kept, self.sent, self.bit = kept.reshape(shape), sent.reshape(shape), 1
        self.got, self.total = None, None

    def exchange(self):
        if self.total is not None or self.got is not None:
            return
        if self.bit:
            pairs = [(i, i ^ self.bit) for i in range(self.count)]
            self.got = lax.ppermute(self.sent, "dp", pairs)
        else:
            self.got = lax.ppermute(self.kept, "seq", SWAP)

    def add(self):
        if self.got is None:
            return
        total = self.kept.astype(jnp.float32) + self.got.astype(jnp.float32)
        self.got = None
        if not self.bit:
            self.total = total
            return
        total = total.astype(jnp.bfloat16)
        if not self.order:
            self.bit, self.kept = 0, total
            return
        self.bit = self.order.pop(0)
        mine = (lax.axis_index("dp") // self.bit) % 2
        self.kept = lax.dynamic_index_in_dim(total, mine, 0, keepdims=False)
        self.sent = lax.dynamic_index_in_dim(total, 1 - mine, 0, keepdims=False)


class Whole:
    def __init__(self, rows):
        self.count = lax.axis_size("dp")
        self.rows, self.bit, self.got, self.total = rows, 1, None, None

    def exchange(self):
        if self.total is not None or self.got is not None:
            return
        if self.bit < self.count:
            steps = [step * self.bit for step in (1, 2, 3) if step * self.bit < self.count]
            self.got = [
                lax.ppermute(self.rows, "dp", [(i, i ^ step) for i in range(self.count)])
                for step in steps
            ]
        else:
            self.got = [lax.ppermute(self.rows, "seq", SWAP)]

    def add(self):
        if self.got is None:
            return
        self.rows = sum(self.got, self.rows)
        self.got = None
        if self.bit >= self.count:
            self.total = self.rows
        self.bit *= 4


def exchange(trees):
    for tree in trees:
        tree.exchange()


def settle(trees, values):
    trees = [tree for tree in trees if tree.got is not None]
    gots, values = lax.optimization_barrier(([tree.got for tree in trees], values))
    for tree, got in zip(trees, gots):
        tree.got = got
        tree.add()
    return values


def finish(trees):
    while any(tree.total is None for tree in trees):
        exchange(trees)
        settle(trees, ())


def whole_sequences(
    targets,
    memory,
    row_kind,
    loss_mask,
    cotangent,
    norm_self_gain,
    norm_self_bias,
    self_input,
    self_query_bias,
    self_value_bias,
    self_output,
    self_output_bias,
    norm_cross_gain,
    norm_cross_bias,
    cross_query,
    cross_query_bias,
    cross_input,
    cross_value_bias,
    cross_output,
    cross_output_bias,
    norm_feed_gain,
    norm_feed_bias,
    feed_in,
    feed_in_bias,
    feed_out,
    feed_out_bias,
):
    micros, _, own, width = targets.shape
    held = micros // 2
    side = lax.axis_index("seq")
    parts = lax.axis_size("dp")
    place = lax.axis_index("dp")
    length = 2 * own
    pairs = HEADS * HEAD // 128

    def swap(rows, at, count, after=()):
        sent = lax.dynamic_slice_in_dim(rows, (1 - side) * held + at, count, axis=0)
        sent, after = lax.optimization_barrier((sent, after))
        return lax.ppermute(sent, "seq", SWAP), after

    def give(owns, got, at):
        got = got.astype(owns.dtype)
        return lax.dynamic_update_slice_in_dim(owns, got, (1 - side) * held + at, axis=0)

    def pack(*rows):
        zero = jnp.zeros((8 - len(rows), width), jnp.float32)
        return jnp.concatenate([jnp.stack(rows), zero])

    def batch(rows):
        return rows.reshape(held, length, -1)

    def flat(rows):
        return rows.reshape(held * length, -1)

    targets, memory = targets[:, 0], memory[:, 0]
    upstreams = (
        cotangent[:, 0].astype(jnp.float32) * loss_mask[:, 0].astype(jnp.float32)[..., None]
    ).astype(jnp.bfloat16)
    target_gots, last_got = [], ()
    for at in range(held):
        got, last_got = swap(targets, at, 1, last_got)
        target_gots.append(got)
        if at:
            target_gots[at - 1] = last_got
        last_got = got
    memory_gots, target_gots[-1] = swap(memory, 0, held, last_got)
    upstream_gots, memory_gots = swap(upstreams, 0, held, memory_gots)
    kinds = lax.dynamic_slice_in_dim(row_kind[:, 0], side * held, held, axis=0)
    info = jnp.concatenate([jnp.stack([side, place % 2]).astype(jnp.int32), kinds])

    self_vectors = pack(norm_self_gain, norm_self_bias)
    zero = jnp.zeros_like(self_query_bias)
    joint_bias = jnp.concatenate([self_query_bias, zero, self_value_bias])[None]
    entered, attended = (), ()
    for at in range(held):
        entered = enter(
            info, at, entered, held, targets, target_gots[at], self_input, self_vectors,
            joint_bias, True,
        )
        joint = batch(entered[1])
        attended = attend(info, at, 1, attended, joint, joint, joint, True, (0, 1, 2))
        entered, attended = lax.optimization_barrier((entered, attended))
    inputs, joint = entered[0], batch(entered[1])
    self_mixed, self_raised, self_inverse = attended
    after_self, cross_queries = middle(
        info,
        inputs,
        flat(self_mixed),
        self_output,
        cross_query,
        pack(self_output_bias, norm_cross_gain, norm_cross_bias, cross_query_bias),
        own,
    )
    pair_bias = jnp.concatenate([zero, cross_value_bias])[None]
    sources, cross_pairs = enter(
        info, 0, (), held, memory, memory_gots, cross_input, self_vectors, pair_bias, False
    )
    cross_queries, cross_pairs = batch(cross_queries), batch(cross_pairs)
    cross_mixed, cross_raised, cross_inverse = attend(
        info, 0, held, (), cross_queries, cross_pairs, cross_pairs, False, (0, 0, 1)
    )
    results, result_gots, grad_cross, cross_upstream, feed_sums, hidden_sums, *feed_parts = feed(
        info,
        after_self,
        flat(cross_mixed),
        upstreams,
        upstream_gots,
        cross_output,
        feed_in,
        feed_out,
        pack(cross_output_bias, norm_feed_gain, norm_feed_bias, feed_out_bias),
        feed_in_bias[None],
        parts,
    )
    feed_trees = [Tree(*feed_parts, low_first)]
    first = pairs // 2
    cross_inputs = (
        cross_queries, cross_pairs, cross_pairs, (0, 0, 1), cross_mixed, batch(cross_upstream),
        cross_raised, cross_inverse,
    )
    exchange(feed_trees)
    result_gots = lax.ppermute(result_gots, "seq", SWAP)
    half_grads, result_gots = settle(
        feed_trees, (attend_back((0, 0), (held, first), (), *cross_inputs), result_gots)
    )
    exchange(feed_trees)
    cross_grads = attend_back((0, first), (held, pairs - first), half_grads, *cross_inputs)
    source_grads, source_gots, grad_self, self_upstream, return_sums, *mid_parts = settle(
        feed_trees,
        return_rows(
            info,
            [flat(rows) for rows in cross_grads],
            after_self,
            grad_cross,
            flat(self_mixed),
            sources,
            cross_query,
            cross_input,
            self_output,
            pack(norm_cross_gain, norm_cross_bias),
            own,
            micros,
            parts,
        ),
    )
    early_sums = Whole(
        jnp.concatenate([feed_sums, return_sums, hidden_sums.reshape(-1, width)], axis=0)
    )
    mid_trees = [Tree(*mid_parts, low_first), early_sums]
    exchange(feed_trees + mid_trees)
    self_inputs = (
        joint, joint, joint, (0, 1, 2), self_mixed, batch(self_upstream), self_raised, self_inverse
    )
    source_gots = lax.ppermute(source_gots, "seq", SWAP)
    grads, source_gots = settle(
        feed_trees + mid_trees,
        (attend_back((0, 0), (1, pairs), (), *self_inputs), source_gots),
    )
    exchange(feed_trees + mid_trees)
    kept, leave_sums = (), []
    trees = feed_trees + mid_trees
    for at in range(held):
        if at == held - 1:
            late_parts = last_weight(
                info, [flat(rows) for rows in grads], inputs, self_vectors, own, parts
            )
            late_trees = [
                Tree(*late_parts[0:2], low_first),
                Tree(*late_parts[2:4], second_first),
            ]
            grads = settle(trees, lax.optimization_barrier((grads, late_parts[0]))[0])
            trees = trees + late_trees
            exchange(trees)
            grads = settle(late_trees, grads)
            exchange(trees)
        kept, got, sums = leave(
            info, at, kept, [flat(rows) for rows in grads], inputs, grad_self,
            self_input, self_vectors, own, micros,
        )
        leave_sums.append(sums)
        if at < held - 1:
            grads, kept = lax.optimization_barrier((grads, kept))
            back = lax.ppermute(got, "seq", SWAP)
            grads, back = settle(
                trees,
                (attend_back((at + 1, 0), (1, pairs), grads, *self_inputs), back),
            )
            exchange(trees)
            back = back.astype(kept.dtype)[None]
            kept = (
                lax.dynamic_update_slice_in_dim(kept, back, (1 - side) * held + at, axis=0),
            )
    input_grads, got, sums = settle(trees, (kept, got, sum(leave_sums)))
    late_sums = Whole(sums)
    trees = trees + [late_sums]
    exchange(trees)
    back = lax.ppermute(got, "seq", SWAP)
    settle(trees, ())
    exchange(trees)
    back = settle(trees, back)
    exchange(trees)
    input_grads = give(input_grads, back[None], held - 1)
    finish(trees)
    rows = width // parts
    inner_rows = feed_in.shape[1] // parts
    final = [None] * 21

    def mine(row):
        return lax.dynamic_slice_in_dim(row, place * (row.shape[0] // parts), row.shape[0] // parts)

    def widen(block):
        return jnp.concatenate([block[i : i + rows] for i in range(0, len(block), rows)], axis=1)

    for index, at in ((14, 0), (15, 1), (16, 2), (20, 3), (7, 8), (8, 9), (6, 10), (10, 11), (12, 12)):
        final[index] = mine(early_sums.total[at])
    final[18] = mine(early_sums.total[16:].reshape(-1))
    for index, at in ((0, 0), (1, 1), (3, 2), (4, 3)):
        final[index] = mine(late_sums.total[at])
    feed_total, mid_total = feed_trees[0].total, mid_trees[0].total
    final[19] = feed_total[:inner_rows]
    final[13] = feed_total[inner_rows : inner_rows + rows]
    final[17] = widen(feed_total[inner_rows + rows :])
    final[9] = mid_total[:rows]
    final[5] = mid_total[rows : 2 * rows]
    final[11] = widen(mid_total[2 * rows :])
    final[2] = jnp.concatenate([tree.total for tree in late_trees], axis=1)
    results = give(results, result_gots, 0)
    source_grads = give(source_grads, source_gots, 0)
    return (results[:, None], input_grads[:, None], source_grads[:, None]) + tuple(final)


def solution(mesh):
    in_specs = (
        P(None, "dp", "seq", None),
        P(None, "dp", "seq", None),
        P(None, "dp"),
        P(None, "dp", "seq"),
        P(None, "dp", "seq", None),
        P(),
        P(),
        P(),
        P(),
        P(),
        P(),
        P(),
        P(),
        P(),
        P(),
        P(),
        P(),
        P(),
        P(),
        P(),
        P(),
        P(),
        P(),
        P(),
        P(),
        P(),
    )
    out_specs = (
        P(None, "dp", "seq", None),
        P(None, "dp", "seq", None),
        P(None, "dp", "seq", None),
        P("dp"),
        P("dp"),
        P("dp", None),
        P("dp"),
        P("dp"),
        P("dp", None),
        P("dp"),
        P("dp"),
        P("dp"),
        P("dp", None),
        P("dp"),
        P("dp", None),
        P("dp"),
        P("dp", None),
        P("dp"),
        P("dp"),
        P("dp"),
        P("dp", None),
        P("dp"),
        P("dp", None),
        P("dp"),
    )

    def on_device(*arguments):
        micros = arguments[0].shape[0]
        rows = lax.axis_size("dp")
        pairs = lax.axis_size("seq") == 2 and micros % 2 == 0
        whole = pairs and rows & (rows - 1) == 0
        return (whole_sequences if whole else split_sequences)(*arguments)

    return jax.shard_map(
        on_device, mesh=mesh, in_specs=in_specs, out_specs=out_specs, check_vma=False
    )
```

```python
import functools

import jax
import jax.numpy as jnp
from jax import lax
from jax.experimental import pallas as pl
from jax.experimental.pallas import tpu as pltpu
from jax.sharding import PartitionSpec as P

HEADS = 12
HEAD = 64


epsilon = 1e-05
blocked_score = -1e30


def normed(values, norm_gain, norm_shift):
    center = values - jnp.mean(values, axis=-1, keepdims=True)
    spread = jnp.mean(center * center, axis=-1, keepdims=True)
    return center * lax.rsqrt(spread + epsilon) * norm_gain + norm_shift


def normed_back(values, norm_gain, norm_shift, upstream):
    unused, pullback = jax.vjp(normed, values, norm_gain, norm_shift)
    return pullback(upstream)


def gelu_exact(values):
    return jax.nn.gelu(values, approximate=False)


def project_rows(row_block, weight):
    return jnp.einsum("bpd,de->bpe", row_block, weight, preferred_element_type=jnp.float32)


def project_back(row_block, weight):
    return jnp.einsum("bpe,de->bpd", row_block, weight, preferred_element_type=jnp.float32)


def outer_sum(first_rows, second_rows):
    return jnp.einsum("bpd,bpe->de", first_rows, second_rows, preferred_element_type=jnp.float32)


def split_heads(row_block):
    return row_block.reshape(row_block.shape[0], row_block.shape[1], HEADS, HEAD)


def masked_scores(queries, key_rows, allowed):
    scores = jnp.einsum(
        "bphe,bshe->bhps",
        split_heads(queries),
        split_heads(key_rows),
        preferred_element_type=jnp.float32,
    )
    if allowed is None:
        return scores
    return jnp.where(allowed[:, None], scores, blocked_score)


def attend_forward(queries, key_rows, values, allowed):
    scores = masked_scores(queries, key_rows, allowed)
    highest_score = jnp.max(scores, axis=-1, keepdims=True)
    raised = jnp.exp(scores - highest_score)
    totals = jnp.sum(raised, axis=-1, keepdims=True)
    weights = (raised / totals).astype(jnp.bfloat16)
    mixed = jnp.einsum(
        "bhps,bshe->bphe", weights, split_heads(values), preferred_element_type=jnp.float32
    )
    return (mixed.reshape(queries.shape).astype(jnp.bfloat16), highest_score + jnp.log(totals))


def attend_backward(queries, key_rows, values, allowed, log_totals, upstream):
    weights = jnp.exp(masked_scores(queries, key_rows, allowed) - log_totals)
    upstream_heads = split_heads(upstream)
    value_grads = jnp.einsum(
        "bhps,bphe->bshe",
        weights.astype(jnp.bfloat16),
        upstream_heads,
        preferred_element_type=jnp.float32,
    )
    weight_grads = jnp.einsum(
        "bphe,bshe->bhps", upstream_heads, split_heads(values), preferred_element_type=jnp.float32
    )
    score_grads = weights * (weight_grads - jnp.sum(weight_grads * weights, axis=-1, keepdims=True))
    score_low = score_grads.astype(jnp.bfloat16)
    query_grads = jnp.einsum(
        "bhps,bshe->bphe", score_low, split_heads(key_rows), preferred_element_type=jnp.float32
    ).reshape(queries.shape)
    key_grads = jnp.einsum(
        "bhps,bphe->bshe", score_low, split_heads(queries), preferred_element_type=jnp.float32
    ).reshape(key_rows.shape)
    return (query_grads, jnp.concatenate([key_grads, value_grads.reshape(key_rows.shape)], axis=-1))


def split_sequences(
    targets,
    memory,
    row_kind,
    loss_mask,
    cotangent,
    norm_self_gain,
    norm_self_bias,
    self_input,
    self_query_bias,
    self_value_bias,
    self_output,
    self_output_bias,
    norm_cross_gain,
    norm_cross_bias,
    cross_query,
    cross_query_bias,
    cross_input,
    cross_value_bias,
    cross_output,
    cross_output_bias,
    norm_feed_gain,
    norm_feed_bias,
    feed_in,
    feed_in_bias,
    feed_out,
    feed_out_bias,
):
    model_width = targets.shape[3]
    part_rows = targets.shape[2]
    key_span = part_rows * lax.axis_size("seq")
    query_scale = HEAD ** (-0.5)
    places = lax.axis_index("seq") * part_rows + jnp.arange(part_rows)
    causal = jnp.arange(key_span)[None, :] <= places[:, None]
    results, input_grads, source_grads = ([], [], [])
    totals = None
    for micro_index in range(targets.shape[0]):
        inputs = targets[micro_index].astype(jnp.float32)
        memory_local = memory[micro_index]
        allowed = causal[None] | (row_kind[micro_index] == 1)[:, None, None]
        first_normed = normed(inputs, norm_self_gain, norm_self_bias).astype(jnp.bfloat16)
        self_joint = project_rows(first_normed, self_input)
        queries = ((self_joint[..., :model_width] + self_query_bias) * query_scale).astype(
            jnp.bfloat16
        )
        own_pairs = jnp.concatenate(
            [
                self_joint[..., model_width : 2 * model_width],
                self_joint[..., 2 * model_width :] + self_value_bias,
            ],
            axis=-1,
        ).astype(jnp.bfloat16)
        gathered_self = lax.all_gather(own_pairs, "seq", axis=1, tiled=True)
        key_rows = gathered_self[..., :model_width]
        value_rows = gathered_self[..., model_width:]
        self_mixed, self_totals = attend_forward(queries, key_rows, value_rows, allowed)
        after_self = inputs + project_rows(self_mixed, self_output) + self_output_bias
        second_normed = normed(after_self, norm_cross_gain, norm_cross_bias).astype(jnp.bfloat16)
        cross_queries = (
            (project_rows(second_normed, cross_query) + cross_query_bias) * query_scale
        ).astype(jnp.bfloat16)
        joined = project_rows(lax.all_gather(memory_local, "seq", axis=1, tiled=True), cross_input)
        gathered_cross = jnp.concatenate(
            [joined[..., :model_width], joined[..., model_width:] + cross_value_bias], axis=-1
        ).astype(jnp.bfloat16)
        cross_keys = gathered_cross[..., :model_width]
        cross_values = gathered_cross[..., model_width:]
        cross_mixed, cross_totals = attend_forward(cross_queries, cross_keys, cross_values, None)
        after_cross = after_self + project_rows(cross_mixed, cross_output) + cross_output_bias
        third_normed = normed(after_cross, norm_feed_gain, norm_feed_bias).astype(jnp.bfloat16)
        activated, gelu_pullback = jax.vjp(
            gelu_exact, project_rows(third_normed, feed_in) + feed_in_bias
        )
        activated_low = activated.astype(jnp.bfloat16)
        results.append(
            (after_cross + project_rows(activated_low, feed_out) + feed_out_bias).astype(
                jnp.bfloat16
            )
        )
        pieces = [None] * 21
        grad_output = (
            cotangent[micro_index].astype(jnp.float32)
            * loss_mask[micro_index].astype(jnp.float32)[..., None]
        )
        output_low = grad_output.astype(jnp.bfloat16)
        pieces[19] = outer_sum(activated_low, output_low)
        pieces[20] = jnp.sum(grad_output, axis=(0, 1))
        grad_hidden = gelu_pullback(project_back(output_low, feed_out))[0]
        hidden_low = grad_hidden.astype(jnp.bfloat16)
        pieces[17] = outer_sum(third_normed, hidden_low)
        pieces[18] = jnp.sum(grad_hidden, axis=(0, 1))
        through_feed, pieces[15], pieces[16] = normed_back(
            after_cross, norm_feed_gain, norm_feed_bias, project_back(hidden_low, feed_in)
        )
        grad_cross = grad_output + through_feed
        cross_low = grad_cross.astype(jnp.bfloat16)
        pieces[13] = outer_sum(cross_mixed, cross_low)
        pieces[14] = jnp.sum(grad_cross, axis=(0, 1))
        cross_upstream = project_back(cross_low, cross_output).astype(jnp.bfloat16)
        cross_query_grads, cross_pair_grads = attend_backward(
            cross_queries, cross_keys, cross_values, None, cross_totals, cross_upstream
        )
        own_cross = lax.psum_scatter(
            cross_pair_grads.astype(jnp.bfloat16), "seq", scatter_dimension=1, tiled=True
        ).astype(jnp.float32)
        pieces[12] = jnp.sum(own_cross[..., model_width:], axis=(0, 1))
        own_cross_low = own_cross.astype(jnp.bfloat16)
        pieces[11] = outer_sum(memory_local, own_cross_low)
        source_grads.append(project_back(own_cross_low, cross_input))
        scaled_cross = cross_query_grads * query_scale
        pieces[10] = jnp.sum(scaled_cross, axis=(0, 1))
        scaled_cross_low = scaled_cross.astype(jnp.bfloat16)
        pieces[9] = outer_sum(second_normed, scaled_cross_low)
        through_cross, pieces[7], pieces[8] = normed_back(
            after_self,
            norm_cross_gain,
            norm_cross_bias,
            project_back(scaled_cross_low, cross_query),
        )
        grad_self = grad_cross + through_cross
        self_low = grad_self.astype(jnp.bfloat16)
        pieces[5] = outer_sum(self_mixed, self_low)
        pieces[6] = jnp.sum(grad_self, axis=(0, 1))
        self_upstream = project_back(self_low, self_output).astype(jnp.bfloat16)
        self_query_grads, self_pair_grads = attend_backward(
            queries, key_rows, value_rows, allowed, self_totals, self_upstream
        )
        own_self = lax.psum_scatter(
            self_pair_grads.astype(jnp.bfloat16), "seq", scatter_dimension=1, tiled=True
        ).astype(jnp.float32)
        scaled_self = self_query_grads * query_scale
        pieces[3] = jnp.sum(scaled_self, axis=(0, 1))
        pieces[4] = jnp.sum(own_self[..., model_width:], axis=(0, 1))
        joint_low = jnp.concatenate([scaled_self, own_self], axis=-1).astype(jnp.bfloat16)
        pieces[2] = outer_sum(first_normed, joint_low)
        through_first, pieces[0], pieces[1] = normed_back(
            inputs, norm_self_gain, norm_self_bias, project_back(joint_low, self_input)
        )
        input_grads.append(grad_self + through_first)
        totals = (
            pieces
            if totals is None
            else [running + added for running, added in zip(totals, pieces)]
        )
    def reduced(total):
        block = lax.psum_scatter(
            total.astype(jnp.bfloat16), "dp", scatter_dimension=0, tiled=True
        )
        return lax.psum(block, "seq").astype(jnp.float32)

    final = [reduced(total) for total in totals]
    return (jnp.stack(results), jnp.stack(input_grads), jnp.stack(source_grads)) + tuple(final)


def contract(first, second, first_dim, second_dim):
    return lax.dot_general(
        first, second, (((first_dim,), (second_dim,)), ((), ())), preferred_element_type=jnp.float32
    )


def head_masks(pair):
    lane = lax.broadcasted_iota(jnp.int32, (1, pair.shape[1]), 1)
    zero = jnp.zeros((), pair.dtype)
    return (jnp.where(lane < HEAD, pair, zero), jnp.where(lane < HEAD, zero, pair))


LIMIT = 62 * 2**20


def attend_kernel(info_ref, q_ref, k_ref, v_ref, *refs, use_mask, start):
    o_ref, e_ref, r_ref, mask_ref = refs[-4:]
    length = k_ref.shape[1]
    half = length // 2
    values_turned = v_ref[0].T
    ones = jnp.ones((16, length), jnp.bfloat16)

    def run(masked, shifted):
        lowest, highest = None, None
        for at in range(2):
            queries_at = slice(at * half, (at + 1) * half)
            mixed = []
            for head, queries in enumerate(head_masks(q_ref[0, queries_at, :])):
                scores = contract(k_ref[0], queries, 1, 1)
                if shifted:
                    if masked:
                        seen = mask_ref[:, queries_at].astype(jnp.float32) > 0
                        scores = jnp.where(seen, scores, blocked_score)
                    scores = scores - jnp.max(scores, axis=0, keepdims=True)
                low = jnp.exp(scores).astype(jnp.bfloat16)
                if masked:
                    low = low * mask_ref[:, queries_at]
                e_ref[0, head, :, queries_at] = low
                turned = jnp.concatenate(
                    [values_turned[head * HEAD : (head + 1) * HEAD], ones], axis=0
                )
                sums = contract(turned, low, 1, 0)
                total = sums[HEAD : HEAD + 1]
                if not shifted:
                    lowest = total if lowest is None else jnp.minimum(lowest, total)
                    highest = total if highest is None else jnp.maximum(highest, total)
                inverse = 1.0 / total
                r_ref[0, 0, head : head + 1, queries_at] = inverse
                mixed.append(sums[:HEAD] * inverse)
            o_ref[0, queries_at, :] = jnp.concatenate(mixed, axis=0).T.astype(jnp.bfloat16)
        if not shifted:
            in_range = (jnp.min(lowest) > 1e-20) & (jnp.max(highest) < 1e30)

            @pl.when(jnp.logical_not(in_range))
            def _():
                run(masked, True)

    if not use_mask:
        run(False, False)
        return
    causal = info_ref[2 + start + pl.program_id(0)] == 0

    @pl.when(causal & (pl.program_id(1) == 0))
    def _():
        later = info_ref[0] * half
        query = lax.broadcasted_iota(jnp.int32, (1, length), 1)
        query = jnp.where(query < half, query + later, query - later)

        @pl.loop(0, length, step=64)
        def _(row):
            key = lax.broadcasted_iota(jnp.int32, (64, 1), 0) + row
            key = jnp.where(key < half, key + later, key - later)
            seen = jnp.where(key <= query, 1.0, 0.0)
            mask_ref[pl.ds(pl.multiple_of(row, 64), 64), :] = seen.astype(jnp.bfloat16)

    @pl.when(causal)
    def _():
        run(True, False)

    @pl.when(jnp.logical_not(causal))
    def _():
        run(False, False)


def attend(info, start, count_now, previous, queries, keys, values, use_mask, offsets):
    count, length = queries.shape[:2]
    pairs = HEADS * HEAD // 128
    width = HEADS * HEAD

    def spec(offset):
        return pl.BlockSpec((1, length, 128), lambda s, p, info: (start + s, 0, offset * pairs + p))

    place = lambda s, p, info: (start + s, p, 0, 0)
    return pl.pallas_call(
        functools.partial(attend_kernel, use_mask=use_mask, start=start),
        grid_spec=pltpu.PrefetchScalarGridSpec(
            num_scalar_prefetch=1,
            grid=(count_now, pairs),
            in_specs=[spec(offset) for offset in offsets]
            + [pl.BlockSpec(memory_space=pl.ANY)] * len(previous),
            out_specs=[
                spec(0),
                pl.BlockSpec((1, 2, length, length), place),
                pl.BlockSpec((1, 1, 2, length), place),
            ],
            scratch_shapes=[pltpu.VMEM((length, length), jnp.bfloat16)],
        ),
        out_shape=[
            jax.ShapeDtypeStruct((count, length, width), jnp.bfloat16),
            jax.ShapeDtypeStruct((count, HEADS, length, length), jnp.bfloat16),
            jax.ShapeDtypeStruct((count, pairs, 2, length), jnp.float32),
        ],
        input_output_aliases={4: 0, 5: 1, 6: 2} if previous else {},
        compiler_params=pltpu.CompilerParams(vmem_limit_bytes=LIMIT),
        cost_estimate=pl.CostEstimate(
            flops=4 * count_now * HEADS * length * length * 256,
            bytes_accessed=count_now * HEADS * length * length * 2,
            transcendentals=count_now * HEADS * length * length,
        ),
        name="attend",
    )(info, queries, keys, values, *previous)


def attend_back_kernel(q_ref, k_ref, v_ref, o_ref, g_ref, e_ref, r_ref, dq_ref, dk_ref, dv_ref):
    length = k_ref.shape[1]
    keys_turned = k_ref[0].T
    upstream = g_ref[0].astype(jnp.float32)
    products = (o_ref[0].astype(jnp.float32) * upstream).T
    upstream = upstream.T
    parts, deltas = [], []
    for head in range(2):
        rows = slice(head * HEAD, (head + 1) * HEAD)
        inverse = r_ref[0, 0, head : head + 1, :]
        parts.append(upstream[rows] * inverse)
        deltas.append(jnp.sum(products[rows], axis=0, keepdims=True) * inverse)
    scaled = head_masks(jnp.concatenate(parts, axis=0).T.astype(jnp.bfloat16))
    queries = head_masks(q_ref[0])
    key_sum, value_sum, query_parts = 0.0, 0.0, []
    for head in range(2):
        rows = slice(head * HEAD, (head + 1) * HEAD)
        low = e_ref[0, head]
        grads = contract(v_ref[0], scaled[head], 1, 1)
        score_low = (low.astype(jnp.float32) * (grads - deltas[head])).astype(jnp.bfloat16)
        value_sum += contract(low, scaled[head], 1, 0)
        key_sum += contract(score_low, queries[head], 1, 0)
        query_parts.append(contract(keys_turned[rows], score_low, 1, 0))
    turned = jnp.concatenate(query_parts, axis=0) * (HEAD**-0.5)
    dq_ref[0] = turned.T.astype(jnp.bfloat16)
    dk_ref[0] = key_sum.astype(jnp.bfloat16)
    dv_ref[0] = value_sum.astype(jnp.bfloat16)


def attend_back(place, size, previous, queries, keys, values, offsets, *rest):
    count, length = queries.shape[:2]
    pairs = HEADS * HEAD // 128
    width = HEADS * HEAD

    start, first = place

    def spec(offset):
        return pl.BlockSpec(
            (1, length, 128), lambda s, p: (start + s, 0, offset * pairs + first + p)
        )

    kernel = attend_back_kernel
    aliases = {}
    if previous:
        kernel = lambda *refs: attend_back_kernel(*refs[3:])
        aliases = {0: 0, 1: 1, 2: 2}
    return pl.pallas_call(
        kernel,
        grid=size,
        in_specs=[pl.BlockSpec(memory_space=pl.ANY)] * len(previous)
        + [spec(offset) for offset in offsets]
        + [
            spec(0),
            spec(0),
            pl.BlockSpec((1, 2, length, length), lambda s, p: (start + s, first + p, 0, 0)),
            pl.BlockSpec((1, 1, 2, length), lambda s, p: (start + s, first + p, 0, 0)),
        ],
        out_specs=[spec(0)] * 3,
        out_shape=[jax.ShapeDtypeStruct((count, length, width), jnp.bfloat16)] * 3,
        input_output_aliases=aliases,
        compiler_params=pltpu.CompilerParams(vmem_limit_bytes=LIMIT),
        cost_estimate=pl.CostEstimate(
            flops=16 * size[0] * size[1] * length * length * 256,
            bytes_accessed=4 * size[0] * size[1] * length * length,
            transcendentals=0,
        ),
        name="attend_back",
    )(*previous, queries, keys, values, *rest)


def normal_parts(values):
    center = values - jnp.mean(values, axis=-1, keepdims=True)
    inverse = lax.rsqrt(jnp.mean(center * center, axis=-1, keepdims=True) + epsilon)
    return center * inverse, inverse


def normal_back(unit, inverse, norm_gain, upstream):
    inner = upstream * norm_gain
    shift = jnp.mean(inner, axis=-1, keepdims=True)
    tilt = jnp.mean(inner * unit, axis=-1, keepdims=True)
    return inverse * (inner - shift - unit * tilt)


def gelu_parts(values):
    size = jnp.abs(values)
    ratio = 1.0 / (1.0 + 0.2316418882663604 * size)
    series = 0.5307027145
    for weight in (-0.7265760135, 0.7107068705, -0.142248368, 0.127414796):
        series = series * ratio + weight
    bell = jnp.exp(-0.5 * values * values)
    upper = series * ratio * bell
    chance = jnp.where(values < 0, upper, 1.0 - upper)
    return values * chance, chance + values * (0.3989422804014327 * bell)


def column_sum(values):
    return jnp.sum(values, axis=0, keepdims=True)


def resident(array):
    return pl.BlockSpec(array.shape, lambda *_: (0,) * array.ndim, pipeline_mode=pl.Buffered(1))


def whole_block(array):
    return pl.BlockSpec(array.shape, lambda *_: (0,) * len(array.shape))


def like(shape, dtype=jnp.float32):
    return jax.ShapeDtypeStruct(tuple(shape), dtype)


def pick(take_first, first_ref, second_ref):
    return jnp.where(take_first, first_ref[...], second_ref[...])


ONCE = {"pipeline_mode": pl.Buffered(1)}


def own_spec(own, width, held, last, **more):
    def place(step, info):
        return (info[0] * held + jnp.minimum(step, last) // 2, 0, 0)

    return pl.BlockSpec((None, own, width), place, **more)


def got_spec(own, width, last, **more):
    return pl.BlockSpec(
        (None, own, width), lambda step, info: (jnp.minimum(step, last) // 2, 0, 0), **more
    )


def row_spec(own, width, last, **more):
    return pl.BlockSpec((own, width), lambda step, info: (jnp.minimum(step, last), 0), **more)


def kernel_call(kernel, name, info, arrays, in_specs, outs, out_specs, grid, flops, moved, **more):
    scratch = more.pop("scratch", [])
    return pl.pallas_call(
        kernel,
        grid_spec=pltpu.PrefetchScalarGridSpec(
            num_scalar_prefetch=1,
            grid=(grid,),
            in_specs=in_specs,
            out_specs=out_specs,
            scratch_shapes=scratch,
        ),
        out_shape=outs,
        compiler_params=pltpu.CompilerParams(
            vmem_limit_bytes=more.pop("limit", LIMIT)
        ),
        cost_estimate=pl.CostEstimate(flops=flops, bytes_accessed=moved, transcendentals=0),
        name=name,
        **more,
    )(info, *arrays)


def enter_kernel(info_ref, source_ref, w_ref, vec_ref, bias_ref, *refs, norm):
    x_ref, out_ref = refs[-2:]
    x = source_ref[...]
    x_ref[...] = x
    if norm:
        unit, _ = normal_parts(x.astype(jnp.float32))
        x = (unit * vec_ref[0:1, :] + vec_ref[1:2, :]).astype(jnp.bfloat16)
    width = x.shape[1]
    for start in range(0, w_ref.shape[1], width):
        part = slice(start, start + width)
        total = contract(x, w_ref[:, part], 1, 0) + bias_ref[:, part]
        if norm and start == 0:
            total = total * (HEAD**-0.5)
        out_ref[:, part] = total.astype(jnp.bfloat16)


def enter(info, first, count, previous, held, rows_in, weight, vectors, bias, norm):
    own, width = rows_in.shape[1:]
    rows = 2 * held * own
    wide = weight.shape[1]
    if first is None:
        place = lambda step, info: (info[0] * held + step, 0, 0)
        row = lambda step, info: (2 * step, 0)
    else:
        place = lambda step, info: (step, 0, 0)
        row = lambda step, info: (2 * (first + step) + 1, 0)
    return kernel_call(
        functools.partial(enter_kernel, norm=norm),
        "enter",
        info,
        (rows_in, weight, vectors, bias, *previous),
        [pl.BlockSpec((None, own, width), place)]
        + [resident(a) for a in (weight, vectors, bias)]
        + [pl.BlockSpec(memory_space=pl.ANY)] * len(previous),
        [like((rows, width), jnp.bfloat16), like((rows, wide), jnp.bfloat16)],
        [pl.BlockSpec((own, width), row), pl.BlockSpec((own, wide), row)],
        count,
        2 * count * own * width * wide,
        2 * count * own * (2 * width + wide),
        input_output_aliases={5: 0, 6: 1} if previous else {},
    )


def middle_kernel(info_ref, x_ref, mixed_ref, wo_ref, wq_ref, vec_ref, after_ref, q_ref):
    out_bias, gain, shift, query_bias = (vec_ref[i : i + 1, :] for i in range(4))
    after = (
        x_ref[...].astype(jnp.float32) + contract(mixed_ref[...], wo_ref[...], 1, 0) + out_bias
    )
    after_ref[...] = after
    unit, _ = normal_parts(after)
    normal = (unit * gain + shift).astype(jnp.bfloat16)
    queries = (contract(normal, wq_ref[...], 1, 0) + query_bias) * (HEAD**-0.5)
    q_ref[...] = queries.astype(jnp.bfloat16)


def middle(info, x, mixed, wo, wq, vectors, own):
    rows, width = x.shape
    last = rows // own - 1
    spec = row_spec(own, width, last)
    return kernel_call(
        middle_kernel,
        "middle",
        info,
        (x, mixed, wo, wq, vectors),
        [spec, spec] + [resident(a) for a in (wo, wq, vectors)],
        [like((rows, width)), like((rows, width), jnp.bfloat16)],
        [spec, spec],
        rows // own,
        4 * rows * width * width,
        10 * rows * width,
    )


def write_split(core, rows, kept_ref, sent_ref, start):
    half = rows.shape[0] // 2
    low = rows.astype(jnp.bfloat16)
    place = slice(start, start + half)

    @pl.when(core == 0)
    def _():
        kept_ref[0, place, :] = low[:half]
        sent_ref[0, place, :] = low[half:]

    @pl.when(core != 0)
    def _():
        kept_ref[0, place, :] = low[half:]
        sent_ref[0, place, :] = low[:half]


def write_wide(core, rows, kept_ref, sent_ref, start):
    half, width = rows.shape[0] // 2, kept_ref.shape[2]
    for at in range(rows.shape[1] // width):
        part = rows[:, at * width : (at + 1) * width]
        write_split(core, part, kept_ref, sent_ref, start + at * half)


def acc_rows(ref, at, rows):
    return ref[pl.ds(pl.multiple_of(at * rows, 16), rows), :]


def piece(parts, high, wide, steps, order):
    bits = parts.bit_length() - 2

    def late(step, info):
        at = jnp.maximum(step - steps, 0)
        place = 0
        for bit in order(bits):
            place = 2 * place + (at // 2**bit) % 2
        return (place, 0, 0)

    return (
        [pl.BlockSpec((1, high, wide), late)] * 2,
        [like((parts // 2, high, wide), jnp.bfloat16)] * 2,
    )


def low_first(bits):
    return list(range(bits))


def second_first(bits):
    return list(range(bits))[1:2] + [0] + list(range(2, bits))


def put_rows(step, value, own_ref, got_ref):
    @pl.when(step % 2 == 0)
    def _():
        own_ref[...] = value.astype(own_ref.dtype)

    @pl.when(step % 2 != 0)
    def _():
        got_ref[...] = value.astype(got_ref.dtype)


def feed_kernel(
    info_ref, x_ref, mixed_ref, dyo_ref, dyg_ref, wc_ref, wi_ref, wo_ref, vec_ref, bi_ref,
    own_ref, got_ref, dx_ref, do_ref, vsum_ref, bsum_ref, kept_ref, sent_ref, ai_ref, ao_ref,
    ac_ref, *, steps, chunk, parts,
):
    step = pl.program_id(0)

    @pl.when(step == 0)
    def _():
        for ref in (vsum_ref, bsum_ref, ai_ref, ao_ref, ac_ref):
            ref[...] = jnp.zeros_like(ref)

    @pl.when(step < steps)
    def _():
        cross_bias, gain, shift, out_bias = (vec_ref[i : i + 1, :] for i in range(4))
        mixed = mixed_ref[...]
        x2 = x_ref[...] + contract(mixed, wc_ref[...], 1, 0) + cross_bias
        unit, inverse = normal_parts(x2)
        normal = (unit * gain + shift).astype(jnp.bfloat16)
        normal_turned = normal.T
        dy = pick(step % 2 == 0, dyo_ref, dyg_ref)
        dy_turned = dy.T
        result, upstream = None, None
        for start in range(0, wi_ref.shape[1], chunk):
            part = slice(start, start + chunk)
            hidden = contract(normal, wi_ref[:, part], 1, 0) + bi_ref[:, part]
            active, slope = gelu_parts(hidden)
            active = active.astype(jnp.bfloat16)
            down = contract(active, wo_ref[part, :], 1, 0)
            result = down if result is None else result + down
            grads = contract(dy, wo_ref[part, :], 1, 1) * slope
            bsum_ref[:, part] += column_sum(grads)
            low = grads.astype(jnp.bfloat16)
            up = contract(low, wi_ref[:, part], 1, 1)
            upstream = up if upstream is None else upstream + up
            ao_ref[:, part] += contract(dy_turned, active, 1, 0)
            ai_ref[:, part] += contract(normal_turned, low, 1, 0)
        put_rows(step, x2 + result + out_bias, own_ref, got_ref)
        wide = dy.astype(jnp.float32)
        dx = wide + normal_back(unit, inverse, gain, upstream)
        dx_ref[...] = dx
        dx_low = dx.astype(jnp.bfloat16)
        do_ref[...] = contract(dx_low, wc_ref[...], 1, 1).astype(jnp.bfloat16)
        ac_ref[...] += contract(mixed.T, dx_low, 1, 0)
        vsum_ref[0:1, :] += column_sum(dx)
        vsum_ref[1:2, :] += column_sum(upstream * unit)
        vsum_ref[2:3, :] += column_sum(upstream)
        vsum_ref[3:4, :] += column_sum(wide)

    @pl.when(step >= steps)
    def _():
        at = step - steps
        core = info_ref[1]
        width, wide = ai_ref.shape
        rows = 2 * width // parts
        inner = 2 * wide // parts
        columns = ao_ref[:, pl.ds(pl.multiple_of(at * inner, 128), inner)]
        write_split(core, columns.astype(jnp.bfloat16).T, kept_ref, sent_ref, 0)
        write_split(core, acc_rows(ac_ref, at, rows), kept_ref, sent_ref, inner // 2)
        write_wide(core, acc_rows(ai_ref, at, rows), kept_ref, sent_ref, (inner + rows) // 2)


def feed(info, x1, mixed, dys, dy_gots, wc, wi, wo, vectors, bi, parts, chunk=768):
    rows, width = x1.shape
    held, own = dy_gots.shape[:2]
    micros = dys.shape[0]
    inner = wi.shape[1]
    steps = 2 * held
    last = steps - 1
    row = row_spec(own, width, last)
    pieces = [piece(parts, (2 * inner + width) // parts, width, steps, low_first)]
    sums = [like((8, width)), like((1, inner))]
    return kernel_call(
        functools.partial(feed_kernel, steps=steps, chunk=chunk, parts=parts),
        "feed",
        info,
        (x1, mixed, dys, dy_gots, wc, wi, wo, vectors, bi),
        [row_spec(own, width, last, **ONCE)] * 2
        + [own_spec(own, width, held, last, **ONCE), got_spec(own, width, last, **ONCE)]
        + [resident(a) for a in (wc, wi, wo, vectors, bi)],
        [
            like((micros, own, width), jnp.bfloat16),
            like((held, own, width), jnp.bfloat16),
            like((rows, width)),
            like((rows, width), jnp.bfloat16),
        ]
        + sums
        + sum([p[1] for p in pieces], []),
        [own_spec(own, width, held, last), got_spec(own, width, last), row, row]
        + [whole_block(a) for a in sums]
        + sum([p[0] for p in pieces], []),
        steps + parts // 2,
        2 * rows * width * (6 * inner + 3 * width),
        60 * 2**20,
        scratch=[
            pltpu.VMEM((width, inner), jnp.float32),
            pltpu.VMEM((width, inner), jnp.float32),
            pltpu.VMEM((width, width), jnp.float32),
        ],
        limit=LIMIT,
    )


def return_kernel(
    info_ref, dq_ref, dk_ref, dv_ref, x_ref, dx_ref, mixed_ref, src_ref, wq_ref, wi_ref, wo_ref,
    vec_ref, own_ref, got_ref, dxo_ref, do_ref, vsum_ref, kept_ref, sent_ref, aq_ref, ao_ref,
    ai_ref, *, steps, parts,
):
    step = pl.program_id(0)

    @pl.when(step == 0)
    def _():
        for ref in (vsum_ref, aq_ref, ao_ref, ai_ref):
            ref[...] = jnp.zeros_like(ref)

    @pl.when(step < steps)
    def _():
        width = x_ref.shape[1]
        gain, shift = vec_ref[0:1, :], vec_ref[1:2, :]
        dq, dk, dv = dq_ref[...], dk_ref[...], dv_ref[...]
        upstream = contract(dq, wq_ref[...], 1, 1)
        unit, inverse = normal_parts(x_ref[...])
        normal = (unit * gain + shift).astype(jnp.bfloat16)
        dx = dx_ref[...] + normal_back(unit, inverse, gain, upstream)
        dxo_ref[...] = dx
        low = dx.astype(jnp.bfloat16)
        do_ref[...] = contract(low, wo_ref[...], 1, 1).astype(jnp.bfloat16)
        source = contract(dk, wi_ref[:, :width], 1, 1) + contract(dv, wi_ref[:, width:], 1, 1)
        put_rows(step, source, own_ref, got_ref)
        aq_ref[...] += contract(normal.T, dq, 1, 0)
        ao_ref[...] += contract(mixed_ref[...].T, low, 1, 0)
        turned = src_ref[...].T
        ai_ref[:, :width] += contract(turned, dk, 1, 0)
        ai_ref[:, width:] += contract(turned, dv, 1, 0)
        vsum_ref[0:1, :] += column_sum(upstream * unit)
        vsum_ref[1:2, :] += column_sum(upstream)
        vsum_ref[2:3, :] += column_sum(dx)
        vsum_ref[3:4, :] += column_sum(dq.astype(jnp.float32))
        vsum_ref[4:5, :] += column_sum(dv.astype(jnp.float32))

    @pl.when(step >= steps)
    def _():
        at = step - steps
        core = info_ref[1]
        rows = 2 * aq_ref.shape[0] // parts
        write_split(core, acc_rows(aq_ref, at, rows), kept_ref, sent_ref, 0)
        write_split(core, acc_rows(ao_ref, at, rows), kept_ref, sent_ref, rows // 2)
        write_wide(core, acc_rows(ai_ref, at, rows), kept_ref, sent_ref, rows)


def return_rows(info, grads, x1, dx2, mixed, sources, wq, wi, wo, vectors, own, micros, parts):
    rows, width = x1.shape
    held = rows // own // 2
    steps = 2 * held
    last = steps - 1
    row = row_spec(own, width, last)
    pieces = [piece(parts, 4 * width // parts, width, steps, low_first)]
    sums = like((8, width))
    return kernel_call(
        functools.partial(return_kernel, steps=steps, parts=parts),
        "return_rows",
        info,
        (*grads, x1, dx2, mixed, sources, wq, wi, wo, vectors),
        [row] * 7 + [resident(a) for a in (wq, wi, wo, vectors)],
        [
            like((micros, own, width)),
            like((held, own, width), jnp.bfloat16),
            like((rows, width)),
            like((rows, width), jnp.bfloat16),
            sums,
        ]
        + sum([p[1] for p in pieces], []),
        [own_spec(own, width, held, last), got_spec(own, width, last), row, row, whole_block(sums)]
        + sum([p[0] for p in pieces], []),
        steps + parts // 2,
        16 * rows * width * width,
        40 * 2**20,
        scratch=[
            pltpu.VMEM((width, width), jnp.float32),
            pltpu.VMEM((width, width), jnp.float32),
            pltpu.VMEM((width, 2 * width), jnp.float32),
        ],
    )


def last_weight_kernel(
    info_ref, dq_ref, dk_ref, dv_ref, x_ref, vec_ref, ka_ref, sa_ref, kb_ref, sb_ref, acc_ref,
    *, steps,
):
    step = pl.program_id(0)

    @pl.when(step == 0)
    def _():
        acc_ref[...] = jnp.zeros_like(acc_ref)

    @pl.when(step < steps)
    def _():
        unit, _ = normal_parts(x_ref[...].astype(jnp.float32))
        turned = (unit * vec_ref[0:1, :] + vec_ref[1:2, :]).astype(jnp.bfloat16).T
        width = x_ref.shape[1]
        for at, ref in enumerate((dq_ref, dk_ref, dv_ref)):
            acc_ref[:, at * width : (at + 1) * width] += contract(turned, ref[...], 1, 0)

    @pl.when(step >= steps)
    def _():
        rows = acc_rows(acc_ref, step - steps, 2 * ka_ref.shape[1])
        half = ka_ref.shape[2]
        write_split(info_ref[1], rows[:, :half], ka_ref, sa_ref, 0)
        write_split(info_ref[1], rows[:, half:], kb_ref, sb_ref, 0)


def last_weight(info, grads, x, vectors, own, parts):
    rows, width = x.shape
    steps = rows // own
    row = row_spec(own, width, steps - 1)
    pieces = [
        piece(parts, width // parts, 3 * width // 2, steps, order)
        for order in (low_first, second_first)
    ]
    return kernel_call(
        functools.partial(last_weight_kernel, steps=steps),
        "last_weight",
        info,
        (*grads, x, vectors),
        [row] * 4 + [resident(vectors)],
        sum([p[1] for p in pieces], []),
        sum([p[0] for p in pieces], []),
        steps + parts // 2,
        6 * rows * width * width,
        20 * 2**20,
        scratch=[pltpu.VMEM((width, 3 * width), jnp.float32)],
    )


def leave_kernel(
    info_ref, dq_ref, dk_ref, dv_ref, x_ref, dx_ref, w_ref, vec_ref, *refs
):
    own_ref, got_ref, vsum_ref = refs[-3:]
    step = pl.program_id(0)

    @pl.when(step == 0)
    def _():
        vsum_ref[...] = jnp.zeros_like(vsum_ref)

    width = x_ref.shape[1]
    dq, dk, dv = dq_ref[...], dk_ref[...], dv_ref[...]
    upstream = (
        contract(dq, w_ref[:, :width], 1, 1)
        + contract(dk, w_ref[:, width : 2 * width], 1, 1)
        + contract(dv, w_ref[:, 2 * width :], 1, 1)
    )
    unit, inverse = normal_parts(x_ref[...].astype(jnp.float32))
    dx = dx_ref[...] + normal_back(unit, inverse, vec_ref[0:1, :], upstream)
    put_rows(step, dx, own_ref, got_ref)
    vsum_ref[0:1, :] += column_sum(upstream * unit)
    vsum_ref[1:2, :] += column_sum(upstream)
    vsum_ref[2:3, :] += column_sum(dq.astype(jnp.float32))
    vsum_ref[3:4, :] += column_sum(dv.astype(jnp.float32))


def leave(info, at, previous, grads, x, dx1, weight, vectors, own, micros):
    rows, width = x.shape
    held = rows // own // 2
    row = pl.BlockSpec((own, width), lambda step, info: (2 * at + step, 0))
    more = {"input_output_aliases": {8: 0}} if previous else {}
    sums = like((8, width))
    return kernel_call(
        leave_kernel,
        "leave",
        info,
        (*grads, x, dx1, weight, vectors, *previous),
        [row] * 5
        + [resident(a) for a in (weight, vectors)]
        + [pl.BlockSpec(memory_space=pl.ANY)] * len(previous),
        [like((micros, own, width)), like((own, width), jnp.bfloat16), sums],
        [
            pl.BlockSpec((None, own, width), lambda step, info: (info[0] * held + at, 0, 0)),
            pl.BlockSpec((own, width), lambda step, info: (0, 0)),
            whole_block(sums),
        ],
        2,
        12 * own * width * width,
        16 * 2**20,
        **more,
    )


SWAP = ((0, 1), (1, 0))


class Tree:
    def __init__(self, kept, sent, order):
        self.count = lax.axis_size("dp")
        bits = self.count.bit_length() - 2
        shape = (2,) * bits + kept.shape[1:]
        self.order = [2 << bit for bit in order(bits)]
        self.kept, self.sent, self.bit = kept.reshape(shape), sent.reshape(shape), 1
        self.got, self.total = None, None

    def exchange(self):
        if self.total is not None or self.got is not None:
            return
        if self.bit:
            pairs = [(i, i ^ self.bit) for i in range(self.count)]
            self.got = lax.ppermute(self.sent, "dp", pairs)
        else:
            self.got = lax.ppermute(self.kept, "seq", SWAP)

    def add(self):
        if self.got is None:
            return
        total = self.kept.astype(jnp.float32) + self.got.astype(jnp.float32)
        self.got = None
        if not self.bit:
            self.total = total
            return
        total = total.astype(jnp.bfloat16)
        if not self.order:
            self.bit, self.kept = 0, total
            return
        self.bit = self.order.pop(0)
        mine = (lax.axis_index("dp") // self.bit) % 2
        self.kept = lax.dynamic_index_in_dim(total, mine, 0, keepdims=False)
        self.sent = lax.dynamic_index_in_dim(total, 1 - mine, 0, keepdims=False)


class Whole:
    def __init__(self, rows):
        self.count = lax.axis_size("dp")
        self.rows, self.bit, self.got, self.total = rows, 1, None, None

    def exchange(self):
        if self.total is not None or self.got is not None:
            return
        if self.bit < self.count:
            steps = [step * self.bit for step in (1, 2, 3) if step * self.bit < self.count]
            self.got = [
                lax.ppermute(self.rows, "dp", [(i, i ^ step) for i in range(self.count)])
                for step in steps
            ]
        else:
            self.got = [lax.ppermute(self.rows, "seq", SWAP)]

    def add(self):
        if self.got is None:
            return
        self.rows = sum(self.got, self.rows)
        self.got = None
        if self.bit >= self.count:
            self.total = self.rows
        self.bit *= 4


def exchange(trees):
    for tree in trees:
        tree.exchange()


def settle(trees, values):
    trees = [tree for tree in trees if tree.got is not None]
    gots, values = lax.optimization_barrier(([tree.got for tree in trees], values))
    for tree, got in zip(trees, gots):
        tree.got = got
        tree.add()
    return values


def finish(trees):
    while any(tree.total is None for tree in trees):
        exchange(trees)
        settle(trees, ())


def whole_sequences(
    targets,
    memory,
    row_kind,
    loss_mask,
    cotangent,
    norm_self_gain,
    norm_self_bias,
    self_input,
    self_query_bias,
    self_value_bias,
    self_output,
    self_output_bias,
    norm_cross_gain,
    norm_cross_bias,
    cross_query,
    cross_query_bias,
    cross_input,
    cross_value_bias,
    cross_output,
    cross_output_bias,
    norm_feed_gain,
    norm_feed_bias,
    feed_in,
    feed_in_bias,
    feed_out,
    feed_out_bias,
):
    micros, _, own, width = targets.shape
    held = micros // 2
    side = lax.axis_index("seq")
    parts = lax.axis_size("dp")
    place = lax.axis_index("dp")
    length = 2 * own
    pairs = HEADS * HEAD // 128

    def swap(rows, at, count, after=()):
        sent = lax.dynamic_slice_in_dim(rows, (1 - side) * held + at, count, axis=0)
        sent, after = lax.optimization_barrier((sent, after))
        return lax.ppermute(sent, "seq", SWAP), after

    def give(owns, got, at):
        got = got.astype(owns.dtype)
        return lax.dynamic_update_slice_in_dim(owns, got, (1 - side) * held + at, axis=0)

    def pack(*rows):
        zero = jnp.zeros((8 - len(rows), width), jnp.float32)
        return jnp.concatenate([jnp.stack(rows), zero])

    def batch(rows):
        return rows.reshape(held, length, -1)

    def flat(rows):
        return rows.reshape(held * length, -1)

    targets, memory = targets[:, 0], memory[:, 0]
    upstreams = (
        cotangent[:, 0].astype(jnp.float32) * loss_mask[:, 0].astype(jnp.float32)[..., None]
    ).astype(jnp.bfloat16)
    kinds = lax.dynamic_slice_in_dim(row_kind[:, 0], side * held, held, axis=0)
    info = jnp.concatenate([jnp.stack([side, place % 2]).astype(jnp.int32), kinds])

    self_vectors = pack(norm_self_gain, norm_self_bias)
    zero = jnp.zeros_like(self_query_bias)
    joint_bias = jnp.concatenate([self_query_bias, zero, self_value_bias])[None]
    pair_bias = jnp.concatenate([zero, cross_value_bias])[None]
    got, _ = swap(targets, 0, 1)
    entered = enter(
        info, None, held, (), held, targets, self_input, self_vectors, joint_bias, True
    )
    source_parts = enter(
        info, None, held, (), held, memory, cross_input, self_vectors, pair_bias, False
    )
    got, entered, source_parts = lax.optimization_barrier((got, entered, source_parts))
    attended = ()
    for at in range(held):
        if at + 1 < held:
            later, got = swap(targets, at + 1, 1, got)
        entered = enter(
            info, at, 1, entered, held, got, self_input, self_vectors, joint_bias, True
        )
        joint = batch(entered[1])
        attended = attend(info, at, 1, attended, joint, joint, joint, True, (0, 1, 2))
        if at + 1 < held:
            entered, attended, got = lax.optimization_barrier((entered, attended, later))
        if at + 2 == held:
            memory_gots, got = swap(memory, 0, held, got)
    inputs, joint = entered[0], batch(entered[1])
    self_mixed, self_raised, self_inverse = attended
    after_self, cross_queries = middle(
        info,
        inputs,
        flat(self_mixed),
        self_output,
        cross_query,
        pack(self_output_bias, norm_cross_gain, norm_cross_bias, cross_query_bias),
        own,
    )
    cross_queries, source_parts, memory_gots = lax.optimization_barrier(
        (cross_queries, source_parts, memory_gots)
    )
    upstream_gots, memory_gots = swap(upstreams, 0, held, memory_gots)
    sources, cross_pairs = enter(
        info, 0, held, source_parts, held, memory_gots, cross_input, self_vectors, pair_bias, False
    )
    cross_queries, cross_pairs = batch(cross_queries), batch(cross_pairs)
    cross_mixed, cross_raised, cross_inverse = attend(
        info, 0, held, (), cross_queries, cross_pairs, cross_pairs, False, (0, 0, 1)
    )
    results, result_gots, grad_cross, cross_upstream, feed_sums, hidden_sums, *feed_parts = feed(
        info,
        after_self,
        flat(cross_mixed),
        upstreams,
        upstream_gots,
        cross_output,
        feed_in,
        feed_out,
        pack(cross_output_bias, norm_feed_gain, norm_feed_bias, feed_out_bias),
        feed_in_bias[None],
        parts,
    )
    feed_trees = [Tree(*feed_parts, low_first)]
    first = pairs // 2
    cross_inputs = (
        cross_queries, cross_pairs, cross_pairs, (0, 0, 1), cross_mixed, batch(cross_upstream),
        cross_raised, cross_inverse,
    )
    exchange(feed_trees)
    result_gots = lax.ppermute(result_gots, "seq", SWAP)
    half_grads = settle(feed_trees, attend_back((0, 0), (held, first), (), *cross_inputs))
    exchange(feed_trees)
    cross_grads = attend_back((0, first), (held, pairs - first), half_grads, *cross_inputs)
    (source_grads, source_gots, grad_self, self_upstream, return_sums, *mid_parts), back = settle(
        feed_trees,
        (return_rows(
            info,
            [flat(rows) for rows in cross_grads],
            after_self,
            grad_cross,
            flat(self_mixed),
            sources,
            cross_query,
            cross_input,
            self_output,
            pack(norm_cross_gain, norm_cross_bias),
            own,
            micros,
            parts,
        ), result_gots),
    )
    results = give(results, back, 0)
    mid_trees = [Tree(*mid_parts, low_first)]
    exchange(feed_trees + mid_trees)
    self_inputs = (
        joint, joint, joint, (0, 1, 2), self_mixed, batch(self_upstream), self_raised, self_inverse
    )
    source_gots = lax.ppermute(source_gots, "seq", SWAP)
    grads = settle(feed_trees + mid_trees, attend_back((0, 0), (1, pairs), (), *self_inputs))
    exchange(feed_trees + mid_trees)
    kept, leave_sums = (), []
    trees = feed_trees + mid_trees
    for at in range(held):
        if at == held - 1:
            late_parts = last_weight(
                info, [flat(rows) for rows in grads], inputs, self_vectors, own, parts
            )
            late_trees = [
                Tree(*late_parts[0:2], low_first),
                Tree(*late_parts[2:4], second_first),
            ]
            grads = settle(trees, lax.optimization_barrier((grads, late_parts[0]))[0])
            trees = trees + late_trees
            exchange(trees)
            grads = settle(late_trees, grads)
            exchange(trees)
        kept, got, sums = leave(
            info, at, kept, [flat(rows) for rows in grads], inputs, grad_self,
            self_input, self_vectors, own, micros,
        )
        leave_sums.append(sums)
        if at < held - 1:
            grads, kept = lax.optimization_barrier((grads, kept))
            back = lax.ppermute(got, "seq", SWAP)
            grads, back, source_gots = settle(
                trees,
                (attend_back((at + 1, 0), (1, pairs), grads, *self_inputs), back, source_gots),
            )
            exchange(trees)
            back = back.astype(kept.dtype)[None]
            kept = (
                lax.dynamic_update_slice_in_dim(kept, back, (1 - side) * held + at, axis=0),
            )
    input_grads, got, sums = settle(trees, (kept, got, sum(leave_sums)))
    late_sums = Whole(
        jnp.concatenate([sums, feed_sums, return_sums, hidden_sums.reshape(-1, width)], axis=0)
    )
    trees = trees + [late_sums]
    exchange(trees)
    back = lax.ppermute(got, "seq", SWAP)
    settle(trees, ())
    exchange(trees)
    back = settle(trees, back)
    exchange(trees)
    input_grads = give(input_grads, back[None], held - 1)
    finish(trees)
    rows = width // parts
    inner_rows = feed_in.shape[1] // parts
    final = [None] * 21

    def mine(row):
        return lax.dynamic_slice_in_dim(row, place * (row.shape[0] // parts), row.shape[0] // parts)

    def widen(block):
        return jnp.concatenate([block[i : i + rows] for i in range(0, len(block), rows)], axis=1)

    for at, index in enumerate((0, 1, 3, 4, 14, 15, 16, 20, 7, 8, 6, 10, 12)):
        row = at if at < 4 else at + 4 if at < 8 else at + 8
        final[index] = mine(late_sums.total[row])
    final[18] = mine(late_sums.total[24:].reshape(-1))
    feed_total, mid_total = feed_trees[0].total, mid_trees[0].total
    final[19] = feed_total[:inner_rows]
    final[13] = feed_total[inner_rows : inner_rows + rows]
    final[17] = widen(feed_total[inner_rows + rows :])
    final[9] = mid_total[:rows]
    final[5] = mid_total[rows : 2 * rows]
    final[11] = widen(mid_total[2 * rows :])
    final[2] = jnp.concatenate([tree.total for tree in late_trees], axis=1)
    source_grads = give(source_grads, source_gots, 0)
    return (results[:, None], input_grads[:, None], source_grads[:, None]) + tuple(final)


def solution(mesh):
    in_specs = (
        P(None, "dp", "seq", None),
        P(None, "dp", "seq", None),
        P(None, "dp"),
        P(None, "dp", "seq"),
        P(None, "dp", "seq", None),
        P(),
        P(),
        P(),
        P(),
        P(),
        P(),
        P(),
        P(),
        P(),
        P(),
        P(),
        P(),
        P(),
        P(),
        P(),
        P(),
        P(),
        P(),
        P(),
        P(),
        P(),
    )
    out_specs = (
        P(None, "dp", "seq", None),
        P(None, "dp", "seq", None),
        P(None, "dp", "seq", None),
        P("dp"),
        P("dp"),
        P("dp", None),
        P("dp"),
        P("dp"),
        P("dp", None),
        P("dp"),
        P("dp"),
        P("dp"),
        P("dp", None),
        P("dp"),
        P("dp", None),
        P("dp"),
        P("dp", None),
        P("dp"),
        P("dp"),
        P("dp"),
        P("dp", None),
        P("dp"),
        P("dp", None),
        P("dp"),
    )

    def on_device(*arguments):
        micros = arguments[0].shape[0]
        rows = lax.axis_size("dp")
        pairs = lax.axis_size("seq") == 2 and micros % 2 == 0
        whole = pairs and rows & (rows - 1) == 0
        return (whole_sequences if whole else split_sequences)(*arguments)

    return jax.shard_map(
        on_device, mesh=mesh, in_specs=in_specs, out_specs=out_specs, check_vma=False
    )
```

```python
import functools

import jax
import jax.numpy as jnp
from jax import lax
from jax.experimental import pallas as pl
from jax.experimental.pallas import tpu as pltpu
from jax.sharding import PartitionSpec as P

HEADS = 12
HEAD = 64


epsilon = 1e-05
blocked_score = -1e30


def normed(values, norm_gain, norm_shift):
    center = values - jnp.mean(values, axis=-1, keepdims=True)
    spread = jnp.mean(center * center, axis=-1, keepdims=True)
    return center * lax.rsqrt(spread + epsilon) * norm_gain + norm_shift


def normed_back(values, norm_gain, norm_shift, upstream):
    unused, pullback = jax.vjp(normed, values, norm_gain, norm_shift)
    return pullback(upstream)


def gelu_exact(values):
    return jax.nn.gelu(values, approximate=False)


def project_rows(row_block, weight):
    return jnp.einsum("bpd,de->bpe", row_block, weight, preferred_element_type=jnp.float32)


def project_back(row_block, weight):
    return jnp.einsum("bpe,de->bpd", row_block, weight, preferred_element_type=jnp.float32)


def outer_sum(first_rows, second_rows):
    return jnp.einsum("bpd,bpe->de", first_rows, second_rows, preferred_element_type=jnp.float32)


def split_heads(row_block):
    return row_block.reshape(row_block.shape[0], row_block.shape[1], HEADS, HEAD)


def masked_scores(queries, key_rows, allowed):
    scores = jnp.einsum(
        "bphe,bshe->bhps",
        split_heads(queries),
        split_heads(key_rows),
        preferred_element_type=jnp.float32,
    )
    if allowed is None:
        return scores
    return jnp.where(allowed[:, None], scores, blocked_score)


def attend_forward(queries, key_rows, values, allowed):
    scores = masked_scores(queries, key_rows, allowed)
    highest_score = jnp.max(scores, axis=-1, keepdims=True)
    raised = jnp.exp(scores - highest_score)
    totals = jnp.sum(raised, axis=-1, keepdims=True)
    weights = (raised / totals).astype(jnp.bfloat16)
    mixed = jnp.einsum(
        "bhps,bshe->bphe", weights, split_heads(values), preferred_element_type=jnp.float32
    )
    return (mixed.reshape(queries.shape).astype(jnp.bfloat16), highest_score + jnp.log(totals))


def attend_backward(queries, key_rows, values, allowed, log_totals, upstream):
    weights = jnp.exp(masked_scores(queries, key_rows, allowed) - log_totals)
    upstream_heads = split_heads(upstream)
    value_grads = jnp.einsum(
        "bhps,bphe->bshe",
        weights.astype(jnp.bfloat16),
        upstream_heads,
        preferred_element_type=jnp.float32,
    )
    weight_grads = jnp.einsum(
        "bphe,bshe->bhps", upstream_heads, split_heads(values), preferred_element_type=jnp.float32
    )
    score_grads = weights * (weight_grads - jnp.sum(weight_grads * weights, axis=-1, keepdims=True))
    score_low = score_grads.astype(jnp.bfloat16)
    query_grads = jnp.einsum(
        "bhps,bshe->bphe", score_low, split_heads(key_rows), preferred_element_type=jnp.float32
    ).reshape(queries.shape)
    key_grads = jnp.einsum(
        "bhps,bphe->bshe", score_low, split_heads(queries), preferred_element_type=jnp.float32
    ).reshape(key_rows.shape)
    return (query_grads, jnp.concatenate([key_grads, value_grads.reshape(key_rows.shape)], axis=-1))


def split_sequences(
    targets,
    memory,
    row_kind,
    loss_mask,
    cotangent,
    norm_self_gain,
    norm_self_bias,
    self_input,
    self_query_bias,
    self_value_bias,
    self_output,
    self_output_bias,
    norm_cross_gain,
    norm_cross_bias,
    cross_query,
    cross_query_bias,
    cross_input,
    cross_value_bias,
    cross_output,
    cross_output_bias,
    norm_feed_gain,
    norm_feed_bias,
    feed_in,
    feed_in_bias,
    feed_out,
    feed_out_bias,
):
    model_width = targets.shape[3]
    part_rows = targets.shape[2]
    key_span = part_rows * lax.axis_size("seq")
    query_scale = HEAD ** (-0.5)
    places = lax.axis_index("seq") * part_rows + jnp.arange(part_rows)
    causal = jnp.arange(key_span)[None, :] <= places[:, None]
    results, input_grads, source_grads = ([], [], [])
    totals = None
    for micro_index in range(targets.shape[0]):
        inputs = targets[micro_index].astype(jnp.float32)
        memory_local = memory[micro_index]
        allowed = causal[None] | (row_kind[micro_index] == 1)[:, None, None]
        first_normed = normed(inputs, norm_self_gain, norm_self_bias).astype(jnp.bfloat16)
        self_joint = project_rows(first_normed, self_input)
        queries = ((self_joint[..., :model_width] + self_query_bias) * query_scale).astype(
            jnp.bfloat16
        )
        own_pairs = jnp.concatenate(
            [
                self_joint[..., model_width : 2 * model_width],
                self_joint[..., 2 * model_width :] + self_value_bias,
            ],
            axis=-1,
        ).astype(jnp.bfloat16)
        gathered_self = lax.all_gather(own_pairs, "seq", axis=1, tiled=True)
        key_rows = gathered_self[..., :model_width]
        value_rows = gathered_self[..., model_width:]
        self_mixed, self_totals = attend_forward(queries, key_rows, value_rows, allowed)
        after_self = inputs + project_rows(self_mixed, self_output) + self_output_bias
        second_normed = normed(after_self, norm_cross_gain, norm_cross_bias).astype(jnp.bfloat16)
        cross_queries = (
            (project_rows(second_normed, cross_query) + cross_query_bias) * query_scale
        ).astype(jnp.bfloat16)
        joined = project_rows(lax.all_gather(memory_local, "seq", axis=1, tiled=True), cross_input)
        gathered_cross = jnp.concatenate(
            [joined[..., :model_width], joined[..., model_width:] + cross_value_bias], axis=-1
        ).astype(jnp.bfloat16)
        cross_keys = gathered_cross[..., :model_width]
        cross_values = gathered_cross[..., model_width:]
        cross_mixed, cross_totals = attend_forward(cross_queries, cross_keys, cross_values, None)
        after_cross = after_self + project_rows(cross_mixed, cross_output) + cross_output_bias
        third_normed = normed(after_cross, norm_feed_gain, norm_feed_bias).astype(jnp.bfloat16)
        activated, gelu_pullback = jax.vjp(
            gelu_exact, project_rows(third_normed, feed_in) + feed_in_bias
        )
        activated_low = activated.astype(jnp.bfloat16)
        results.append(
            (after_cross + project_rows(activated_low, feed_out) + feed_out_bias).astype(
                jnp.bfloat16
            )
        )
        pieces = [None] * 21
        grad_output = (
            cotangent[micro_index].astype(jnp.float32)
            * loss_mask[micro_index].astype(jnp.float32)[..., None]
        )
        output_low = grad_output.astype(jnp.bfloat16)
        pieces[19] = outer_sum(activated_low, output_low)
        pieces[20] = jnp.sum(grad_output, axis=(0, 1))
        grad_hidden = gelu_pullback(project_back(output_low, feed_out))[0]
        hidden_low = grad_hidden.astype(jnp.bfloat16)
        pieces[17] = outer_sum(third_normed, hidden_low)
        pieces[18] = jnp.sum(grad_hidden, axis=(0, 1))
        through_feed, pieces[15], pieces[16] = normed_back(
            after_cross, norm_feed_gain, norm_feed_bias, project_back(hidden_low, feed_in)
        )
        grad_cross = grad_output + through_feed
        cross_low = grad_cross.astype(jnp.bfloat16)
        pieces[13] = outer_sum(cross_mixed, cross_low)
        pieces[14] = jnp.sum(grad_cross, axis=(0, 1))
        cross_upstream = project_back(cross_low, cross_output).astype(jnp.bfloat16)
        cross_query_grads, cross_pair_grads = attend_backward(
            cross_queries, cross_keys, cross_values, None, cross_totals, cross_upstream
        )
        own_cross = lax.psum_scatter(
            cross_pair_grads.astype(jnp.bfloat16), "seq", scatter_dimension=1, tiled=True
        ).astype(jnp.float32)
        pieces[12] = jnp.sum(own_cross[..., model_width:], axis=(0, 1))
        own_cross_low = own_cross.astype(jnp.bfloat16)
        pieces[11] = outer_sum(memory_local, own_cross_low)
        source_grads.append(project_back(own_cross_low, cross_input))
        scaled_cross = cross_query_grads * query_scale
        pieces[10] = jnp.sum(scaled_cross, axis=(0, 1))
        scaled_cross_low = scaled_cross.astype(jnp.bfloat16)
        pieces[9] = outer_sum(second_normed, scaled_cross_low)
        through_cross, pieces[7], pieces[8] = normed_back(
            after_self,
            norm_cross_gain,
            norm_cross_bias,
            project_back(scaled_cross_low, cross_query),
        )
        grad_self = grad_cross + through_cross
        self_low = grad_self.astype(jnp.bfloat16)
        pieces[5] = outer_sum(self_mixed, self_low)
        pieces[6] = jnp.sum(grad_self, axis=(0, 1))
        self_upstream = project_back(self_low, self_output).astype(jnp.bfloat16)
        self_query_grads, self_pair_grads = attend_backward(
            queries, key_rows, value_rows, allowed, self_totals, self_upstream
        )
        own_self = lax.psum_scatter(
            self_pair_grads.astype(jnp.bfloat16), "seq", scatter_dimension=1, tiled=True
        ).astype(jnp.float32)
        scaled_self = self_query_grads * query_scale
        pieces[3] = jnp.sum(scaled_self, axis=(0, 1))
        pieces[4] = jnp.sum(own_self[..., model_width:], axis=(0, 1))
        joint_low = jnp.concatenate([scaled_self, own_self], axis=-1).astype(jnp.bfloat16)
        pieces[2] = outer_sum(first_normed, joint_low)
        through_first, pieces[0], pieces[1] = normed_back(
            inputs, norm_self_gain, norm_self_bias, project_back(joint_low, self_input)
        )
        input_grads.append(grad_self + through_first)
        totals = (
            pieces
            if totals is None
            else [running + added for running, added in zip(totals, pieces)]
        )
    def reduced(total):
        block = lax.psum_scatter(
            total.astype(jnp.bfloat16), "dp", scatter_dimension=0, tiled=True
        )
        return lax.psum(block, "seq").astype(jnp.float32)

    final = [reduced(total) for total in totals]
    return (jnp.stack(results), jnp.stack(input_grads), jnp.stack(source_grads)) + tuple(final)


def contract(first, second, first_dim, second_dim):
    return lax.dot_general(
        first, second, (((first_dim,), (second_dim,)), ((), ())), preferred_element_type=jnp.float32
    )


def head_masks(pair):
    lane = lax.broadcasted_iota(jnp.int32, (1, pair.shape[1]), 1)
    zero = jnp.zeros((), pair.dtype)
    return (jnp.where(lane < HEAD, pair, zero), jnp.where(lane < HEAD, zero, pair))


LIMIT = 62 * 2**20


def attend_kernel(info_ref, q_ref, k_ref, v_ref, *refs, use_mask, start):
    o_ref, e_ref, r_ref, mask_ref = refs[-4:]
    length = k_ref.shape[1]
    half = length // 2
    values_turned = v_ref[0].T
    ones = jnp.ones((16, length), jnp.bfloat16)

    def run(masked, shifted):
        lowest, highest = None, None
        for at in range(2):
            queries_at = slice(at * half, (at + 1) * half)
            mixed = []
            for head, queries in enumerate(head_masks(q_ref[0, queries_at, :])):
                scores = contract(k_ref[0], queries, 1, 1)
                if shifted:
                    if masked:
                        seen = mask_ref[:, queries_at].astype(jnp.float32) > 0
                        scores = jnp.where(seen, scores, blocked_score)
                    scores = scores - jnp.max(scores, axis=0, keepdims=True)
                low = jnp.exp(scores).astype(jnp.bfloat16)
                if masked:
                    low = low * mask_ref[:, queries_at]
                e_ref[0, head, :, queries_at] = low
                turned = jnp.concatenate(
                    [values_turned[head * HEAD : (head + 1) * HEAD], ones], axis=0
                )
                sums = contract(turned, low, 1, 0)
                total = sums[HEAD : HEAD + 1]
                if not shifted:
                    lowest = total if lowest is None else jnp.minimum(lowest, total)
                    highest = total if highest is None else jnp.maximum(highest, total)
                inverse = 1.0 / total
                r_ref[0, 0, head : head + 1, queries_at] = inverse
                mixed.append(sums[:HEAD] * inverse)
            o_ref[0, queries_at, :] = jnp.concatenate(mixed, axis=0).T.astype(jnp.bfloat16)
        if not shifted:
            in_range = (jnp.min(lowest) > 1e-20) & (jnp.max(highest) < 1e30)

            @pl.when(jnp.logical_not(in_range))
            def _():
                run(masked, True)

    if not use_mask:
        run(False, False)
        return
    causal = info_ref[2 + start + pl.program_id(0)] == 0

    @pl.when(causal & (pl.program_id(1) == 0))
    def _():
        later = info_ref[0] * half
        query = lax.broadcasted_iota(jnp.int32, (1, length), 1)
        query = jnp.where(query < half, query + later, query - later)

        @pl.loop(0, length, step=64)
        def _(row):
            key = lax.broadcasted_iota(jnp.int32, (64, 1), 0) + row
            key = jnp.where(key < half, key + later, key - later)
            seen = jnp.where(key <= query, 1.0, 0.0)
            mask_ref[pl.ds(pl.multiple_of(row, 64), 64), :] = seen.astype(jnp.bfloat16)

    @pl.when(causal)
    def _():
        run(True, False)

    @pl.when(jnp.logical_not(causal))
    def _():
        run(False, False)


def attend(info, start, count_now, previous, queries, keys, values, use_mask, offsets):
    count, length = queries.shape[:2]
    pairs = HEADS * HEAD // 128
    width = HEADS * HEAD

    def spec(offset):
        return pl.BlockSpec((1, length, 128), lambda s, p, info: (start + s, 0, offset * pairs + p))

    place = lambda s, p, info: (start + s, p, 0, 0)
    return pl.pallas_call(
        functools.partial(attend_kernel, use_mask=use_mask, start=start),
        grid_spec=pltpu.PrefetchScalarGridSpec(
            num_scalar_prefetch=1,
            grid=(count_now, pairs),
            in_specs=[spec(offset) for offset in offsets]
            + [pl.BlockSpec(memory_space=pl.ANY)] * len(previous),
            out_specs=[
                spec(0),
                pl.BlockSpec((1, 2, length, length), place),
                pl.BlockSpec((1, 1, 2, length), place),
            ],
            scratch_shapes=[pltpu.VMEM((length, length), jnp.bfloat16)],
        ),
        out_shape=[
            jax.ShapeDtypeStruct((count, length, width), jnp.bfloat16),
            jax.ShapeDtypeStruct((count, HEADS, length, length), jnp.bfloat16),
            jax.ShapeDtypeStruct((count, pairs, 2, length), jnp.float32),
        ],
        input_output_aliases={4: 0, 5: 1, 6: 2} if previous else {},
        compiler_params=pltpu.CompilerParams(vmem_limit_bytes=LIMIT),
        cost_estimate=pl.CostEstimate(
            flops=4 * count_now * HEADS * length * length * 256,
            bytes_accessed=count_now * HEADS * length * length * 2,
            transcendentals=count_now * HEADS * length * length,
        ),
        name="attend",
    )(info, queries, keys, values, *previous)


def attend_back_kernel(q_ref, k_ref, v_ref, o_ref, g_ref, e_ref, r_ref, dq_ref, dk_ref, dv_ref):
    length = k_ref.shape[1]
    keys_turned = k_ref[0].T
    upstream = g_ref[0].astype(jnp.float32)
    products = (o_ref[0].astype(jnp.float32) * upstream).T
    upstream = upstream.T
    parts, deltas = [], []
    for head in range(2):
        rows = slice(head * HEAD, (head + 1) * HEAD)
        inverse = r_ref[0, 0, head : head + 1, :]
        parts.append(upstream[rows] * inverse)
        deltas.append(jnp.sum(products[rows], axis=0, keepdims=True) * inverse)
    scaled = head_masks(jnp.concatenate(parts, axis=0).T.astype(jnp.bfloat16))
    queries = head_masks(q_ref[0])
    key_sum, value_sum, query_parts = 0.0, 0.0, []
    for head in range(2):
        rows = slice(head * HEAD, (head + 1) * HEAD)
        low = e_ref[0, head]
        grads = contract(v_ref[0], scaled[head], 1, 1)
        score_low = (low.astype(jnp.float32) * (grads - deltas[head])).astype(jnp.bfloat16)
        value_sum += contract(low, scaled[head], 1, 0)
        key_sum += contract(score_low, queries[head], 1, 0)
        query_parts.append(contract(keys_turned[rows], score_low, 1, 0))
    turned = jnp.concatenate(query_parts, axis=0) * (HEAD**-0.5)
    dq_ref[0] = turned.T.astype(jnp.bfloat16)
    dk_ref[0] = key_sum.astype(jnp.bfloat16)
    dv_ref[0] = value_sum.astype(jnp.bfloat16)


def attend_back(place, size, previous, queries, keys, values, offsets, *rest):
    count, length = queries.shape[:2]
    pairs = HEADS * HEAD // 128
    width = HEADS * HEAD

    start, first = place

    def spec(offset):
        return pl.BlockSpec(
            (1, length, 128), lambda s, p: (start + s, 0, offset * pairs + first + p)
        )

    kernel = attend_back_kernel
    aliases = {}
    if previous:
        kernel = lambda *refs: attend_back_kernel(*refs[3:])
        aliases = {0: 0, 1: 1, 2: 2}
    return pl.pallas_call(
        kernel,
        grid=size,
        in_specs=[pl.BlockSpec(memory_space=pl.ANY)] * len(previous)
        + [spec(offset) for offset in offsets]
        + [
            spec(0),
            spec(0),
            pl.BlockSpec((1, 2, length, length), lambda s, p: (start + s, first + p, 0, 0)),
            pl.BlockSpec((1, 1, 2, length), lambda s, p: (start + s, first + p, 0, 0)),
        ],
        out_specs=[spec(0)] * 3,
        out_shape=[jax.ShapeDtypeStruct((count, length, width), jnp.bfloat16)] * 3,
        input_output_aliases=aliases,
        compiler_params=pltpu.CompilerParams(vmem_limit_bytes=LIMIT),
        cost_estimate=pl.CostEstimate(
            flops=16 * size[0] * size[1] * length * length * 256,
            bytes_accessed=4 * size[0] * size[1] * length * length,
            transcendentals=0,
        ),
        name="attend_back",
    )(*previous, queries, keys, values, *rest)


def normal_parts(values):
    center = values - jnp.mean(values, axis=-1, keepdims=True)
    inverse = lax.rsqrt(jnp.mean(center * center, axis=-1, keepdims=True) + epsilon)
    return center * inverse, inverse


def normal_back(unit, inverse, norm_gain, upstream):
    inner = upstream * norm_gain
    shift = jnp.mean(inner, axis=-1, keepdims=True)
    tilt = jnp.mean(inner * unit, axis=-1, keepdims=True)
    return inverse * (inner - shift - unit * tilt)


def gelu_parts(values):
    size = jnp.abs(values)
    ratio = 1.0 / (1.0 + 0.2316418882663604 * size)
    series = 0.5307027145
    for weight in (-0.7265760135, 0.7107068705, -0.142248368, 0.127414796):
        series = series * ratio + weight
    bell = jnp.exp(-0.5 * values * values)
    upper = series * ratio * bell
    chance = jnp.where(values < 0, upper, 1.0 - upper)
    return values * chance, chance + values * (0.3989422804014327 * bell)


def column_sum(values):
    return jnp.sum(values, axis=0, keepdims=True)


def resident(array):
    return pl.BlockSpec(array.shape, lambda *_: (0,) * array.ndim, pipeline_mode=pl.Buffered(1))


def whole_block(array):
    return pl.BlockSpec(array.shape, lambda *_: (0,) * len(array.shape))


def like(shape, dtype=jnp.float32):
    return jax.ShapeDtypeStruct(tuple(shape), dtype)


def pick(take_first, first_ref, second_ref):
    return jnp.where(take_first, first_ref[...], second_ref[...])


ONCE = {"pipeline_mode": pl.Buffered(1)}


def own_spec(own, width, held, last, **more):
    def place(step, info):
        return (info[0] * held + jnp.minimum(step, last) // 2, 0, 0)

    return pl.BlockSpec((None, own, width), place, **more)


def got_spec(own, width, last, **more):
    return pl.BlockSpec(
        (None, own, width), lambda step, info: (jnp.minimum(step, last) // 2, 0, 0), **more
    )


def row_spec(own, width, last, **more):
    return pl.BlockSpec((own, width), lambda step, info: (jnp.minimum(step, last), 0), **more)


def kernel_call(kernel, name, info, arrays, in_specs, outs, out_specs, grid, flops, moved, **more):
    scratch = more.pop("scratch", [])
    return pl.pallas_call(
        kernel,
        grid_spec=pltpu.PrefetchScalarGridSpec(
            num_scalar_prefetch=1,
            grid=(grid,),
            in_specs=in_specs,
            out_specs=out_specs,
            scratch_shapes=scratch,
        ),
        out_shape=outs,
        compiler_params=pltpu.CompilerParams(
            vmem_limit_bytes=more.pop("limit", LIMIT)
        ),
        cost_estimate=pl.CostEstimate(flops=flops, bytes_accessed=moved, transcendentals=0),
        name=name,
        **more,
    )(info, *arrays)


def enter_kernel(info_ref, source_ref, w_ref, vec_ref, bias_ref, *refs, norm):
    x_ref, out_ref = refs[-2:]
    x = source_ref[...]
    x_ref[...] = x
    if norm:
        unit, _ = normal_parts(x.astype(jnp.float32))
        x = (unit * vec_ref[0:1, :] + vec_ref[1:2, :]).astype(jnp.bfloat16)
    width = x.shape[1]
    for start in range(0, w_ref.shape[1], width):
        part = slice(start, start + width)
        total = contract(x, w_ref[:, part], 1, 0) + bias_ref[:, part]
        if norm and start == 0:
            total = total * (HEAD**-0.5)
        out_ref[:, part] = total.astype(jnp.bfloat16)


def enter(info, first, count, previous, held, rows_in, weight, vectors, bias, norm):
    own, width = rows_in.shape[1:]
    rows = 2 * held * own
    wide = weight.shape[1]
    if first is None:
        place = lambda step, info: (info[0] * held + step, 0, 0)
        row = lambda step, info: (2 * step, 0)
    else:
        place = lambda step, info: (step, 0, 0)
        row = lambda step, info: (2 * (first + step) + 1, 0)
    return kernel_call(
        functools.partial(enter_kernel, norm=norm),
        "enter",
        info,
        (rows_in, weight, vectors, bias, *previous),
        [pl.BlockSpec((None, own, width), place)]
        + [resident(a) for a in (weight, vectors, bias)]
        + [pl.BlockSpec(memory_space=pl.ANY)] * len(previous),
        [like((rows, width), jnp.bfloat16), like((rows, wide), jnp.bfloat16)],
        [pl.BlockSpec((own, width), row), pl.BlockSpec((own, wide), row)],
        count,
        2 * count * own * width * wide,
        2 * count * own * (2 * width + wide),
        input_output_aliases={5: 0, 6: 1} if previous else {},
    )


def middle_kernel(info_ref, x_ref, mixed_ref, wo_ref, wq_ref, vec_ref, after_ref, q_ref):
    out_bias, gain, shift, query_bias = (vec_ref[i : i + 1, :] for i in range(4))
    after = (
        x_ref[...].astype(jnp.float32) + contract(mixed_ref[...], wo_ref[...], 1, 0) + out_bias
    )
    after_ref[...] = after
    unit, _ = normal_parts(after)
    normal = (unit * gain + shift).astype(jnp.bfloat16)
    queries = (contract(normal, wq_ref[...], 1, 0) + query_bias) * (HEAD**-0.5)
    q_ref[...] = queries.astype(jnp.bfloat16)


def middle(info, x, mixed, wo, wq, vectors, own):
    rows, width = x.shape
    last = rows // own - 1
    spec = row_spec(own, width, last)
    return kernel_call(
        middle_kernel,
        "middle",
        info,
        (x, mixed, wo, wq, vectors),
        [spec, spec] + [resident(a) for a in (wo, wq, vectors)],
        [like((rows, width)), like((rows, width), jnp.bfloat16)],
        [spec, spec],
        rows // own,
        4 * rows * width * width,
        10 * rows * width,
    )


def write_split(core, rows, kept_ref, sent_ref, start):
    half = rows.shape[0] // 2
    low = rows.astype(jnp.bfloat16)
    place = slice(start, start + half)

    @pl.when(core == 0)
    def _():
        kept_ref[0, place, :] = low[:half]
        sent_ref[0, place, :] = low[half:]

    @pl.when(core != 0)
    def _():
        kept_ref[0, place, :] = low[half:]
        sent_ref[0, place, :] = low[:half]


def write_wide(core, rows, kept_ref, sent_ref, start):
    half, width = rows.shape[0] // 2, kept_ref.shape[2]
    for at in range(rows.shape[1] // width):
        part = rows[:, at * width : (at + 1) * width]
        write_split(core, part, kept_ref, sent_ref, start + at * half)


def acc_rows(ref, at, rows):
    return ref[pl.ds(pl.multiple_of(at * rows, 16), rows), :]


def piece(parts, high, wide, steps, order):
    bits = parts.bit_length() - 2

    def late(step, info):
        at = jnp.maximum(step - steps, 0)
        place = 0
        for bit in order(bits):
            place = 2 * place + (at // 2**bit) % 2
        return (place, 0, 0)

    return (
        [pl.BlockSpec((1, high, wide), late)] * 2,
        [like((parts // 2, high, wide), jnp.bfloat16)] * 2,
    )


def low_first(bits):
    return list(range(bits))


def second_first(bits):
    return list(range(bits))[1:2] + [0] + list(range(2, bits))


def put_rows(step, value, own_ref, got_ref):
    @pl.when(step % 2 == 0)
    def _():
        own_ref[...] = value.astype(own_ref.dtype)

    @pl.when(step % 2 != 0)
    def _():
        got_ref[...] = value.astype(got_ref.dtype)


def feed_kernel(
    info_ref, x_ref, mixed_ref, dyo_ref, dyg_ref, wc_ref, wi_ref, wo_ref, vec_ref, bi_ref,
    own_ref, got_ref, dx_ref, do_ref, vsum_ref, bsum_ref, kept_ref, sent_ref, ai_ref, ao_ref,
    ac_ref, *, steps, chunk, parts,
):
    step = pl.program_id(0)

    @pl.when(step == 0)
    def _():
        for ref in (vsum_ref, bsum_ref, ai_ref, ao_ref, ac_ref):
            ref[...] = jnp.zeros_like(ref)

    @pl.when(step < steps)
    def _():
        cross_bias, gain, shift, out_bias = (vec_ref[i : i + 1, :] for i in range(4))
        mixed = mixed_ref[...]
        x2 = x_ref[...] + contract(mixed, wc_ref[...], 1, 0) + cross_bias
        unit, inverse = normal_parts(x2)
        normal = (unit * gain + shift).astype(jnp.bfloat16)
        normal_turned = normal.T
        dy = pick(step % 2 == 0, dyo_ref, dyg_ref)
        dy_turned = dy.T
        result, upstream = None, None
        for start in range(0, wi_ref.shape[1], chunk):
            part = slice(start, start + chunk)
            hidden = contract(normal, wi_ref[:, part], 1, 0) + bi_ref[:, part]
            active, slope = gelu_parts(hidden)
            active = active.astype(jnp.bfloat16)
            down = contract(active, wo_ref[part, :], 1, 0)
            result = down if result is None else result + down
            grads = contract(dy, wo_ref[part, :], 1, 1) * slope
            bsum_ref[:, part] += column_sum(grads)
            low = grads.astype(jnp.bfloat16)
            up = contract(low, wi_ref[:, part], 1, 1)
            upstream = up if upstream is None else upstream + up
            ao_ref[:, part] += contract(dy_turned, active, 1, 0)
            ai_ref[:, part] += contract(normal_turned, low, 1, 0)
        put_rows(step, x2 + result + out_bias, own_ref, got_ref)
        wide = dy.astype(jnp.float32)
        dx = wide + normal_back(unit, inverse, gain, upstream)
        dx_ref[...] = dx
        dx_low = dx.astype(jnp.bfloat16)
        do_ref[...] = contract(dx_low, wc_ref[...], 1, 1).astype(jnp.bfloat16)
        ac_ref[...] += contract(mixed.T, dx_low, 1, 0)
        vsum_ref[0:1, :] += column_sum(dx)
        vsum_ref[1:2, :] += column_sum(upstream * unit)
        vsum_ref[2:3, :] += column_sum(upstream)
        vsum_ref[3:4, :] += column_sum(wide)

    @pl.when(step >= steps)
    def _():
        at = step - steps
        core = info_ref[1]
        width, wide = ai_ref.shape
        rows = 2 * width // parts
        inner = 2 * wide // parts
        columns = ao_ref[:, pl.ds(pl.multiple_of(at * inner, 128), inner)]
        write_split(core, columns.astype(jnp.bfloat16).T, kept_ref, sent_ref, 0)
        write_split(core, acc_rows(ac_ref, at, rows), kept_ref, sent_ref, inner // 2)
        write_wide(core, acc_rows(ai_ref, at, rows), kept_ref, sent_ref, (inner + rows) // 2)


def feed(info, x1, mixed, dys, dy_gots, wc, wi, wo, vectors, bi, parts, chunk=768):
    rows, width = x1.shape
    held, own = dy_gots.shape[:2]
    micros = dys.shape[0]
    inner = wi.shape[1]
    steps = 2 * held
    last = steps - 1
    row = row_spec(own, width, last)
    pieces = [piece(parts, (2 * inner + width) // parts, width, steps, low_first)]
    sums = [like((8, width)), like((1, inner))]
    return kernel_call(
        functools.partial(feed_kernel, steps=steps, chunk=chunk, parts=parts),
        "feed",
        info,
        (x1, mixed, dys, dy_gots, wc, wi, wo, vectors, bi),
        [row_spec(own, width, last, **ONCE)] * 2
        + [own_spec(own, width, held, last, **ONCE), got_spec(own, width, last, **ONCE)]
        + [resident(a) for a in (wc, wi, wo, vectors, bi)],
        [
            like((micros, own, width), jnp.bfloat16),
            like((held, own, width), jnp.bfloat16),
            like((rows, width)),
            like((rows, width), jnp.bfloat16),
        ]
        + sums
        + sum([p[1] for p in pieces], []),
        [own_spec(own, width, held, last), got_spec(own, width, last), row, row]
        + [whole_block(a) for a in sums]
        + sum([p[0] for p in pieces], []),
        steps + parts // 2,
        2 * rows * width * (6 * inner + 3 * width),
        60 * 2**20,
        scratch=[
            pltpu.VMEM((width, inner), jnp.float32),
            pltpu.VMEM((width, inner), jnp.float32),
            pltpu.VMEM((width, width), jnp.float32),
        ],
        limit=LIMIT,
    )


def return_kernel(
    info_ref, dq_ref, dk_ref, dv_ref, x_ref, dx_ref, mixed_ref, src_ref, wq_ref, wi_ref, wo_ref,
    vec_ref, own_ref, got_ref, dxo_ref, do_ref, vsum_ref, kept_ref, sent_ref, aq_ref, ao_ref,
    ai_ref, *, steps, parts,
):
    step = pl.program_id(0)

    @pl.when(step == 0)
    def _():
        for ref in (vsum_ref, aq_ref, ao_ref, ai_ref):
            ref[...] = jnp.zeros_like(ref)

    @pl.when(step < steps)
    def _():
        width = x_ref.shape[1]
        gain, shift = vec_ref[0:1, :], vec_ref[1:2, :]
        dq, dk, dv = dq_ref[...], dk_ref[...], dv_ref[...]
        upstream = contract(dq, wq_ref[...], 1, 1)
        unit, inverse = normal_parts(x_ref[...])
        normal = (unit * gain + shift).astype(jnp.bfloat16)
        dx = dx_ref[...] + normal_back(unit, inverse, gain, upstream)
        dxo_ref[...] = dx
        low = dx.astype(jnp.bfloat16)
        do_ref[...] = contract(low, wo_ref[...], 1, 1).astype(jnp.bfloat16)
        source = contract(dk, wi_ref[:, :width], 1, 1) + contract(dv, wi_ref[:, width:], 1, 1)
        put_rows(step, source, own_ref, got_ref)
        aq_ref[...] += contract(normal.T, dq, 1, 0)
        ao_ref[...] += contract(mixed_ref[...].T, low, 1, 0)
        turned = src_ref[...].T
        ai_ref[:, :width] += contract(turned, dk, 1, 0)
        ai_ref[:, width:] += contract(turned, dv, 1, 0)
        vsum_ref[0:1, :] += column_sum(upstream * unit)
        vsum_ref[1:2, :] += column_sum(upstream)
        vsum_ref[2:3, :] += column_sum(dx)
        vsum_ref[3:4, :] += column_sum(dq.astype(jnp.float32))
        vsum_ref[4:5, :] += column_sum(dv.astype(jnp.float32))

    @pl.when(step >= steps)
    def _():
        at = step - steps
        core = info_ref[1]
        rows = 2 * aq_ref.shape[0] // parts
        write_split(core, acc_rows(aq_ref, at, rows), kept_ref, sent_ref, 0)
        write_split(core, acc_rows(ao_ref, at, rows), kept_ref, sent_ref, rows // 2)
        write_wide(core, acc_rows(ai_ref, at, rows), kept_ref, sent_ref, rows)


def return_rows(info, grads, x1, dx2, mixed, sources, wq, wi, wo, vectors, own, micros, parts):
    rows, width = x1.shape
    held = rows // own // 2
    steps = 2 * held
    last = steps - 1
    row = row_spec(own, width, last)
    pieces = [piece(parts, 4 * width // parts, width, steps, low_first)]
    sums = like((8, width))
    return kernel_call(
        functools.partial(return_kernel, steps=steps, parts=parts),
        "return_rows",
        info,
        (*grads, x1, dx2, mixed, sources, wq, wi, wo, vectors),
        [row] * 7 + [resident(a) for a in (wq, wi, wo, vectors)],
        [
            like((micros, own, width)),
            like((held, own, width), jnp.bfloat16),
            like((rows, width)),
            like((rows, width), jnp.bfloat16),
            sums,
        ]
        + sum([p[1] for p in pieces], []),
        [own_spec(own, width, held, last), got_spec(own, width, last), row, row, whole_block(sums)]
        + sum([p[0] for p in pieces], []),
        steps + parts // 2,
        16 * rows * width * width,
        40 * 2**20,
        scratch=[
            pltpu.VMEM((width, width), jnp.float32),
            pltpu.VMEM((width, width), jnp.float32),
            pltpu.VMEM((width, 2 * width), jnp.float32),
        ],
    )


def last_weight_kernel(
    info_ref, dq_ref, dk_ref, dv_ref, x_ref, vec_ref, ka_ref, sa_ref, kb_ref, sb_ref, acc_ref,
    *, steps,
):
    step = pl.program_id(0)

    @pl.when(step == 0)
    def _():
        acc_ref[...] = jnp.zeros_like(acc_ref)

    @pl.when(step < steps)
    def _():
        unit, _ = normal_parts(x_ref[...].astype(jnp.float32))
        turned = (unit * vec_ref[0:1, :] + vec_ref[1:2, :]).astype(jnp.bfloat16).T
        width = x_ref.shape[1]
        for at, ref in enumerate((dq_ref, dk_ref, dv_ref)):
            acc_ref[:, at * width : (at + 1) * width] += contract(turned, ref[...], 1, 0)

    @pl.when(step >= steps)
    def _():
        rows = acc_rows(acc_ref, step - steps, 2 * ka_ref.shape[1])
        half = ka_ref.shape[2]
        write_split(info_ref[1], rows[:, :half], ka_ref, sa_ref, 0)
        write_split(info_ref[1], rows[:, half:], kb_ref, sb_ref, 0)


def last_weight(info, grads, x, vectors, own, parts):
    rows, width = x.shape
    steps = rows // own
    row = row_spec(own, width, steps - 1)
    pieces = [
        piece(parts, width // parts, 3 * width // 2, steps, order)
        for order in (low_first, second_first)
    ]
    return kernel_call(
        functools.partial(last_weight_kernel, steps=steps),
        "last_weight",
        info,
        (*grads, x, vectors),
        [row] * 4 + [resident(vectors)],
        sum([p[1] for p in pieces], []),
        sum([p[0] for p in pieces], []),
        steps + parts // 2,
        6 * rows * width * width,
        20 * 2**20,
        scratch=[pltpu.VMEM((width, 3 * width), jnp.float32)],
    )


def leave_kernel(
    info_ref, dq_ref, dk_ref, dv_ref, x_ref, dx_ref, w_ref, vec_ref, *refs
):
    own_ref, got_ref, vsum_ref = refs[-3:]
    step = pl.program_id(0)

    @pl.when(step == 0)
    def _():
        vsum_ref[...] = jnp.zeros_like(vsum_ref)

    width = x_ref.shape[1]
    dq, dk, dv = dq_ref[...], dk_ref[...], dv_ref[...]
    upstream = (
        contract(dq, w_ref[:, :width], 1, 1)
        + contract(dk, w_ref[:, width : 2 * width], 1, 1)
        + contract(dv, w_ref[:, 2 * width :], 1, 1)
    )
    unit, inverse = normal_parts(x_ref[...].astype(jnp.float32))
    dx = dx_ref[...] + normal_back(unit, inverse, vec_ref[0:1, :], upstream)
    put_rows(step, dx, own_ref, got_ref)
    vsum_ref[0:1, :] += column_sum(upstream * unit)
    vsum_ref[1:2, :] += column_sum(upstream)
    vsum_ref[2:3, :] += column_sum(dq.astype(jnp.float32))
    vsum_ref[3:4, :] += column_sum(dv.astype(jnp.float32))


def leave(info, at, previous, grads, x, dx1, weight, vectors, own, micros):
    rows, width = x.shape
    held = rows // own // 2
    row = pl.BlockSpec((own, width), lambda step, info: (2 * at + step, 0))
    more = {"input_output_aliases": {8: 0}} if previous else {}
    sums = like((8, width))
    return kernel_call(
        leave_kernel,
        "leave",
        info,
        (*grads, x, dx1, weight, vectors, *previous),
        [row] * 5
        + [resident(a) for a in (weight, vectors)]
        + [pl.BlockSpec(memory_space=pl.ANY)] * len(previous),
        [like((micros, own, width)), like((own, width), jnp.bfloat16), sums],
        [
            pl.BlockSpec((None, own, width), lambda step, info: (info[0] * held + at, 0, 0)),
            pl.BlockSpec((own, width), lambda step, info: (0, 0)),
            whole_block(sums),
        ],
        2,
        12 * own * width * width,
        16 * 2**20,
        **more,
    )


SWAP = ((0, 1), (1, 0))


class Tree:
    def __init__(self, kept, sent, order):
        self.count = lax.axis_size("dp")
        bits = self.count.bit_length() - 2
        shape = (2,) * bits + kept.shape[1:]
        self.order = [2 << bit for bit in order(bits)]
        self.kept, self.sent, self.bit = kept.reshape(shape), sent.reshape(shape), 1
        self.got, self.total = None, None

    def exchange(self):
        if self.total is not None or self.got is not None:
            return
        if self.bit:
            pairs = [(i, i ^ self.bit) for i in range(self.count)]
            self.got = lax.ppermute(self.sent, "dp", pairs)
        else:
            self.got = lax.ppermute(self.kept, "seq", SWAP)

    def add(self):
        if self.got is None:
            return
        total = self.kept.astype(jnp.float32) + self.got.astype(jnp.float32)
        self.got = None
        if not self.bit:
            self.total = total
            return
        total = total.astype(jnp.bfloat16)
        if not self.order:
            self.bit, self.kept = 0, total
            return
        self.bit = self.order.pop(0)
        mine = (lax.axis_index("dp") // self.bit) % 2
        self.kept = lax.dynamic_index_in_dim(total, mine, 0, keepdims=False)
        self.sent = lax.dynamic_index_in_dim(total, 1 - mine, 0, keepdims=False)


def exchange(trees):
    for tree in trees:
        tree.exchange()


def settle(trees, values):
    trees = [tree for tree in trees if tree.got is not None]
    gots, values = lax.optimization_barrier(([tree.got for tree in trees], values))
    for tree, got in zip(trees, gots):
        tree.got = got
        tree.add()
    return values


def receive(trees, values):
    gots, values = lax.optimization_barrier(([tree.got for tree in trees], values))
    for tree, got in zip(trees, gots):
        tree.got = got
    return values


def finish(trees):
    while any(tree.total is None for tree in trees):
        exchange(trees)
        settle(trees, ())


MESH = pl.DeviceIdType.MESH


def partner(place, offset):
    bit = 1
    while bit <= offset:
        if offset & bit:
            place = place + bit * (1 - 2 * ((place // bit) % 2))
        bit *= 2
    return place


def tail_kernel(*refs, orders, groups):
    trees = len(orders)
    ins, refs = refs[: 2 * trees + 2], refs[2 * trees + 2 :]
    outs, refs = refs[: trees + 2], refs[trees + 2 :]
    send_sems, recv_sems = refs[-2:]
    scratch = list(refs[:-2])
    place = lax.axis_index("dp")
    side = lax.axis_index("seq")
    offsets = sorted({bit for order in orders for bit in order} | {o for g in groups for o in g})
    peers = [{"dp": partner(place, offset)} for offset in offsets] + [{"seq": 1 - side}]
    barrier = pltpu.get_barrier_semaphore()
    for peer in peers:
        pl.semaphore_signal(barrier, inc=1, device_id=peer, device_id_type=MESH)
    pl.semaphore_wait(barrier, len(peers))
    used = []

    def send(source, target, peer):
        at = len(used)
        copy = pltpu.make_async_remote_copy(
            src_ref=source,
            dst_ref=target,
            send_sem=send_sems.at[at],
            recv_sem=recv_sems.at[at],
            device_id=peer,
            device_id_type=MESH,
        )
        used.append(copy)
        copy.start()
        return copy

    other = {"seq": 1 - side}
    rows_copy = send(ins[-1], outs[-1], other)
    totals = []
    for at in range(trees):
        total = scratch.pop(0)
        total[...] = (
            ins[2 * at][...].astype(jnp.float32) + ins[2 * at + 1][...].astype(jnp.float32)
        ).astype(jnp.bfloat16)
        totals.append(total)
    sums = scratch.pop(0)
    sums[...] = ins[2 * trees][...]
    rounds = max(max(len(order) for order in orders) + 1, len(groups) + 1)
    for step in range(rounds):
        copies = []
        for at, order in enumerate(orders):
            if step < len(order):
                mine = (place // order[step]) % 2
                got = scratch.pop(0)
                peer = {"dp": partner(place, order[step])}
                copy = send(totals[at].at[1 - mine], got, peer)
                copies.append((copy, at, mine, got, scratch.pop(0)))
            elif step == len(order):
                got = scratch.pop(0)
                copies.append((send(totals[at], got, other), at, None, got, outs[at]))
        summed = []
        if step < len(groups):
            for offset in groups[step]:
                got = scratch.pop(0)
                summed.append((send(sums, got, {"dp": partner(place, offset)}), got))
        elif step == len(groups):
            got = scratch.pop(0)
            summed.append((send(sums, got, other), got))
        for copy, at, mine, got, target in copies:
            copy.wait()
            held = totals[at][...] if mine is None else totals[at][mine]
            total = held.astype(jnp.float32) + got[...].astype(jnp.float32)
            target[...] = total.astype(target.dtype)
            totals[at] = target
        if summed:
            target = scratch.pop(0) if step < len(groups) else outs[trees]
            total = sums[...]
            for copy, got in summed:
                copy.wait()
                total = total + got[...]
            target[...] = total
            sums = target
    rows_copy.wait()


def tail(trees, sums, rows, parts):
    orders = [tuple(tree.order) for tree in trees]
    groups, bit = [], 1
    while bit < parts:
        groups.append(tuple(step * bit for step in (1, 2, 3) if step * bit < parts))
        bit *= 4
    arrays = []
    for tree in trees:
        arrays += [tree.kept, tree.got]
    arrays += [sums, rows]
    totals = [pltpu.VMEM(tree.kept.shape, jnp.bfloat16) for tree in trees]
    scratch = totals + [pltpu.VMEM(sums.shape, jnp.float32)]
    shapes = [tree.kept.shape for tree in trees]
    copies = 1
    for step in range(max(max(len(order) for order in orders) + 1, len(groups) + 1)):
        for at, order in enumerate(orders):
            if step < len(order):
                shapes[at] = shapes[at][1:]
                scratch += [pltpu.VMEM(shapes[at], jnp.bfloat16)] * 2
                copies += 1
            elif step == len(order):
                scratch += [pltpu.VMEM(shapes[at], jnp.bfloat16)]
                copies += 1
        if step < len(groups):
            scratch += [pltpu.VMEM(sums.shape, jnp.float32)] * (len(groups[step]) + 1)
            copies += len(groups[step])
        elif step == len(groups):
            scratch += [pltpu.VMEM(sums.shape, jnp.float32)]
            copies += 1
    outs = [like(shape) for shape in shapes] + [like(sums.shape), like(rows.shape, rows.dtype)]
    vmem = pl.BlockSpec(memory_space=pltpu.VMEM)
    return pl.pallas_call(
        functools.partial(tail_kernel, orders=orders, groups=groups),
        in_specs=[vmem] * len(arrays),
        out_specs=[vmem] * len(outs),
        out_shape=outs,
        scratch_shapes=scratch + [pltpu.SemaphoreType.DMA((copies,))] * 2,
        compiler_params=pltpu.CompilerParams(
            collective_id=0, has_side_effects=True, vmem_limit_bytes=LIMIT
        ),
        cost_estimate=pl.CostEstimate(
            flops=2 * 10**10, bytes_accessed=10**7, transcendentals=0
        ),
        name="tail",
    )(*arrays)


def whole_sequences(
    targets,
    memory,
    row_kind,
    loss_mask,
    cotangent,
    norm_self_gain,
    norm_self_bias,
    self_input,
    self_query_bias,
    self_value_bias,
    self_output,
    self_output_bias,
    norm_cross_gain,
    norm_cross_bias,
    cross_query,
    cross_query_bias,
    cross_input,
    cross_value_bias,
    cross_output,
    cross_output_bias,
    norm_feed_gain,
    norm_feed_bias,
    feed_in,
    feed_in_bias,
    feed_out,
    feed_out_bias,
):
    micros, _, own, width = targets.shape
    held = micros // 2
    side = lax.axis_index("seq")
    parts = lax.axis_size("dp")
    place = lax.axis_index("dp")
    length = 2 * own
    pairs = HEADS * HEAD // 128

    def swap(rows, at, count, after=()):
        sent = lax.dynamic_slice_in_dim(rows, (1 - side) * held + at, count, axis=0)
        sent, after = lax.optimization_barrier((sent, after))
        return lax.ppermute(sent, "seq", SWAP), after

    def give(owns, got, at):
        got = got.astype(owns.dtype)
        return lax.dynamic_update_slice_in_dim(owns, got, (1 - side) * held + at, axis=0)

    def pack(*rows):
        zero = jnp.zeros((8 - len(rows), width), jnp.float32)
        return jnp.concatenate([jnp.stack(rows), zero])

    def batch(rows):
        return rows.reshape(held, length, -1)

    def flat(rows):
        return rows.reshape(held * length, -1)

    targets, memory = targets[:, 0], memory[:, 0]
    upstreams = (
        cotangent[:, 0].astype(jnp.float32) * loss_mask[:, 0].astype(jnp.float32)[..., None]
    ).astype(jnp.bfloat16)
    kinds = lax.dynamic_slice_in_dim(row_kind[:, 0], side * held, held, axis=0)
    info = jnp.concatenate([jnp.stack([side, place % 2]).astype(jnp.int32), kinds])

    self_vectors = pack(norm_self_gain, norm_self_bias)
    zero = jnp.zeros_like(self_query_bias)
    joint_bias = jnp.concatenate([self_query_bias, zero, self_value_bias])[None]
    pair_bias = jnp.concatenate([zero, cross_value_bias])[None]
    got, _ = swap(targets, 0, 1)
    entered = enter(
        info, None, held, (), held, targets, self_input, self_vectors, joint_bias, True
    )
    source_parts = enter(
        info, None, held, (), held, memory, cross_input, self_vectors, pair_bias, False
    )
    got, entered, source_parts = lax.optimization_barrier((got, entered, source_parts))
    attended = ()
    for at in range(held):
        if at + 1 < held:
            later, got = swap(targets, at + 1, 1, got)
        entered = enter(
            info, at, 1, entered, held, got, self_input, self_vectors, joint_bias, True
        )
        joint = batch(entered[1])
        attended = attend(info, at, 1, attended, joint, joint, joint, True, (0, 1, 2))
        if at + 1 < held:
            entered, attended, got = lax.optimization_barrier((entered, attended, later))
        if at + 2 == held:
            memory_gots, got = swap(memory, 0, held, got)
    inputs, joint = entered[0], batch(entered[1])
    self_mixed, self_raised, self_inverse = attended
    after_self, cross_queries = middle(
        info,
        inputs,
        flat(self_mixed),
        self_output,
        cross_query,
        pack(self_output_bias, norm_cross_gain, norm_cross_bias, cross_query_bias),
        own,
    )
    cross_queries, source_parts, memory_gots = lax.optimization_barrier(
        (cross_queries, source_parts, memory_gots)
    )
    upstream_gots, memory_gots = swap(upstreams, 0, held, memory_gots)
    sources, cross_pairs = enter(
        info, 0, held, source_parts, held, memory_gots, cross_input, self_vectors, pair_bias, False
    )
    cross_queries, cross_pairs = batch(cross_queries), batch(cross_pairs)
    cross_mixed, cross_raised, cross_inverse = attend(
        info, 0, held, (), cross_queries, cross_pairs, cross_pairs, False, (0, 0, 1)
    )
    results, result_gots, grad_cross, cross_upstream, feed_sums, hidden_sums, *feed_parts = feed(
        info,
        after_self,
        flat(cross_mixed),
        upstreams,
        upstream_gots,
        cross_output,
        feed_in,
        feed_out,
        pack(cross_output_bias, norm_feed_gain, norm_feed_bias, feed_out_bias),
        feed_in_bias[None],
        parts,
    )
    feed_trees = [Tree(*feed_parts, low_first)]
    first = pairs // 2
    cross_inputs = (
        cross_queries, cross_pairs, cross_pairs, (0, 0, 1), cross_mixed, batch(cross_upstream),
        cross_raised, cross_inverse,
    )
    exchange(feed_trees)
    result_gots = lax.ppermute(result_gots, "seq", SWAP)
    half_grads = settle(feed_trees, attend_back((0, 0), (held, first), (), *cross_inputs))
    exchange(feed_trees)
    cross_grads = attend_back((0, first), (held, pairs - first), half_grads, *cross_inputs)
    (source_grads, source_gots, grad_self, self_upstream, return_sums, *mid_parts), back = settle(
        feed_trees,
        (return_rows(
            info,
            [flat(rows) for rows in cross_grads],
            after_self,
            grad_cross,
            flat(self_mixed),
            sources,
            cross_query,
            cross_input,
            self_output,
            pack(norm_cross_gain, norm_cross_bias),
            own,
            micros,
            parts,
        ), result_gots),
    )
    results = give(results, back, 0)
    mid_trees = [Tree(*mid_parts, low_first)]
    exchange(feed_trees + mid_trees)
    self_inputs = (
        joint, joint, joint, (0, 1, 2), self_mixed, batch(self_upstream), self_raised, self_inverse
    )
    source_gots = lax.ppermute(source_gots, "seq", SWAP)
    grads = settle(feed_trees + mid_trees, attend_back((0, 0), (1, pairs), (), *self_inputs))
    exchange(feed_trees + mid_trees)
    kept, leave_sums = (), []
    trees = feed_trees + mid_trees
    for at in range(held):
        if at == held - 1:
            late_parts = last_weight(
                info, [flat(rows) for rows in grads], inputs, self_vectors, own, parts
            )
            late_trees = [
                Tree(*late_parts[0:2], low_first),
                Tree(*late_parts[2:4], second_first),
            ]
            exchange(late_trees)
            grads, _ = lax.optimization_barrier((grads, late_parts[0]))
            grads = settle(late_trees, grads)
            exchange(late_trees)
        kept, got, sums = leave(
            info, at, kept, [flat(rows) for rows in grads], inputs, grad_self,
            self_input, self_vectors, own, micros,
        )
        leave_sums.append(sums)
        if at < held - 1:
            grads, kept = lax.optimization_barrier((grads, kept))
            back = lax.ppermute(got, "seq", SWAP)
            grads, back, source_gots = settle(
                trees,
                (attend_back((at + 1, 0), (1, pairs), grads, *self_inputs), back, source_gots),
            )
            exchange(trees)
            back = back.astype(kept.dtype)[None]
            kept = (
                lax.dynamic_update_slice_in_dim(kept, back, (1 - side) * held + at, axis=0),
            )
    input_grads, got, sums = settle(
        feed_trees, receive(mid_trees + late_trees, (kept, got, sum(leave_sums)))
    )
    finish(feed_trees)
    sums = jnp.concatenate([sums, feed_sums, return_sums, hidden_sums.reshape(-1, width)], axis=0)
    mid_total, *late_totals, sums, back = tail(mid_trees + late_trees, sums, got, parts)
    input_grads = give(input_grads, back[None], held - 1)
    rows = width // parts
    inner_rows = feed_in.shape[1] // parts
    final = [None] * 21

    def mine(row):
        return lax.dynamic_slice_in_dim(row, place * (row.shape[0] // parts), row.shape[0] // parts)

    def widen(block):
        return jnp.concatenate([block[i : i + rows] for i in range(0, len(block), rows)], axis=1)

    for at, index in enumerate((0, 1, 3, 4, 14, 15, 16, 20, 7, 8, 6, 10, 12)):
        row = at if at < 4 else at + 4 if at < 8 else at + 8
        final[index] = mine(sums[row])
    final[18] = mine(sums[24:].reshape(-1))
    feed_total = feed_trees[0].total
    final[19] = feed_total[:inner_rows]
    final[13] = feed_total[inner_rows : inner_rows + rows]
    final[17] = widen(feed_total[inner_rows + rows :])
    final[9] = mid_total[:rows]
    final[5] = mid_total[rows : 2 * rows]
    final[11] = widen(mid_total[2 * rows :])
    final[2] = jnp.concatenate(late_totals, axis=1)
    source_grads = give(source_grads, source_gots, 0)
    return (results[:, None], input_grads[:, None], source_grads[:, None]) + tuple(final)


def solution(mesh):
    in_specs = (
        P(None, "dp", "seq", None),
        P(None, "dp", "seq", None),
        P(None, "dp"),
        P(None, "dp", "seq"),
        P(None, "dp", "seq", None),
        P(),
        P(),
        P(),
        P(),
        P(),
        P(),
        P(),
        P(),
        P(),
        P(),
        P(),
        P(),
        P(),
        P(),
        P(),
        P(),
        P(),
        P(),
        P(),
        P(),
        P(),
    )
    out_specs = (
        P(None, "dp", "seq", None),
        P(None, "dp", "seq", None),
        P(None, "dp", "seq", None),
        P("dp"),
        P("dp"),
        P("dp", None),
        P("dp"),
        P("dp"),
        P("dp", None),
        P("dp"),
        P("dp"),
        P("dp"),
        P("dp", None),
        P("dp"),
        P("dp", None),
        P("dp"),
        P("dp", None),
        P("dp"),
        P("dp"),
        P("dp"),
        P("dp", None),
        P("dp"),
        P("dp", None),
        P("dp"),
    )

    def on_device(*arguments):
        micros = arguments[0].shape[0]
        rows = lax.axis_size("dp")
        pairs = lax.axis_size("seq") == 2 and micros % 2 == 0
        whole = pairs and rows == 16
        return (whole_sequences if whole else split_sequences)(*arguments)

    return jax.shard_map(
        on_device, mesh=mesh, in_specs=in_specs, out_specs=out_specs, check_vma=False
    )
```

```python
import functools

import jax
import jax.numpy as jnp
from jax import lax
from jax.experimental import pallas as pl
from jax.experimental.pallas import tpu as pltpu
from jax.sharding import PartitionSpec as P

HEADS = 12
HEAD = 64


epsilon = 1e-05
blocked_score = -1e30


def normed(values, norm_gain, norm_shift):
    center = values - jnp.mean(values, axis=-1, keepdims=True)
    spread = jnp.mean(center * center, axis=-1, keepdims=True)
    return center * lax.rsqrt(spread + epsilon) * norm_gain + norm_shift


def normed_back(values, norm_gain, norm_shift, upstream):
    unused, pullback = jax.vjp(normed, values, norm_gain, norm_shift)
    return pullback(upstream)


def gelu_exact(values):
    return jax.nn.gelu(values, approximate=False)


def project_rows(row_block, weight):
    return jnp.einsum("bpd,de->bpe", row_block, weight, preferred_element_type=jnp.float32)


def project_back(row_block, weight):
    return jnp.einsum("bpe,de->bpd", row_block, weight, preferred_element_type=jnp.float32)


def outer_sum(first_rows, second_rows):
    return jnp.einsum("bpd,bpe->de", first_rows, second_rows, preferred_element_type=jnp.float32)


def split_heads(row_block):
    return row_block.reshape(row_block.shape[0], row_block.shape[1], HEADS, HEAD)


def masked_scores(queries, key_rows, allowed):
    scores = jnp.einsum(
        "bphe,bshe->bhps",
        split_heads(queries),
        split_heads(key_rows),
        preferred_element_type=jnp.float32,
    )
    if allowed is None:
        return scores
    return jnp.where(allowed[:, None], scores, blocked_score)


def attend_forward(queries, key_rows, values, allowed):
    scores = masked_scores(queries, key_rows, allowed)
    highest_score = jnp.max(scores, axis=-1, keepdims=True)
    raised = jnp.exp(scores - highest_score)
    totals = jnp.sum(raised, axis=-1, keepdims=True)
    weights = (raised / totals).astype(jnp.bfloat16)
    mixed = jnp.einsum(
        "bhps,bshe->bphe", weights, split_heads(values), preferred_element_type=jnp.float32
    )
    return (mixed.reshape(queries.shape).astype(jnp.bfloat16), highest_score + jnp.log(totals))


def attend_backward(queries, key_rows, values, allowed, log_totals, upstream):
    weights = jnp.exp(masked_scores(queries, key_rows, allowed) - log_totals)
    upstream_heads = split_heads(upstream)
    value_grads = jnp.einsum(
        "bhps,bphe->bshe",
        weights.astype(jnp.bfloat16),
        upstream_heads,
        preferred_element_type=jnp.float32,
    )
    weight_grads = jnp.einsum(
        "bphe,bshe->bhps", upstream_heads, split_heads(values), preferred_element_type=jnp.float32
    )
    score_grads = weights * (weight_grads - jnp.sum(weight_grads * weights, axis=-1, keepdims=True))
    score_low = score_grads.astype(jnp.bfloat16)
    query_grads = jnp.einsum(
        "bhps,bshe->bphe", score_low, split_heads(key_rows), preferred_element_type=jnp.float32
    ).reshape(queries.shape)
    key_grads = jnp.einsum(
        "bhps,bphe->bshe", score_low, split_heads(queries), preferred_element_type=jnp.float32
    ).reshape(key_rows.shape)
    return (query_grads, jnp.concatenate([key_grads, value_grads.reshape(key_rows.shape)], axis=-1))


def split_sequences(
    targets,
    memory,
    row_kind,
    loss_mask,
    cotangent,
    norm_self_gain,
    norm_self_bias,
    self_input,
    self_query_bias,
    self_value_bias,
    self_output,
    self_output_bias,
    norm_cross_gain,
    norm_cross_bias,
    cross_query,
    cross_query_bias,
    cross_input,
    cross_value_bias,
    cross_output,
    cross_output_bias,
    norm_feed_gain,
    norm_feed_bias,
    feed_in,
    feed_in_bias,
    feed_out,
    feed_out_bias,
):
    model_width = targets.shape[3]
    part_rows = targets.shape[2]
    key_span = part_rows * lax.axis_size("seq")
    query_scale = HEAD ** (-0.5)
    places = lax.axis_index("seq") * part_rows + jnp.arange(part_rows)
    causal = jnp.arange(key_span)[None, :] <= places[:, None]
    results, input_grads, source_grads = ([], [], [])
    totals = None
    for micro_index in range(targets.shape[0]):
        inputs = targets[micro_index].astype(jnp.float32)
        memory_local = memory[micro_index]
        allowed = causal[None] | (row_kind[micro_index] == 1)[:, None, None]
        first_normed = normed(inputs, norm_self_gain, norm_self_bias).astype(jnp.bfloat16)
        self_joint = project_rows(first_normed, self_input)
        queries = ((self_joint[..., :model_width] + self_query_bias) * query_scale).astype(
            jnp.bfloat16
        )
        own_pairs = jnp.concatenate(
            [
                self_joint[..., model_width : 2 * model_width],
                self_joint[..., 2 * model_width :] + self_value_bias,
            ],
            axis=-1,
        ).astype(jnp.bfloat16)
        gathered_self = lax.all_gather(own_pairs, "seq", axis=1, tiled=True)
        key_rows = gathered_self[..., :model_width]
        value_rows = gathered_self[..., model_width:]
        self_mixed, self_totals = attend_forward(queries, key_rows, value_rows, allowed)
        after_self = inputs + project_rows(self_mixed, self_output) + self_output_bias
        second_normed = normed(after_self, norm_cross_gain, norm_cross_bias).astype(jnp.bfloat16)
        cross_queries = (
            (project_rows(second_normed, cross_query) + cross_query_bias) * query_scale
        ).astype(jnp.bfloat16)
        joined = project_rows(lax.all_gather(memory_local, "seq", axis=1, tiled=True), cross_input)
        gathered_cross = jnp.concatenate(
            [joined[..., :model_width], joined[..., model_width:] + cross_value_bias], axis=-1
        ).astype(jnp.bfloat16)
        cross_keys = gathered_cross[..., :model_width]
        cross_values = gathered_cross[..., model_width:]
        cross_mixed, cross_totals = attend_forward(cross_queries, cross_keys, cross_values, None)
        after_cross = after_self + project_rows(cross_mixed, cross_output) + cross_output_bias
        third_normed = normed(after_cross, norm_feed_gain, norm_feed_bias).astype(jnp.bfloat16)
        activated, gelu_pullback = jax.vjp(
            gelu_exact, project_rows(third_normed, feed_in) + feed_in_bias
        )
        activated_low = activated.astype(jnp.bfloat16)
        results.append(
            (after_cross + project_rows(activated_low, feed_out) + feed_out_bias).astype(
                jnp.bfloat16
            )
        )
        pieces = [None] * 21
        grad_output = (
            cotangent[micro_index].astype(jnp.float32)
            * loss_mask[micro_index].astype(jnp.float32)[..., None]
        )
        output_low = grad_output.astype(jnp.bfloat16)
        pieces[19] = outer_sum(activated_low, output_low)
        pieces[20] = jnp.sum(grad_output, axis=(0, 1))
        grad_hidden = gelu_pullback(project_back(output_low, feed_out))[0]
        hidden_low = grad_hidden.astype(jnp.bfloat16)
        pieces[17] = outer_sum(third_normed, hidden_low)
        pieces[18] = jnp.sum(grad_hidden, axis=(0, 1))
        through_feed, pieces[15], pieces[16] = normed_back(
            after_cross, norm_feed_gain, norm_feed_bias, project_back(hidden_low, feed_in)
        )
        grad_cross = grad_output + through_feed
        cross_low = grad_cross.astype(jnp.bfloat16)
        pieces[13] = outer_sum(cross_mixed, cross_low)
        pieces[14] = jnp.sum(grad_cross, axis=(0, 1))
        cross_upstream = project_back(cross_low, cross_output).astype(jnp.bfloat16)
        cross_query_grads, cross_pair_grads = attend_backward(
            cross_queries, cross_keys, cross_values, None, cross_totals, cross_upstream
        )
        own_cross = lax.psum_scatter(
            cross_pair_grads.astype(jnp.bfloat16), "seq", scatter_dimension=1, tiled=True
        ).astype(jnp.float32)
        pieces[12] = jnp.sum(own_cross[..., model_width:], axis=(0, 1))
        own_cross_low = own_cross.astype(jnp.bfloat16)
        pieces[11] = outer_sum(memory_local, own_cross_low)
        source_grads.append(project_back(own_cross_low, cross_input))
        scaled_cross = cross_query_grads * query_scale
        pieces[10] = jnp.sum(scaled_cross, axis=(0, 1))
        scaled_cross_low = scaled_cross.astype(jnp.bfloat16)
        pieces[9] = outer_sum(second_normed, scaled_cross_low)
        through_cross, pieces[7], pieces[8] = normed_back(
            after_self,
            norm_cross_gain,
            norm_cross_bias,
            project_back(scaled_cross_low, cross_query),
        )
        grad_self = grad_cross + through_cross
        self_low = grad_self.astype(jnp.bfloat16)
        pieces[5] = outer_sum(self_mixed, self_low)
        pieces[6] = jnp.sum(grad_self, axis=(0, 1))
        self_upstream = project_back(self_low, self_output).astype(jnp.bfloat16)
        self_query_grads, self_pair_grads = attend_backward(
            queries, key_rows, value_rows, allowed, self_totals, self_upstream
        )
        own_self = lax.psum_scatter(
            self_pair_grads.astype(jnp.bfloat16), "seq", scatter_dimension=1, tiled=True
        ).astype(jnp.float32)
        scaled_self = self_query_grads * query_scale
        pieces[3] = jnp.sum(scaled_self, axis=(0, 1))
        pieces[4] = jnp.sum(own_self[..., model_width:], axis=(0, 1))
        joint_low = jnp.concatenate([scaled_self, own_self], axis=-1).astype(jnp.bfloat16)
        pieces[2] = outer_sum(first_normed, joint_low)
        through_first, pieces[0], pieces[1] = normed_back(
            inputs, norm_self_gain, norm_self_bias, project_back(joint_low, self_input)
        )
        input_grads.append(grad_self + through_first)
        totals = (
            pieces
            if totals is None
            else [running + added for running, added in zip(totals, pieces)]
        )
    def reduced(total):
        block = lax.psum_scatter(
            total.astype(jnp.bfloat16), "dp", scatter_dimension=0, tiled=True
        )
        return lax.psum(block, "seq").astype(jnp.float32)

    final = [reduced(total) for total in totals]
    return (jnp.stack(results), jnp.stack(input_grads), jnp.stack(source_grads)) + tuple(final)


def contract(first, second, first_dim, second_dim):
    return lax.dot_general(
        first, second, (((first_dim,), (second_dim,)), ((), ())), preferred_element_type=jnp.float32
    )


def head_masks(pair):
    lane = lax.broadcasted_iota(jnp.int32, (1, pair.shape[1]), 1)
    zero = jnp.zeros((), pair.dtype)
    return (jnp.where(lane < HEAD, pair, zero), jnp.where(lane < HEAD, zero, pair))


LIMIT = 62 * 2**20


def attend_kernel(info_ref, q_ref, k_ref, v_ref, *refs, use_mask, start):
    o_ref, e_ref, r_ref, mask_ref = refs[-4:]
    length = k_ref.shape[1]
    half = length // 2
    values_turned = v_ref[0].T
    ones = jnp.ones((16, length), jnp.bfloat16)

    def run(masked, shifted):
        lowest, highest = None, None
        for at in range(2):
            queries_at = slice(at * half, (at + 1) * half)
            mixed = []
            for head, queries in enumerate(head_masks(q_ref[0, queries_at, :])):
                scores = contract(k_ref[0], queries, 1, 1)
                if shifted:
                    if masked:
                        seen = mask_ref[:, queries_at].astype(jnp.float32) > 0
                        scores = jnp.where(seen, scores, blocked_score)
                    scores = scores - jnp.max(scores, axis=0, keepdims=True)
                low = jnp.exp(scores).astype(jnp.bfloat16)
                if masked:
                    low = low * mask_ref[:, queries_at]
                e_ref[0, head, :, queries_at] = low
                turned = jnp.concatenate(
                    [values_turned[head * HEAD : (head + 1) * HEAD], ones], axis=0
                )
                sums = contract(turned, low, 1, 0)
                total = sums[HEAD : HEAD + 1]
                if not shifted:
                    lowest = total if lowest is None else jnp.minimum(lowest, total)
                    highest = total if highest is None else jnp.maximum(highest, total)
                inverse = 1.0 / total
                r_ref[0, 0, head : head + 1, queries_at] = inverse
                mixed.append(sums[:HEAD] * inverse)
            o_ref[0, queries_at, :] = jnp.concatenate(mixed, axis=0).T.astype(jnp.bfloat16)
        if not shifted:
            in_range = (jnp.min(lowest) > 1e-20) & (jnp.max(highest) < 1e30)

            @pl.when(jnp.logical_not(in_range))
            def _():
                run(masked, True)

    if not use_mask:
        run(False, False)
        return
    causal = info_ref[2 + start + pl.program_id(0)] == 0

    @pl.when(causal & (pl.program_id(1) == 0))
    def _():
        later = info_ref[0] * half
        query = lax.broadcasted_iota(jnp.int32, (1, length), 1)
        query = jnp.where(query < half, query + later, query - later)

        @pl.loop(0, length, step=64)
        def _(row):
            key = lax.broadcasted_iota(jnp.int32, (64, 1), 0) + row
            key = jnp.where(key < half, key + later, key - later)
            seen = jnp.where(key <= query, 1.0, 0.0)
            mask_ref[pl.ds(pl.multiple_of(row, 64), 64), :] = seen.astype(jnp.bfloat16)

    @pl.when(causal)
    def _():
        run(True, False)

    @pl.when(jnp.logical_not(causal))
    def _():
        run(False, False)


def attend(info, start, count_now, previous, queries, keys, values, use_mask, offsets):
    count, length = queries.shape[:2]
    pairs = HEADS * HEAD // 128
    width = HEADS * HEAD

    def spec(offset):
        return pl.BlockSpec((1, length, 128), lambda s, p, info: (start + s, 0, offset * pairs + p))

    place = lambda s, p, info: (start + s, p, 0, 0)
    return pl.pallas_call(
        functools.partial(attend_kernel, use_mask=use_mask, start=start),
        grid_spec=pltpu.PrefetchScalarGridSpec(
            num_scalar_prefetch=1,
            grid=(count_now, pairs),
            in_specs=[spec(offset) for offset in offsets]
            + [pl.BlockSpec(memory_space=pl.ANY)] * len(previous),
            out_specs=[
                spec(0),
                pl.BlockSpec((1, 2, length, length), place),
                pl.BlockSpec((1, 1, 2, length), place),
            ],
            scratch_shapes=[pltpu.VMEM((length, length), jnp.bfloat16)],
        ),
        out_shape=[
            jax.ShapeDtypeStruct((count, length, width), jnp.bfloat16),
            jax.ShapeDtypeStruct((count, HEADS, length, length), jnp.bfloat16),
            jax.ShapeDtypeStruct((count, pairs, 2, length), jnp.float32),
        ],
        input_output_aliases={4: 0, 5: 1, 6: 2} if previous else {},
        compiler_params=pltpu.CompilerParams(vmem_limit_bytes=LIMIT),
        cost_estimate=pl.CostEstimate(
            flops=4 * count_now * HEADS * length * length * 256,
            bytes_accessed=count_now * HEADS * length * length * 2,
            transcendentals=count_now * HEADS * length * length,
        ),
        name="attend",
    )(info, queries, keys, values, *previous)


def attend_back_kernel(q_ref, k_ref, v_ref, o_ref, g_ref, e_ref, r_ref, dq_ref, dk_ref, dv_ref):
    length = k_ref.shape[1]
    keys_turned = k_ref[0].T
    upstream = g_ref[0].astype(jnp.float32)
    products = (o_ref[0].astype(jnp.float32) * upstream).T
    upstream = upstream.T
    parts, deltas = [], []
    for head in range(2):
        rows = slice(head * HEAD, (head + 1) * HEAD)
        inverse = r_ref[0, 0, head : head + 1, :]
        parts.append(upstream[rows] * inverse)
        deltas.append(jnp.sum(products[rows], axis=0, keepdims=True) * inverse)
    scaled = head_masks(jnp.concatenate(parts, axis=0).T.astype(jnp.bfloat16))
    queries = head_masks(q_ref[0])
    key_sum, value_sum, query_parts = 0.0, 0.0, []
    for head in range(2):
        rows = slice(head * HEAD, (head + 1) * HEAD)
        low = e_ref[0, head]
        grads = contract(v_ref[0], scaled[head], 1, 1)
        score_low = (low.astype(jnp.float32) * (grads - deltas[head])).astype(jnp.bfloat16)
        value_sum += contract(low, scaled[head], 1, 0)
        key_sum += contract(score_low, queries[head], 1, 0)
        query_parts.append(contract(keys_turned[rows], score_low, 1, 0))
    turned = jnp.concatenate(query_parts, axis=0) * (HEAD**-0.5)
    dq_ref[0] = turned.T.astype(jnp.bfloat16)
    dk_ref[0] = key_sum.astype(jnp.bfloat16)
    dv_ref[0] = value_sum.astype(jnp.bfloat16)


def attend_back(place, size, previous, queries, keys, values, offsets, *rest):
    count, length = queries.shape[:2]
    pairs = HEADS * HEAD // 128
    width = HEADS * HEAD

    start, first = place

    def spec(offset):
        return pl.BlockSpec(
            (1, length, 128), lambda s, p: (start + s, 0, offset * pairs + first + p)
        )

    kernel = attend_back_kernel
    aliases = {}
    if previous:
        kernel = lambda *refs: attend_back_kernel(*refs[3:])
        aliases = {0: 0, 1: 1, 2: 2}
    return pl.pallas_call(
        kernel,
        grid=size,
        in_specs=[pl.BlockSpec(memory_space=pl.ANY)] * len(previous)
        + [spec(offset) for offset in offsets]
        + [
            spec(0),
            spec(0),
            pl.BlockSpec((1, 2, length, length), lambda s, p: (start + s, first + p, 0, 0)),
            pl.BlockSpec((1, 1, 2, length), lambda s, p: (start + s, first + p, 0, 0)),
        ],
        out_specs=[spec(0)] * 3,
        out_shape=[jax.ShapeDtypeStruct((count, length, width), jnp.bfloat16)] * 3,
        input_output_aliases=aliases,
        compiler_params=pltpu.CompilerParams(vmem_limit_bytes=LIMIT),
        cost_estimate=pl.CostEstimate(
            flops=16 * size[0] * size[1] * length * length * 256,
            bytes_accessed=4 * size[0] * size[1] * length * length,
            transcendentals=0,
        ),
        name="attend_back",
    )(*previous, queries, keys, values, *rest)


def normal_parts(values):
    center = values - jnp.mean(values, axis=-1, keepdims=True)
    inverse = lax.rsqrt(jnp.mean(center * center, axis=-1, keepdims=True) + epsilon)
    return center * inverse, inverse


def normal_back(unit, inverse, norm_gain, upstream):
    inner = upstream * norm_gain
    shift = jnp.mean(inner, axis=-1, keepdims=True)
    tilt = jnp.mean(inner * unit, axis=-1, keepdims=True)
    return inverse * (inner - shift - unit * tilt)


def gelu_parts(values):
    size = jnp.abs(values)
    ratio = 1.0 / (1.0 + 0.2316418882663604 * size)
    series = 0.5307027145
    for weight in (-0.7265760135, 0.7107068705, -0.142248368, 0.127414796):
        series = series * ratio + weight
    bell = jnp.exp(-0.5 * values * values)
    upper = series * ratio * bell
    chance = jnp.where(values < 0, upper, 1.0 - upper)
    return values * chance, chance + values * (0.3989422804014327 * bell)


def column_sum(values):
    return jnp.sum(values, axis=0, keepdims=True)


def resident(array):
    return pl.BlockSpec(array.shape, lambda *_: (0,) * array.ndim, pipeline_mode=pl.Buffered(1))


def whole_block(array):
    return pl.BlockSpec(array.shape, lambda *_: (0,) * len(array.shape))


def like(shape, dtype=jnp.float32):
    return jax.ShapeDtypeStruct(tuple(shape), dtype)


def pick(take_first, first_ref, second_ref):
    return jnp.where(take_first, first_ref[...], second_ref[...])


ONCE = {"pipeline_mode": pl.Buffered(1)}


def own_spec(own, width, held, last, **more):
    def place(step, info):
        return (info[0] * held + jnp.minimum(step, last) // 2, 0, 0)

    return pl.BlockSpec((None, own, width), place, **more)


def got_spec(own, width, last, **more):
    return pl.BlockSpec(
        (None, own, width), lambda step, info: (jnp.minimum(step, last) // 2, 0, 0), **more
    )


def row_spec(own, width, last, **more):
    return pl.BlockSpec((own, width), lambda step, info: (jnp.minimum(step, last), 0), **more)


def kernel_call(kernel, name, info, arrays, in_specs, outs, out_specs, grid, flops, moved, **more):
    scratch = more.pop("scratch", [])
    return pl.pallas_call(
        kernel,
        grid_spec=pltpu.PrefetchScalarGridSpec(
            num_scalar_prefetch=1,
            grid=(grid,),
            in_specs=in_specs,
            out_specs=out_specs,
            scratch_shapes=scratch,
        ),
        out_shape=outs,
        compiler_params=pltpu.CompilerParams(
            vmem_limit_bytes=more.pop("limit", LIMIT)
        ),
        cost_estimate=pl.CostEstimate(flops=flops, bytes_accessed=moved, transcendentals=0),
        name=name,
        **more,
    )(info, *arrays)


def enter_kernel(info_ref, source_ref, w_ref, vec_ref, bias_ref, *refs, norm):
    x_ref, out_ref = refs[-2:]
    x = source_ref[...]
    x_ref[...] = x
    if norm:
        unit, _ = normal_parts(x.astype(jnp.float32))
        x = (unit * vec_ref[0:1, :] + vec_ref[1:2, :]).astype(jnp.bfloat16)
    width = x.shape[1]
    for start in range(0, w_ref.shape[1], width):
        part = slice(start, start + width)
        total = contract(x, w_ref[:, part], 1, 0) + bias_ref[:, part]
        if norm and start == 0:
            total = total * (HEAD**-0.5)
        out_ref[:, part] = total.astype(jnp.bfloat16)


def enter(info, first, count, previous, held, rows_in, weight, vectors, bias, norm):
    own, width = rows_in.shape[1:]
    rows = 2 * held * own
    wide = weight.shape[1]
    if first is None:
        place = lambda step, info: (info[0] * held + step, 0, 0)
        row = lambda step, info: (2 * step, 0)
    else:
        place = lambda step, info: (step, 0, 0)
        row = lambda step, info: (2 * (first + step) + 1, 0)
    return kernel_call(
        functools.partial(enter_kernel, norm=norm),
        "enter",
        info,
        (rows_in, weight, vectors, bias, *previous),
        [pl.BlockSpec((None, own, width), place)]
        + [resident(a) for a in (weight, vectors, bias)]
        + [pl.BlockSpec(memory_space=pl.ANY)] * len(previous),
        [like((rows, width), jnp.bfloat16), like((rows, wide), jnp.bfloat16)],
        [pl.BlockSpec((own, width), row), pl.BlockSpec((own, wide), row)],
        count,
        2 * count * own * width * wide,
        2 * count * own * (2 * width + wide),
        input_output_aliases={5: 0, 6: 1} if previous else {},
    )


def middle_kernel(info_ref, x_ref, mixed_ref, wo_ref, wq_ref, vec_ref, after_ref, q_ref):
    out_bias, gain, shift, query_bias = (vec_ref[i : i + 1, :] for i in range(4))
    after = (
        x_ref[...].astype(jnp.float32) + contract(mixed_ref[...], wo_ref[...], 1, 0) + out_bias
    )
    after_ref[...] = after
    unit, _ = normal_parts(after)
    normal = (unit * gain + shift).astype(jnp.bfloat16)
    queries = (contract(normal, wq_ref[...], 1, 0) + query_bias) * (HEAD**-0.5)
    q_ref[...] = queries.astype(jnp.bfloat16)


def middle(info, x, mixed, wo, wq, vectors, own):
    rows, width = x.shape
    last = rows // own - 1
    spec = row_spec(own, width, last)
    return kernel_call(
        middle_kernel,
        "middle",
        info,
        (x, mixed, wo, wq, vectors),
        [spec, spec] + [resident(a) for a in (wo, wq, vectors)],
        [like((rows, width)), like((rows, width), jnp.bfloat16)],
        [spec, spec],
        rows // own,
        4 * rows * width * width,
        10 * rows * width,
    )


def write_split(core, rows, kept_ref, sent_ref, start):
    half = rows.shape[0] // 2
    low = rows.astype(jnp.bfloat16)
    place = slice(start, start + half)

    @pl.when(core == 0)
    def _():
        kept_ref[0, place, :] = low[:half]
        sent_ref[0, place, :] = low[half:]

    @pl.when(core != 0)
    def _():
        kept_ref[0, place, :] = low[half:]
        sent_ref[0, place, :] = low[:half]


def write_wide(core, rows, kept_ref, sent_ref, start):
    half, width = rows.shape[0] // 2, kept_ref.shape[2]
    for at in range(rows.shape[1] // width):
        part = rows[:, at * width : (at + 1) * width]
        write_split(core, part, kept_ref, sent_ref, start + at * half)


def acc_rows(ref, at, rows):
    return ref[pl.ds(pl.multiple_of(at * rows, 16), rows), :]


def piece(parts, high, wide, steps, order):
    bits = parts.bit_length() - 2

    def late(step, info):
        at = jnp.maximum(step - steps, 0)
        place = 0
        for bit in order(bits):
            place = 2 * place + (at // 2**bit) % 2
        return (place, 0, 0)

    return (
        [pl.BlockSpec((1, high, wide), late)] * 2,
        [like((parts // 2, high, wide), jnp.bfloat16)] * 2,
    )


def low_first(bits):
    return list(range(bits))


def second_first(bits):
    return list(range(bits))[1:2] + [0] + list(range(2, bits))


def put_rows(step, value, own_ref, got_ref):
    @pl.when(step % 2 == 0)
    def _():
        own_ref[...] = value.astype(own_ref.dtype)

    @pl.when(step % 2 != 0)
    def _():
        got_ref[...] = value.astype(got_ref.dtype)


def feed_kernel(
    info_ref, x_ref, mixed_ref, dyo_ref, dyg_ref, wc_ref, wi_ref, wo_ref, vec_ref, bi_ref,
    own_ref, got_ref, dx_ref, do_ref, vsum_ref, bsum_ref, kept_ref, sent_ref, ai_ref, ao_ref,
    ac_ref, *, steps, chunk, parts,
):
    step = pl.program_id(0)

    @pl.when(step == 0)
    def _():
        for ref in (vsum_ref, bsum_ref, ai_ref, ao_ref, ac_ref):
            ref[...] = jnp.zeros_like(ref)

    @pl.when(step < steps)
    def _():
        cross_bias, gain, shift, out_bias = (vec_ref[i : i + 1, :] for i in range(4))
        mixed = mixed_ref[...]
        x2 = x_ref[...] + contract(mixed, wc_ref[...], 1, 0) + cross_bias
        unit, inverse = normal_parts(x2)
        normal = (unit * gain + shift).astype(jnp.bfloat16)
        normal_turned = normal.T
        dy = pick(step % 2 == 0, dyo_ref, dyg_ref)
        dy_turned = dy.T
        result, upstream = None, None
        for start in range(0, wi_ref.shape[1], chunk):
            part = slice(start, start + chunk)
            hidden = contract(normal, wi_ref[:, part], 1, 0) + bi_ref[:, part]
            active, slope = gelu_parts(hidden)
            active = active.astype(jnp.bfloat16)
            down = contract(active, wo_ref[part, :], 1, 0)
            result = down if result is None else result + down
            grads = contract(dy, wo_ref[part, :], 1, 1) * slope
            bsum_ref[:, part] += column_sum(grads)
            low = grads.astype(jnp.bfloat16)
            up = contract(low, wi_ref[:, part], 1, 1)
            upstream = up if upstream is None else upstream + up
            ao_ref[:, part] += contract(dy_turned, active, 1, 0)
            ai_ref[:, part] += contract(normal_turned, low, 1, 0)
        put_rows(step, x2 + result + out_bias, own_ref, got_ref)
        wide = dy.astype(jnp.float32)
        dx = wide + normal_back(unit, inverse, gain, upstream)
        dx_ref[...] = dx
        dx_low = dx.astype(jnp.bfloat16)
        do_ref[...] = contract(dx_low, wc_ref[...], 1, 1).astype(jnp.bfloat16)
        ac_ref[...] += contract(mixed.T, dx_low, 1, 0)
        vsum_ref[0:1, :] += column_sum(dx)
        vsum_ref[1:2, :] += column_sum(upstream * unit)
        vsum_ref[2:3, :] += column_sum(upstream)
        vsum_ref[3:4, :] += column_sum(wide)

    @pl.when(step >= steps)
    def _():
        at = step - steps
        core = info_ref[1]
        width, wide = ai_ref.shape
        rows = 2 * width // parts
        inner = 2 * wide // parts
        columns = ao_ref[:, pl.ds(pl.multiple_of(at * inner, 128), inner)]
        write_split(core, columns.astype(jnp.bfloat16).T, kept_ref, sent_ref, 0)
        write_split(core, acc_rows(ac_ref, at, rows), kept_ref, sent_ref, inner // 2)
        write_wide(core, acc_rows(ai_ref, at, rows), kept_ref, sent_ref, (inner + rows) // 2)


def feed(info, x1, mixed, dys, dy_gots, wc, wi, wo, vectors, bi, parts, chunk=768):
    rows, width = x1.shape
    held, own = dy_gots.shape[:2]
    micros = dys.shape[0]
    inner = wi.shape[1]
    steps = 2 * held
    last = steps - 1
    row = row_spec(own, width, last)
    pieces = [piece(parts, (2 * inner + width) // parts, width, steps, low_first)]
    sums = [like((8, width)), like((1, inner))]
    return kernel_call(
        functools.partial(feed_kernel, steps=steps, chunk=chunk, parts=parts),
        "feed",
        info,
        (x1, mixed, dys, dy_gots, wc, wi, wo, vectors, bi),
        [row_spec(own, width, last, **ONCE)] * 2
        + [own_spec(own, width, held, last, **ONCE), got_spec(own, width, last, **ONCE)]
        + [resident(a) for a in (wc, wi, wo, vectors, bi)],
        [
            like((micros, own, width), jnp.bfloat16),
            like((held, own, width), jnp.bfloat16),
            like((rows, width)),
            like((rows, width), jnp.bfloat16),
        ]
        + sums
        + sum([p[1] for p in pieces], []),
        [own_spec(own, width, held, last), got_spec(own, width, last), row, row]
        + [whole_block(a) for a in sums]
        + sum([p[0] for p in pieces], []),
        steps + parts // 2,
        2 * rows * width * (6 * inner + 3 * width),
        60 * 2**20,
        scratch=[
            pltpu.VMEM((width, inner), jnp.float32),
            pltpu.VMEM((width, inner), jnp.float32),
            pltpu.VMEM((width, width), jnp.float32),
        ],
        limit=LIMIT,
    )


def return_kernel(
    info_ref, dq_ref, dk_ref, dv_ref, x_ref, dx_ref, mixed_ref, src_ref, wq_ref, wi_ref, wo_ref,
    vec_ref, own_ref, got_ref, dxo_ref, do_ref, vsum_ref, kept_ref, sent_ref, aq_ref, ao_ref,
    ai_ref, *, steps, parts,
):
    step = pl.program_id(0)

    @pl.when(step == 0)
    def _():
        for ref in (vsum_ref, aq_ref, ao_ref, ai_ref):
            ref[...] = jnp.zeros_like(ref)

    @pl.when(step < steps)
    def _():
        width = x_ref.shape[1]
        gain, shift = vec_ref[0:1, :], vec_ref[1:2, :]
        dq, dk, dv = dq_ref[...], dk_ref[...], dv_ref[...]
        upstream = contract(dq, wq_ref[...], 1, 1)
        unit, inverse = normal_parts(x_ref[...])
        normal = (unit * gain + shift).astype(jnp.bfloat16)
        dx = dx_ref[...] + normal_back(unit, inverse, gain, upstream)
        dxo_ref[...] = dx
        low = dx.astype(jnp.bfloat16)
        do_ref[...] = contract(low, wo_ref[...], 1, 1).astype(jnp.bfloat16)
        source = contract(dk, wi_ref[:, :width], 1, 1) + contract(dv, wi_ref[:, width:], 1, 1)
        put_rows(step, source, own_ref, got_ref)
        aq_ref[...] += contract(normal.T, dq, 1, 0)
        ao_ref[...] += contract(mixed_ref[...].T, low, 1, 0)
        turned = src_ref[...].T
        ai_ref[:, :width] += contract(turned, dk, 1, 0)
        ai_ref[:, width:] += contract(turned, dv, 1, 0)
        vsum_ref[0:1, :] += column_sum(upstream * unit)
        vsum_ref[1:2, :] += column_sum(upstream)
        vsum_ref[2:3, :] += column_sum(dx)
        vsum_ref[3:4, :] += column_sum(dq.astype(jnp.float32))
        vsum_ref[4:5, :] += column_sum(dv.astype(jnp.float32))

    @pl.when(step >= steps)
    def _():
        at = step - steps
        core = info_ref[1]
        rows = 2 * aq_ref.shape[0] // parts
        write_split(core, acc_rows(aq_ref, at, rows), kept_ref, sent_ref, 0)
        write_split(core, acc_rows(ao_ref, at, rows), kept_ref, sent_ref, rows // 2)
        write_wide(core, acc_rows(ai_ref, at, rows), kept_ref, sent_ref, rows)


def return_rows(info, grads, x1, dx2, mixed, sources, wq, wi, wo, vectors, own, micros, parts):
    rows, width = x1.shape
    held = rows // own // 2
    steps = 2 * held
    last = steps - 1
    row = row_spec(own, width, last)
    pieces = [piece(parts, 4 * width // parts, width, steps, low_first)]
    sums = like((8, width))
    return kernel_call(
        functools.partial(return_kernel, steps=steps, parts=parts),
        "return_rows",
        info,
        (*grads, x1, dx2, mixed, sources, wq, wi, wo, vectors),
        [row] * 7 + [resident(a) for a in (wq, wi, wo, vectors)],
        [
            like((micros, own, width)),
            like((held, own, width), jnp.bfloat16),
            like((rows, width)),
            like((rows, width), jnp.bfloat16),
            sums,
        ]
        + sum([p[1] for p in pieces], []),
        [own_spec(own, width, held, last), got_spec(own, width, last), row, row, whole_block(sums)]
        + sum([p[0] for p in pieces], []),
        steps + parts // 2,
        16 * rows * width * width,
        40 * 2**20,
        scratch=[
            pltpu.VMEM((width, width), jnp.float32),
            pltpu.VMEM((width, width), jnp.float32),
            pltpu.VMEM((width, 2 * width), jnp.float32),
        ],
    )


def last_weight_kernel(
    info_ref, dq_ref, dk_ref, dv_ref, x_ref, vec_ref, ka_ref, sa_ref, kb_ref, sb_ref, acc_ref,
    *, steps,
):
    step = pl.program_id(0)

    @pl.when(step == 0)
    def _():
        acc_ref[...] = jnp.zeros_like(acc_ref)

    @pl.when(step < steps)
    def _():
        unit, _ = normal_parts(x_ref[...].astype(jnp.float32))
        turned = (unit * vec_ref[0:1, :] + vec_ref[1:2, :]).astype(jnp.bfloat16).T
        width = x_ref.shape[1]
        for at, ref in enumerate((dq_ref, dk_ref, dv_ref)):
            acc_ref[:, at * width : (at + 1) * width] += contract(turned, ref[...], 1, 0)

    @pl.when(step >= steps)
    def _():
        rows = acc_rows(acc_ref, step - steps, 2 * ka_ref.shape[1])
        half = ka_ref.shape[2]
        write_split(info_ref[1], rows[:, :half], ka_ref, sa_ref, 0)
        write_split(info_ref[1], rows[:, half:], kb_ref, sb_ref, 0)


def last_weight(info, grads, x, vectors, own, parts):
    rows, width = x.shape
    steps = rows // own
    row = row_spec(own, width, steps - 1)
    pieces = [
        piece(parts, width // parts, 3 * width // 2, steps, order)
        for order in (low_first, second_first)
    ]
    return kernel_call(
        functools.partial(last_weight_kernel, steps=steps),
        "last_weight",
        info,
        (*grads, x, vectors),
        [row] * 4 + [resident(vectors)],
        sum([p[1] for p in pieces], []),
        sum([p[0] for p in pieces], []),
        steps + parts // 2,
        24 * rows * width * width,
        20 * 2**20,
        scratch=[pltpu.VMEM((width, 3 * width), jnp.float32)],
    )


def leave_kernel(
    info_ref, dq_ref, dk_ref, dv_ref, x_ref, dx_ref, w_ref, vec_ref, *refs, halves
):
    refs = list(refs)
    up_ref, vsum_ref = refs.pop(), refs.pop()
    got_ref = refs.pop() if 1 in halves else None
    own_ref = refs.pop() if 0 in halves else None
    step = pl.program_id(0)

    @pl.when(step == 0)
    def _():
        vsum_ref[...] = jnp.zeros_like(vsum_ref)

    width = x_ref.shape[1]
    dq, dk, dv = dq_ref[...], dk_ref[...], dv_ref[...]
    upstream = (
        contract(dq, w_ref[:, :width], 1, 1)
        + contract(dk, w_ref[:, width : 2 * width], 1, 1)
        + contract(dv, w_ref[:, 2 * width :], 1, 1)
    )
    unit, inverse = normal_parts(x_ref[...].astype(jnp.float32))
    dx = dx_ref[...] + normal_back(unit, inverse, vec_ref[0:1, :], upstream)
    if len(halves) == 2:
        put_rows(step, dx, own_ref, got_ref)
    else:
        out_ref = got_ref if own_ref is None else own_ref
        out_ref[...] = dx.astype(out_ref.dtype)
    vsum_ref[0:1, :] += column_sum(upstream * unit)
    vsum_ref[1:2, :] += column_sum(upstream)
    vsum_ref[2:3, :] += column_sum(dq.astype(jnp.float32))
    vsum_ref[3:4, :] += column_sum(dv.astype(jnp.float32))


def leave(info, at, halves, previous, grads, x, dx1, weight, vectors, own, micros):
    rows, width = x.shape
    held = rows // own // 2
    row = pl.BlockSpec((own, width), lambda step, info: (2 * at + halves[0] + step, 0))
    more = {"input_output_aliases": {8: 0}} if previous else {}
    sums = like((8, width))
    outs, out_specs = [], []
    if 0 in halves:
        outs.append(like((micros, own, width)))
        out_specs.append(
            pl.BlockSpec((None, own, width), lambda step, info: (info[0] * held + at, 0, 0))
        )
    if 1 in halves:
        outs.append(like((own, width), jnp.bfloat16))
        out_specs.append(pl.BlockSpec((own, width), lambda step, info: (0, 0)))
    return kernel_call(
        functools.partial(leave_kernel, halves=halves),
        "leave",
        info,
        (*grads, x, dx1, weight, vectors, *previous),
        [row] * 5
        + [resident(a) for a in (weight, vectors)]
        + [pl.BlockSpec(memory_space=pl.ANY)] * len(previous),
        outs + [sums],
        out_specs + [whole_block(sums)],
        len(halves),
        12 * len(halves) * own * width * width,
        8 * len(halves) * 2**20,
        scratch=[pltpu.VMEM((8, 128), jnp.float32)],
        **more,
    )


SWAP = ((0, 1), (1, 0))


class Tree:
    def __init__(self, kept, sent, order):
        self.count = lax.axis_size("dp")
        bits = self.count.bit_length() - 2
        shape = (2,) * bits + kept.shape[1:]
        self.order = [2 << bit for bit in order(bits)]
        self.kept, self.sent, self.bit = kept.reshape(shape), sent.reshape(shape), 1
        self.got, self.total = None, None

    def exchange(self):
        if self.total is not None or self.got is not None:
            return
        if self.bit:
            pairs = [(i, i ^ self.bit) for i in range(self.count)]
            self.got = lax.ppermute(self.sent, "dp", pairs)
        else:
            self.got = lax.ppermute(self.kept, "seq", SWAP)

    def add(self):
        if self.got is None:
            return
        total = self.kept.astype(jnp.float32) + self.got.astype(jnp.float32)
        self.got = None
        if not self.bit:
            self.total = total
            return
        total = total.astype(jnp.bfloat16)
        if not self.order:
            self.bit, self.kept = 0, total
            return
        self.bit = self.order.pop(0)
        mine = (lax.axis_index("dp") // self.bit) % 2
        self.kept = lax.dynamic_index_in_dim(total, mine, 0, keepdims=False)
        self.sent = lax.dynamic_index_in_dim(total, 1 - mine, 0, keepdims=False)


def exchange(trees):
    for tree in trees:
        tree.exchange()


def settle(trees, values):
    trees = [tree for tree in trees if tree.got is not None]
    gots, values = lax.optimization_barrier(([tree.got for tree in trees], values))
    for tree, got in zip(trees, gots):
        tree.got = got
        tree.add()
    return values


def receive(trees, values):
    gots, values = lax.optimization_barrier(([tree.got for tree in trees], values))
    for tree, got in zip(trees, gots):
        tree.got = got
    return values


def finish(trees):
    while any(tree.total is None for tree in trees):
        exchange(trees)
        settle(trees, ())


MESH = pl.DeviceIdType.MESH


def partner(place, offset):
    bit = 1
    while bit <= offset:
        if offset & bit:
            place = place + bit * (1 - 2 * ((place // bit) % 2))
        bit *= 2
    return place


def tail_kernel(*refs, orders, groups):
    trees = len(orders)
    ins, refs = refs[: 2 * trees + 1], refs[2 * trees + 1 :]
    outs, refs = refs[: trees + 1], refs[trees + 1 :]
    send_sems, recv_sems = refs[-2:]
    scratch = list(refs[:-2])
    place = lax.axis_index("dp")
    side = lax.axis_index("seq")
    offsets = sorted({bit for order in orders for bit in order} | {o for g in groups for o in g})
    peers = [{"dp": partner(place, offset)} for offset in offsets] + [{"seq": 1 - side}]
    barrier = pltpu.get_barrier_semaphore()
    for peer in peers:
        pl.semaphore_signal(barrier, inc=1, device_id=peer, device_id_type=MESH)
    pl.semaphore_wait(barrier, len(peers))
    used = []

    def send(source, target, peer):
        at = len(used)
        copy = pltpu.make_async_remote_copy(
            src_ref=source,
            dst_ref=target,
            send_sem=send_sems.at[at],
            recv_sem=recv_sems.at[at],
            device_id=peer,
            device_id_type=MESH,
        )
        used.append(copy)
        copy.start()
        return copy

    other = {"seq": 1 - side}
    totals = []
    for at in range(trees):
        total = scratch.pop(0)
        total[...] = (
            ins[2 * at][...].astype(jnp.float32) + ins[2 * at + 1][...].astype(jnp.float32)
        ).astype(jnp.bfloat16)
        totals.append(total)
    sums = scratch.pop(0)
    sums[...] = ins[2 * trees][...]
    rounds = max(max(len(order) for order in orders) + 1, len(groups) + 1)
    for step in range(rounds):
        copies = []
        for at, order in enumerate(orders):
            if step < len(order):
                mine = (place // order[step]) % 2
                got = scratch.pop(0)
                peer = {"dp": partner(place, order[step])}
                copy = send(totals[at].at[1 - mine], got, peer)
                copies.append((copy, at, mine, got, scratch.pop(0)))
            elif step == len(order):
                got = scratch.pop(0)
                copies.append((send(totals[at], got, other), at, None, got, outs[at]))
        summed = []
        if step < len(groups):
            for offset in groups[step]:
                got = scratch.pop(0)
                summed.append((send(sums, got, {"dp": partner(place, offset)}), got))
        elif step == len(groups):
            got = scratch.pop(0)
            summed.append((send(sums, got, other), got))
        for copy, at, mine, got, target in copies:
            copy.wait()
            held = totals[at][...] if mine is None else totals[at][mine]
            total = held.astype(jnp.float32) + got[...].astype(jnp.float32)
            target[...] = total.astype(target.dtype)
            totals[at] = target
        if summed:
            target = scratch.pop(0) if step < len(groups) else outs[trees]
            total = sums[...]
            for copy, got in summed:
                copy.wait()
                total = total + got[...]
            target[...] = total
            sums = target


def tail(trees, sums, parts):
    orders = [tuple(tree.order) for tree in trees]
    groups, bit = [], 1
    while bit < parts:
        groups.append(tuple(step * bit for step in (1, 2, 3) if step * bit < parts))
        bit *= 4
    arrays = []
    for tree in trees:
        arrays += [tree.kept, tree.got]
    arrays += [sums]
    totals = [pltpu.VMEM(tree.kept.shape, jnp.bfloat16) for tree in trees]
    scratch = totals + [pltpu.VMEM(sums.shape, jnp.float32)]
    shapes = [tree.kept.shape for tree in trees]
    copies = 0
    for step in range(max(max(len(order) for order in orders) + 1, len(groups) + 1)):
        for at, order in enumerate(orders):
            if step < len(order):
                shapes[at] = shapes[at][1:]
                scratch += [pltpu.VMEM(shapes[at], jnp.bfloat16)] * 2
                copies += 1
            elif step == len(order):
                scratch += [pltpu.VMEM(shapes[at], jnp.bfloat16)]
                copies += 1
        if step < len(groups):
            scratch += [pltpu.VMEM(sums.shape, jnp.float32)] * (len(groups[step]) + 1)
            copies += len(groups[step])
        elif step == len(groups):
            scratch += [pltpu.VMEM(sums.shape, jnp.float32)]
            copies += 1
    outs = [like(shape) for shape in shapes] + [like(sums.shape)]
    vmem = pl.BlockSpec(memory_space=pltpu.VMEM)
    return pl.pallas_call(
        functools.partial(tail_kernel, orders=orders, groups=groups),
        in_specs=[vmem] * len(arrays),
        out_specs=[vmem] * len(outs),
        out_shape=outs,
        scratch_shapes=scratch + [pltpu.SemaphoreType.DMA((copies,))] * 2,
        compiler_params=pltpu.CompilerParams(
            collective_id=0, has_side_effects=True, vmem_limit_bytes=LIMIT
        ),
        cost_estimate=pl.CostEstimate(
            flops=2 * 10**10, bytes_accessed=10**7, transcendentals=0
        ),
        name="tail",
    )(*arrays)


def final_kernel(info_ref, kept_ref, got_ref, mid_ref, first_ref, second_ref, sums_ref, *outs, rows, vectors):
    place = info_ref[info_ref.shape[0] - 1]
    width = mid_ref.shape[1]
    high = kept_ref.shape[0]

    def feed_rows(start, count):
        at = slice(start, start + count)
        return kept_ref[at, :].astype(jnp.float32) + got_ref[at, :].astype(jnp.float32)

    wide = outs[17].shape[1] // width
    inner = high - (wide + 1) * rows
    outs[19][...] = feed_rows(0, inner)
    outs[13][...] = feed_rows(inner, rows)
    for at in range(wide):
        outs[17][:, at * width : (at + 1) * width] = feed_rows(inner + (at + 1) * rows, rows)
    outs[9][...] = mid_ref[:rows, :]
    outs[5][...] = mid_ref[rows : 2 * rows, :]
    for at in range(2):
        outs[11][:, at * width : (at + 1) * width] = mid_ref[(2 + at) * rows : (3 + at) * rows, :]
    half = first_ref.shape[1]
    outs[2][:, :half] = first_ref[...]
    outs[2][:, half:] = second_ref[...]
    turn = lax.rem(width - place * rows, width)
    for group in range(3):
        turned = pltpu.roll(sums_ref[8 * group : 8 * group + 8, :], turn, 1)
        for index, row in vectors:
            if row // 8 == group:
                outs[index][...] = turned[row % 8 : row % 8 + 1, :rows]
    each = width // inner
    hidden = sums_ref[24 : 24 + wide, :]
    turned = pltpu.roll(
        jnp.concatenate([hidden] * (8 // wide), axis=0),
        lax.rem(width - lax.rem(place, each) * inner, width),
        1,
    )[:, :inner]
    mine = lax.broadcasted_iota(jnp.int32, turned.shape, 0) == place // each
    outs[18][...] = jnp.sum(jnp.where(mine, turned, 0.0), axis=0, keepdims=True)


def final_outputs(info, kept, got, mid, first, second, sums, inner, rows):
    width = mid.shape[1]
    block = inner * rows // width
    vectors = tuple(
        (index, at if at < 4 else at + 4 if at < 8 else at + 8)
        for at, index in enumerate((0, 1, 3, 4, 14, 15, 16, 20, 7, 8, 6, 10, 12))
    )
    shapes = [(1, rows)] * 21
    shapes[18] = (1, block)
    shapes[2], shapes[5], shapes[9], shapes[13] = (rows, 3 * width), *[(rows, width)] * 3
    shapes[11], shapes[17], shapes[19] = (rows, 2 * width), (rows, inner), (block, width)
    arrays = (kept, got, mid, first, second, sums)
    outs = [like(shape) for shape in shapes]
    results = kernel_call(
        functools.partial(final_kernel, rows=rows, vectors=vectors),
        "final",
        info,
        arrays,
        [whole_block(a) for a in arrays],
        outs,
        [whole_block(a) for a in outs],
        1,
        10**6,
        10**7,
    )
    return [out[0] if out.shape[0] == 1 else out for out in results]


def whole_sequences(
    targets,
    memory,
    row_kind,
    loss_mask,
    cotangent,
    norm_self_gain,
    norm_self_bias,
    self_input,
    self_query_bias,
    self_value_bias,
    self_output,
    self_output_bias,
    norm_cross_gain,
    norm_cross_bias,
    cross_query,
    cross_query_bias,
    cross_input,
    cross_value_bias,
    cross_output,
    cross_output_bias,
    norm_feed_gain,
    norm_feed_bias,
    feed_in,
    feed_in_bias,
    feed_out,
    feed_out_bias,
):
    micros, _, own, width = targets.shape
    held = micros // 2
    side = lax.axis_index("seq")
    parts = lax.axis_size("dp")
    place = lax.axis_index("dp")
    length = 2 * own
    pairs = HEADS * HEAD // 128

    def swap(rows, at, count, after=()):
        sent = lax.dynamic_slice_in_dim(rows, (1 - side) * held + at, count, axis=0)
        sent, after = lax.optimization_barrier((sent, after))
        return lax.ppermute(sent, "seq", SWAP), after

    def give(owns, got, at):
        got = got.astype(owns.dtype)
        return lax.dynamic_update_slice_in_dim(owns, got, (1 - side) * held + at, axis=0)

    def pack(*rows):
        zero = jnp.zeros((8 - len(rows), width), jnp.float32)
        return jnp.concatenate([jnp.stack(rows), zero])

    def batch(rows):
        return rows.reshape(held, length, -1)

    def flat(rows):
        return rows.reshape(held * length, -1)

    targets, memory = targets[:, 0], memory[:, 0]
    upstreams = (
        cotangent[:, 0].astype(jnp.float32) * loss_mask[:, 0].astype(jnp.float32)[..., None]
    ).astype(jnp.bfloat16)
    kinds = lax.dynamic_slice_in_dim(row_kind[:, 0], side * held, held, axis=0)
    info = jnp.concatenate(
        [jnp.stack([side, place % 2]), kinds, place[None]], dtype=jnp.int32
    )

    self_vectors = pack(norm_self_gain, norm_self_bias)
    zero = jnp.zeros_like(self_query_bias)
    joint_bias = jnp.concatenate([self_query_bias, zero, self_value_bias])[None]
    pair_bias = jnp.concatenate([zero, cross_value_bias])[None]
    got, _ = swap(targets, 0, 1)
    entered = enter(
        info, None, held, (), held, targets, self_input, self_vectors, joint_bias, True
    )
    source_parts = enter(
        info, None, held, (), held, memory, cross_input, self_vectors, pair_bias, False
    )
    got, entered, source_parts = lax.optimization_barrier((got, entered, source_parts))
    attended = ()
    for at in range(held):
        if at + 1 < held:
            later, got = swap(targets, at + 1, 1, got)
        entered = enter(
            info, at, 1, entered, held, got, self_input, self_vectors, joint_bias, True
        )
        joint = batch(entered[1])
        attended = attend(info, at, 1, attended, joint, joint, joint, True, (0, 1, 2))
        if at + 1 < held:
            entered, attended, got = lax.optimization_barrier((entered, attended, later))
        if at + 2 == held:
            memory_gots, got = swap(memory, 0, held, got)
    inputs, joint = entered[0], batch(entered[1])
    self_mixed, self_raised, self_inverse = attended
    after_self, cross_queries = middle(
        info,
        inputs,
        flat(self_mixed),
        self_output,
        cross_query,
        pack(self_output_bias, norm_cross_gain, norm_cross_bias, cross_query_bias),
        own,
    )
    cross_queries, source_parts, memory_gots = lax.optimization_barrier(
        (cross_queries, source_parts, memory_gots)
    )
    upstream_gots, memory_gots = swap(upstreams, 0, held, memory_gots)
    sources, cross_pairs = enter(
        info, 0, held, source_parts, held, memory_gots, cross_input, self_vectors, pair_bias, False
    )
    cross_queries, cross_pairs = batch(cross_queries), batch(cross_pairs)
    cross_mixed, cross_raised, cross_inverse = attend(
        info, 0, held, (), cross_queries, cross_pairs, cross_pairs, False, (0, 0, 1)
    )
    results, result_gots, grad_cross, cross_upstream, feed_sums, hidden_sums, *feed_parts = feed(
        info,
        after_self,
        flat(cross_mixed),
        upstreams,
        upstream_gots,
        cross_output,
        feed_in,
        feed_out,
        pack(cross_output_bias, norm_feed_gain, norm_feed_bias, feed_out_bias),
        feed_in_bias[None],
        parts,
    )
    feed_trees = [Tree(*feed_parts, low_first)]
    first = pairs // 2
    cross_inputs = (
        cross_queries, cross_pairs, cross_pairs, (0, 0, 1), cross_mixed, batch(cross_upstream),
        cross_raised, cross_inverse,
    )
    exchange(feed_trees)
    result_gots = lax.ppermute(result_gots, "seq", SWAP)
    half_grads = settle(feed_trees, attend_back((0, 0), (held, first), (), *cross_inputs))
    exchange(feed_trees)
    cross_grads = attend_back((0, first), (held, pairs - first), half_grads, *cross_inputs)
    (source_grads, source_gots, grad_self, self_upstream, return_sums, *mid_parts), back = settle(
        feed_trees,
        (return_rows(
            info,
            [flat(rows) for rows in cross_grads],
            after_self,
            grad_cross,
            flat(self_mixed),
            sources,
            cross_query,
            cross_input,
            self_output,
            pack(norm_cross_gain, norm_cross_bias),
            own,
            micros,
            parts,
        ), result_gots),
    )
    results = give(results, back, 0)
    mid_trees = [Tree(*mid_parts, low_first)]
    exchange(feed_trees + mid_trees)
    self_inputs = (
        joint, joint, joint, (0, 1, 2), self_mixed, batch(self_upstream), self_raised, self_inverse
    )
    source_gots = lax.ppermute(source_gots, "seq", SWAP)
    grads = settle(feed_trees + mid_trees, attend_back((0, 0), (1, pairs), (), *self_inputs))
    exchange(feed_trees + mid_trees)
    kept, sums = (), 0.0
    trees = feed_trees + mid_trees

    def leave_now(at, halves, kept, grads):
        return leave(
            info, at, halves, kept, [flat(rows) for rows in grads], inputs, grad_self,
            self_input, self_vectors, own, micros,
        )

    for at in range(held - 1):
        kept, got, new_sums = leave_now(at, (0, 1), kept, grads)
        sums = sums + new_sums
        grads, kept = lax.optimization_barrier((grads, kept))
        back = lax.ppermute(got, "seq", SWAP)
        grads, back, source_gots = settle(
            trees, (attend_back((at + 1, 0), (1, pairs), grads, *self_inputs), back, source_gots)
        )
        exchange(trees)
        back = back.astype(kept.dtype)[None]
        kept = (lax.dynamic_update_slice_in_dim(kept, back, (1 - side) * held + at, axis=0),)
    got, new_sums = leave_now(held - 1, (1,), (), grads)
    sums = sums + new_sums
    back = lax.ppermute(got, "seq", SWAP)
    grads, _ = lax.optimization_barrier((grads, got))
    late_parts = last_weight(info, [flat(rows) for rows in grads], inputs, self_vectors, own, parts)
    late_trees = [Tree(*late_parts[0:2], low_first), Tree(*late_parts[2:4], second_first)]
    exchange(late_trees)
    (grads, _), back = lax.optimization_barrier(((grads, late_parts[0]), back))
    grads = settle(late_trees, grads)
    exchange(late_trees)
    input_grads, new_sums = leave_now(held - 1, (0,), kept, grads)
    input_grads, new_sums = receive(trees + late_trees, (input_grads, new_sums))
    sums = jnp.concatenate(
        [sums + new_sums, feed_sums, return_sums, hidden_sums.reshape(-1, width)], axis=0
    )
    mid_total, *late_totals, sums = tail(mid_trees + late_trees, sums, parts)
    input_grads = give(input_grads, back[None], held - 1)
    final = final_outputs(
        info, feed_trees[0].kept, feed_trees[0].got, mid_total, *late_totals, sums,
        feed_in.shape[1], width // parts,
    )
    source_grads = give(source_grads, source_gots, 0)
    return (results[:, None], input_grads[:, None], source_grads[:, None]) + tuple(final)


def solution(mesh):
    in_specs = (
        P(None, "dp", "seq", None),
        P(None, "dp", "seq", None),
        P(None, "dp"),
        P(None, "dp", "seq"),
        P(None, "dp", "seq", None),
        P(),
        P(),
        P(),
        P(),
        P(),
        P(),
        P(),
        P(),
        P(),
        P(),
        P(),
        P(),
        P(),
        P(),
        P(),
        P(),
        P(),
        P(),
        P(),
        P(),
        P(),
    )
    out_specs = (
        P(None, "dp", "seq", None),
        P(None, "dp", "seq", None),
        P(None, "dp", "seq", None),
        P("dp"),
        P("dp"),
        P("dp", None),
        P("dp"),
        P("dp"),
        P("dp", None),
        P("dp"),
        P("dp"),
        P("dp"),
        P("dp", None),
        P("dp"),
        P("dp", None),
        P("dp"),
        P("dp", None),
        P("dp"),
        P("dp"),
        P("dp"),
        P("dp", None),
        P("dp"),
        P("dp", None),
        P("dp"),
    )

    def on_device(*arguments):
        micros = arguments[0].shape[0]
        rows = lax.axis_size("dp")
        pairs = lax.axis_size("seq") == 2 and micros % 2 == 0
        whole = pairs and rows == 16
        return (whole_sequences if whole else split_sequences)(*arguments)

    return jax.shard_map(
        on_device, mesh=mesh, in_specs=in_specs, out_specs=out_specs, check_vma=False
    )
```

```python
import functools

import jax
import jax.numpy as jnp
from jax import lax
from jax.experimental import pallas as pl
from jax.experimental.pallas import tpu as pltpu
from jax.sharding import PartitionSpec as P

HEADS = 12
HEAD = 64


epsilon = 1e-05
blocked_score = -1e30


def normed(values, norm_gain, norm_shift):
    center = values - jnp.mean(values, axis=-1, keepdims=True)
    spread = jnp.mean(center * center, axis=-1, keepdims=True)
    return center * lax.rsqrt(spread + epsilon) * norm_gain + norm_shift


def normed_back(values, norm_gain, norm_shift, upstream):
    unused, pullback = jax.vjp(normed, values, norm_gain, norm_shift)
    return pullback(upstream)


def gelu_exact(values):
    return jax.nn.gelu(values, approximate=False)


def project_rows(row_block, weight):
    return jnp.einsum("bpd,de->bpe", row_block, weight, preferred_element_type=jnp.float32)


def project_back(row_block, weight):
    return jnp.einsum("bpe,de->bpd", row_block, weight, preferred_element_type=jnp.float32)


def outer_sum(first_rows, second_rows):
    return jnp.einsum("bpd,bpe->de", first_rows, second_rows, preferred_element_type=jnp.float32)


def split_heads(row_block):
    return row_block.reshape(row_block.shape[0], row_block.shape[1], HEADS, HEAD)


def masked_scores(queries, key_rows, allowed):
    scores = jnp.einsum(
        "bphe,bshe->bhps",
        split_heads(queries),
        split_heads(key_rows),
        preferred_element_type=jnp.float32,
    )
    if allowed is None:
        return scores
    return jnp.where(allowed[:, None], scores, blocked_score)


def attend_forward(queries, key_rows, values, allowed):
    scores = masked_scores(queries, key_rows, allowed)
    highest_score = jnp.max(scores, axis=-1, keepdims=True)
    raised = jnp.exp(scores - highest_score)
    totals = jnp.sum(raised, axis=-1, keepdims=True)
    weights = (raised / totals).astype(jnp.bfloat16)
    mixed = jnp.einsum(
        "bhps,bshe->bphe", weights, split_heads(values), preferred_element_type=jnp.float32
    )
    return (mixed.reshape(queries.shape).astype(jnp.bfloat16), highest_score + jnp.log(totals))


def attend_backward(queries, key_rows, values, allowed, log_totals, upstream):
    weights = jnp.exp(masked_scores(queries, key_rows, allowed) - log_totals)
    upstream_heads = split_heads(upstream)
    value_grads = jnp.einsum(
        "bhps,bphe->bshe",
        weights.astype(jnp.bfloat16),
        upstream_heads,
        preferred_element_type=jnp.float32,
    )
    weight_grads = jnp.einsum(
        "bphe,bshe->bhps", upstream_heads, split_heads(values), preferred_element_type=jnp.float32
    )
    score_grads = weights * (weight_grads - jnp.sum(weight_grads * weights, axis=-1, keepdims=True))
    score_low = score_grads.astype(jnp.bfloat16)
    query_grads = jnp.einsum(
        "bhps,bshe->bphe", score_low, split_heads(key_rows), preferred_element_type=jnp.float32
    ).reshape(queries.shape)
    key_grads = jnp.einsum(
        "bhps,bphe->bshe", score_low, split_heads(queries), preferred_element_type=jnp.float32
    ).reshape(key_rows.shape)
    return (query_grads, jnp.concatenate([key_grads, value_grads.reshape(key_rows.shape)], axis=-1))


def split_sequences(
    targets,
    memory,
    row_kind,
    loss_mask,
    cotangent,
    norm_self_gain,
    norm_self_bias,
    self_input,
    self_query_bias,
    self_value_bias,
    self_output,
    self_output_bias,
    norm_cross_gain,
    norm_cross_bias,
    cross_query,
    cross_query_bias,
    cross_input,
    cross_value_bias,
    cross_output,
    cross_output_bias,
    norm_feed_gain,
    norm_feed_bias,
    feed_in,
    feed_in_bias,
    feed_out,
    feed_out_bias,
):
    model_width = targets.shape[3]
    part_rows = targets.shape[2]
    key_span = part_rows * lax.axis_size("seq")
    query_scale = HEAD ** (-0.5)
    places = lax.axis_index("seq") * part_rows + jnp.arange(part_rows)
    causal = jnp.arange(key_span)[None, :] <= places[:, None]
    results, input_grads, source_grads = ([], [], [])
    totals = None
    for micro_index in range(targets.shape[0]):
        inputs = targets[micro_index].astype(jnp.float32)
        memory_local = memory[micro_index]
        allowed = causal[None] | (row_kind[micro_index] == 1)[:, None, None]
        first_normed = normed(inputs, norm_self_gain, norm_self_bias).astype(jnp.bfloat16)
        self_joint = project_rows(first_normed, self_input)
        queries = ((self_joint[..., :model_width] + self_query_bias) * query_scale).astype(
            jnp.bfloat16
        )
        own_pairs = jnp.concatenate(
            [
                self_joint[..., model_width : 2 * model_width],
                self_joint[..., 2 * model_width :] + self_value_bias,
            ],
            axis=-1,
        ).astype(jnp.bfloat16)
        gathered_self = lax.all_gather(own_pairs, "seq", axis=1, tiled=True)
        key_rows = gathered_self[..., :model_width]
        value_rows = gathered_self[..., model_width:]
        self_mixed, self_totals = attend_forward(queries, key_rows, value_rows, allowed)
        after_self = inputs + project_rows(self_mixed, self_output) + self_output_bias
        second_normed = normed(after_self, norm_cross_gain, norm_cross_bias).astype(jnp.bfloat16)
        cross_queries = (
            (project_rows(second_normed, cross_query) + cross_query_bias) * query_scale
        ).astype(jnp.bfloat16)
        joined = project_rows(lax.all_gather(memory_local, "seq", axis=1, tiled=True), cross_input)
        gathered_cross = jnp.concatenate(
            [joined[..., :model_width], joined[..., model_width:] + cross_value_bias], axis=-1
        ).astype(jnp.bfloat16)
        cross_keys = gathered_cross[..., :model_width]
        cross_values = gathered_cross[..., model_width:]
        cross_mixed, cross_totals = attend_forward(cross_queries, cross_keys, cross_values, None)
        after_cross = after_self + project_rows(cross_mixed, cross_output) + cross_output_bias
        third_normed = normed(after_cross, norm_feed_gain, norm_feed_bias).astype(jnp.bfloat16)
        activated, gelu_pullback = jax.vjp(
            gelu_exact, project_rows(third_normed, feed_in) + feed_in_bias
        )
        activated_low = activated.astype(jnp.bfloat16)
        results.append(
            (after_cross + project_rows(activated_low, feed_out) + feed_out_bias).astype(
                jnp.bfloat16
            )
        )
        pieces = [None] * 21
        grad_output = (
            cotangent[micro_index].astype(jnp.float32)
            * loss_mask[micro_index].astype(jnp.float32)[..., None]
        )
        output_low = grad_output.astype(jnp.bfloat16)
        pieces[19] = outer_sum(activated_low, output_low)
        pieces[20] = jnp.sum(grad_output, axis=(0, 1))
        grad_hidden = gelu_pullback(project_back(output_low, feed_out))[0]
        hidden_low = grad_hidden.astype(jnp.bfloat16)
        pieces[17] = outer_sum(third_normed, hidden_low)
        pieces[18] = jnp.sum(grad_hidden, axis=(0, 1))
        through_feed, pieces[15], pieces[16] = normed_back(
            after_cross, norm_feed_gain, norm_feed_bias, project_back(hidden_low, feed_in)
        )
        grad_cross = grad_output + through_feed
        cross_low = grad_cross.astype(jnp.bfloat16)
        pieces[13] = outer_sum(cross_mixed, cross_low)
        pieces[14] = jnp.sum(grad_cross, axis=(0, 1))
        cross_upstream = project_back(cross_low, cross_output).astype(jnp.bfloat16)
        cross_query_grads, cross_pair_grads = attend_backward(
            cross_queries, cross_keys, cross_values, None, cross_totals, cross_upstream
        )
        own_cross = lax.psum_scatter(
            cross_pair_grads.astype(jnp.bfloat16), "seq", scatter_dimension=1, tiled=True
        ).astype(jnp.float32)
        pieces[12] = jnp.sum(own_cross[..., model_width:], axis=(0, 1))
        own_cross_low = own_cross.astype(jnp.bfloat16)
        pieces[11] = outer_sum(memory_local, own_cross_low)
        source_grads.append(project_back(own_cross_low, cross_input))
        scaled_cross = cross_query_grads * query_scale
        pieces[10] = jnp.sum(scaled_cross, axis=(0, 1))
        scaled_cross_low = scaled_cross.astype(jnp.bfloat16)
        pieces[9] = outer_sum(second_normed, scaled_cross_low)
        through_cross, pieces[7], pieces[8] = normed_back(
            after_self,
            norm_cross_gain,
            norm_cross_bias,
            project_back(scaled_cross_low, cross_query),
        )
        grad_self = grad_cross + through_cross
        self_low = grad_self.astype(jnp.bfloat16)
        pieces[5] = outer_sum(self_mixed, self_low)
        pieces[6] = jnp.sum(grad_self, axis=(0, 1))
        self_upstream = project_back(self_low, self_output).astype(jnp.bfloat16)
        self_query_grads, self_pair_grads = attend_backward(
            queries, key_rows, value_rows, allowed, self_totals, self_upstream
        )
        own_self = lax.psum_scatter(
            self_pair_grads.astype(jnp.bfloat16), "seq", scatter_dimension=1, tiled=True
        ).astype(jnp.float32)
        scaled_self = self_query_grads * query_scale
        pieces[3] = jnp.sum(scaled_self, axis=(0, 1))
        pieces[4] = jnp.sum(own_self[..., model_width:], axis=(0, 1))
        joint_low = jnp.concatenate([scaled_self, own_self], axis=-1).astype(jnp.bfloat16)
        pieces[2] = outer_sum(first_normed, joint_low)
        through_first, pieces[0], pieces[1] = normed_back(
            inputs, norm_self_gain, norm_self_bias, project_back(joint_low, self_input)
        )
        input_grads.append(grad_self + through_first)
        totals = (
            pieces
            if totals is None
            else [running + added for running, added in zip(totals, pieces)]
        )
    def reduced(total):
        block = lax.psum_scatter(
            total.astype(jnp.bfloat16), "dp", scatter_dimension=0, tiled=True
        )
        return lax.psum(block, "seq").astype(jnp.float32)

    final = [reduced(total) for total in totals]
    return (jnp.stack(results), jnp.stack(input_grads), jnp.stack(source_grads)) + tuple(final)


def contract(first, second, first_dim, second_dim):
    return lax.dot_general(
        first, second, (((first_dim,), (second_dim,)), ((), ())), preferred_element_type=jnp.float32
    )


def head_masks(pair):
    lane = lax.broadcasted_iota(jnp.int32, (1, pair.shape[1]), 1)
    zero = jnp.zeros((), pair.dtype)
    return (jnp.where(lane < HEAD, pair, zero), jnp.where(lane < HEAD, zero, pair))


LIMIT = 62 * 2**20


def attend_kernel(info_ref, q_ref, k_ref, v_ref, *refs, use_mask, start):
    o_ref, e_ref, r_ref, mask_ref = refs[-4:]
    length = k_ref.shape[1]
    half = length // 2
    values_turned = v_ref[0].T
    ones = jnp.ones((16, length), jnp.bfloat16)

    def run(masked, shifted):
        lowest, highest = None, None
        for at in range(2):
            queries_at = slice(at * half, (at + 1) * half)
            mixed = []
            for head, queries in enumerate(head_masks(q_ref[0, queries_at, :])):
                scores = contract(k_ref[0], queries, 1, 1)
                if shifted:
                    if masked:
                        seen = mask_ref[:, queries_at].astype(jnp.float32) > 0
                        scores = jnp.where(seen, scores, blocked_score)
                    scores = scores - jnp.max(scores, axis=0, keepdims=True)
                low = jnp.exp(scores).astype(jnp.bfloat16)
                if masked:
                    low = low * mask_ref[:, queries_at]
                e_ref[0, head, :, queries_at] = low
                turned = jnp.concatenate(
                    [values_turned[head * HEAD : (head + 1) * HEAD], ones], axis=0
                )
                sums = contract(turned, low, 1, 0)
                total = sums[HEAD : HEAD + 1]
                if not shifted:
                    lowest = total if lowest is None else jnp.minimum(lowest, total)
                    highest = total if highest is None else jnp.maximum(highest, total)
                inverse = 1.0 / total
                r_ref[0, 0, head : head + 1, queries_at] = inverse
                mixed.append(sums[:HEAD] * inverse)
            o_ref[0, queries_at, :] = jnp.concatenate(mixed, axis=0).T.astype(jnp.bfloat16)
        if not shifted:
            in_range = (jnp.min(lowest) > 1e-20) & (jnp.max(highest) < 1e30)

            @pl.when(jnp.logical_not(in_range))
            def _():
                run(masked, True)

    if not use_mask:
        run(False, False)
        return
    causal = info_ref[2 + start + pl.program_id(0)] == 0

    @pl.when(causal & (pl.program_id(1) == 0))
    def _():
        later = info_ref[0] * half
        query = lax.broadcasted_iota(jnp.int32, (1, length), 1)
        query = jnp.where(query < half, query + later, query - later)

        @pl.loop(0, length, step=64)
        def _(row):
            key = lax.broadcasted_iota(jnp.int32, (64, 1), 0) + row
            key = jnp.where(key < half, key + later, key - later)
            seen = jnp.where(key <= query, 1.0, 0.0)
            mask_ref[pl.ds(pl.multiple_of(row, 64), 64), :] = seen.astype(jnp.bfloat16)

    @pl.when(causal)
    def _():
        run(True, False)

    @pl.when(jnp.logical_not(causal))
    def _():
        run(False, False)


def attend(info, start, count_now, previous, queries, keys, values, use_mask, offsets):
    count, length = queries.shape[:2]
    pairs = HEADS * HEAD // 128
    width = HEADS * HEAD

    def spec(offset):
        return pl.BlockSpec((1, length, 128), lambda s, p, info: (start + s, 0, offset * pairs + p))

    place = lambda s, p, info: (start + s, p, 0, 0)
    return pl.pallas_call(
        functools.partial(attend_kernel, use_mask=use_mask, start=start),
        grid_spec=pltpu.PrefetchScalarGridSpec(
            num_scalar_prefetch=1,
            grid=(count_now, pairs),
            in_specs=[spec(offset) for offset in offsets]
            + [pl.BlockSpec(memory_space=pl.ANY)] * len(previous),
            out_specs=[
                spec(0),
                pl.BlockSpec((1, 2, length, length), place),
                pl.BlockSpec((1, 1, 2, length), place),
            ],
            scratch_shapes=[pltpu.VMEM((length, length), jnp.bfloat16)],
        ),
        out_shape=[
            jax.ShapeDtypeStruct((count, length, width), jnp.bfloat16),
            jax.ShapeDtypeStruct((count, HEADS, length, length), jnp.bfloat16),
            jax.ShapeDtypeStruct((count, pairs, 2, length), jnp.float32),
        ],
        input_output_aliases={4: 0, 5: 1, 6: 2} if previous else {},
        compiler_params=pltpu.CompilerParams(vmem_limit_bytes=LIMIT),
        cost_estimate=pl.CostEstimate(
            flops=4 * count_now * HEADS * length * length * 256,
            bytes_accessed=count_now * HEADS * length * length * 2,
            transcendentals=count_now * HEADS * length * length,
        ),
        name="attend",
    )(info, queries, keys, values, *previous)


def attend_back_kernel(q_ref, k_ref, v_ref, o_ref, g_ref, e_ref, r_ref, dq_ref, dk_ref, dv_ref):
    length = k_ref.shape[1]
    keys_turned = k_ref[0].T
    upstream = g_ref[0].astype(jnp.float32)
    products = (o_ref[0].astype(jnp.float32) * upstream).T
    upstream = upstream.T
    parts, deltas = [], []
    for head in range(2):
        rows = slice(head * HEAD, (head + 1) * HEAD)
        inverse = r_ref[0, 0, head : head + 1, :]
        parts.append(upstream[rows] * inverse)
        deltas.append(jnp.sum(products[rows], axis=0, keepdims=True) * inverse)
    scaled = head_masks(jnp.concatenate(parts, axis=0).T.astype(jnp.bfloat16))
    queries = head_masks(q_ref[0])
    key_sum, value_sum, query_parts = 0.0, 0.0, []
    for head in range(2):
        rows = slice(head * HEAD, (head + 1) * HEAD)
        low = e_ref[0, head]
        grads = contract(v_ref[0], scaled[head], 1, 1)
        score_low = (low.astype(jnp.float32) * (grads - deltas[head])).astype(jnp.bfloat16)
        value_sum += contract(low, scaled[head], 1, 0)
        key_sum += contract(score_low, queries[head], 1, 0)
        query_parts.append(contract(keys_turned[rows], score_low, 1, 0))
    turned = jnp.concatenate(query_parts, axis=0) * (HEAD**-0.5)
    dq_ref[0] = turned.T.astype(jnp.bfloat16)
    dk_ref[0] = key_sum.astype(jnp.bfloat16)
    dv_ref[0] = value_sum.astype(jnp.bfloat16)


def attend_back(place, size, previous, queries, keys, values, offsets, *rest):
    count, length = queries.shape[:2]
    pairs = HEADS * HEAD // 128
    width = HEADS * HEAD

    start, first = place

    def spec(offset):
        return pl.BlockSpec(
            (1, length, 128), lambda s, p: (start + s, 0, offset * pairs + first + p)
        )

    kernel = attend_back_kernel
    aliases = {}
    if previous:
        kernel = lambda *refs: attend_back_kernel(*refs[3:])
        aliases = {0: 0, 1: 1, 2: 2}
    return pl.pallas_call(
        kernel,
        grid=size,
        in_specs=[pl.BlockSpec(memory_space=pl.ANY)] * len(previous)
        + [spec(offset) for offset in offsets]
        + [
            spec(0),
            spec(0),
            pl.BlockSpec((1, 2, length, length), lambda s, p: (start + s, first + p, 0, 0)),
            pl.BlockSpec((1, 1, 2, length), lambda s, p: (start + s, first + p, 0, 0)),
        ],
        out_specs=[spec(0)] * 3,
        out_shape=[jax.ShapeDtypeStruct((count, length, width), jnp.bfloat16)] * 3,
        input_output_aliases=aliases,
        compiler_params=pltpu.CompilerParams(vmem_limit_bytes=LIMIT),
        cost_estimate=pl.CostEstimate(
            flops=16 * size[0] * size[1] * length * length * 256,
            bytes_accessed=4 * size[0] * size[1] * length * length,
            transcendentals=0,
        ),
        name="attend_back",
    )(*previous, queries, keys, values, *rest)


def normal_parts(values):
    center = values - jnp.mean(values, axis=-1, keepdims=True)
    inverse = lax.rsqrt(jnp.mean(center * center, axis=-1, keepdims=True) + epsilon)
    return center * inverse, inverse


def normal_back(unit, inverse, norm_gain, upstream):
    inner = upstream * norm_gain
    shift = jnp.mean(inner, axis=-1, keepdims=True)
    tilt = jnp.mean(inner * unit, axis=-1, keepdims=True)
    return inverse * (inner - shift - unit * tilt)


def gelu_parts(values):
    size = jnp.abs(values)
    ratio = 1.0 / (1.0 + 0.2316418882663604 * size)
    series = 0.5307027145
    for weight in (-0.7265760135, 0.7107068705, -0.142248368, 0.127414796):
        series = series * ratio + weight
    bell = jnp.exp(-0.5 * values * values)
    upper = series * ratio * bell
    chance = jnp.where(values < 0, upper, 1.0 - upper)
    return values * chance, chance + values * (0.3989422804014327 * bell)


def column_sum(values):
    return jnp.sum(values, axis=0, keepdims=True)


def resident(array):
    return pl.BlockSpec(array.shape, lambda *_: (0,) * array.ndim, pipeline_mode=pl.Buffered(1))


def whole_block(array):
    return pl.BlockSpec(array.shape, lambda *_: (0,) * len(array.shape))


def like(shape, dtype=jnp.float32):
    return jax.ShapeDtypeStruct(tuple(shape), dtype)


def pick(take_first, first_ref, second_ref):
    return jnp.where(take_first, first_ref[...], second_ref[...])


ONCE = {"pipeline_mode": pl.Buffered(1)}


def own_spec(own, width, held, last, **more):
    def place(step, info):
        return (info[0] * held + jnp.minimum(step, last) // 2, 0, 0)

    return pl.BlockSpec((None, own, width), place, **more)


def got_spec(own, width, last, **more):
    return pl.BlockSpec(
        (None, own, width), lambda step, info: (jnp.minimum(step, last) // 2, 0, 0), **more
    )


def row_spec(own, width, last, **more):
    return pl.BlockSpec((own, width), lambda step, info: (jnp.minimum(step, last), 0), **more)


def kernel_call(kernel, name, info, arrays, in_specs, outs, out_specs, grid, flops, moved, **more):
    scratch = more.pop("scratch", [])
    return pl.pallas_call(
        kernel,
        grid_spec=pltpu.PrefetchScalarGridSpec(
            num_scalar_prefetch=1,
            grid=(grid,),
            in_specs=in_specs,
            out_specs=out_specs,
            scratch_shapes=scratch,
        ),
        out_shape=outs,
        compiler_params=pltpu.CompilerParams(
            vmem_limit_bytes=more.pop("limit", LIMIT)
        ),
        cost_estimate=pl.CostEstimate(flops=flops, bytes_accessed=moved, transcendentals=0),
        name=name,
        **more,
    )(info, *arrays)


def enter_kernel(info_ref, source_ref, w_ref, vec_ref, bias_ref, *refs, norm):
    x_ref, out_ref = refs[-2:]
    x = source_ref[...]
    x_ref[...] = x
    if norm:
        unit, _ = normal_parts(x.astype(jnp.float32))
        x = (unit * vec_ref[0:1, :] + vec_ref[1:2, :]).astype(jnp.bfloat16)
    width = x.shape[1]
    for start in range(0, w_ref.shape[1], width):
        part = slice(start, start + width)
        total = contract(x, w_ref[:, part], 1, 0) + bias_ref[:, part]
        if norm and start == 0:
            total = total * (HEAD**-0.5)
        out_ref[:, part] = total.astype(jnp.bfloat16)


def enter(info, first, count, previous, held, rows_in, weight, vectors, bias, norm):
    own, width = rows_in.shape[1:]
    rows = 2 * held * own
    wide = weight.shape[1]
    if first is None:
        place = lambda step, info: (info[0] * held + step, 0, 0)
        row = lambda step, info: (2 * step, 0)
    else:
        place = lambda step, info: (step, 0, 0)
        row = lambda step, info: (2 * (first + step) + 1, 0)
    return kernel_call(
        functools.partial(enter_kernel, norm=norm),
        "enter",
        info,
        (rows_in, weight, vectors, bias, *previous),
        [pl.BlockSpec((None, own, width), place)]
        + [resident(a) for a in (weight, vectors, bias)]
        + [pl.BlockSpec(memory_space=pl.ANY)] * len(previous),
        [like((rows, width), jnp.bfloat16), like((rows, wide), jnp.bfloat16)],
        [pl.BlockSpec((own, width), row), pl.BlockSpec((own, wide), row)],
        count,
        2 * count * own * width * wide,
        2 * count * own * (2 * width + wide),
        input_output_aliases={5: 0, 6: 1} if previous else {},
    )


def middle_kernel(info_ref, x_ref, mixed_ref, wo_ref, wq_ref, vec_ref, after_ref, q_ref):
    out_bias, gain, shift, query_bias = (vec_ref[i : i + 1, :] for i in range(4))
    after = (
        x_ref[...].astype(jnp.float32) + contract(mixed_ref[...], wo_ref[...], 1, 0) + out_bias
    )
    after_ref[...] = after
    unit, _ = normal_parts(after)
    normal = (unit * gain + shift).astype(jnp.bfloat16)
    queries = (contract(normal, wq_ref[...], 1, 0) + query_bias) * (HEAD**-0.5)
    q_ref[...] = queries.astype(jnp.bfloat16)


def middle(info, x, mixed, wo, wq, vectors, own):
    rows, width = x.shape
    last = rows // own - 1
    spec = row_spec(own, width, last)
    return kernel_call(
        middle_kernel,
        "middle",
        info,
        (x, mixed, wo, wq, vectors),
        [spec, spec] + [resident(a) for a in (wo, wq, vectors)],
        [like((rows, width)), like((rows, width), jnp.bfloat16)],
        [spec, spec],
        rows // own,
        4 * rows * width * width,
        10 * rows * width,
    )


def write_split(core, rows, kept_ref, sent_ref, start):
    half = rows.shape[0] // 2
    low = rows.astype(jnp.bfloat16)
    place = slice(start, start + half)

    @pl.when(core == 0)
    def _():
        kept_ref[0, place, :] = low[:half]
        sent_ref[0, place, :] = low[half:]

    @pl.when(core != 0)
    def _():
        kept_ref[0, place, :] = low[half:]
        sent_ref[0, place, :] = low[:half]


def write_wide(core, rows, kept_ref, sent_ref, start):
    half, width = rows.shape[0] // 2, kept_ref.shape[2]
    for at in range(rows.shape[1] // width):
        part = rows[:, at * width : (at + 1) * width]
        write_split(core, part, kept_ref, sent_ref, start + at * half)


def acc_rows(ref, at, rows):
    return ref[pl.ds(pl.multiple_of(at * rows, 16), rows), :]


def piece(parts, high, wide, steps, order):
    bits = parts.bit_length() - 2

    def late(step, info):
        at = jnp.maximum(step - steps, 0)
        place = 0
        for bit in order(bits):
            place = 2 * place + (at // 2**bit) % 2
        return (place, 0, 0)

    return (
        [pl.BlockSpec((1, high, wide), late)] * 2,
        [like((parts // 2, high, wide), jnp.bfloat16)] * 2,
    )


def low_first(bits):
    return list(range(bits))


def second_first(bits):
    return list(range(bits))[1:2] + [0] + list(range(2, bits))


def put_rows(step, value, own_ref, got_ref):
    @pl.when(step % 2 == 0)
    def _():
        own_ref[...] = value.astype(own_ref.dtype)

    @pl.when(step % 2 != 0)
    def _():
        got_ref[...] = value.astype(got_ref.dtype)


def feed_kernel(
    info_ref, x_ref, mixed_ref, dyo_ref, dyg_ref, wc_ref, wi_ref, wo_ref, vec_ref, bi_ref,
    own_ref, got_ref, dx_ref, do_ref, vsum_ref, bsum_ref, kept_ref, sent_ref, ai_ref, ao_ref,
    ac_ref, *, steps, chunk, parts,
):
    step = pl.program_id(0)

    @pl.when(step == 0)
    def _():
        for ref in (vsum_ref, bsum_ref, ai_ref, ao_ref, ac_ref):
            ref[...] = jnp.zeros_like(ref)

    @pl.when(step < steps)
    def _():
        cross_bias, gain, shift, out_bias = (vec_ref[i : i + 1, :] for i in range(4))
        mixed = mixed_ref[...]
        x2 = x_ref[...] + contract(mixed, wc_ref[...], 1, 0) + cross_bias
        unit, inverse = normal_parts(x2)
        normal = (unit * gain + shift).astype(jnp.bfloat16)
        normal_turned = normal.T
        dy = pick(step % 2 == 0, dyo_ref, dyg_ref)
        dy_turned = dy.T
        result, upstream = None, None
        for start in range(0, wi_ref.shape[1], chunk):
            part = slice(start, start + chunk)
            hidden = contract(normal, wi_ref[:, part], 1, 0) + bi_ref[:, part]
            active, slope = gelu_parts(hidden)
            active = active.astype(jnp.bfloat16)
            down = contract(active, wo_ref[part, :], 1, 0)
            result = down if result is None else result + down
            grads = contract(dy, wo_ref[part, :], 1, 1) * slope
            bsum_ref[:, part] += column_sum(grads)
            low = grads.astype(jnp.bfloat16)
            up = contract(low, wi_ref[:, part], 1, 1)
            upstream = up if upstream is None else upstream + up
            ao_ref[:, part] += contract(dy_turned, active, 1, 0)
            ai_ref[:, part] += contract(normal_turned, low, 1, 0)
        put_rows(step, x2 + result + out_bias, own_ref, got_ref)
        wide = dy.astype(jnp.float32)
        dx = wide + normal_back(unit, inverse, gain, upstream)
        dx_ref[...] = dx
        dx_low = dx.astype(jnp.bfloat16)
        do_ref[...] = contract(dx_low, wc_ref[...], 1, 1).astype(jnp.bfloat16)
        ac_ref[...] += contract(mixed.T, dx_low, 1, 0)
        vsum_ref[0:1, :] += column_sum(dx)
        vsum_ref[1:2, :] += column_sum(upstream * unit)
        vsum_ref[2:3, :] += column_sum(upstream)
        vsum_ref[3:4, :] += column_sum(wide)

    @pl.when(step >= steps)
    def _():
        at = step - steps
        core = info_ref[1]
        width, wide = ai_ref.shape
        rows = 2 * width // parts
        inner = 2 * wide // parts
        columns = ao_ref[:, pl.ds(pl.multiple_of(at * inner, 128), inner)]
        write_split(core, columns.astype(jnp.bfloat16).T, kept_ref, sent_ref, 0)
        write_split(core, acc_rows(ac_ref, at, rows), kept_ref, sent_ref, inner // 2)
        write_wide(core, acc_rows(ai_ref, at, rows), kept_ref, sent_ref, (inner + rows) // 2)


def feed(info, x1, mixed, dys, dy_gots, wc, wi, wo, vectors, bi, parts, chunk=768):
    rows, width = x1.shape
    held, own = dy_gots.shape[:2]
    micros = dys.shape[0]
    inner = wi.shape[1]
    steps = 2 * held
    last = steps - 1
    row = row_spec(own, width, last)
    pieces = [piece(parts, (2 * inner + width) // parts, width, steps, low_first)]
    sums = [like((8, width)), like((1, inner))]
    return kernel_call(
        functools.partial(feed_kernel, steps=steps, chunk=chunk, parts=parts),
        "feed",
        info,
        (x1, mixed, dys, dy_gots, wc, wi, wo, vectors, bi),
        [row_spec(own, width, last, **ONCE)] * 2
        + [own_spec(own, width, held, last, **ONCE), got_spec(own, width, last, **ONCE)]
        + [resident(a) for a in (wc, wi, wo, vectors, bi)],
        [
            like((micros, own, width), jnp.bfloat16),
            like((held, own, width), jnp.bfloat16),
            like((rows, width)),
            like((rows, width), jnp.bfloat16),
        ]
        + sums
        + sum([p[1] for p in pieces], []),
        [own_spec(own, width, held, last), got_spec(own, width, last), row, row]
        + [whole_block(a) for a in sums]
        + sum([p[0] for p in pieces], []),
        steps + parts // 2,
        2 * rows * width * (6 * inner + 3 * width),
        60 * 2**20,
        scratch=[
            pltpu.VMEM((width, inner), jnp.float32),
            pltpu.VMEM((width, inner), jnp.float32),
            pltpu.VMEM((width, width), jnp.float32),
        ],
        limit=LIMIT,
    )


def return_kernel(
    info_ref, dq_ref, dk_ref, dv_ref, x_ref, dx_ref, mixed_ref, src_ref, wq_ref, wi_ref, wo_ref,
    vec_ref, own_ref, got_ref, dxo_ref, do_ref, vsum_ref, kept_ref, sent_ref, aq_ref, ao_ref,
    ai_ref, *, steps, parts,
):
    step = pl.program_id(0)

    @pl.when(step == 0)
    def _():
        for ref in (vsum_ref, aq_ref, ao_ref, ai_ref):
            ref[...] = jnp.zeros_like(ref)

    @pl.when(step < steps)
    def _():
        width = x_ref.shape[1]
        gain, shift = vec_ref[0:1, :], vec_ref[1:2, :]
        dq, dk, dv = dq_ref[...], dk_ref[...], dv_ref[...]
        upstream = contract(dq, wq_ref[...], 1, 1)
        unit, inverse = normal_parts(x_ref[...])
        normal = (unit * gain + shift).astype(jnp.bfloat16)
        dx = dx_ref[...] + normal_back(unit, inverse, gain, upstream)
        dxo_ref[...] = dx
        low = dx.astype(jnp.bfloat16)
        do_ref[...] = contract(low, wo_ref[...], 1, 1).astype(jnp.bfloat16)
        source = contract(dk, wi_ref[:, :width], 1, 1) + contract(dv, wi_ref[:, width:], 1, 1)
        put_rows(step, source, own_ref, got_ref)
        aq_ref[...] += contract(normal.T, dq, 1, 0)
        ao_ref[...] += contract(mixed_ref[...].T, low, 1, 0)
        turned = src_ref[...].T
        ai_ref[:, :width] += contract(turned, dk, 1, 0)
        ai_ref[:, width:] += contract(turned, dv, 1, 0)
        vsum_ref[0:1, :] += column_sum(upstream * unit)
        vsum_ref[1:2, :] += column_sum(upstream)
        vsum_ref[2:3, :] += column_sum(dx)
        vsum_ref[3:4, :] += column_sum(dq.astype(jnp.float32))
        vsum_ref[4:5, :] += column_sum(dv.astype(jnp.float32))

    @pl.when(step >= steps)
    def _():
        at = step - steps
        core = info_ref[1]
        rows = 2 * aq_ref.shape[0] // parts
        write_split(core, acc_rows(aq_ref, at, rows), kept_ref, sent_ref, 0)
        write_split(core, acc_rows(ao_ref, at, rows), kept_ref, sent_ref, rows // 2)
        write_wide(core, acc_rows(ai_ref, at, rows), kept_ref, sent_ref, rows)


def return_rows(info, grads, x1, dx2, mixed, sources, wq, wi, wo, vectors, own, micros, parts):
    rows, width = x1.shape
    held = rows // own // 2
    steps = 2 * held
    last = steps - 1
    row = row_spec(own, width, last)
    pieces = [piece(parts, 4 * width // parts, width, steps, low_first)]
    sums = like((8, width))
    return kernel_call(
        functools.partial(return_kernel, steps=steps, parts=parts),
        "return_rows",
        info,
        (*grads, x1, dx2, mixed, sources, wq, wi, wo, vectors),
        [row] * 7 + [resident(a) for a in (wq, wi, wo, vectors)],
        [
            like((micros, own, width)),
            like((held, own, width), jnp.bfloat16),
            like((rows, width)),
            like((rows, width), jnp.bfloat16),
            sums,
        ]
        + sum([p[1] for p in pieces], []),
        [own_spec(own, width, held, last), got_spec(own, width, last), row, row, whole_block(sums)]
        + sum([p[0] for p in pieces], []),
        steps + parts // 2,
        16 * rows * width * width,
        40 * 2**20,
        scratch=[
            pltpu.VMEM((width, width), jnp.float32),
            pltpu.VMEM((width, width), jnp.float32),
            pltpu.VMEM((width, 2 * width), jnp.float32),
        ],
    )


def last_weight_kernel(
    info_ref, dq_ref, dk_ref, dv_ref, x_ref, vec_ref, ka_ref, sa_ref, kb_ref, sb_ref, acc_ref,
    *, steps,
):
    step = pl.program_id(0)

    @pl.when(step == 0)
    def _():
        acc_ref[...] = jnp.zeros_like(acc_ref)

    @pl.when(step < steps)
    def _():
        unit, _ = normal_parts(x_ref[...].astype(jnp.float32))
        turned = (unit * vec_ref[0:1, :] + vec_ref[1:2, :]).astype(jnp.bfloat16).T
        width = x_ref.shape[1]
        for at, ref in enumerate((dq_ref, dk_ref, dv_ref)):
            acc_ref[:, at * width : (at + 1) * width] += contract(turned, ref[...], 1, 0)

    @pl.when(step >= steps)
    def _():
        rows = acc_rows(acc_ref, step - steps, 2 * ka_ref.shape[1])
        half = ka_ref.shape[2]
        write_split(info_ref[1], rows[:, :half], ka_ref, sa_ref, 0)
        write_split(info_ref[1], rows[:, half:], kb_ref, sb_ref, 0)


def last_weight(info, grads, x, vectors, own, parts):
    rows, width = x.shape
    steps = rows // own
    row = row_spec(own, width, steps - 1)
    pieces = [
        piece(parts, width // parts, 3 * width // 2, steps, order)
        for order in (low_first, second_first)
    ]
    return kernel_call(
        functools.partial(last_weight_kernel, steps=steps),
        "last_weight",
        info,
        (*grads, x, vectors),
        [row] * 4 + [resident(vectors)],
        sum([p[1] for p in pieces], []),
        sum([p[0] for p in pieces], []),
        steps + parts // 2,
        24 * rows * width * width,
        20 * 2**20,
        scratch=[pltpu.VMEM((width, 3 * width), jnp.float32)],
    )


def leave_kernel(
    info_ref, dq_ref, dk_ref, dv_ref, x_ref, dx_ref, w_ref, vec_ref, *refs, halves
):
    refs = list(refs)
    up_ref, vsum_ref = refs.pop(), refs.pop()
    got_ref = refs.pop() if 1 in halves else None
    own_ref = refs.pop() if 0 in halves else None
    step = pl.program_id(0)

    @pl.when(step == 0)
    def _():
        vsum_ref[...] = jnp.zeros_like(vsum_ref)

    width = x_ref.shape[1]
    dq, dk, dv = dq_ref[...], dk_ref[...], dv_ref[...]
    upstream = (
        contract(dq, w_ref[:, :width], 1, 1)
        + contract(dk, w_ref[:, width : 2 * width], 1, 1)
        + contract(dv, w_ref[:, 2 * width :], 1, 1)
    )
    unit, inverse = normal_parts(x_ref[...].astype(jnp.float32))
    dx = dx_ref[...] + normal_back(unit, inverse, vec_ref[0:1, :], upstream)
    if len(halves) == 2:
        put_rows(step, dx, own_ref, got_ref)
    else:
        out_ref = got_ref if own_ref is None else own_ref
        out_ref[...] = dx.astype(out_ref.dtype)
    vsum_ref[0:1, :] += column_sum(upstream * unit)
    vsum_ref[1:2, :] += column_sum(upstream)
    vsum_ref[2:3, :] += column_sum(dq.astype(jnp.float32))
    vsum_ref[3:4, :] += column_sum(dv.astype(jnp.float32))


def leave(info, at, halves, previous, grads, x, dx1, weight, vectors, own, micros):
    rows, width = x.shape
    held = rows // own // 2
    row = pl.BlockSpec((own, width), lambda step, info: (2 * at + halves[0] + step, 0))
    more = {"input_output_aliases": {8: 0}} if previous else {}
    sums = like((8, width))
    outs, out_specs = [], []
    if 0 in halves:
        outs.append(like((micros, own, width)))
        out_specs.append(
            pl.BlockSpec((None, own, width), lambda step, info: (info[0] * held + at, 0, 0))
        )
    if 1 in halves:
        outs.append(like((own, width), jnp.bfloat16))
        out_specs.append(pl.BlockSpec((own, width), lambda step, info: (0, 0)))
    return kernel_call(
        functools.partial(leave_kernel, halves=halves),
        "leave",
        info,
        (*grads, x, dx1, weight, vectors, *previous),
        [row] * 5
        + [resident(a) for a in (weight, vectors)]
        + [pl.BlockSpec(memory_space=pl.ANY)] * len(previous),
        outs + [sums],
        out_specs + [whole_block(sums)],
        len(halves),
        12 * len(halves) * own * width * width,
        8 * len(halves) * 2**20,
        scratch=[pltpu.VMEM((8, 128), jnp.float32)],
        **more,
    )


SWAP = ((0, 1), (1, 0))


class Tree:
    def __init__(self, kept, sent, order):
        self.count = lax.axis_size("dp")
        bits = self.count.bit_length() - 2
        shape = (2,) * bits + kept.shape[1:]
        self.order = [2 << bit for bit in order(bits)]
        self.kept, self.sent, self.bit = kept.reshape(shape), sent.reshape(shape), 1
        self.got, self.total = None, None

    def exchange(self):
        if self.total is not None or self.got is not None:
            return
        if self.bit:
            pairs = [(i, i ^ self.bit) for i in range(self.count)]
            self.got = lax.ppermute(self.sent, "dp", pairs)
        else:
            self.got = lax.ppermute(self.kept, "seq", SWAP)

    def add(self):
        if self.got is None:
            return
        total = self.kept.astype(jnp.float32) + self.got.astype(jnp.float32)
        self.got = None
        if not self.bit:
            self.total = total
            return
        total = total.astype(jnp.bfloat16)
        if not self.order:
            self.bit, self.kept = 0, total
            return
        self.bit = self.order.pop(0)
        mine = (lax.axis_index("dp") // self.bit) % 2
        self.kept = lax.dynamic_index_in_dim(total, mine, 0, keepdims=False)
        self.sent = lax.dynamic_index_in_dim(total, 1 - mine, 0, keepdims=False)


def exchange(trees):
    for tree in trees:
        tree.exchange()


def settle(trees, values):
    trees = [tree for tree in trees if tree.got is not None]
    gots, values = lax.optimization_barrier(([tree.got for tree in trees], values))
    for tree, got in zip(trees, gots):
        tree.got = got
        tree.add()
    return values


def receive(trees, values):
    gots, values = lax.optimization_barrier(([tree.got for tree in trees], values))
    for tree, got in zip(trees, gots):
        tree.got = got
    return values


def finish(trees):
    while any(tree.total is None for tree in trees):
        exchange(trees)
        settle(trees, ())


MESH = pl.DeviceIdType.MESH


def partner(place, offset):
    bit = 1
    while bit <= offset:
        if offset & bit:
            place = place + bit * (1 - 2 * ((place // bit) % 2))
        bit *= 2
    return place


def tail_kernel(*refs, orders, groups):
    trees = len(orders)
    ins, refs = refs[: 2 * trees + 1], refs[2 * trees + 1 :]
    outs, refs = refs[: trees + 1], refs[trees + 1 :]
    send_sems, recv_sems = refs[-2:]
    scratch = list(refs[:-2])
    place = lax.axis_index("dp")
    side = lax.axis_index("seq")
    offsets = sorted({bit for order in orders for bit in order} | {o for g in groups for o in g})
    peers = [{"dp": partner(place, offset)} for offset in offsets] + [{"seq": 1 - side}]
    barrier = pltpu.get_barrier_semaphore()
    for peer in peers:
        pl.semaphore_signal(barrier, inc=1, device_id=peer, device_id_type=MESH)
    pl.semaphore_wait(barrier, len(peers))
    used = []

    def send(source, target, peer):
        at = len(used)
        copy = pltpu.make_async_remote_copy(
            src_ref=source,
            dst_ref=target,
            send_sem=send_sems.at[at],
            recv_sem=recv_sems.at[at],
            device_id=peer,
            device_id_type=MESH,
        )
        used.append(copy)
        copy.start()
        return copy

    other = {"seq": 1 - side}
    totals = []
    for at in range(trees):
        total = scratch.pop(0)
        total[...] = (
            ins[2 * at][...].astype(jnp.float32) + ins[2 * at + 1][...].astype(jnp.float32)
        ).astype(jnp.bfloat16)
        totals.append(total)
    sums = ins[2 * trees][...]
    rounds = max(max(len(order) for order in orders) + 1, len(groups) + 1)
    for step in range(rounds):
        copies = []
        for at, order in enumerate(orders):
            if step < len(order):
                mine = (place // order[step]) % 2
                got = scratch.pop(0)
                peer = {"dp": partner(place, order[step])}
                copy = send(totals[at].at[1 - mine], got, peer)
                copies.append((copy, at, mine, got, scratch.pop(0)))
            elif step == len(order):
                got = scratch.pop(0)
                copies.append((send(totals[at], got, other), at, None, got, outs[at]))
        summed = []
        if step <= len(groups):
            low = scratch.pop(0)
            low[...] = sums.astype(jnp.bfloat16)
            goals = [other]
            if step < len(groups):
                goals = [{"dp": partner(place, offset)} for offset in groups[step]]
            for goal in goals:
                got = scratch.pop(0)
                summed.append((send(low, got, goal), got))
        for copy, at, mine, got, target in copies:
            copy.wait()
            held = totals[at][...] if mine is None else totals[at][mine]
            total = held.astype(jnp.float32) + got[...].astype(jnp.float32)
            target[...] = total.astype(target.dtype)
            totals[at] = target
        for copy, got in summed:
            copy.wait()
            sums = sums + got[...].astype(jnp.float32)
    outs[trees][...] = sums


def tail(trees, sums, parts):
    orders = [tuple(tree.order) for tree in trees]
    groups, bit = [], 1
    while bit < parts:
        groups.append(tuple(step * bit for step in (1, 2, 3) if step * bit < parts))
        bit *= 4
    arrays = []
    for tree in trees:
        arrays += [tree.kept, tree.got]
    arrays += [sums]
    totals = [pltpu.VMEM(tree.kept.shape, jnp.bfloat16) for tree in trees]
    scratch = totals
    shapes = [tree.kept.shape for tree in trees]
    copies = 0
    for step in range(max(max(len(order) for order in orders) + 1, len(groups) + 1)):
        for at, order in enumerate(orders):
            if step < len(order):
                shapes[at] = shapes[at][1:]
                scratch += [pltpu.VMEM(shapes[at], jnp.bfloat16)] * 2
                copies += 1
            elif step == len(order):
                scratch += [pltpu.VMEM(shapes[at], jnp.bfloat16)]
                copies += 1
        if step <= len(groups):
            each = len(groups[step]) if step < len(groups) else 1
            scratch += [pltpu.VMEM(sums.shape, jnp.bfloat16)] * (each + 1)
            copies += each
    outs = [like(shape) for shape in shapes] + [like(sums.shape)]
    vmem = pl.BlockSpec(memory_space=pltpu.VMEM)
    return pl.pallas_call(
        functools.partial(tail_kernel, orders=orders, groups=groups),
        in_specs=[vmem] * len(arrays),
        out_specs=[vmem] * len(outs),
        out_shape=outs,
        scratch_shapes=scratch + [pltpu.SemaphoreType.DMA((copies,))] * 2,
        compiler_params=pltpu.CompilerParams(
            collective_id=0, has_side_effects=True, vmem_limit_bytes=LIMIT
        ),
        cost_estimate=pl.CostEstimate(
            flops=2 * 10**10, bytes_accessed=10**7, transcendentals=0
        ),
        name="tail",
    )(*arrays)


def final_kernel(info_ref, kept_ref, got_ref, mid_ref, first_ref, second_ref, sums_ref, *outs, rows, vectors):
    place = info_ref[info_ref.shape[0] - 1]
    width = mid_ref.shape[1]
    high = kept_ref.shape[0]

    def feed_rows(start, count):
        at = slice(start, start + count)
        return kept_ref[at, :].astype(jnp.float32) + got_ref[at, :].astype(jnp.float32)

    wide = outs[17].shape[1] // width
    inner = high - (wide + 1) * rows
    outs[19][...] = feed_rows(0, inner)
    outs[13][...] = feed_rows(inner, rows)
    for at in range(wide):
        outs[17][:, at * width : (at + 1) * width] = feed_rows(inner + (at + 1) * rows, rows)
    outs[9][...] = mid_ref[:rows, :]
    outs[5][...] = mid_ref[rows : 2 * rows, :]
    for at in range(2):
        outs[11][:, at * width : (at + 1) * width] = mid_ref[(2 + at) * rows : (3 + at) * rows, :]
    half = first_ref.shape[1]
    outs[2][:, :half] = first_ref[...]
    outs[2][:, half:] = second_ref[...]
    turn = lax.rem(width - place * rows, width)
    for group in range(3):
        turned = pltpu.roll(sums_ref[8 * group : 8 * group + 8, :], turn, 1)
        for index, row in vectors:
            if row // 8 == group:
                outs[index][...] = turned[row % 8 : row % 8 + 1, :rows]
    each = width // inner
    hidden = sums_ref[24 : 24 + wide, :]
    turned = pltpu.roll(
        jnp.concatenate([hidden] * (8 // wide), axis=0),
        lax.rem(width - lax.rem(place, each) * inner, width),
        1,
    )[:, :inner]
    mine = lax.broadcasted_iota(jnp.int32, turned.shape, 0) == place // each
    outs[18][...] = jnp.sum(jnp.where(mine, turned, 0.0), axis=0, keepdims=True)


def final_outputs(info, kept, got, mid, first, second, sums, inner, rows):
    width = mid.shape[1]
    block = inner * rows // width
    vectors = tuple(
        (index, at if at < 4 else at + 4 if at < 8 else at + 8)
        for at, index in enumerate((0, 1, 3, 4, 14, 15, 16, 20, 7, 8, 6, 10, 12))
    )
    shapes = [(1, rows)] * 21
    shapes[18] = (1, block)
    shapes[2], shapes[5], shapes[9], shapes[13] = (rows, 3 * width), *[(rows, width)] * 3
    shapes[11], shapes[17], shapes[19] = (rows, 2 * width), (rows, inner), (block, width)
    arrays = (kept, got, mid, first, second, sums)
    outs = [like(shape) for shape in shapes]
    results = kernel_call(
        functools.partial(final_kernel, rows=rows, vectors=vectors),
        "final",
        info,
        arrays,
        [whole_block(a) for a in arrays],
        outs,
        [whole_block(a) for a in outs],
        1,
        10**6,
        10**7,
    )
    return [out[0] if out.shape[0] == 1 else out for out in results]


def whole_sequences(
    targets,
    memory,
    row_kind,
    loss_mask,
    cotangent,
    norm_self_gain,
    norm_self_bias,
    self_input,
    self_query_bias,
    self_value_bias,
    self_output,
    self_output_bias,
    norm_cross_gain,
    norm_cross_bias,
    cross_query,
    cross_query_bias,
    cross_input,
    cross_value_bias,
    cross_output,
    cross_output_bias,
    norm_feed_gain,
    norm_feed_bias,
    feed_in,
    feed_in_bias,
    feed_out,
    feed_out_bias,
):
    micros, _, own, width = targets.shape
    held = micros // 2
    side = lax.axis_index("seq")
    parts = lax.axis_size("dp")
    place = lax.axis_index("dp")
    length = 2 * own
    pairs = HEADS * HEAD // 128

    def swap(rows, at, count, after=()):
        sent = lax.dynamic_slice_in_dim(rows, (1 - side) * held + at, count, axis=0)
        sent, after = lax.optimization_barrier((sent, after))
        return lax.ppermute(sent, "seq", SWAP), after

    def give(owns, got, at):
        got = got.astype(owns.dtype)
        return lax.dynamic_update_slice_in_dim(owns, got, (1 - side) * held + at, axis=0)

    def pack(*rows):
        zero = jnp.zeros((8 - len(rows), width), jnp.float32)
        return jnp.concatenate([jnp.stack(rows), zero])

    def batch(rows):
        return rows.reshape(held, length, -1)

    def flat(rows):
        return rows.reshape(held * length, -1)

    targets, memory = targets[:, 0], memory[:, 0]
    upstreams = (
        cotangent[:, 0].astype(jnp.float32) * loss_mask[:, 0].astype(jnp.float32)[..., None]
    ).astype(jnp.bfloat16)
    kinds = lax.dynamic_slice_in_dim(row_kind[:, 0], side * held, held, axis=0)
    info = jnp.concatenate(
        [jnp.stack([side, place % 2]), kinds, place[None]], dtype=jnp.int32
    )

    self_vectors = pack(norm_self_gain, norm_self_bias)
    zero = jnp.zeros_like(self_query_bias)
    joint_bias = jnp.concatenate([self_query_bias, zero, self_value_bias])[None]
    pair_bias = jnp.concatenate([zero, cross_value_bias])[None]
    got, _ = swap(targets, 0, 1)
    entered = enter(
        info, None, held, (), held, targets, self_input, self_vectors, joint_bias, True
    )
    source_parts = enter(
        info, None, held, (), held, memory, cross_input, self_vectors, pair_bias, False
    )
    got, entered, source_parts = lax.optimization_barrier((got, entered, source_parts))
    attended = ()
    for at in range(held):
        if at + 1 < held:
            later, got = swap(targets, at + 1, 1, got)
        entered = enter(
            info, at, 1, entered, held, got, self_input, self_vectors, joint_bias, True
        )
        joint = batch(entered[1])
        attended = attend(info, at, 1, attended, joint, joint, joint, True, (0, 1, 2))
        if at + 1 < held:
            entered, attended, got = lax.optimization_barrier((entered, attended, later))
        if at + 2 == held:
            memory_gots, got = swap(memory, 0, held, got)
    inputs, joint = entered[0], batch(entered[1])
    self_mixed, self_raised, self_inverse = attended
    after_self, cross_queries = middle(
        info,
        inputs,
        flat(self_mixed),
        self_output,
        cross_query,
        pack(self_output_bias, norm_cross_gain, norm_cross_bias, cross_query_bias),
        own,
    )
    cross_queries, source_parts, memory_gots = lax.optimization_barrier(
        (cross_queries, source_parts, memory_gots)
    )
    upstream_gots, memory_gots = swap(upstreams, 0, held, memory_gots)
    sources, cross_pairs = enter(
        info, 0, held, source_parts, held, memory_gots, cross_input, self_vectors, pair_bias, False
    )
    cross_queries, cross_pairs = batch(cross_queries), batch(cross_pairs)
    cross_mixed, cross_raised, cross_inverse = attend(
        info, 0, held, (), cross_queries, cross_pairs, cross_pairs, False, (0, 0, 1)
    )
    results, result_gots, grad_cross, cross_upstream, feed_sums, hidden_sums, *feed_parts = feed(
        info,
        after_self,
        flat(cross_mixed),
        upstreams,
        upstream_gots,
        cross_output,
        feed_in,
        feed_out,
        pack(cross_output_bias, norm_feed_gain, norm_feed_bias, feed_out_bias),
        feed_in_bias[None],
        parts,
    )
    feed_trees = [Tree(*feed_parts, low_first)]
    first = pairs // 2
    cross_inputs = (
        cross_queries, cross_pairs, cross_pairs, (0, 0, 1), cross_mixed, batch(cross_upstream),
        cross_raised, cross_inverse,
    )
    exchange(feed_trees)
    result_gots = lax.ppermute(result_gots, "seq", SWAP)
    half_grads = settle(feed_trees, attend_back((0, 0), (held, first), (), *cross_inputs))
    exchange(feed_trees)
    cross_grads = attend_back((0, first), (held, pairs - first), half_grads, *cross_inputs)
    (source_grads, source_gots, grad_self, self_upstream, return_sums, *mid_parts), back = settle(
        feed_trees,
        (return_rows(
            info,
            [flat(rows) for rows in cross_grads],
            after_self,
            grad_cross,
            flat(self_mixed),
            sources,
            cross_query,
            cross_input,
            self_output,
            pack(norm_cross_gain, norm_cross_bias),
            own,
            micros,
            parts,
        ), result_gots),
    )
    results = give(results, back, 0)
    mid_trees = [Tree(*mid_parts, low_first)]
    exchange(feed_trees + mid_trees)
    self_inputs = (
        joint, joint, joint, (0, 1, 2), self_mixed, batch(self_upstream), self_raised, self_inverse
    )
    source_gots = lax.ppermute(source_gots, "seq", SWAP)
    grads = settle(feed_trees + mid_trees, attend_back((0, 0), (1, pairs), (), *self_inputs))
    exchange(feed_trees + mid_trees)
    kept, sums = (), 0.0
    trees = feed_trees + mid_trees

    def leave_now(at, halves, kept, grads):
        return leave(
            info, at, halves, kept, [flat(rows) for rows in grads], inputs, grad_self,
            self_input, self_vectors, own, micros,
        )

    for at in range(held - 1):
        kept, got, new_sums = leave_now(at, (0, 1), kept, grads)
        sums = sums + new_sums
        grads, kept = lax.optimization_barrier((grads, kept))
        back = lax.ppermute(got, "seq", SWAP)
        grads, back, source_gots = settle(
            trees, (attend_back((at + 1, 0), (1, pairs), grads, *self_inputs), back, source_gots)
        )
        exchange(trees)
        back = back.astype(kept.dtype)[None]
        kept = (lax.dynamic_update_slice_in_dim(kept, back, (1 - side) * held + at, axis=0),)
    got, new_sums = leave_now(held - 1, (1,), (), grads)
    sums = sums + new_sums
    back = lax.ppermute(got, "seq", SWAP)
    grads, _ = lax.optimization_barrier((grads, got))
    late_parts = last_weight(info, [flat(rows) for rows in grads], inputs, self_vectors, own, parts)
    late_trees = [Tree(*late_parts[0:2], low_first), Tree(*late_parts[2:4], second_first)]
    exchange(late_trees)
    (grads, _), back = lax.optimization_barrier(((grads, late_parts[0]), back))
    grads = settle(mid_trees + late_trees, grads)
    exchange(mid_trees + late_trees)
    input_grads, new_sums = leave_now(held - 1, (0,), kept, grads)
    input_grads, new_sums = receive(trees + late_trees, (input_grads, new_sums))
    sums = jnp.concatenate(
        [sums + new_sums, feed_sums, return_sums, hidden_sums.reshape(-1, width), jnp.zeros((4, width))],
        axis=0,
    )
    mid_total, *late_totals, sums = tail(mid_trees + late_trees, sums, parts)
    input_grads = give(input_grads, back[None], held - 1)
    final = final_outputs(
        info, feed_trees[0].kept, feed_trees[0].got, mid_total, *late_totals, sums,
        feed_in.shape[1], width // parts,
    )
    source_grads = give(source_grads, source_gots, 0)
    return (results[:, None], input_grads[:, None], source_grads[:, None]) + tuple(final)


def solution(mesh):
    in_specs = (
        P(None, "dp", "seq", None),
        P(None, "dp", "seq", None),
        P(None, "dp"),
        P(None, "dp", "seq"),
        P(None, "dp", "seq", None),
        P(),
        P(),
        P(),
        P(),
        P(),
        P(),
        P(),
        P(),
        P(),
        P(),
        P(),
        P(),
        P(),
        P(),
        P(),
        P(),
        P(),
        P(),
        P(),
        P(),
        P(),
    )
    out_specs = (
        P(None, "dp", "seq", None),
        P(None, "dp", "seq", None),
        P(None, "dp", "seq", None),
        P("dp"),
        P("dp"),
        P("dp", None),
        P("dp"),
        P("dp"),
        P("dp", None),
        P("dp"),
        P("dp"),
        P("dp"),
        P("dp", None),
        P("dp"),
        P("dp", None),
        P("dp"),
        P("dp", None),
        P("dp"),
        P("dp"),
        P("dp"),
        P("dp", None),
        P("dp"),
        P("dp", None),
        P("dp"),
    )

    def on_device(*arguments):
        micros = arguments[0].shape[0]
        rows = lax.axis_size("dp")
        pairs = lax.axis_size("seq") == 2 and micros % 2 == 0
        whole = pairs and rows == 16
        return (whole_sequences if whole else split_sequences)(*arguments)

    return jax.shard_map(
        on_device, mesh=mesh, in_specs=in_specs, out_specs=out_specs, check_vma=False
    )
```

```python
import functools

import jax
import jax.numpy as jnp
from jax import lax
from jax.experimental import pallas as pl
from jax.experimental.pallas import tpu as pltpu
from jax.sharding import PartitionSpec as P

HEADS = 12
HEAD = 64


epsilon = 1e-05
blocked_score = -1e30


def normed(values, norm_gain, norm_shift):
    center = values - jnp.mean(values, axis=-1, keepdims=True)
    spread = jnp.mean(center * center, axis=-1, keepdims=True)
    return center * lax.rsqrt(spread + epsilon) * norm_gain + norm_shift


def normed_back(values, norm_gain, norm_shift, upstream):
    unused, pullback = jax.vjp(normed, values, norm_gain, norm_shift)
    return pullback(upstream)


def gelu_exact(values):
    return jax.nn.gelu(values, approximate=False)


def project_rows(row_block, weight):
    return jnp.einsum("bpd,de->bpe", row_block, weight, preferred_element_type=jnp.float32)


def project_back(row_block, weight):
    return jnp.einsum("bpe,de->bpd", row_block, weight, preferred_element_type=jnp.float32)


def outer_sum(first_rows, second_rows):
    return jnp.einsum("bpd,bpe->de", first_rows, second_rows, preferred_element_type=jnp.float32)


def split_heads(row_block):
    return row_block.reshape(row_block.shape[0], row_block.shape[1], HEADS, HEAD)


def masked_scores(queries, key_rows, allowed):
    scores = jnp.einsum(
        "bphe,bshe->bhps",
        split_heads(queries),
        split_heads(key_rows),
        preferred_element_type=jnp.float32,
    )
    if allowed is None:
        return scores
    return jnp.where(allowed[:, None], scores, blocked_score)


def attend_forward(queries, key_rows, values, allowed):
    scores = masked_scores(queries, key_rows, allowed)
    highest_score = jnp.max(scores, axis=-1, keepdims=True)
    raised = jnp.exp(scores - highest_score)
    totals = jnp.sum(raised, axis=-1, keepdims=True)
    weights = (raised / totals).astype(jnp.bfloat16)
    mixed = jnp.einsum(
        "bhps,bshe->bphe", weights, split_heads(values), preferred_element_type=jnp.float32
    )
    return (mixed.reshape(queries.shape).astype(jnp.bfloat16), highest_score + jnp.log(totals))


def attend_backward(queries, key_rows, values, allowed, log_totals, upstream):
    weights = jnp.exp(masked_scores(queries, key_rows, allowed) - log_totals)
    upstream_heads = split_heads(upstream)
    value_grads = jnp.einsum(
        "bhps,bphe->bshe",
        weights.astype(jnp.bfloat16),
        upstream_heads,
        preferred_element_type=jnp.float32,
    )
    weight_grads = jnp.einsum(
        "bphe,bshe->bhps", upstream_heads, split_heads(values), preferred_element_type=jnp.float32
    )
    score_grads = weights * (weight_grads - jnp.sum(weight_grads * weights, axis=-1, keepdims=True))
    score_low = score_grads.astype(jnp.bfloat16)
    query_grads = jnp.einsum(
        "bhps,bshe->bphe", score_low, split_heads(key_rows), preferred_element_type=jnp.float32
    ).reshape(queries.shape)
    key_grads = jnp.einsum(
        "bhps,bphe->bshe", score_low, split_heads(queries), preferred_element_type=jnp.float32
    ).reshape(key_rows.shape)
    return (query_grads, jnp.concatenate([key_grads, value_grads.reshape(key_rows.shape)], axis=-1))


def split_sequences(
    targets,
    memory,
    row_kind,
    loss_mask,
    cotangent,
    norm_self_gain,
    norm_self_bias,
    self_input,
    self_query_bias,
    self_value_bias,
    self_output,
    self_output_bias,
    norm_cross_gain,
    norm_cross_bias,
    cross_query,
    cross_query_bias,
    cross_input,
    cross_value_bias,
    cross_output,
    cross_output_bias,
    norm_feed_gain,
    norm_feed_bias,
    feed_in,
    feed_in_bias,
    feed_out,
    feed_out_bias,
):
    model_width = targets.shape[3]
    part_rows = targets.shape[2]
    key_span = part_rows * lax.axis_size("seq")
    query_scale = HEAD ** (-0.5)
    places = lax.axis_index("seq") * part_rows + jnp.arange(part_rows)
    causal = jnp.arange(key_span)[None, :] <= places[:, None]
    results, input_grads, source_grads = ([], [], [])
    totals = None
    for micro_index in range(targets.shape[0]):
        inputs = targets[micro_index].astype(jnp.float32)
        memory_local = memory[micro_index]
        allowed = causal[None] | (row_kind[micro_index] == 1)[:, None, None]
        first_normed = normed(inputs, norm_self_gain, norm_self_bias).astype(jnp.bfloat16)
        self_joint = project_rows(first_normed, self_input)
        queries = ((self_joint[..., :model_width] + self_query_bias) * query_scale).astype(
            jnp.bfloat16
        )
        own_pairs = jnp.concatenate(
            [
                self_joint[..., model_width : 2 * model_width],
                self_joint[..., 2 * model_width :] + self_value_bias,
            ],
            axis=-1,
        ).astype(jnp.bfloat16)
        gathered_self = lax.all_gather(own_pairs, "seq", axis=1, tiled=True)
        key_rows = gathered_self[..., :model_width]
        value_rows = gathered_self[..., model_width:]
        self_mixed, self_totals = attend_forward(queries, key_rows, value_rows, allowed)
        after_self = inputs + project_rows(self_mixed, self_output) + self_output_bias
        second_normed = normed(after_self, norm_cross_gain, norm_cross_bias).astype(jnp.bfloat16)
        cross_queries = (
            (project_rows(second_normed, cross_query) + cross_query_bias) * query_scale
        ).astype(jnp.bfloat16)
        joined = project_rows(lax.all_gather(memory_local, "seq", axis=1, tiled=True), cross_input)
        gathered_cross = jnp.concatenate(
            [joined[..., :model_width], joined[..., model_width:] + cross_value_bias], axis=-1
        ).astype(jnp.bfloat16)
        cross_keys = gathered_cross[..., :model_width]
        cross_values = gathered_cross[..., model_width:]
        cross_mixed, cross_totals = attend_forward(cross_queries, cross_keys, cross_values, None)
        after_cross = after_self + project_rows(cross_mixed, cross_output) + cross_output_bias
        third_normed = normed(after_cross, norm_feed_gain, norm_feed_bias).astype(jnp.bfloat16)
        activated, gelu_pullback = jax.vjp(
            gelu_exact, project_rows(third_normed, feed_in) + feed_in_bias
        )
        activated_low = activated.astype(jnp.bfloat16)
        results.append(
            (after_cross + project_rows(activated_low, feed_out) + feed_out_bias).astype(
                jnp.bfloat16
            )
        )
        pieces = [None] * 21
        grad_output = (
            cotangent[micro_index].astype(jnp.float32)
            * loss_mask[micro_index].astype(jnp.float32)[..., None]
        )
        output_low = grad_output.astype(jnp.bfloat16)
        pieces[19] = outer_sum(activated_low, output_low)
        pieces[20] = jnp.sum(grad_output, axis=(0, 1))
        grad_hidden = gelu_pullback(project_back(output_low, feed_out))[0]
        hidden_low = grad_hidden.astype(jnp.bfloat16)
        pieces[17] = outer_sum(third_normed, hidden_low)
        pieces[18] = jnp.sum(grad_hidden, axis=(0, 1))
        through_feed, pieces[15], pieces[16] = normed_back(
            after_cross, norm_feed_gain, norm_feed_bias, project_back(hidden_low, feed_in)
        )
        grad_cross = grad_output + through_feed
        cross_low = grad_cross.astype(jnp.bfloat16)
        pieces[13] = outer_sum(cross_mixed, cross_low)
        pieces[14] = jnp.sum(grad_cross, axis=(0, 1))
        cross_upstream = project_back(cross_low, cross_output).astype(jnp.bfloat16)
        cross_query_grads, cross_pair_grads = attend_backward(
            cross_queries, cross_keys, cross_values, None, cross_totals, cross_upstream
        )
        own_cross = lax.psum_scatter(
            cross_pair_grads.astype(jnp.bfloat16), "seq", scatter_dimension=1, tiled=True
        ).astype(jnp.float32)
        pieces[12] = jnp.sum(own_cross[..., model_width:], axis=(0, 1))
        own_cross_low = own_cross.astype(jnp.bfloat16)
        pieces[11] = outer_sum(memory_local, own_cross_low)
        source_grads.append(project_back(own_cross_low, cross_input))
        scaled_cross = cross_query_grads * query_scale
        pieces[10] = jnp.sum(scaled_cross, axis=(0, 1))
        scaled_cross_low = scaled_cross.astype(jnp.bfloat16)
        pieces[9] = outer_sum(second_normed, scaled_cross_low)
        through_cross, pieces[7], pieces[8] = normed_back(
            after_self,
            norm_cross_gain,
            norm_cross_bias,
            project_back(scaled_cross_low, cross_query),
        )
        grad_self = grad_cross + through_cross
        self_low = grad_self.astype(jnp.bfloat16)
        pieces[5] = outer_sum(self_mixed, self_low)
        pieces[6] = jnp.sum(grad_self, axis=(0, 1))
        self_upstream = project_back(self_low, self_output).astype(jnp.bfloat16)
        self_query_grads, self_pair_grads = attend_backward(
            queries, key_rows, value_rows, allowed, self_totals, self_upstream
        )
        own_self = lax.psum_scatter(
            self_pair_grads.astype(jnp.bfloat16), "seq", scatter_dimension=1, tiled=True
        ).astype(jnp.float32)
        scaled_self = self_query_grads * query_scale
        pieces[3] = jnp.sum(scaled_self, axis=(0, 1))
        pieces[4] = jnp.sum(own_self[..., model_width:], axis=(0, 1))
        joint_low = jnp.concatenate([scaled_self, own_self], axis=-1).astype(jnp.bfloat16)
        pieces[2] = outer_sum(first_normed, joint_low)
        through_first, pieces[0], pieces[1] = normed_back(
            inputs, norm_self_gain, norm_self_bias, project_back(joint_low, self_input)
        )
        input_grads.append(grad_self + through_first)
        totals = (
            pieces
            if totals is None
            else [running + added for running, added in zip(totals, pieces)]
        )
    def reduced(total):
        block = lax.psum_scatter(
            total.astype(jnp.bfloat16), "dp", scatter_dimension=0, tiled=True
        )
        return lax.psum(block, "seq").astype(jnp.float32)

    final = [reduced(total) for total in totals]
    return (jnp.stack(results), jnp.stack(input_grads), jnp.stack(source_grads)) + tuple(final)


def contract(first, second, first_dim, second_dim):
    return lax.dot_general(
        first, second, (((first_dim,), (second_dim,)), ((), ())), preferred_element_type=jnp.float32
    )


def head_masks(pair):
    lane = lax.broadcasted_iota(jnp.int32, (1, pair.shape[1]), 1)
    zero = jnp.zeros((), pair.dtype)
    return (jnp.where(lane < HEAD, pair, zero), jnp.where(lane < HEAD, zero, pair))


LIMIT = 62 * 2**20


def attend_kernel(info_ref, q_ref, k_ref, v_ref, *refs, use_mask, start):
    o_ref, e_ref, r_ref, mask_ref = refs[-4:]
    length = k_ref.shape[1]
    half = length // 2
    values_turned = v_ref[0].T
    ones = jnp.ones((16, length), jnp.bfloat16)

    def run(masked, shifted):
        lowest, highest = None, None
        for at in range(2):
            queries_at = slice(at * half, (at + 1) * half)
            mixed = []
            for head, queries in enumerate(head_masks(q_ref[0, queries_at, :])):
                scores = contract(k_ref[0], queries, 1, 1)
                if shifted:
                    if masked:
                        seen = mask_ref[:, queries_at].astype(jnp.float32) > 0
                        scores = jnp.where(seen, scores, blocked_score)
                    scores = scores - jnp.max(scores, axis=0, keepdims=True)
                low = jnp.exp(scores).astype(jnp.bfloat16)
                if masked:
                    low = low * mask_ref[:, queries_at]
                e_ref[0, head, :, queries_at] = low
                turned = jnp.concatenate(
                    [values_turned[head * HEAD : (head + 1) * HEAD], ones], axis=0
                )
                sums = contract(turned, low, 1, 0)
                total = sums[HEAD : HEAD + 1]
                if not shifted:
                    lowest = total if lowest is None else jnp.minimum(lowest, total)
                    highest = total if highest is None else jnp.maximum(highest, total)
                inverse = 1.0 / total
                r_ref[0, 0, head : head + 1, queries_at] = inverse
                mixed.append(sums[:HEAD] * inverse)
            o_ref[0, queries_at, :] = jnp.concatenate(mixed, axis=0).T.astype(jnp.bfloat16)
        if not shifted:
            in_range = (jnp.min(lowest) > 1e-20) & (jnp.max(highest) < 1e30)

            @pl.when(jnp.logical_not(in_range))
            def _():
                run(masked, True)

    if not use_mask:
        run(False, False)
        return
    causal = info_ref[2 + start + pl.program_id(0)] == 0

    @pl.when(causal & (pl.program_id(1) == 0))
    def _():
        later = info_ref[0] * half
        query = lax.broadcasted_iota(jnp.int32, (1, length), 1)
        query = jnp.where(query < half, query + later, query - later)

        @pl.loop(0, length, step=64)
        def _(row):
            key = lax.broadcasted_iota(jnp.int32, (64, 1), 0) + row
            key = jnp.where(key < half, key + later, key - later)
            seen = jnp.where(key <= query, 1.0, 0.0)
            mask_ref[pl.ds(pl.multiple_of(row, 64), 64), :] = seen.astype(jnp.bfloat16)

    @pl.when(causal)
    def _():
        run(True, False)

    @pl.when(jnp.logical_not(causal))
    def _():
        run(False, False)


def attend(info, start, count_now, previous, queries, keys, values, use_mask, offsets):
    count, length = queries.shape[:2]
    pairs = HEADS * HEAD // 128
    width = HEADS * HEAD

    def spec(offset):
        return pl.BlockSpec((1, length, 128), lambda s, p, info: (start + s, 0, offset * pairs + p))

    place = lambda s, p, info: (start + s, p, 0, 0)
    return pl.pallas_call(
        functools.partial(attend_kernel, use_mask=use_mask, start=start),
        grid_spec=pltpu.PrefetchScalarGridSpec(
            num_scalar_prefetch=1,
            grid=(count_now, pairs),
            in_specs=[spec(offset) for offset in offsets]
            + [pl.BlockSpec(memory_space=pl.ANY)] * len(previous),
            out_specs=[
                spec(0),
                pl.BlockSpec((1, 2, length, length), place),
                pl.BlockSpec((1, 1, 2, length), place),
            ],
            scratch_shapes=[pltpu.VMEM((length, length), jnp.bfloat16)],
        ),
        out_shape=[
            jax.ShapeDtypeStruct((count, length, width), jnp.bfloat16),
            jax.ShapeDtypeStruct((count, HEADS, length, length), jnp.bfloat16),
            jax.ShapeDtypeStruct((count, pairs, 2, length), jnp.float32),
        ],
        input_output_aliases={4: 0, 5: 1, 6: 2} if previous else {},
        compiler_params=pltpu.CompilerParams(vmem_limit_bytes=LIMIT),
        cost_estimate=pl.CostEstimate(
            flops=4 * count_now * HEADS * length * length * 256,
            bytes_accessed=count_now * HEADS * length * length * 2,
            transcendentals=count_now * HEADS * length * length,
        ),
        name="attend",
    )(info, queries, keys, values, *previous)


def attend_back_kernel(q_ref, k_ref, v_ref, o_ref, g_ref, e_ref, r_ref, dq_ref, dk_ref, dv_ref):
    length = k_ref.shape[1]
    keys_turned = k_ref[0].T
    upstream = g_ref[0].astype(jnp.float32)
    products = (o_ref[0].astype(jnp.float32) * upstream).T
    upstream = upstream.T
    parts, deltas = [], []
    for head in range(2):
        rows = slice(head * HEAD, (head + 1) * HEAD)
        inverse = r_ref[0, 0, head : head + 1, :]
        parts.append(upstream[rows] * inverse)
        deltas.append(jnp.sum(products[rows], axis=0, keepdims=True) * inverse)
    scaled = head_masks(jnp.concatenate(parts, axis=0).T.astype(jnp.bfloat16))
    queries = head_masks(q_ref[0])
    key_sum, value_sum, query_parts = 0.0, 0.0, []
    for head in range(2):
        rows = slice(head * HEAD, (head + 1) * HEAD)
        low = e_ref[0, head]
        grads = contract(v_ref[0], scaled[head], 1, 1)
        score_low = (low.astype(jnp.float32) * (grads - deltas[head])).astype(jnp.bfloat16)
        value_sum += contract(low, scaled[head], 1, 0)
        key_sum += contract(score_low, queries[head], 1, 0)
        query_parts.append(contract(keys_turned[rows], score_low, 1, 0))
    turned = jnp.concatenate(query_parts, axis=0) * (HEAD**-0.5)
    dq_ref[0] = turned.T.astype(jnp.bfloat16)
    dk_ref[0] = key_sum.astype(jnp.bfloat16)
    dv_ref[0] = value_sum.astype(jnp.bfloat16)


def attend_back(place, size, previous, queries, keys, values, offsets, *rest):
    count, length = queries.shape[:2]
    pairs = HEADS * HEAD // 128
    width = HEADS * HEAD

    start, first = place

    def spec(offset):
        return pl.BlockSpec(
            (1, length, 128), lambda s, p: (start + s, 0, offset * pairs + first + p)
        )

    kernel = attend_back_kernel
    aliases = {}
    if previous:
        kernel = lambda *refs: attend_back_kernel(*refs[3:])
        aliases = {0: 0, 1: 1, 2: 2}
    return pl.pallas_call(
        kernel,
        grid=size,
        in_specs=[pl.BlockSpec(memory_space=pl.ANY)] * len(previous)
        + [spec(offset) for offset in offsets]
        + [
            spec(0),
            spec(0),
            pl.BlockSpec((1, 2, length, length), lambda s, p: (start + s, first + p, 0, 0)),
            pl.BlockSpec((1, 1, 2, length), lambda s, p: (start + s, first + p, 0, 0)),
        ],
        out_specs=[spec(0)] * 3,
        out_shape=[jax.ShapeDtypeStruct((count, length, width), jnp.bfloat16)] * 3,
        input_output_aliases=aliases,
        compiler_params=pltpu.CompilerParams(vmem_limit_bytes=LIMIT),
        cost_estimate=pl.CostEstimate(
            flops=16 * size[0] * size[1] * length * length * 256,
            bytes_accessed=4 * size[0] * size[1] * length * length,
            transcendentals=0,
        ),
        name="attend_back",
    )(*previous, queries, keys, values, *rest)


def normal_parts(values):
    center = values - jnp.mean(values, axis=-1, keepdims=True)
    inverse = lax.rsqrt(jnp.mean(center * center, axis=-1, keepdims=True) + epsilon)
    return center * inverse, inverse


def normal_back(unit, inverse, norm_gain, upstream):
    inner = upstream * norm_gain
    shift = jnp.mean(inner, axis=-1, keepdims=True)
    tilt = jnp.mean(inner * unit, axis=-1, keepdims=True)
    return inverse * (inner - shift - unit * tilt)


def gelu_parts(values):
    size = jnp.abs(values)
    ratio = 1.0 / (1.0 + 0.2316418882663604 * size)
    series = 0.5307027145
    for weight in (-0.7265760135, 0.7107068705, -0.142248368, 0.127414796):
        series = series * ratio + weight
    bell = jnp.exp(-0.5 * values * values)
    upper = series * ratio * bell
    chance = jnp.where(values < 0, upper, 1.0 - upper)
    return values * chance, chance + values * (0.3989422804014327 * bell)


def column_sum(values):
    return jnp.sum(values, axis=0, keepdims=True)


def resident(array):
    return pl.BlockSpec(array.shape, lambda *_: (0,) * array.ndim, pipeline_mode=pl.Buffered(1))


def whole_block(array):
    return pl.BlockSpec(array.shape, lambda *_: (0,) * len(array.shape))


def like(shape, dtype=jnp.float32):
    return jax.ShapeDtypeStruct(tuple(shape), dtype)


def pick(take_first, first_ref, second_ref):
    return jnp.where(take_first, first_ref[...], second_ref[...])


ONCE = {"pipeline_mode": pl.Buffered(1)}


def own_spec(own, width, held, last, **more):
    def place(step, info):
        return (info[0] * held + jnp.minimum(step, last) // 2, 0, 0)

    return pl.BlockSpec((None, own, width), place, **more)


def got_spec(own, width, last, **more):
    return pl.BlockSpec(
        (None, own, width), lambda step, info: (jnp.minimum(step, last) // 2, 0, 0), **more
    )


def row_spec(own, width, last, **more):
    return pl.BlockSpec((own, width), lambda step, info: (jnp.minimum(step, last), 0), **more)


def kernel_call(kernel, name, info, arrays, in_specs, outs, out_specs, grid, flops, moved, **more):
    scratch = more.pop("scratch", [])
    return pl.pallas_call(
        kernel,
        grid_spec=pltpu.PrefetchScalarGridSpec(
            num_scalar_prefetch=1,
            grid=(grid,),
            in_specs=in_specs,
            out_specs=out_specs,
            scratch_shapes=scratch,
        ),
        out_shape=outs,
        compiler_params=pltpu.CompilerParams(
            vmem_limit_bytes=more.pop("limit", LIMIT)
        ),
        cost_estimate=pl.CostEstimate(flops=flops, bytes_accessed=moved, transcendentals=0),
        name=name,
        **more,
    )(info, *arrays)


def enter_kernel(info_ref, source_ref, w_ref, vec_ref, bias_ref, *refs, norm):
    x_ref, out_ref = refs[-2:]
    x = source_ref[...]
    x_ref[...] = x
    if norm:
        unit, _ = normal_parts(x.astype(jnp.float32))
        x = (unit * vec_ref[0:1, :] + vec_ref[1:2, :]).astype(jnp.bfloat16)
    width = x.shape[1]
    for start in range(0, w_ref.shape[1], width):
        part = slice(start, start + width)
        total = contract(x, w_ref[:, part], 1, 0) + bias_ref[:, part]
        if norm and start == 0:
            total = total * (HEAD**-0.5)
        out_ref[:, part] = total.astype(jnp.bfloat16)


def enter(info, first, count, previous, held, rows_in, weight, vectors, bias, norm):
    own, width = rows_in.shape[1:]
    rows = 2 * held * own
    wide = weight.shape[1]
    if first is None:
        place = lambda step, info: (info[0] * held + step, 0, 0)
        row = lambda step, info: (2 * step, 0)
    else:
        place = lambda step, info: (step, 0, 0)
        row = lambda step, info: (2 * (first + step) + 1, 0)
    return kernel_call(
        functools.partial(enter_kernel, norm=norm),
        "enter",
        info,
        (rows_in, weight, vectors, bias, *previous),
        [pl.BlockSpec((None, own, width), place)]
        + [resident(a) for a in (weight, vectors, bias)]
        + [pl.BlockSpec(memory_space=pl.ANY)] * len(previous),
        [like((rows, width), jnp.bfloat16), like((rows, wide), jnp.bfloat16)],
        [pl.BlockSpec((own, width), row), pl.BlockSpec((own, wide), row)],
        count,
        2 * count * own * width * wide,
        2 * count * own * (2 * width + wide),
        input_output_aliases={5: 0, 6: 1} if previous else {},
    )


def middle_kernel(info_ref, x_ref, mixed_ref, wo_ref, wq_ref, vec_ref, after_ref, q_ref):
    out_bias, gain, shift, query_bias = (vec_ref[i : i + 1, :] for i in range(4))
    after = (
        x_ref[...].astype(jnp.float32) + contract(mixed_ref[...], wo_ref[...], 1, 0) + out_bias
    )
    after_ref[...] = after
    unit, _ = normal_parts(after)
    normal = (unit * gain + shift).astype(jnp.bfloat16)
    queries = (contract(normal, wq_ref[...], 1, 0) + query_bias) * (HEAD**-0.5)
    q_ref[...] = queries.astype(jnp.bfloat16)


def middle(info, x, mixed, wo, wq, vectors, own):
    rows, width = x.shape
    last = rows // own - 1
    spec = row_spec(own, width, last)
    return kernel_call(
        middle_kernel,
        "middle",
        info,
        (x, mixed, wo, wq, vectors),
        [spec, spec] + [resident(a) for a in (wo, wq, vectors)],
        [like((rows, width)), like((rows, width), jnp.bfloat16)],
        [spec, spec],
        rows // own,
        4 * rows * width * width,
        10 * rows * width,
    )


def write_split(core, rows, kept_ref, sent_ref, start):
    half = rows.shape[0] // 2
    low = rows.astype(jnp.bfloat16)
    place = slice(start, start + half)

    @pl.when(core == 0)
    def _():
        kept_ref[0, place, :] = low[:half]
        sent_ref[0, place, :] = low[half:]

    @pl.when(core != 0)
    def _():
        kept_ref[0, place, :] = low[half:]
        sent_ref[0, place, :] = low[:half]


def write_wide(core, rows, kept_ref, sent_ref, start):
    half, width = rows.shape[0] // 2, kept_ref.shape[2]
    for at in range(rows.shape[1] // width):
        part = rows[:, at * width : (at + 1) * width]
        write_split(core, part, kept_ref, sent_ref, start + at * half)


def acc_rows(ref, at, rows):
    return ref[pl.ds(pl.multiple_of(at * rows, 16), rows), :]


def piece(parts, high, wide, steps, order):
    bits = parts.bit_length() - 2

    def late(step, info):
        at = jnp.maximum(step - steps, 0)
        place = 0
        for bit in order(bits):
            place = 2 * place + (at // 2**bit) % 2
        return (place, 0, 0)

    return (
        [pl.BlockSpec((1, high, wide), late)] * 2,
        [like((parts // 2, high, wide), jnp.bfloat16)] * 2,
    )


def low_first(bits):
    return list(range(bits))


def second_first(bits):
    return list(range(bits))[1:2] + [0] + list(range(2, bits))


def put_rows(step, value, own_ref, got_ref):
    @pl.when(step % 2 == 0)
    def _():
        own_ref[...] = value.astype(own_ref.dtype)

    @pl.when(step % 2 != 0)
    def _():
        got_ref[...] = value.astype(got_ref.dtype)


def feed_kernel(
    info_ref, x_ref, mixed_ref, dyo_ref, dyg_ref, wc_ref, wi_ref, wo_ref, vec_ref, bi_ref,
    own_ref, got_ref, dx_ref, do_ref, vsum_ref, bsum_ref, kept_ref, sent_ref, ai_ref, ao_ref,
    ac_ref, *, steps, chunk, parts,
):
    step = pl.program_id(0)

    @pl.when(step == 0)
    def _():
        for ref in (vsum_ref, bsum_ref, ai_ref, ao_ref, ac_ref):
            ref[...] = jnp.zeros_like(ref)

    @pl.when(step < steps)
    def _():
        cross_bias, gain, shift, out_bias = (vec_ref[i : i + 1, :] for i in range(4))
        mixed = mixed_ref[...]
        x2 = x_ref[...] + contract(mixed, wc_ref[...], 1, 0) + cross_bias
        unit, inverse = normal_parts(x2)
        normal = (unit * gain + shift).astype(jnp.bfloat16)
        normal_turned = normal.T
        dy = pick(step % 2 == 0, dyo_ref, dyg_ref)
        dy_turned = dy.T
        result, upstream = None, None
        for start in range(0, wi_ref.shape[1], chunk):
            part = slice(start, start + chunk)
            hidden = contract(normal, wi_ref[:, part], 1, 0) + bi_ref[:, part]
            active, slope = gelu_parts(hidden)
            active = active.astype(jnp.bfloat16)
            down = contract(active, wo_ref[part, :], 1, 0)
            result = down if result is None else result + down
            grads = contract(dy, wo_ref[part, :], 1, 1) * slope
            bsum_ref[:, part] += column_sum(grads)
            low = grads.astype(jnp.bfloat16)
            up = contract(low, wi_ref[:, part], 1, 1)
            upstream = up if upstream is None else upstream + up
            ao_ref[:, part] += contract(dy_turned, active, 1, 0)
            ai_ref[:, part] += contract(normal_turned, low, 1, 0)
        put_rows(step, x2 + result + out_bias, own_ref, got_ref)
        wide = dy.astype(jnp.float32)
        dx = wide + normal_back(unit, inverse, gain, upstream)
        dx_ref[...] = dx
        dx_low = dx.astype(jnp.bfloat16)
        do_ref[...] = contract(dx_low, wc_ref[...], 1, 1).astype(jnp.bfloat16)
        ac_ref[...] += contract(mixed.T, dx_low, 1, 0)
        vsum_ref[0:1, :] += column_sum(dx)
        vsum_ref[1:2, :] += column_sum(upstream * unit)
        vsum_ref[2:3, :] += column_sum(upstream)
        vsum_ref[3:4, :] += column_sum(wide)

    @pl.when(step >= steps)
    def _():
        at = step - steps
        core = info_ref[1]
        width, wide = ai_ref.shape
        rows = 2 * width // parts
        inner = 2 * wide // parts
        columns = ao_ref[:, pl.ds(pl.multiple_of(at * inner, 128), inner)]
        write_split(core, columns.astype(jnp.bfloat16).T, kept_ref, sent_ref, 0)
        write_split(core, acc_rows(ac_ref, at, rows), kept_ref, sent_ref, inner // 2)
        write_wide(core, acc_rows(ai_ref, at, rows), kept_ref, sent_ref, (inner + rows) // 2)


def feed(info, x1, mixed, dys, dy_gots, wc, wi, wo, vectors, bi, parts, chunk=768):
    rows, width = x1.shape
    held, own = dy_gots.shape[:2]
    micros = dys.shape[0]
    inner = wi.shape[1]
    steps = 2 * held
    last = steps - 1
    row = row_spec(own, width, last)
    pieces = [piece(parts, (2 * inner + width) // parts, width, steps, low_first)]
    sums = [like((8, width)), like((1, inner))]
    return kernel_call(
        functools.partial(feed_kernel, steps=steps, chunk=chunk, parts=parts),
        "feed",
        info,
        (x1, mixed, dys, dy_gots, wc, wi, wo, vectors, bi),
        [row_spec(own, width, last, **ONCE)] * 2
        + [own_spec(own, width, held, last, **ONCE), got_spec(own, width, last, **ONCE)]
        + [resident(a) for a in (wc, wi, wo, vectors, bi)],
        [
            like((micros, own, width), jnp.bfloat16),
            like((held, own, width), jnp.bfloat16),
            like((rows, width)),
            like((rows, width), jnp.bfloat16),
        ]
        + sums
        + sum([p[1] for p in pieces], []),
        [own_spec(own, width, held, last), got_spec(own, width, last), row, row]
        + [whole_block(a) for a in sums]
        + sum([p[0] for p in pieces], []),
        steps + parts // 2,
        2 * rows * width * (6 * inner + 3 * width),
        60 * 2**20,
        scratch=[
            pltpu.VMEM((width, inner), jnp.float32),
            pltpu.VMEM((width, inner), jnp.float32),
            pltpu.VMEM((width, width), jnp.float32),
        ],
        limit=LIMIT,
    )


def return_kernel(
    info_ref, dq_ref, dk_ref, dv_ref, x_ref, dx_ref, mixed_ref, src_ref, wq_ref, wi_ref, wo_ref,
    vec_ref, own_ref, got_ref, dxo_ref, do_ref, vsum_ref, kept_ref, sent_ref, aq_ref, ao_ref,
    ai_ref, *, steps, parts,
):
    step = pl.program_id(0)

    @pl.when(step == 0)
    def _():
        for ref in (vsum_ref, aq_ref, ao_ref, ai_ref):
            ref[...] = jnp.zeros_like(ref)

    @pl.when(step < steps)
    def _():
        width = x_ref.shape[1]
        gain, shift = vec_ref[0:1, :], vec_ref[1:2, :]
        dq, dk, dv = dq_ref[...], dk_ref[...], dv_ref[...]
        upstream = contract(dq, wq_ref[...], 1, 1)
        unit, inverse = normal_parts(x_ref[...])
        normal = (unit * gain + shift).astype(jnp.bfloat16)
        dx = dx_ref[...] + normal_back(unit, inverse, gain, upstream)
        dxo_ref[...] = dx
        low = dx.astype(jnp.bfloat16)
        do_ref[...] = contract(low, wo_ref[...], 1, 1).astype(jnp.bfloat16)
        source = contract(dk, wi_ref[:, :width], 1, 1) + contract(dv, wi_ref[:, width:], 1, 1)
        put_rows(step, source, own_ref, got_ref)
        aq_ref[...] += contract(normal.T, dq, 1, 0)
        ao_ref[...] += contract(mixed_ref[...].T, low, 1, 0)
        turned = src_ref[...].T
        ai_ref[:, :width] += contract(turned, dk, 1, 0)
        ai_ref[:, width:] += contract(turned, dv, 1, 0)
        vsum_ref[0:1, :] += column_sum(upstream * unit)
        vsum_ref[1:2, :] += column_sum(upstream)
        vsum_ref[2:3, :] += column_sum(dx)
        vsum_ref[3:4, :] += column_sum(dq.astype(jnp.float32))
        vsum_ref[4:5, :] += column_sum(dv.astype(jnp.float32))

    @pl.when(step >= steps)
    def _():
        at = step - steps
        core = info_ref[1]
        rows = 2 * aq_ref.shape[0] // parts
        write_split(core, acc_rows(aq_ref, at, rows), kept_ref, sent_ref, 0)
        write_split(core, acc_rows(ao_ref, at, rows), kept_ref, sent_ref, rows // 2)
        write_wide(core, acc_rows(ai_ref, at, rows), kept_ref, sent_ref, rows)


def return_rows(info, grads, x1, dx2, mixed, sources, wq, wi, wo, vectors, own, micros, parts):
    rows, width = x1.shape
    held = rows // own // 2
    steps = 2 * held
    last = steps - 1
    row = row_spec(own, width, last)
    pieces = [piece(parts, 4 * width // parts, width, steps, low_first)]
    sums = like((8, width))
    return kernel_call(
        functools.partial(return_kernel, steps=steps, parts=parts),
        "return_rows",
        info,
        (*grads, x1, dx2, mixed, sources, wq, wi, wo, vectors),
        [row] * 7 + [resident(a) for a in (wq, wi, wo, vectors)],
        [
            like((micros, own, width)),
            like((held, own, width), jnp.bfloat16),
            like((rows, width)),
            like((rows, width), jnp.bfloat16),
            sums,
        ]
        + sum([p[1] for p in pieces], []),
        [own_spec(own, width, held, last), got_spec(own, width, last), row, row, whole_block(sums)]
        + sum([p[0] for p in pieces], []),
        steps + parts // 2,
        16 * rows * width * width,
        40 * 2**20,
        scratch=[
            pltpu.VMEM((width, width), jnp.float32),
            pltpu.VMEM((width, width), jnp.float32),
            pltpu.VMEM((width, 2 * width), jnp.float32),
        ],
    )


def last_weight_kernel(
    info_ref, dq_ref, dk_ref, dv_ref, x_ref, vec_ref, ka_ref, sa_ref, kb_ref, sb_ref, acc_ref,
    *, steps,
):
    step = pl.program_id(0)

    @pl.when(step == 0)
    def _():
        acc_ref[...] = jnp.zeros_like(acc_ref)

    @pl.when(step < steps)
    def _():
        unit, _ = normal_parts(x_ref[...].astype(jnp.float32))
        turned = (unit * vec_ref[0:1, :] + vec_ref[1:2, :]).astype(jnp.bfloat16).T
        width = x_ref.shape[1]
        for at, ref in enumerate((dq_ref, dk_ref, dv_ref)):
            acc_ref[:, at * width : (at + 1) * width] += contract(turned, ref[...], 1, 0)

    @pl.when(step >= steps)
    def _():
        rows = acc_rows(acc_ref, step - steps, 2 * ka_ref.shape[1])
        half = ka_ref.shape[2]
        write_split(info_ref[1], rows[:, :half], ka_ref, sa_ref, 0)
        write_split(info_ref[1], rows[:, half:], kb_ref, sb_ref, 0)


def last_weight(info, grads, x, vectors, own, parts):
    rows, width = x.shape
    steps = rows // own
    row = row_spec(own, width, steps - 1)
    pieces = [
        piece(parts, width // parts, 3 * width // 2, steps, order)
        for order in (low_first, second_first)
    ]
    return kernel_call(
        functools.partial(last_weight_kernel, steps=steps),
        "last_weight",
        info,
        (*grads, x, vectors),
        [row] * 4 + [resident(vectors)],
        sum([p[1] for p in pieces], []),
        sum([p[0] for p in pieces], []),
        steps + parts // 2,
        24 * rows * width * width,
        20 * 2**20,
        scratch=[pltpu.VMEM((width, 3 * width), jnp.float32)],
    )


def leave_kernel(
    info_ref, dq_ref, dk_ref, dv_ref, x_ref, dx_ref, w_ref, vec_ref, *refs, halves
):
    refs = list(refs)
    up_ref, vsum_ref = refs.pop(), refs.pop()
    got_ref = refs.pop() if 1 in halves else None
    own_ref = refs.pop() if 0 in halves else None
    step = pl.program_id(0)

    @pl.when(step == 0)
    def _():
        vsum_ref[...] = jnp.zeros_like(vsum_ref)

    width = x_ref.shape[1]
    dq, dk, dv = dq_ref[...], dk_ref[...], dv_ref[...]
    upstream = (
        contract(dq, w_ref[:, :width], 1, 1)
        + contract(dk, w_ref[:, width : 2 * width], 1, 1)
        + contract(dv, w_ref[:, 2 * width :], 1, 1)
    )
    unit, inverse = normal_parts(x_ref[...].astype(jnp.float32))
    dx = dx_ref[...] + normal_back(unit, inverse, vec_ref[0:1, :], upstream)
    if len(halves) == 2:
        put_rows(step, dx, own_ref, got_ref)
    else:
        out_ref = got_ref if own_ref is None else own_ref
        out_ref[...] = dx.astype(out_ref.dtype)
    vsum_ref[0:1, :] += column_sum(upstream * unit)
    vsum_ref[1:2, :] += column_sum(upstream)
    vsum_ref[2:3, :] += column_sum(dq.astype(jnp.float32))
    vsum_ref[3:4, :] += column_sum(dv.astype(jnp.float32))


def leave(info, at, halves, previous, grads, x, dx1, weight, vectors, own, micros):
    rows, width = x.shape
    held = rows // own // 2
    row = pl.BlockSpec((own, width), lambda step, info: (2 * at + halves[0] + step, 0))
    more = {"input_output_aliases": {8: 0}} if previous else {}
    sums = like((8, width))
    outs, out_specs = [], []
    if 0 in halves:
        outs.append(like((micros, own, width)))
        out_specs.append(
            pl.BlockSpec((None, own, width), lambda step, info: (info[0] * held + at, 0, 0))
        )
    if 1 in halves:
        outs.append(like((own, width), jnp.bfloat16))
        out_specs.append(pl.BlockSpec((own, width), lambda step, info: (0, 0)))
    return kernel_call(
        functools.partial(leave_kernel, halves=halves),
        "leave",
        info,
        (*grads, x, dx1, weight, vectors, *previous),
        [row] * 5
        + [resident(a) for a in (weight, vectors)]
        + [pl.BlockSpec(memory_space=pl.ANY)] * len(previous),
        outs + [sums],
        out_specs + [whole_block(sums)],
        len(halves),
        12 * len(halves) * own * width * width,
        8 * len(halves) * 2**20,
        scratch=[pltpu.VMEM((8, 128), jnp.float32)],
        **more,
    )


SWAP = ((0, 1), (1, 0))


class Tree:
    def __init__(self, kept, sent, order):
        self.count = lax.axis_size("dp")
        bits = self.count.bit_length() - 2
        shape = (2,) * bits + kept.shape[1:]
        self.order = [2 << bit for bit in order(bits)]
        self.kept, self.sent, self.bit = kept.reshape(shape), sent.reshape(shape), 1
        self.got, self.total = None, None

    def exchange(self):
        if self.total is not None or self.got is not None:
            return
        if self.bit:
            pairs = [(i, i ^ self.bit) for i in range(self.count)]
            self.got = lax.ppermute(self.sent, "dp", pairs)
        else:
            self.got = lax.ppermute(self.kept, "seq", SWAP)

    def add(self):
        if self.got is None:
            return
        total = self.kept.astype(jnp.float32) + self.got.astype(jnp.float32)
        self.got = None
        if not self.bit:
            self.total = total
            return
        total = total.astype(jnp.bfloat16)
        if not self.order:
            self.bit, self.kept = 0, total
            return
        self.bit = self.order.pop(0)
        mine = (lax.axis_index("dp") // self.bit) % 2
        self.kept = lax.dynamic_index_in_dim(total, mine, 0, keepdims=False)
        self.sent = lax.dynamic_index_in_dim(total, 1 - mine, 0, keepdims=False)


def exchange(trees):
    for tree in trees:
        tree.exchange()


def settle(trees, values):
    trees = [tree for tree in trees if tree.got is not None]
    gots, values = lax.optimization_barrier(([tree.got for tree in trees], values))
    for tree, got in zip(trees, gots):
        tree.got = got
        tree.add()
    return values


def receive(trees, values):
    gots, values = lax.optimization_barrier(([tree.got for tree in trees], values))
    for tree, got in zip(trees, gots):
        tree.got = got
    return values


def finish(trees):
    while any(tree.total is None for tree in trees):
        exchange(trees)
        settle(trees, ())


MESH = pl.DeviceIdType.MESH


def partner(place, offset):
    bit = 1
    while bit <= offset:
        if offset & bit:
            place = place + bit * (1 - 2 * ((place // bit) % 2))
        bit *= 2
    return place


def tail_kernel(*refs, orders, groups):
    trees = len(orders)
    ins, refs = refs[: 2 * trees + 4], refs[2 * trees + 4 :]
    outs, refs = refs[: trees + 1], refs[trees + 1 :]
    send_sems, recv_sems = refs[-2:]
    scratch = list(refs[:-2])
    place = lax.axis_index("dp")
    side = lax.axis_index("seq")
    offsets = sorted({bit for order in orders for bit in order} | {o for g in groups for o in g})
    peers = [{"dp": partner(place, offset)} for offset in offsets] + [{"seq": 1 - side}]
    barrier = pltpu.get_barrier_semaphore()
    for peer in peers:
        pl.semaphore_signal(barrier, inc=1, device_id=peer, device_id_type=MESH)
    pl.semaphore_wait(barrier, len(peers))
    used = []

    def send(source, target, peer):
        at = len(used)
        copy = pltpu.make_async_remote_copy(
            src_ref=source,
            dst_ref=target,
            send_sem=send_sems.at[at],
            recv_sem=recv_sems.at[at],
            device_id=peer,
            device_id_type=MESH,
        )
        used.append(copy)
        copy.start()
        return copy

    other = {"seq": 1 - side}
    totals = []
    for at in range(trees):
        total = scratch.pop(0)
        total[...] = (
            ins[2 * at][...].astype(jnp.float32) + ins[2 * at + 1][...].astype(jnp.float32)
        ).astype(jnp.bfloat16)
        totals.append(total)
    sums = [ref[...] for ref in ins[2 * trees : 2 * trees + 3]]
    hidden, width = ins[-1][...], sums[0].shape[1]
    sums += [hidden[:, at : at + width] for at in range(0, hidden.shape[1], width)]
    spare = outs[trees].shape[0] - sum(rows.shape[0] for rows in sums)
    sums = jnp.concatenate(sums + [jnp.zeros((spare, width), jnp.float32)], axis=0)
    rounds = max(max(len(order) for order in orders) + 1, len(groups) + 1)
    for step in range(rounds):
        copies = []
        for at, order in enumerate(orders):
            if step < len(order):
                mine = (place // order[step]) % 2
                got = scratch.pop(0)
                peer = {"dp": partner(place, order[step])}
                copy = send(totals[at].at[1 - mine], got, peer)
                copies.append((copy, at, mine, got, scratch.pop(0)))
            elif step == len(order):
                got = scratch.pop(0)
                copies.append((send(totals[at], got, other), at, None, got, outs[at]))
        summed = []
        if step <= len(groups):
            low = scratch.pop(0)
            low[...] = sums.astype(jnp.bfloat16)
            goals = [other]
            if step < len(groups):
                goals = [{"dp": partner(place, offset)} for offset in groups[step]]
            for goal in goals:
                got = scratch.pop(0)
                summed.append((send(low, got, goal), got))
        for copy, at, mine, got, target in copies:
            copy.wait()
            held = totals[at][...] if mine is None else totals[at][mine]
            total = held.astype(jnp.float32) + got[...].astype(jnp.float32)
            target[...] = total.astype(target.dtype)
            totals[at] = target
        for copy, got in summed:
            copy.wait()
            sums = sums + got[...].astype(jnp.float32)
    outs[trees][...] = sums


def tail(trees, sums, parts):
    orders = [tuple(tree.order) for tree in trees]
    groups, bit = [], 1
    while bit < parts:
        groups.append(tuple(step * bit for step in (1, 2, 3) if step * bit < parts))
        bit *= 4
    arrays = []
    for tree in trees:
        arrays += [tree.kept, tree.got]
    arrays += sums
    sums = like((32, sums[0].shape[1]))
    totals = [pltpu.VMEM(tree.kept.shape, jnp.bfloat16) for tree in trees]
    scratch = totals
    shapes = [tree.kept.shape for tree in trees]
    copies = 0
    for step in range(max(max(len(order) for order in orders) + 1, len(groups) + 1)):
        for at, order in enumerate(orders):
            if step < len(order):
                shapes[at] = shapes[at][1:]
                scratch += [pltpu.VMEM(shapes[at], jnp.bfloat16)] * 2
                copies += 1
            elif step == len(order):
                scratch += [pltpu.VMEM(shapes[at], jnp.bfloat16)]
                copies += 1
        if step <= len(groups):
            each = len(groups[step]) if step < len(groups) else 1
            scratch += [pltpu.VMEM(sums.shape, jnp.bfloat16)] * (each + 1)
            copies += each
    outs = [like(shape) for shape in shapes] + [like(sums.shape)]
    vmem = pl.BlockSpec(memory_space=pltpu.VMEM)
    return pl.pallas_call(
        functools.partial(tail_kernel, orders=orders, groups=groups),
        in_specs=[vmem] * len(arrays),
        out_specs=[vmem] * len(outs),
        out_shape=outs,
        scratch_shapes=scratch + [pltpu.SemaphoreType.DMA((copies,))] * 2,
        compiler_params=pltpu.CompilerParams(
            collective_id=0, has_side_effects=True, vmem_limit_bytes=LIMIT
        ),
        cost_estimate=pl.CostEstimate(
            flops=2 * 10**10, bytes_accessed=10**7, transcendentals=0
        ),
        name="tail",
    )(*arrays)


def final_kernel(info_ref, kept_ref, got_ref, mid_ref, first_ref, second_ref, sums_ref, *outs, rows, vectors):
    place = info_ref[info_ref.shape[0] - 1]
    width = mid_ref.shape[1]
    high = kept_ref.shape[0]

    def feed_rows(start, count):
        at = slice(start, start + count)
        return kept_ref[at, :].astype(jnp.float32) + got_ref[at, :].astype(jnp.float32)

    wide = outs[17].shape[1] // width
    inner = high - (wide + 1) * rows
    outs[19][...] = feed_rows(0, inner)
    outs[13][...] = feed_rows(inner, rows)
    for at in range(wide):
        outs[17][:, at * width : (at + 1) * width] = feed_rows(inner + (at + 1) * rows, rows)
    outs[9][...] = mid_ref[:rows, :]
    outs[5][...] = mid_ref[rows : 2 * rows, :]
    for at in range(2):
        outs[11][:, at * width : (at + 1) * width] = mid_ref[(2 + at) * rows : (3 + at) * rows, :]
    half = first_ref.shape[1]
    outs[2][:, :half] = first_ref[...]
    outs[2][:, half:] = second_ref[...]
    turn = lax.rem(width - place * rows, width)
    for group in range(3):
        turned = pltpu.roll(sums_ref[8 * group : 8 * group + 8, :], turn, 1)
        for index, row in vectors:
            if row // 8 == group:
                outs[index][...] = turned[row % 8 : row % 8 + 1, :rows]
    each = width // inner
    hidden = sums_ref[24 : 24 + wide, :]
    turned = pltpu.roll(
        jnp.concatenate([hidden] * (8 // wide), axis=0),
        lax.rem(width - lax.rem(place, each) * inner, width),
        1,
    )[:, :inner]
    mine = lax.broadcasted_iota(jnp.int32, turned.shape, 0) == place // each
    outs[18][...] = jnp.sum(jnp.where(mine, turned, 0.0), axis=0, keepdims=True)


def final_outputs(info, kept, got, mid, first, second, sums, inner, rows):
    width = mid.shape[1]
    block = inner * rows // width
    vectors = tuple(
        (index, at if at < 4 else at + 4 if at < 8 else at + 8)
        for at, index in enumerate((0, 1, 3, 4, 14, 15, 16, 20, 7, 8, 6, 10, 12))
    )
    shapes = [(1, rows)] * 21
    shapes[18] = (1, block)
    shapes[2], shapes[5], shapes[9], shapes[13] = (rows, 3 * width), *[(rows, width)] * 3
    shapes[11], shapes[17], shapes[19] = (rows, 2 * width), (rows, inner), (block, width)
    arrays = (kept, got, mid, first, second, sums)
    outs = [like(shape) for shape in shapes]
    results = kernel_call(
        functools.partial(final_kernel, rows=rows, vectors=vectors),
        "final",
        info,
        arrays,
        [whole_block(a) for a in arrays],
        outs,
        [whole_block(a) for a in outs],
        1,
        10**6,
        10**7,
    )
    return [out[0] if out.shape[0] == 1 else out for out in results]


def whole_sequences(
    targets,
    memory,
    row_kind,
    loss_mask,
    cotangent,
    norm_self_gain,
    norm_self_bias,
    self_input,
    self_query_bias,
    self_value_bias,
    self_output,
    self_output_bias,
    norm_cross_gain,
    norm_cross_bias,
    cross_query,
    cross_query_bias,
    cross_input,
    cross_value_bias,
    cross_output,
    cross_output_bias,
    norm_feed_gain,
    norm_feed_bias,
    feed_in,
    feed_in_bias,
    feed_out,
    feed_out_bias,
):
    micros, _, own, width = targets.shape
    held = micros // 2
    side = lax.axis_index("seq")
    parts = lax.axis_size("dp")
    place = lax.axis_index("dp")
    length = 2 * own
    pairs = HEADS * HEAD // 128

    def swap(rows, at, count, after=()):
        sent = lax.dynamic_slice_in_dim(rows, (1 - side) * held + at, count, axis=0)
        sent, after = lax.optimization_barrier((sent, after))
        return lax.ppermute(sent, "seq", SWAP), after

    def give(owns, got, at):
        got = got.astype(owns.dtype)
        return lax.dynamic_update_slice_in_dim(owns, got, (1 - side) * held + at, axis=0)

    def pack(*rows):
        zero = jnp.zeros((8 - len(rows), width), jnp.float32)
        return jnp.concatenate([jnp.stack(rows), zero])

    def batch(rows):
        return rows.reshape(held, length, -1)

    def flat(rows):
        return rows.reshape(held * length, -1)

    targets, memory = targets[:, 0], memory[:, 0]
    upstreams = (
        cotangent[:, 0].astype(jnp.float32) * loss_mask[:, 0].astype(jnp.float32)[..., None]
    ).astype(jnp.bfloat16)
    kinds = lax.dynamic_slice_in_dim(row_kind[:, 0], side * held, held, axis=0)
    info = jnp.concatenate(
        [jnp.stack([side, place % 2]), kinds, place[None]], dtype=jnp.int32
    )

    self_vectors = pack(norm_self_gain, norm_self_bias)
    zero = jnp.zeros_like(self_query_bias)
    joint_bias = jnp.concatenate([self_query_bias, zero, self_value_bias])[None]
    pair_bias = jnp.concatenate([zero, cross_value_bias])[None]
    got, _ = swap(targets, 0, 1)
    entered = enter(
        info, None, held, (), held, targets, self_input, self_vectors, joint_bias, True
    )
    source_parts = enter(
        info, None, held, (), held, memory, cross_input, self_vectors, pair_bias, False
    )
    got, entered, source_parts = lax.optimization_barrier((got, entered, source_parts))
    attended = ()
    for at in range(held):
        if at + 1 < held:
            later, got = swap(targets, at + 1, 1, got)
        entered = enter(
            info, at, 1, entered, held, got, self_input, self_vectors, joint_bias, True
        )
        joint = batch(entered[1])
        attended = attend(info, at, 1, attended, joint, joint, joint, True, (0, 1, 2))
        if at + 1 < held:
            entered, attended, got = lax.optimization_barrier((entered, attended, later))
        if at + 2 == held:
            memory_gots, got = swap(memory, 0, held, got)
    inputs, joint = entered[0], batch(entered[1])
    self_mixed, self_raised, self_inverse = attended
    after_self, cross_queries = middle(
        info,
        inputs,
        flat(self_mixed),
        self_output,
        cross_query,
        pack(self_output_bias, norm_cross_gain, norm_cross_bias, cross_query_bias),
        own,
    )
    cross_queries, source_parts, memory_gots = lax.optimization_barrier(
        (cross_queries, source_parts, memory_gots)
    )
    upstream_gots, memory_gots = swap(upstreams, 0, held, memory_gots)
    sources, cross_pairs = enter(
        info, 0, held, source_parts, held, memory_gots, cross_input, self_vectors, pair_bias, False
    )
    cross_queries, cross_pairs = batch(cross_queries), batch(cross_pairs)
    cross_mixed, cross_raised, cross_inverse = attend(
        info, 0, held, (), cross_queries, cross_pairs, cross_pairs, False, (0, 0, 1)
    )
    results, result_gots, grad_cross, cross_upstream, feed_sums, hidden_sums, *feed_parts = feed(
        info,
        after_self,
        flat(cross_mixed),
        upstreams,
        upstream_gots,
        cross_output,
        feed_in,
        feed_out,
        pack(cross_output_bias, norm_feed_gain, norm_feed_bias, feed_out_bias),
        feed_in_bias[None],
        parts,
    )
    feed_trees = [Tree(*feed_parts, low_first)]
    first = pairs // 2
    cross_inputs = (
        cross_queries, cross_pairs, cross_pairs, (0, 0, 1), cross_mixed, batch(cross_upstream),
        cross_raised, cross_inverse,
    )
    exchange(feed_trees)
    result_gots = lax.ppermute(result_gots, "seq", SWAP)
    half_grads = settle(feed_trees, attend_back((0, 0), (held, first), (), *cross_inputs))
    exchange(feed_trees)
    cross_grads = attend_back((0, first), (held, pairs - first), half_grads, *cross_inputs)
    (source_grads, source_gots, grad_self, self_upstream, return_sums, *mid_parts), back = settle(
        feed_trees,
        (return_rows(
            info,
            [flat(rows) for rows in cross_grads],
            after_self,
            grad_cross,
            flat(self_mixed),
            sources,
            cross_query,
            cross_input,
            self_output,
            pack(norm_cross_gain, norm_cross_bias),
            own,
            micros,
            parts,
        ), result_gots),
    )
    results = give(results, back, 0)
    mid_trees = [Tree(*mid_parts, low_first)]
    exchange(feed_trees + mid_trees)
    self_inputs = (
        joint, joint, joint, (0, 1, 2), self_mixed, batch(self_upstream), self_raised, self_inverse
    )
    source_gots = lax.ppermute(source_gots, "seq", SWAP)
    grads = settle(feed_trees + mid_trees, attend_back((0, 0), (1, pairs), (), *self_inputs))
    exchange(feed_trees + mid_trees)
    kept, sums = (), 0.0
    trees = feed_trees + mid_trees

    def leave_now(at, halves, kept, grads):
        return leave(
            info, at, halves, kept, [flat(rows) for rows in grads], inputs, grad_self,
            self_input, self_vectors, own, micros,
        )

    for at in range(held - 1):
        kept, got, new_sums = leave_now(at, (0, 1), kept, grads)
        sums = sums + new_sums
        grads, kept = lax.optimization_barrier((grads, kept))
        back = lax.ppermute(got, "seq", SWAP)
        grads, back, source_gots = settle(
            trees, (attend_back((at + 1, 0), (1, pairs), grads, *self_inputs), back, source_gots)
        )
        for tree in mid_trees:
            tree.kept, tree.sent, grads = lax.optimization_barrier((tree.kept, tree.sent, grads))
        exchange(trees)
        back = back.astype(kept.dtype)[None]
        kept = (lax.dynamic_update_slice_in_dim(kept, back, (1 - side) * held + at, axis=0),)
    got, new_sums = leave_now(held - 1, (1,), (), grads)
    sums = sums + new_sums
    back = lax.ppermute(got, "seq", SWAP)
    grads, _ = lax.optimization_barrier((grads, got))
    late_parts = last_weight(info, [flat(rows) for rows in grads], inputs, self_vectors, own, parts)
    late_parts = settle(mid_trees, late_parts)
    late_trees = [Tree(*late_parts[0:2], low_first), Tree(*late_parts[2:4], second_first)]
    exchange(mid_trees + late_trees)
    (grads, _), back = lax.optimization_barrier(((grads, late_parts[0]), back))
    grads = settle(late_trees, grads)
    exchange(late_trees)
    input_grads, new_sums = leave_now(held - 1, (0,), kept, grads)
    input_grads, new_sums = receive(trees + late_trees, (input_grads, new_sums))
    sums = [sums + new_sums, feed_sums, return_sums, hidden_sums]
    mid_total, *late_totals, sums = tail(mid_trees + late_trees, sums, parts)
    input_grads = give(input_grads, back[None], held - 1)
    final = final_outputs(
        info, feed_trees[0].kept, feed_trees[0].got, mid_total, *late_totals, sums,
        feed_in.shape[1], width // parts,
    )
    source_grads = give(source_grads, source_gots, 0)
    return (results[:, None], input_grads[:, None], source_grads[:, None]) + tuple(final)


def solution(mesh):
    in_specs = (
        P(None, "dp", "seq", None),
        P(None, "dp", "seq", None),
        P(None, "dp"),
        P(None, "dp", "seq"),
        P(None, "dp", "seq", None),
        P(),
        P(),
        P(),
        P(),
        P(),
        P(),
        P(),
        P(),
        P(),
        P(),
        P(),
        P(),
        P(),
        P(),
        P(),
        P(),
        P(),
        P(),
        P(),
        P(),
        P(),
    )
    out_specs = (
        P(None, "dp", "seq", None),
        P(None, "dp", "seq", None),
        P(None, "dp", "seq", None),
        P("dp"),
        P("dp"),
        P("dp", None),
        P("dp"),
        P("dp"),
        P("dp", None),
        P("dp"),
        P("dp"),
        P("dp"),
        P("dp", None),
        P("dp"),
        P("dp", None),
        P("dp"),
        P("dp", None),
        P("dp"),
        P("dp"),
        P("dp"),
        P("dp", None),
        P("dp"),
        P("dp", None),
        P("dp"),
    )

    def on_device(*arguments):
        micros = arguments[0].shape[0]
        rows = lax.axis_size("dp")
        pairs = lax.axis_size("seq") == 2 and micros % 2 == 0
        whole = pairs and rows == 16
        return (whole_sequences if whole else split_sequences)(*arguments)

    return jax.shard_map(
        on_device, mesh=mesh, in_specs=in_specs, out_specs=out_specs, check_vma=False
    )
```

```python
import functools

import jax
import jax.numpy as jnp
from jax import lax
from jax.experimental import pallas as pl
from jax.experimental.pallas import tpu as pltpu
from jax.sharding import PartitionSpec as P

HEADS = 12
HEAD = 64


epsilon = 1e-05
blocked_score = -1e30


def normed(values, norm_gain, norm_shift):
    center = values - jnp.mean(values, axis=-1, keepdims=True)
    spread = jnp.mean(center * center, axis=-1, keepdims=True)
    return center * lax.rsqrt(spread + epsilon) * norm_gain + norm_shift


def normed_back(values, norm_gain, norm_shift, upstream):
    unused, pullback = jax.vjp(normed, values, norm_gain, norm_shift)
    return pullback(upstream)


def gelu_exact(values):
    return jax.nn.gelu(values, approximate=False)


def project_rows(row_block, weight):
    return jnp.einsum("bpd,de->bpe", row_block, weight, preferred_element_type=jnp.float32)


def project_back(row_block, weight):
    return jnp.einsum("bpe,de->bpd", row_block, weight, preferred_element_type=jnp.float32)


def outer_sum(first_rows, second_rows):
    return jnp.einsum("bpd,bpe->de", first_rows, second_rows, preferred_element_type=jnp.float32)


def split_heads(row_block):
    return row_block.reshape(row_block.shape[0], row_block.shape[1], HEADS, HEAD)


def masked_scores(queries, key_rows, allowed):
    scores = jnp.einsum(
        "bphe,bshe->bhps",
        split_heads(queries),
        split_heads(key_rows),
        preferred_element_type=jnp.float32,
    )
    if allowed is None:
        return scores
    return jnp.where(allowed[:, None], scores, blocked_score)


def attend_forward(queries, key_rows, values, allowed):
    scores = masked_scores(queries, key_rows, allowed)
    highest_score = jnp.max(scores, axis=-1, keepdims=True)
    raised = jnp.exp(scores - highest_score)
    totals = jnp.sum(raised, axis=-1, keepdims=True)
    weights = (raised / totals).astype(jnp.bfloat16)
    mixed = jnp.einsum(
        "bhps,bshe->bphe", weights, split_heads(values), preferred_element_type=jnp.float32
    )
    return (mixed.reshape(queries.shape).astype(jnp.bfloat16), highest_score + jnp.log(totals))


def attend_backward(queries, key_rows, values, allowed, log_totals, upstream):
    weights = jnp.exp(masked_scores(queries, key_rows, allowed) - log_totals)
    upstream_heads = split_heads(upstream)
    value_grads = jnp.einsum(
        "bhps,bphe->bshe",
        weights.astype(jnp.bfloat16),
        upstream_heads,
        preferred_element_type=jnp.float32,
    )
    weight_grads = jnp.einsum(
        "bphe,bshe->bhps", upstream_heads, split_heads(values), preferred_element_type=jnp.float32
    )
    score_grads = weights * (weight_grads - jnp.sum(weight_grads * weights, axis=-1, keepdims=True))
    score_low = score_grads.astype(jnp.bfloat16)
    query_grads = jnp.einsum(
        "bhps,bshe->bphe", score_low, split_heads(key_rows), preferred_element_type=jnp.float32
    ).reshape(queries.shape)
    key_grads = jnp.einsum(
        "bhps,bphe->bshe", score_low, split_heads(queries), preferred_element_type=jnp.float32
    ).reshape(key_rows.shape)
    return (query_grads, jnp.concatenate([key_grads, value_grads.reshape(key_rows.shape)], axis=-1))


def split_sequences(
    targets,
    memory,
    row_kind,
    loss_mask,
    cotangent,
    norm_self_gain,
    norm_self_bias,
    self_input,
    self_query_bias,
    self_value_bias,
    self_output,
    self_output_bias,
    norm_cross_gain,
    norm_cross_bias,
    cross_query,
    cross_query_bias,
    cross_input,
    cross_value_bias,
    cross_output,
    cross_output_bias,
    norm_feed_gain,
    norm_feed_bias,
    feed_in,
    feed_in_bias,
    feed_out,
    feed_out_bias,
):
    model_width = targets.shape[3]
    part_rows = targets.shape[2]
    key_span = part_rows * lax.axis_size("seq")
    query_scale = HEAD ** (-0.5)
    places = lax.axis_index("seq") * part_rows + jnp.arange(part_rows)
    causal = jnp.arange(key_span)[None, :] <= places[:, None]
    results, input_grads, source_grads = ([], [], [])
    totals = None
    for micro_index in range(targets.shape[0]):
        inputs = targets[micro_index].astype(jnp.float32)
        memory_local = memory[micro_index]
        allowed = causal[None] | (row_kind[micro_index] == 1)[:, None, None]
        first_normed = normed(inputs, norm_self_gain, norm_self_bias).astype(jnp.bfloat16)
        self_joint = project_rows(first_normed, self_input)
        queries = ((self_joint[..., :model_width] + self_query_bias) * query_scale).astype(
            jnp.bfloat16
        )
        own_pairs = jnp.concatenate(
            [
                self_joint[..., model_width : 2 * model_width],
                self_joint[..., 2 * model_width :] + self_value_bias,
            ],
            axis=-1,
        ).astype(jnp.bfloat16)
        gathered_self = lax.all_gather(own_pairs, "seq", axis=1, tiled=True)
        key_rows = gathered_self[..., :model_width]
        value_rows = gathered_self[..., model_width:]
        self_mixed, self_totals = attend_forward(queries, key_rows, value_rows, allowed)
        after_self = inputs + project_rows(self_mixed, self_output) + self_output_bias
        second_normed = normed(after_self, norm_cross_gain, norm_cross_bias).astype(jnp.bfloat16)
        cross_queries = (
            (project_rows(second_normed, cross_query) + cross_query_bias) * query_scale
        ).astype(jnp.bfloat16)
        joined = project_rows(lax.all_gather(memory_local, "seq", axis=1, tiled=True), cross_input)
        gathered_cross = jnp.concatenate(
            [joined[..., :model_width], joined[..., model_width:] + cross_value_bias], axis=-1
        ).astype(jnp.bfloat16)
        cross_keys = gathered_cross[..., :model_width]
        cross_values = gathered_cross[..., model_width:]
        cross_mixed, cross_totals = attend_forward(cross_queries, cross_keys, cross_values, None)
        after_cross = after_self + project_rows(cross_mixed, cross_output) + cross_output_bias
        third_normed = normed(after_cross, norm_feed_gain, norm_feed_bias).astype(jnp.bfloat16)
        activated, gelu_pullback = jax.vjp(
            gelu_exact, project_rows(third_normed, feed_in) + feed_in_bias
        )
        activated_low = activated.astype(jnp.bfloat16)
        results.append(
            (after_cross + project_rows(activated_low, feed_out) + feed_out_bias).astype(
                jnp.bfloat16
            )
        )
        pieces = [None] * 21
        grad_output = (
            cotangent[micro_index].astype(jnp.float32)
            * loss_mask[micro_index].astype(jnp.float32)[..., None]
        )
        output_low = grad_output.astype(jnp.bfloat16)
        pieces[19] = outer_sum(activated_low, output_low)
        pieces[20] = jnp.sum(grad_output, axis=(0, 1))
        grad_hidden = gelu_pullback(project_back(output_low, feed_out))[0]
        hidden_low = grad_hidden.astype(jnp.bfloat16)
        pieces[17] = outer_sum(third_normed, hidden_low)
        pieces[18] = jnp.sum(grad_hidden, axis=(0, 1))
        through_feed, pieces[15], pieces[16] = normed_back(
            after_cross, norm_feed_gain, norm_feed_bias, project_back(hidden_low, feed_in)
        )
        grad_cross = grad_output + through_feed
        cross_low = grad_cross.astype(jnp.bfloat16)
        pieces[13] = outer_sum(cross_mixed, cross_low)
        pieces[14] = jnp.sum(grad_cross, axis=(0, 1))
        cross_upstream = project_back(cross_low, cross_output).astype(jnp.bfloat16)
        cross_query_grads, cross_pair_grads = attend_backward(
            cross_queries, cross_keys, cross_values, None, cross_totals, cross_upstream
        )
        own_cross = lax.psum_scatter(
            cross_pair_grads.astype(jnp.bfloat16), "seq", scatter_dimension=1, tiled=True
        ).astype(jnp.float32)
        pieces[12] = jnp.sum(own_cross[..., model_width:], axis=(0, 1))
        own_cross_low = own_cross.astype(jnp.bfloat16)
        pieces[11] = outer_sum(memory_local, own_cross_low)
        source_grads.append(project_back(own_cross_low, cross_input))
        scaled_cross = cross_query_grads * query_scale
        pieces[10] = jnp.sum(scaled_cross, axis=(0, 1))
        scaled_cross_low = scaled_cross.astype(jnp.bfloat16)
        pieces[9] = outer_sum(second_normed, scaled_cross_low)
        through_cross, pieces[7], pieces[8] = normed_back(
            after_self,
            norm_cross_gain,
            norm_cross_bias,
            project_back(scaled_cross_low, cross_query),
        )
        grad_self = grad_cross + through_cross
        self_low = grad_self.astype(jnp.bfloat16)
        pieces[5] = outer_sum(self_mixed, self_low)
        pieces[6] = jnp.sum(grad_self, axis=(0, 1))
        self_upstream = project_back(self_low, self_output).astype(jnp.bfloat16)
        self_query_grads, self_pair_grads = attend_backward(
            queries, key_rows, value_rows, allowed, self_totals, self_upstream
        )
        own_self = lax.psum_scatter(
            self_pair_grads.astype(jnp.bfloat16), "seq", scatter_dimension=1, tiled=True
        ).astype(jnp.float32)
        scaled_self = self_query_grads * query_scale
        pieces[3] = jnp.sum(scaled_self, axis=(0, 1))
        pieces[4] = jnp.sum(own_self[..., model_width:], axis=(0, 1))
        joint_low = jnp.concatenate([scaled_self, own_self], axis=-1).astype(jnp.bfloat16)
        pieces[2] = outer_sum(first_normed, joint_low)
        through_first, pieces[0], pieces[1] = normed_back(
            inputs, norm_self_gain, norm_self_bias, project_back(joint_low, self_input)
        )
        input_grads.append(grad_self + through_first)
        totals = (
            pieces
            if totals is None
            else [running + added for running, added in zip(totals, pieces)]
        )
    def reduced(total):
        block = lax.psum_scatter(
            total.astype(jnp.bfloat16), "dp", scatter_dimension=0, tiled=True
        )
        return lax.psum(block, "seq").astype(jnp.float32)

    final = [reduced(total) for total in totals]
    return (jnp.stack(results), jnp.stack(input_grads), jnp.stack(source_grads)) + tuple(final)


def contract(first, second, first_dim, second_dim):
    return lax.dot_general(
        first, second, (((first_dim,), (second_dim,)), ((), ())), preferred_element_type=jnp.float32
    )


def head_masks(pair):
    lane = lax.broadcasted_iota(jnp.int32, (1, pair.shape[1]), 1)
    zero = jnp.zeros((), pair.dtype)
    return (jnp.where(lane < HEAD, pair, zero), jnp.where(lane < HEAD, zero, pair))


LIMIT = 62 * 2**20


def attend_kernel(info_ref, q_ref, k_ref, v_ref, *refs, use_mask, start):
    o_ref, e_ref, r_ref, mask_ref = refs[-4:]
    length = k_ref.shape[1]
    half = length // 2
    values_turned = v_ref[0].T
    ones = jnp.ones((16, length), jnp.bfloat16)

    def run(masked, shifted):
        lowest, highest = None, None
        for at in range(2):
            queries_at = slice(at * half, (at + 1) * half)
            mixed = []
            for head, queries in enumerate(head_masks(q_ref[0, queries_at, :])):
                scores = contract(k_ref[0], queries, 1, 1)
                if shifted:
                    if masked:
                        seen = mask_ref[:, queries_at].astype(jnp.float32) > 0
                        scores = jnp.where(seen, scores, blocked_score)
                    scores = scores - jnp.max(scores, axis=0, keepdims=True)
                low = jnp.exp(scores).astype(jnp.bfloat16)
                if masked:
                    low = low * mask_ref[:, queries_at]
                e_ref[0, head, :, queries_at] = low
                turned = jnp.concatenate(
                    [values_turned[head * HEAD : (head + 1) * HEAD], ones], axis=0
                )
                sums = contract(turned, low, 1, 0)
                total = sums[HEAD : HEAD + 1]
                if not shifted:
                    lowest = total if lowest is None else jnp.minimum(lowest, total)
                    highest = total if highest is None else jnp.maximum(highest, total)
                inverse = 1.0 / total
                r_ref[0, 0, head : head + 1, queries_at] = inverse
                mixed.append(sums[:HEAD] * inverse)
            o_ref[0, queries_at, :] = jnp.concatenate(mixed, axis=0).T.astype(jnp.bfloat16)
        if not shifted:
            in_range = (jnp.min(lowest) > 1e-20) & (jnp.max(highest) < 1e30)

            @pl.when(jnp.logical_not(in_range))
            def _():
                run(masked, True)

    if not use_mask:
        run(False, False)
        return
    causal = info_ref[2 + start + pl.program_id(0)] == 0

    @pl.when(causal & (pl.program_id(1) == 0))
    def _():
        later = info_ref[0] * half
        query = lax.broadcasted_iota(jnp.int32, (1, length), 1)
        query = jnp.where(query < half, query + later, query - later)

        @pl.loop(0, length, step=64)
        def _(row):
            key = lax.broadcasted_iota(jnp.int32, (64, 1), 0) + row
            key = jnp.where(key < half, key + later, key - later)
            seen = jnp.where(key <= query, 1.0, 0.0)
            mask_ref[pl.ds(pl.multiple_of(row, 64), 64), :] = seen.astype(jnp.bfloat16)

    @pl.when(causal)
    def _():
        run(True, False)

    @pl.when(jnp.logical_not(causal))
    def _():
        run(False, False)


def attend(info, start, count_now, previous, queries, keys, values, use_mask, offsets):
    count, length = queries.shape[:2]
    pairs = HEADS * HEAD // 128
    width = HEADS * HEAD

    def spec(offset):
        return pl.BlockSpec((1, length, 128), lambda s, p, info: (start + s, 0, offset * pairs + p))

    place = lambda s, p, info: (start + s, p, 0, 0)
    return pl.pallas_call(
        functools.partial(attend_kernel, use_mask=use_mask, start=start),
        grid_spec=pltpu.PrefetchScalarGridSpec(
            num_scalar_prefetch=1,
            grid=(count_now, pairs),
            in_specs=[spec(offset) for offset in offsets]
            + [pl.BlockSpec(memory_space=pl.ANY)] * len(previous),
            out_specs=[
                spec(0),
                pl.BlockSpec((1, 2, length, length), place),
                pl.BlockSpec((1, 1, 2, length), place),
            ],
            scratch_shapes=[pltpu.VMEM((length, length), jnp.bfloat16)],
        ),
        out_shape=[
            jax.ShapeDtypeStruct((count, length, width), jnp.bfloat16),
            jax.ShapeDtypeStruct((count, HEADS, length, length), jnp.bfloat16),
            jax.ShapeDtypeStruct((count, pairs, 2, length), jnp.float32),
        ],
        input_output_aliases={4: 0, 5: 1, 6: 2} if previous else {},
        compiler_params=pltpu.CompilerParams(vmem_limit_bytes=LIMIT),
        cost_estimate=pl.CostEstimate(
            flops=4 * count_now * HEADS * length * length * 256,
            bytes_accessed=count_now * HEADS * length * length * 2,
            transcendentals=count_now * HEADS * length * length,
        ),
        name="attend",
    )(info, queries, keys, values, *previous)


def attend_back_kernel(q_ref, k_ref, v_ref, o_ref, g_ref, e_ref, r_ref, dq_ref, dk_ref, dv_ref):
    length = k_ref.shape[1]
    keys_turned = k_ref[0].T
    upstream = g_ref[0].astype(jnp.float32)
    products = (o_ref[0].astype(jnp.float32) * upstream).T
    upstream = upstream.T
    parts, deltas = [], []
    for head in range(2):
        rows = slice(head * HEAD, (head + 1) * HEAD)
        inverse = r_ref[0, 0, head : head + 1, :]
        parts.append(upstream[rows] * inverse)
        deltas.append(jnp.sum(products[rows], axis=0, keepdims=True) * inverse)
    scaled = head_masks(jnp.concatenate(parts, axis=0).T.astype(jnp.bfloat16))
    queries = head_masks(q_ref[0])
    key_sum, value_sum, query_parts = 0.0, 0.0, []
    for head in range(2):
        rows = slice(head * HEAD, (head + 1) * HEAD)
        low = e_ref[0, head]
        grads = contract(v_ref[0], scaled[head], 1, 1)
        score_low = (low.astype(jnp.float32) * (grads - deltas[head])).astype(jnp.bfloat16)
        value_sum += contract(low, scaled[head], 1, 0)
        key_sum += contract(score_low, queries[head], 1, 0)
        query_parts.append(contract(keys_turned[rows], score_low, 1, 0))
    turned = jnp.concatenate(query_parts, axis=0) * (HEAD**-0.5)
    dq_ref[0] = turned.T.astype(jnp.bfloat16)
    dk_ref[0] = key_sum.astype(jnp.bfloat16)
    dv_ref[0] = value_sum.astype(jnp.bfloat16)


def attend_back(place, size, previous, queries, keys, values, offsets, *rest):
    count, length = queries.shape[:2]
    pairs = HEADS * HEAD // 128
    width = HEADS * HEAD

    start, first = place

    def spec(offset):
        return pl.BlockSpec(
            (1, length, 128), lambda s, p: (start + s, 0, offset * pairs + first + p)
        )

    kernel = attend_back_kernel
    aliases = {}
    if previous:
        kernel = lambda *refs: attend_back_kernel(*refs[3:])
        aliases = {0: 0, 1: 1, 2: 2}
    return pl.pallas_call(
        kernel,
        grid=size,
        in_specs=[pl.BlockSpec(memory_space=pl.ANY)] * len(previous)
        + [spec(offset) for offset in offsets]
        + [
            spec(0),
            spec(0),
            pl.BlockSpec((1, 2, length, length), lambda s, p: (start + s, first + p, 0, 0)),
            pl.BlockSpec((1, 1, 2, length), lambda s, p: (start + s, first + p, 0, 0)),
        ],
        out_specs=[spec(0)] * 3,
        out_shape=[jax.ShapeDtypeStruct((count, length, width), jnp.bfloat16)] * 3,
        input_output_aliases=aliases,
        compiler_params=pltpu.CompilerParams(vmem_limit_bytes=LIMIT),
        cost_estimate=pl.CostEstimate(
            flops=16 * size[0] * size[1] * length * length * 256,
            bytes_accessed=4 * size[0] * size[1] * length * length,
            transcendentals=0,
        ),
        name="attend_back",
    )(*previous, queries, keys, values, *rest)


def normal_parts(values):
    center = values - jnp.mean(values, axis=-1, keepdims=True)
    inverse = lax.rsqrt(jnp.mean(center * center, axis=-1, keepdims=True) + epsilon)
    return center * inverse, inverse


def normal_back(unit, inverse, norm_gain, upstream):
    inner = upstream * norm_gain
    shift = jnp.mean(inner, axis=-1, keepdims=True)
    tilt = jnp.mean(inner * unit, axis=-1, keepdims=True)
    return inverse * (inner - shift - unit * tilt)


def gelu_parts(values):
    size = jnp.abs(values)
    ratio = 1.0 / (1.0 + 0.2316418882663604 * size)
    series = 0.5307027145
    for weight in (-0.7265760135, 0.7107068705, -0.142248368, 0.127414796):
        series = series * ratio + weight
    bell = jnp.exp(-0.5 * values * values)
    upper = series * ratio * bell
    chance = jnp.where(values < 0, upper, 1.0 - upper)
    return values * chance, chance + values * (0.3989422804014327 * bell)


def column_sum(values):
    return jnp.sum(values, axis=0, keepdims=True)


def resident(array):
    return pl.BlockSpec(array.shape, lambda *_: (0,) * array.ndim, pipeline_mode=pl.Buffered(1))


def whole_block(array):
    return pl.BlockSpec(array.shape, lambda *_: (0,) * len(array.shape))


def like(shape, dtype=jnp.float32):
    return jax.ShapeDtypeStruct(tuple(shape), dtype)


def pick(take_first, first_ref, second_ref):
    return jnp.where(take_first, first_ref[...], second_ref[...])


ONCE = {"pipeline_mode": pl.Buffered(1)}


def own_spec(own, width, held, last, **more):
    def place(step, info):
        return (info[0] * held + jnp.minimum(step, last) // 2, 0, 0)

    return pl.BlockSpec((None, own, width), place, **more)


def got_spec(own, width, last, **more):
    return pl.BlockSpec(
        (None, own, width), lambda step, info: (jnp.minimum(step, last) // 2, 0, 0), **more
    )


def row_spec(own, width, last, **more):
    return pl.BlockSpec((own, width), lambda step, info: (jnp.minimum(step, last), 0), **more)


def kernel_call(kernel, name, info, arrays, in_specs, outs, out_specs, grid, flops, moved, **more):
    scratch = more.pop("scratch", [])
    return pl.pallas_call(
        kernel,
        grid_spec=pltpu.PrefetchScalarGridSpec(
            num_scalar_prefetch=1,
            grid=(grid,),
            in_specs=in_specs,
            out_specs=out_specs,
            scratch_shapes=scratch,
        ),
        out_shape=outs,
        compiler_params=pltpu.CompilerParams(
            vmem_limit_bytes=more.pop("limit", LIMIT)
        ),
        cost_estimate=pl.CostEstimate(flops=flops, bytes_accessed=moved, transcendentals=0),
        name=name,
        **more,
    )(info, *arrays)


def enter_kernel(info_ref, source_ref, w_ref, vec_ref, bias_ref, *refs, norm):
    x_ref, out_ref = refs[-2:]
    x = source_ref[...]
    x_ref[...] = x
    if norm:
        unit, _ = normal_parts(x.astype(jnp.float32))
        x = (unit * vec_ref[0:1, :] + vec_ref[1:2, :]).astype(jnp.bfloat16)
    width = x.shape[1]
    for start in range(0, w_ref.shape[1], width):
        part = slice(start, start + width)
        total = contract(x, w_ref[:, part], 1, 0) + bias_ref[:, part]
        if norm and start == 0:
            total = total * (HEAD**-0.5)
        out_ref[:, part] = total.astype(jnp.bfloat16)


def enter(info, first, count, previous, held, rows_in, weight, vectors, bias, norm):
    own, width = rows_in.shape[1:]
    rows = 2 * held * own
    wide = weight.shape[1]
    if first is None:
        place = lambda step, info: (info[0] * held + step, 0, 0)
        row = lambda step, info: (2 * step, 0)
    else:
        place = lambda step, info: (step, 0, 0)
        row = lambda step, info: (2 * (first + step) + 1, 0)
    return kernel_call(
        functools.partial(enter_kernel, norm=norm),
        "enter",
        info,
        (rows_in, weight, vectors, bias, *previous),
        [pl.BlockSpec((None, own, width), place)]
        + [resident(a) for a in (weight, vectors, bias)]
        + [pl.BlockSpec(memory_space=pl.ANY)] * len(previous),
        [like((rows, width), jnp.bfloat16), like((rows, wide), jnp.bfloat16)],
        [pl.BlockSpec((own, width), row), pl.BlockSpec((own, wide), row)],
        count,
        2 * count * own * width * wide,
        2 * count * own * (2 * width + wide),
        input_output_aliases={5: 0, 6: 1} if previous else {},
    )


def middle_kernel(info_ref, x_ref, mixed_ref, wo_ref, wq_ref, vec_ref, after_ref, q_ref):
    out_bias, gain, shift, query_bias = (vec_ref[i : i + 1, :] for i in range(4))
    after = (
        x_ref[...].astype(jnp.float32) + contract(mixed_ref[...], wo_ref[...], 1, 0) + out_bias
    )
    after_ref[...] = after
    unit, _ = normal_parts(after)
    normal = (unit * gain + shift).astype(jnp.bfloat16)
    queries = (contract(normal, wq_ref[...], 1, 0) + query_bias) * (HEAD**-0.5)
    q_ref[...] = queries.astype(jnp.bfloat16)


def middle(info, x, mixed, wo, wq, vectors, own):
    rows, width = x.shape
    last = rows // own - 1
    spec = row_spec(own, width, last)
    return kernel_call(
        middle_kernel,
        "middle",
        info,
        (x, mixed, wo, wq, vectors),
        [spec, spec] + [resident(a) for a in (wo, wq, vectors)],
        [like((rows, width)), like((rows, width), jnp.bfloat16)],
        [spec, spec],
        rows // own,
        4 * rows * width * width,
        10 * rows * width,
    )


def write_split(core, rows, kept_ref, sent_ref, start):
    half = rows.shape[0] // 2
    low = rows.astype(jnp.bfloat16)
    place = slice(start, start + half)

    @pl.when(core == 0)
    def _():
        kept_ref[0, place, :] = low[:half]
        sent_ref[0, place, :] = low[half:]

    @pl.when(core != 0)
    def _():
        kept_ref[0, place, :] = low[half:]
        sent_ref[0, place, :] = low[:half]


def write_wide(core, rows, kept_ref, sent_ref, start):
    half, width = rows.shape[0] // 2, kept_ref.shape[2]
    for at in range(rows.shape[1] // width):
        part = rows[:, at * width : (at + 1) * width]
        write_split(core, part, kept_ref, sent_ref, start + at * half)


def acc_rows(ref, at, rows):
    return ref[pl.ds(pl.multiple_of(at * rows, 16), rows), :]


def piece(parts, high, wide, steps, order):
    bits = parts.bit_length() - 2

    def late(step, info):
        at = jnp.maximum(step - steps, 0)
        place = 0
        for bit in order(bits):
            place = 2 * place + (at // 2**bit) % 2
        return (place, 0, 0)

    return (
        [pl.BlockSpec((1, high, wide), late)] * 2,
        [like((parts // 2, high, wide), jnp.bfloat16)] * 2,
    )


def low_first(bits):
    return list(range(bits))


def second_first(bits):
    return list(range(bits))[1:2] + [0] + list(range(2, bits))


def put_rows(step, value, own_ref, got_ref):
    @pl.when(step % 2 == 0)
    def _():
        own_ref[...] = value.astype(own_ref.dtype)

    @pl.when(step % 2 != 0)
    def _():
        got_ref[...] = value.astype(got_ref.dtype)


def feed_kernel(
    info_ref, x_ref, mixed_ref, dyo_ref, dyg_ref, wc_ref, wi_ref, wo_ref, vec_ref, bi_ref,
    own_ref, got_ref, dx_ref, do_ref, vsum_ref, bsum_ref, kept_ref, sent_ref, ai_ref, ao_ref,
    ac_ref, *, steps, chunk, parts,
):
    step = pl.program_id(0)

    @pl.when(step == 0)
    def _():
        for ref in (vsum_ref, bsum_ref, ai_ref, ao_ref, ac_ref):
            ref[...] = jnp.zeros_like(ref)

    @pl.when(step < steps)
    def _():
        cross_bias, gain, shift, out_bias = (vec_ref[i : i + 1, :] for i in range(4))
        mixed = mixed_ref[...]
        x2 = x_ref[...] + contract(mixed, wc_ref[...], 1, 0) + cross_bias
        unit, inverse = normal_parts(x2)
        normal = (unit * gain + shift).astype(jnp.bfloat16)
        normal_turned = normal.T
        dy = pick(step % 2 == 0, dyo_ref, dyg_ref)
        dy_turned = dy.T
        result, upstream = None, None
        for start in range(0, wi_ref.shape[1], chunk):
            part = slice(start, start + chunk)
            hidden = contract(normal, wi_ref[:, part], 1, 0) + bi_ref[:, part]
            active, slope = gelu_parts(hidden)
            active = active.astype(jnp.bfloat16)
            down = contract(active, wo_ref[part, :], 1, 0)
            result = down if result is None else result + down
            grads = contract(dy, wo_ref[part, :], 1, 1) * slope
            bsum_ref[:, part] += column_sum(grads)
            low = grads.astype(jnp.bfloat16)
            up = contract(low, wi_ref[:, part], 1, 1)
            upstream = up if upstream is None else upstream + up
            ao_ref[:, part] += contract(dy_turned, active, 1, 0)
            ai_ref[:, part] += contract(normal_turned, low, 1, 0)
        result = (x2 + result + out_bias).astype(jnp.bfloat16)
        wide = dy.astype(jnp.float32)
        dx = wide + normal_back(unit, inverse, gain, upstream)
        dx_ref[...] = dx
        dx_low = dx.astype(jnp.bfloat16)
        do_ref[...] = contract(dx_low, wc_ref[...], 1, 1).astype(jnp.bfloat16)
        ac_ref[...] += contract(mixed.T, dx_low, 1, 0)
        vsum_ref[0:1, :] += column_sum(dx)
        vsum_ref[1:2, :] += column_sum(upstream * unit)
        vsum_ref[2:3, :] += column_sum(upstream)
        vsum_ref[3:4, :] += column_sum(wide)
        put_rows(step, result, own_ref, got_ref)

    @pl.when(step >= steps)
    def _():
        at = step - steps
        core = info_ref[1]
        width, wide = ai_ref.shape
        rows = 2 * width // parts
        inner = 2 * wide // parts
        columns = ao_ref[:, pl.ds(pl.multiple_of(at * inner, 128), inner)]
        write_split(core, columns.astype(jnp.bfloat16).T, kept_ref, sent_ref, 0)
        write_split(core, acc_rows(ac_ref, at, rows), kept_ref, sent_ref, inner // 2)
        write_wide(core, acc_rows(ai_ref, at, rows), kept_ref, sent_ref, (inner + rows) // 2)


def feed(info, x1, mixed, dys, dy_gots, wc, wi, wo, vectors, bi, parts, chunk=768):
    rows, width = x1.shape
    held, own = dy_gots.shape[:2]
    micros = dys.shape[0]
    inner = wi.shape[1]
    steps = 2 * held
    last = steps - 1
    row = row_spec(own, width, last)
    pieces = [piece(parts, (2 * inner + width) // parts, width, steps, low_first)]
    sums = [like((8, width)), like((1, inner))]
    return kernel_call(
        functools.partial(feed_kernel, steps=steps, chunk=chunk, parts=parts),
        "feed",
        info,
        (x1, mixed, dys, dy_gots, wc, wi, wo, vectors, bi),
        [row_spec(own, width, last, **ONCE)] * 2
        + [own_spec(own, width, held, last, **ONCE), got_spec(own, width, last, **ONCE)]
        + [resident(a) for a in (wc, wi, wo, vectors, bi)],
        [
            like((micros, own, width), jnp.bfloat16),
            like((held, own, width), jnp.bfloat16),
            like((rows, width)),
            like((rows, width), jnp.bfloat16),
        ]
        + sums
        + sum([p[1] for p in pieces], []),
        [own_spec(own, width, held, last), got_spec(own, width, last), row, row]
        + [whole_block(a) for a in sums]
        + sum([p[0] for p in pieces], []),
        steps + parts // 2,
        2 * rows * width * (6 * inner + 3 * width),
        60 * 2**20,
        scratch=[
            pltpu.VMEM((width, inner), jnp.float32),
            pltpu.VMEM((width, inner), jnp.float32),
            pltpu.VMEM((width, width), jnp.float32),
        ],
        limit=LIMIT,
    )


def return_kernel(
    info_ref, dq_ref, dk_ref, dv_ref, x_ref, dx_ref, mixed_ref, src_ref, wq_ref, wi_ref, wo_ref,
    vec_ref, own_ref, got_ref, dxo_ref, do_ref, vsum_ref, kept_ref, sent_ref, aq_ref, ao_ref,
    ai_ref, *, steps, parts,
):
    step = pl.program_id(0)

    @pl.when(step == 0)
    def _():
        for ref in (vsum_ref, aq_ref, ao_ref, ai_ref):
            ref[...] = jnp.zeros_like(ref)

    @pl.when(step < steps)
    def _():
        width = x_ref.shape[1]
        gain, shift = vec_ref[0:1, :], vec_ref[1:2, :]
        dq, dk, dv = dq_ref[...], dk_ref[...], dv_ref[...]
        upstream = contract(dq, wq_ref[...], 1, 1)
        turned = src_ref[...].T
        ai_ref[:, :width] += contract(turned, dk, 1, 0)
        unit, inverse = normal_parts(x_ref[...])
        normal = (unit * gain + shift).astype(jnp.bfloat16)
        ai_ref[:, width:] += contract(turned, dv, 1, 0)
        dx = dx_ref[...] + normal_back(unit, inverse, gain, upstream)
        source = contract(dk, wi_ref[:, :width], 1, 1) + contract(dv, wi_ref[:, width:], 1, 1)
        dxo_ref[...] = dx
        low = dx.astype(jnp.bfloat16)
        aq_ref[...] += contract(normal.T, dq, 1, 0)
        do_ref[...] = contract(low, wo_ref[...], 1, 1).astype(jnp.bfloat16)
        ao_ref[...] += contract(mixed_ref[...].T, low, 1, 0)
        vsum_ref[0:1, :] += column_sum(upstream * unit)
        vsum_ref[1:2, :] += column_sum(upstream)
        vsum_ref[2:3, :] += column_sum(dx)
        vsum_ref[3:4, :] += column_sum(dq.astype(jnp.float32))
        vsum_ref[4:5, :] += column_sum(dv.astype(jnp.float32))
        put_rows(step, source, own_ref, got_ref)

    @pl.when(step >= steps)
    def _():
        at = step - steps
        core = info_ref[1]
        rows = 2 * aq_ref.shape[0] // parts
        write_split(core, acc_rows(aq_ref, at, rows), kept_ref, sent_ref, 0)
        write_split(core, acc_rows(ao_ref, at, rows), kept_ref, sent_ref, rows // 2)
        write_wide(core, acc_rows(ai_ref, at, rows), kept_ref, sent_ref, rows)


def return_rows(info, grads, x1, dx2, mixed, sources, wq, wi, wo, vectors, own, micros, parts):
    rows, width = x1.shape
    held = rows // own // 2
    steps = 2 * held
    last = steps - 1
    row = row_spec(own, width, last)
    pieces = [piece(parts, 4 * width // parts, width, steps, low_first)]
    sums = like((8, width))
    return kernel_call(
        functools.partial(return_kernel, steps=steps, parts=parts),
        "return_rows",
        info,
        (*grads, x1, dx2, mixed, sources, wq, wi, wo, vectors),
        [row] * 7 + [resident(a) for a in (wq, wi, wo, vectors)],
        [
            like((micros, own, width)),
            like((held, own, width), jnp.bfloat16),
            like((rows, width)),
            like((rows, width), jnp.bfloat16),
            sums,
        ]
        + sum([p[1] for p in pieces], []),
        [own_spec(own, width, held, last), got_spec(own, width, last), row, row, whole_block(sums)]
        + sum([p[0] for p in pieces], []),
        steps + parts // 2,
        16 * rows * width * width,
        40 * 2**20,
        scratch=[
            pltpu.VMEM((width, width), jnp.float32),
            pltpu.VMEM((width, width), jnp.float32),
            pltpu.VMEM((width, 2 * width), jnp.float32),
        ],
    )


def last_weight_kernel(
    info_ref, dq_ref, dk_ref, dv_ref, x_ref, vec_ref, ka_ref, sa_ref, kb_ref, sb_ref, acc_ref,
    *, steps,
):
    step = pl.program_id(0)

    @pl.when(step == 0)
    def _():
        acc_ref[...] = jnp.zeros_like(acc_ref)

    @pl.when(step < steps)
    def _():
        unit, _ = normal_parts(x_ref[...].astype(jnp.float32))
        turned = (unit * vec_ref[0:1, :] + vec_ref[1:2, :]).astype(jnp.bfloat16).T
        width = x_ref.shape[1]
        for at, ref in enumerate((dq_ref, dk_ref, dv_ref)):
            acc_ref[:, at * width : (at + 1) * width] += contract(turned, ref[...], 1, 0)

    @pl.when(step >= steps)
    def _():
        rows = acc_rows(acc_ref, step - steps, 2 * ka_ref.shape[1])
        half = ka_ref.shape[2]
        write_split(info_ref[1], rows[:, :half], ka_ref, sa_ref, 0)
        write_split(info_ref[1], rows[:, half:], kb_ref, sb_ref, 0)


def last_weight(info, grads, x, vectors, own, parts):
    rows, width = x.shape
    steps = rows // own
    row = row_spec(own, width, steps - 1)
    pieces = [
        piece(parts, width // parts, 3 * width // 2, steps, order)
        for order in (low_first, second_first)
    ]
    return kernel_call(
        functools.partial(last_weight_kernel, steps=steps),
        "last_weight",
        info,
        (*grads, x, vectors),
        [row] * 4 + [resident(vectors)],
        sum([p[1] for p in pieces], []),
        sum([p[0] for p in pieces], []),
        steps + parts // 2,
        24 * rows * width * width,
        20 * 2**20,
        scratch=[pltpu.VMEM((width, 3 * width), jnp.float32)],
    )


def leave_kernel(
    info_ref, dq_ref, dk_ref, dv_ref, x_ref, dx_ref, w_ref, vec_ref, *refs, halves
):
    refs = list(refs)
    up_ref, vsum_ref = refs.pop(), refs.pop()
    got_ref = refs.pop() if 1 in halves else None
    own_ref = refs.pop() if 0 in halves else None
    step = pl.program_id(0)

    @pl.when(step == 0)
    def _():
        vsum_ref[...] = jnp.zeros_like(vsum_ref)

    width = x_ref.shape[1]
    dq, dk, dv = dq_ref[...], dk_ref[...], dv_ref[...]
    upstream = (
        contract(dq, w_ref[:, :width], 1, 1)
        + contract(dk, w_ref[:, width : 2 * width], 1, 1)
        + contract(dv, w_ref[:, 2 * width :], 1, 1)
    )
    unit, inverse = normal_parts(x_ref[...].astype(jnp.float32))
    dx = dx_ref[...] + normal_back(unit, inverse, vec_ref[0:1, :], upstream)
    if len(halves) == 2:
        put_rows(step, dx, own_ref, got_ref)
    else:
        out_ref = got_ref if own_ref is None else own_ref
        out_ref[...] = dx.astype(out_ref.dtype)
    vsum_ref[0:1, :] += column_sum(upstream * unit)
    vsum_ref[1:2, :] += column_sum(upstream)
    vsum_ref[2:3, :] += column_sum(dq.astype(jnp.float32))
    vsum_ref[3:4, :] += column_sum(dv.astype(jnp.float32))


def leave(info, at, halves, previous, grads, x, dx1, weight, vectors, own, micros):
    rows, width = x.shape
    held = rows // own // 2
    row = pl.BlockSpec((own, width), lambda step, info: (2 * at + halves[0] + step, 0))
    more = {"input_output_aliases": {8: 0}} if previous else {}
    sums = like((8, width))
    outs, out_specs = [], []
    if 0 in halves:
        outs.append(like((micros, own, width)))
        out_specs.append(
            pl.BlockSpec((None, own, width), lambda step, info: (info[0] * held + at, 0, 0))
        )
    if 1 in halves:
        outs.append(like((own, width), jnp.bfloat16))
        out_specs.append(pl.BlockSpec((own, width), lambda step, info: (0, 0)))
    return kernel_call(
        functools.partial(leave_kernel, halves=halves),
        "leave",
        info,
        (*grads, x, dx1, weight, vectors, *previous),
        [row] * 5
        + [resident(a) for a in (weight, vectors)]
        + [pl.BlockSpec(memory_space=pl.ANY)] * len(previous),
        outs + [sums],
        out_specs + [whole_block(sums)],
        len(halves),
        12 * len(halves) * own * width * width,
        8 * len(halves) * 2**20,
        scratch=[pltpu.VMEM((8, 128), jnp.float32)],
        **more,
    )


SWAP = ((0, 1), (1, 0))


class Tree:
    def __init__(self, kept, sent, order):
        self.count = lax.axis_size("dp")
        bits = self.count.bit_length() - 2
        shape = (2,) * bits + kept.shape[1:]
        self.order = [2 << bit for bit in order(bits)]
        self.kept, self.sent, self.bit = kept.reshape(shape), sent.reshape(shape), 1
        self.got, self.total = None, None

    def exchange(self):
        if self.total is not None or self.got is not None:
            return
        if self.bit:
            pairs = [(i, i ^ self.bit) for i in range(self.count)]
            self.got = lax.ppermute(self.sent, "dp", pairs)
        else:
            self.got = lax.ppermute(self.kept, "seq", SWAP)

    def add(self):
        if self.got is None:
            return
        total = self.kept.astype(jnp.float32) + self.got.astype(jnp.float32)
        self.got = None
        if not self.bit:
            self.total = total
            return
        total = total.astype(jnp.bfloat16)
        if not self.order:
            self.bit, self.kept = 0, total
            return
        self.bit = self.order.pop(0)
        mine = (lax.axis_index("dp") // self.bit) % 2
        self.kept = lax.dynamic_index_in_dim(total, mine, 0, keepdims=False)
        self.sent = lax.dynamic_index_in_dim(total, 1 - mine, 0, keepdims=False)


def exchange(trees):
    for tree in trees:
        tree.exchange()


def settle(trees, values):
    trees = [tree for tree in trees if tree.got is not None]
    gots, values = lax.optimization_barrier(([tree.got for tree in trees], values))
    for tree, got in zip(trees, gots):
        tree.got = got
        tree.add()
    return values


def receive(trees, values):
    gots, values = lax.optimization_barrier(([tree.got for tree in trees], values))
    for tree, got in zip(trees, gots):
        tree.got = got
    return values


def finish(trees):
    while any(tree.total is None for tree in trees):
        exchange(trees)
        settle(trees, ())


MESH = pl.DeviceIdType.MESH


def partner(place, offset):
    bit = 1
    while bit <= offset:
        if offset & bit:
            place = place + bit * (1 - 2 * ((place // bit) % 2))
        bit *= 2
    return place


def tail_kernel(*refs, orders, groups):
    trees = len(orders)
    ins, refs = refs[: 2 * trees + 4], refs[2 * trees + 4 :]
    outs, refs = refs[: trees + 1], refs[trees + 1 :]
    send_sems, recv_sems = refs[-2:]
    scratch = list(refs[:-2])
    place = lax.axis_index("dp")
    side = lax.axis_index("seq")
    offsets = sorted({bit for order in orders for bit in order} | {o for g in groups for o in g})
    peers = [{"dp": partner(place, offset)} for offset in offsets] + [{"seq": 1 - side}]
    barrier = pltpu.get_barrier_semaphore()
    for peer in peers:
        pl.semaphore_signal(barrier, inc=1, device_id=peer, device_id_type=MESH)
    pl.semaphore_wait(barrier, len(peers))
    used = []

    def send(source, target, peer):
        at = len(used)
        copy = pltpu.make_async_remote_copy(
            src_ref=source,
            dst_ref=target,
            send_sem=send_sems.at[at],
            recv_sem=recv_sems.at[at],
            device_id=peer,
            device_id_type=MESH,
        )
        used.append(copy)
        copy.start()
        return copy

    other = {"seq": 1 - side}
    totals = []
    for at in range(trees):
        total = scratch.pop(0)
        total[...] = (
            ins[2 * at][...].astype(jnp.float32) + ins[2 * at + 1][...].astype(jnp.float32)
        ).astype(jnp.bfloat16)
        totals.append(total)
    sums = [ref[...] for ref in ins[2 * trees : 2 * trees + 3]]
    hidden, width = ins[-1][...], sums[0].shape[1]
    sums += [hidden[:, at : at + width] for at in range(0, hidden.shape[1], width)]
    spare = outs[trees].shape[0] - sum(rows.shape[0] for rows in sums)
    sums = jnp.concatenate(sums + [jnp.zeros((spare, width), jnp.float32)], axis=0)
    rounds = max(max(len(order) for order in orders) + 1, len(groups) + 1)
    for step in range(rounds):
        copies = []
        for at, order in enumerate(orders):
            if step < len(order):
                mine = (place // order[step]) % 2
                got = scratch.pop(0)
                peer = {"dp": partner(place, order[step])}
                copy = send(totals[at].at[1 - mine], got, peer)
                copies.append((copy, at, mine, got, scratch.pop(0)))
            elif step == len(order):
                got = scratch.pop(0)
                copies.append((send(totals[at], got, other), at, None, got, outs[at]))
        summed = []
        if step <= len(groups):
            low = scratch.pop(0)
            low[...] = sums.astype(jnp.bfloat16)
            goals = [other]
            if step < len(groups):
                goals = [{"dp": partner(place, offset)} for offset in groups[step]]
            for goal in goals:
                got = scratch.pop(0)
                summed.append((send(low, got, goal), got))
        for copy, at, mine, got, target in copies:
            copy.wait()
            held = totals[at][...] if mine is None else totals[at][mine]
            total = held.astype(jnp.float32) + got[...].astype(jnp.float32)
            target[...] = total.astype(target.dtype)
            totals[at] = target
        for copy, got in summed:
            copy.wait()
            sums = sums + got[...].astype(jnp.float32)
    outs[trees][...] = sums


def tail(trees, sums, parts):
    orders = [tuple(tree.order) for tree in trees]
    groups, bit = [], 1
    while bit < parts:
        groups.append(tuple(step * bit for step in (1, 2, 3) if step * bit < parts))
        bit *= 4
    arrays = []
    for tree in trees:
        arrays += [tree.kept, tree.got]
    arrays += sums
    sums = like((32, sums[0].shape[1]))
    totals = [pltpu.VMEM(tree.kept.shape, jnp.bfloat16) for tree in trees]
    scratch = totals
    shapes = [tree.kept.shape for tree in trees]
    copies = 0
    for step in range(max(max(len(order) for order in orders) + 1, len(groups) + 1)):
        for at, order in enumerate(orders):
            if step < len(order):
                shapes[at] = shapes[at][1:]
                scratch += [pltpu.VMEM(shapes[at], jnp.bfloat16)] * 2
                copies += 1
            elif step == len(order):
                scratch += [pltpu.VMEM(shapes[at], jnp.bfloat16)]
                copies += 1
        if step <= len(groups):
            each = len(groups[step]) if step < len(groups) else 1
            scratch += [pltpu.VMEM(sums.shape, jnp.bfloat16)] * (each + 1)
            copies += each
    outs = [like(shape) for shape in shapes] + [like(sums.shape)]
    vmem = pl.BlockSpec(memory_space=pltpu.VMEM)
    return pl.pallas_call(
        functools.partial(tail_kernel, orders=orders, groups=groups),
        in_specs=[vmem] * len(arrays),
        out_specs=[vmem] * len(outs),
        out_shape=outs,
        scratch_shapes=scratch + [pltpu.SemaphoreType.DMA((copies,))] * 2,
        compiler_params=pltpu.CompilerParams(
            collective_id=0, has_side_effects=True, vmem_limit_bytes=LIMIT
        ),
        cost_estimate=pl.CostEstimate(
            flops=2 * 10**10, bytes_accessed=10**7, transcendentals=0
        ),
        name="tail",
    )(*arrays)


def final_kernel(info_ref, kept_ref, got_ref, mid_ref, first_ref, second_ref, sums_ref, *outs, rows, vectors):
    place = info_ref[info_ref.shape[0] - 1]
    width = mid_ref.shape[1]
    high = kept_ref.shape[0]

    def feed_rows(start, count):
        at = slice(start, start + count)
        return kept_ref[at, :].astype(jnp.float32) + got_ref[at, :].astype(jnp.float32)

    wide = outs[17].shape[1] // width
    inner = high - (wide + 1) * rows
    outs[19][...] = feed_rows(0, inner)
    outs[13][...] = feed_rows(inner, rows)
    for at in range(wide):
        outs[17][:, at * width : (at + 1) * width] = feed_rows(inner + (at + 1) * rows, rows)
    outs[9][...] = mid_ref[:rows, :]
    outs[5][...] = mid_ref[rows : 2 * rows, :]
    for at in range(2):
        outs[11][:, at * width : (at + 1) * width] = mid_ref[(2 + at) * rows : (3 + at) * rows, :]
    half = first_ref.shape[1]
    outs[2][:, :half] = first_ref[...]
    outs[2][:, half:] = second_ref[...]
    turn = lax.rem(width - place * rows, width)
    for group in range(3):
        turned = pltpu.roll(sums_ref[8 * group : 8 * group + 8, :], turn, 1)
        for index, row in vectors:
            if row // 8 == group:
                outs[index][...] = turned[row % 8 : row % 8 + 1, :rows]
    each = width // inner
    hidden = sums_ref[24 : 24 + wide, :]
    turned = pltpu.roll(
        jnp.concatenate([hidden] * (8 // wide), axis=0),
        lax.rem(width - lax.rem(place, each) * inner, width),
        1,
    )[:, :inner]
    mine = lax.broadcasted_iota(jnp.int32, turned.shape, 0) == place // each
    outs[18][...] = jnp.sum(jnp.where(mine, turned, 0.0), axis=0, keepdims=True)


def final_outputs(info, kept, got, mid, first, second, sums, inner, rows):
    width = mid.shape[1]
    block = inner * rows // width
    vectors = tuple(
        (index, at if at < 4 else at + 4 if at < 8 else at + 8)
        for at, index in enumerate((0, 1, 3, 4, 14, 15, 16, 20, 7, 8, 6, 10, 12))
    )
    shapes = [(1, rows)] * 21
    shapes[18] = (1, block)
    shapes[2], shapes[5], shapes[9], shapes[13] = (rows, 3 * width), *[(rows, width)] * 3
    shapes[11], shapes[17], shapes[19] = (rows, 2 * width), (rows, inner), (block, width)
    arrays = (kept, got, mid, first, second, sums)
    outs = [like(shape) for shape in shapes]
    results = kernel_call(
        functools.partial(final_kernel, rows=rows, vectors=vectors),
        "final",
        info,
        arrays,
        [whole_block(a) for a in arrays],
        outs,
        [whole_block(a) for a in outs],
        1,
        10**6,
        10**7,
    )
    return [out[0] if out.shape[0] == 1 else out for out in results]


def whole_sequences(
    targets,
    memory,
    row_kind,
    loss_mask,
    cotangent,
    norm_self_gain,
    norm_self_bias,
    self_input,
    self_query_bias,
    self_value_bias,
    self_output,
    self_output_bias,
    norm_cross_gain,
    norm_cross_bias,
    cross_query,
    cross_query_bias,
    cross_input,
    cross_value_bias,
    cross_output,
    cross_output_bias,
    norm_feed_gain,
    norm_feed_bias,
    feed_in,
    feed_in_bias,
    feed_out,
    feed_out_bias,
):
    micros, _, own, width = targets.shape
    held = micros // 2
    side = lax.axis_index("seq")
    parts = lax.axis_size("dp")
    place = lax.axis_index("dp")
    length = 2 * own
    pairs = HEADS * HEAD // 128

    def swap(rows, at, count, after=()):
        sent = lax.dynamic_slice_in_dim(rows, (1 - side) * held + at, count, axis=0)
        sent, after = lax.optimization_barrier((sent, after))
        return lax.ppermute(sent, "seq", SWAP), after

    def give(owns, got, at):
        got = got.astype(owns.dtype)
        return lax.dynamic_update_slice_in_dim(owns, got, (1 - side) * held + at, axis=0)

    def pack(*rows):
        zero = jnp.zeros((8 - len(rows), width), jnp.float32)
        return jnp.concatenate([jnp.stack(rows), zero])

    def batch(rows):
        return rows.reshape(held, length, -1)

    def flat(rows):
        return rows.reshape(held * length, -1)

    targets, memory = targets[:, 0], memory[:, 0]
    upstreams = (
        cotangent[:, 0].astype(jnp.float32) * loss_mask[:, 0].astype(jnp.float32)[..., None]
    ).astype(jnp.bfloat16)
    kinds = lax.dynamic_slice_in_dim(row_kind[:, 0], side * held, held, axis=0)
    info = jnp.concatenate(
        [jnp.stack([side, place % 2]), kinds, place[None]], dtype=jnp.int32
    )

    self_vectors = pack(norm_self_gain, norm_self_bias)
    zero = jnp.zeros_like(self_query_bias)
    joint_bias = jnp.concatenate([self_query_bias, zero, self_value_bias])[None]
    pair_bias = jnp.concatenate([zero, cross_value_bias])[None]
    got, _ = swap(targets, 0, 1)
    entered = enter(
        info, None, held, (), held, targets, self_input, self_vectors, joint_bias, True
    )
    source_parts = enter(
        info, None, held, (), held, memory, cross_input, self_vectors, pair_bias, False
    )
    got, entered, source_parts = lax.optimization_barrier((got, entered, source_parts))
    attended = ()
    for at in range(held):
        if at + 1 < held:
            later, got = swap(targets, at + 1, 1, got)
        entered = enter(
            info, at, 1, entered, held, got, self_input, self_vectors, joint_bias, True
        )
        joint = batch(entered[1])
        attended = attend(info, at, 1, attended, joint, joint, joint, True, (0, 1, 2))
        if at + 1 < held:
            entered, attended, got = lax.optimization_barrier((entered, attended, later))
        if at + 2 == held:
            memory_gots, got = swap(memory, 0, held, got)
    inputs, joint = entered[0], batch(entered[1])
    self_mixed, self_raised, self_inverse = attended
    after_self, cross_queries = middle(
        info,
        inputs,
        flat(self_mixed),
        self_output,
        cross_query,
        pack(self_output_bias, norm_cross_gain, norm_cross_bias, cross_query_bias),
        own,
    )
    cross_queries, source_parts, memory_gots = lax.optimization_barrier(
        (cross_queries, source_parts, memory_gots)
    )
    upstream_gots, memory_gots = swap(upstreams, 0, held, memory_gots)
    sources, cross_pairs = enter(
        info, 0, held, source_parts, held, memory_gots, cross_input, self_vectors, pair_bias, False
    )
    cross_queries, cross_pairs = batch(cross_queries), batch(cross_pairs)
    cross_mixed, cross_raised, cross_inverse = attend(
        info, 0, held, (), cross_queries, cross_pairs, cross_pairs, False, (0, 0, 1)
    )
    results, result_gots, grad_cross, cross_upstream, feed_sums, hidden_sums, *feed_parts = feed(
        info,
        after_self,
        flat(cross_mixed),
        upstreams,
        upstream_gots,
        cross_output,
        feed_in,
        feed_out,
        pack(cross_output_bias, norm_feed_gain, norm_feed_bias, feed_out_bias),
        feed_in_bias[None],
        parts,
    )
    feed_trees = [Tree(*feed_parts, low_first)]
    first = pairs // 2
    cross_inputs = (
        cross_queries, cross_pairs, cross_pairs, (0, 0, 1), cross_mixed, batch(cross_upstream),
        cross_raised, cross_inverse,
    )
    exchange(feed_trees)
    result_gots = lax.ppermute(result_gots, "seq", SWAP)
    half_grads = settle(feed_trees, attend_back((0, 0), (held, first), (), *cross_inputs))
    exchange(feed_trees)
    cross_grads = attend_back((0, first), (held, pairs - first), half_grads, *cross_inputs)
    (source_grads, source_gots, grad_self, self_upstream, return_sums, *mid_parts), back = settle(
        feed_trees,
        (return_rows(
            info,
            [flat(rows) for rows in cross_grads],
            after_self,
            grad_cross,
            flat(self_mixed),
            sources,
            cross_query,
            cross_input,
            self_output,
            pack(norm_cross_gain, norm_cross_bias),
            own,
            micros,
            parts,
        ), result_gots),
    )
    results = give(results, back, 0)
    mid_trees = [Tree(*mid_parts, low_first)]
    exchange(feed_trees + mid_trees)
    self_inputs = (
        joint, joint, joint, (0, 1, 2), self_mixed, batch(self_upstream), self_raised, self_inverse
    )
    source_gots = lax.ppermute(source_gots, "seq", SWAP)
    grads = settle(feed_trees + mid_trees, attend_back((0, 0), (1, pairs), (), *self_inputs))
    exchange(feed_trees + mid_trees)
    kept, sums = (), 0.0
    trees = feed_trees + mid_trees

    def leave_now(at, halves, kept, grads):
        return leave(
            info, at, halves, kept, [flat(rows) for rows in grads], inputs, grad_self,
            self_input, self_vectors, own, micros,
        )

    for at in range(held - 1):
        kept, got, new_sums = leave_now(at, (0, 1), kept, grads)
        sums = sums + new_sums
        grads, kept = lax.optimization_barrier((grads, kept))
        back = lax.ppermute(got, "seq", SWAP)
        grads, back, source_gots = settle(
            trees, (attend_back((at + 1, 0), (1, pairs), grads, *self_inputs), back, source_gots)
        )
        for tree in mid_trees:
            tree.kept, tree.sent, grads = lax.optimization_barrier((tree.kept, tree.sent, grads))
        exchange(trees)
        back = back.astype(kept.dtype)[None]
        kept = (lax.dynamic_update_slice_in_dim(kept, back, (1 - side) * held + at, axis=0),)
    got, new_sums = leave_now(held - 1, (1,), (), grads)
    sums = sums + new_sums
    back = lax.ppermute(got, "seq", SWAP)
    grads, _ = lax.optimization_barrier((grads, got))
    late_parts = last_weight(info, [flat(rows) for rows in grads], inputs, self_vectors, own, parts)
    late_parts = settle(mid_trees, late_parts)
    late_trees = [Tree(*late_parts[0:2], low_first), Tree(*late_parts[2:4], second_first)]
    exchange(mid_trees + late_trees)
    (grads, _), back = lax.optimization_barrier(((grads, late_parts[0]), back))
    grads = settle(late_trees, grads)
    exchange(late_trees)
    input_grads, new_sums = leave_now(held - 1, (0,), kept, grads)
    input_grads, new_sums = receive(trees + late_trees, (input_grads, new_sums))
    sums = [sums + new_sums, feed_sums, return_sums, hidden_sums]
    mid_total, *late_totals, sums = tail(mid_trees + late_trees, sums, parts)
    input_grads = give(input_grads, back[None], held - 1)
    final = final_outputs(
        info, feed_trees[0].kept, feed_trees[0].got, mid_total, *late_totals, sums,
        feed_in.shape[1], width // parts,
    )
    source_grads = give(source_grads, source_gots, 0)
    return (results[:, None], input_grads[:, None], source_grads[:, None]) + tuple(final)


def solution(mesh):
    in_specs = (
        P(None, "dp", "seq", None),
        P(None, "dp", "seq", None),
        P(None, "dp"),
        P(None, "dp", "seq"),
        P(None, "dp", "seq", None),
        P(),
        P(),
        P(),
        P(),
        P(),
        P(),
        P(),
        P(),
        P(),
        P(),
        P(),
        P(),
        P(),
        P(),
        P(),
        P(),
        P(),
        P(),
        P(),
        P(),
        P(),
    )
    out_specs = (
        P(None, "dp", "seq", None),
        P(None, "dp", "seq", None),
        P(None, "dp", "seq", None),
        P("dp"),
        P("dp"),
        P("dp", None),
        P("dp"),
        P("dp"),
        P("dp", None),
        P("dp"),
        P("dp"),
        P("dp"),
        P("dp", None),
        P("dp"),
        P("dp", None),
        P("dp"),
        P("dp", None),
        P("dp"),
        P("dp"),
        P("dp"),
        P("dp", None),
        P("dp"),
        P("dp", None),
        P("dp"),
    )

    def on_device(*arguments):
        micros = arguments[0].shape[0]
        rows = lax.axis_size("dp")
        pairs = lax.axis_size("seq") == 2 and micros % 2 == 0
        whole = pairs and rows == 16
        return (whole_sequences if whole else split_sequences)(*arguments)

    return jax.shard_map(
        on_device, mesh=mesh, in_specs=in_specs, out_specs=out_specs, check_vma=False
    )
```

```python
import functools

import jax
import jax.numpy as jnp
from jax import lax
from jax.experimental import pallas as pl
from jax.experimental.pallas import tpu as pltpu
from jax.sharding import PartitionSpec as P

HEADS = 12
HEAD = 64


epsilon = 1e-05
blocked_score = -1e30


def normed(values, norm_gain, norm_shift):
    center = values - jnp.mean(values, axis=-1, keepdims=True)
    spread = jnp.mean(center * center, axis=-1, keepdims=True)
    return center * lax.rsqrt(spread + epsilon) * norm_gain + norm_shift


def normed_back(values, norm_gain, norm_shift, upstream):
    unused, pullback = jax.vjp(normed, values, norm_gain, norm_shift)
    return pullback(upstream)


def gelu_exact(values):
    return jax.nn.gelu(values, approximate=False)


def project_rows(row_block, weight):
    return jnp.einsum("bpd,de->bpe", row_block, weight, preferred_element_type=jnp.float32)


def project_back(row_block, weight):
    return jnp.einsum("bpe,de->bpd", row_block, weight, preferred_element_type=jnp.float32)


def outer_sum(first_rows, second_rows):
    return jnp.einsum("bpd,bpe->de", first_rows, second_rows, preferred_element_type=jnp.float32)


def split_heads(row_block):
    return row_block.reshape(row_block.shape[0], row_block.shape[1], HEADS, HEAD)


def masked_scores(queries, key_rows, allowed):
    scores = jnp.einsum(
        "bphe,bshe->bhps",
        split_heads(queries),
        split_heads(key_rows),
        preferred_element_type=jnp.float32,
    )
    if allowed is None:
        return scores
    return jnp.where(allowed[:, None], scores, blocked_score)


def attend_forward(queries, key_rows, values, allowed):
    scores = masked_scores(queries, key_rows, allowed)
    highest_score = jnp.max(scores, axis=-1, keepdims=True)
    raised = jnp.exp(scores - highest_score)
    totals = jnp.sum(raised, axis=-1, keepdims=True)
    weights = (raised / totals).astype(jnp.bfloat16)
    mixed = jnp.einsum(
        "bhps,bshe->bphe", weights, split_heads(values), preferred_element_type=jnp.float32
    )
    return (mixed.reshape(queries.shape).astype(jnp.bfloat16), highest_score + jnp.log(totals))


def attend_backward(queries, key_rows, values, allowed, log_totals, upstream):
    weights = jnp.exp(masked_scores(queries, key_rows, allowed) - log_totals)
    upstream_heads = split_heads(upstream)
    value_grads = jnp.einsum(
        "bhps,bphe->bshe",
        weights.astype(jnp.bfloat16),
        upstream_heads,
        preferred_element_type=jnp.float32,
    )
    weight_grads = jnp.einsum(
        "bphe,bshe->bhps", upstream_heads, split_heads(values), preferred_element_type=jnp.float32
    )
    score_grads = weights * (weight_grads - jnp.sum(weight_grads * weights, axis=-1, keepdims=True))
    score_low = score_grads.astype(jnp.bfloat16)
    query_grads = jnp.einsum(
        "bhps,bshe->bphe", score_low, split_heads(key_rows), preferred_element_type=jnp.float32
    ).reshape(queries.shape)
    key_grads = jnp.einsum(
        "bhps,bphe->bshe", score_low, split_heads(queries), preferred_element_type=jnp.float32
    ).reshape(key_rows.shape)
    return (query_grads, jnp.concatenate([key_grads, value_grads.reshape(key_rows.shape)], axis=-1))


def split_sequences(
    targets,
    memory,
    row_kind,
    loss_mask,
    cotangent,
    norm_self_gain,
    norm_self_bias,
    self_input,
    self_query_bias,
    self_value_bias,
    self_output,
    self_output_bias,
    norm_cross_gain,
    norm_cross_bias,
    cross_query,
    cross_query_bias,
    cross_input,
    cross_value_bias,
    cross_output,
    cross_output_bias,
    norm_feed_gain,
    norm_feed_bias,
    feed_in,
    feed_in_bias,
    feed_out,
    feed_out_bias,
):
    model_width = targets.shape[3]
    part_rows = targets.shape[2]
    key_span = part_rows * lax.axis_size("seq")
    query_scale = HEAD ** (-0.5)
    places = lax.axis_index("seq") * part_rows + jnp.arange(part_rows)
    causal = jnp.arange(key_span)[None, :] <= places[:, None]
    results, input_grads, source_grads = ([], [], [])
    totals = None
    for micro_index in range(targets.shape[0]):
        inputs = targets[micro_index].astype(jnp.float32)
        memory_local = memory[micro_index]
        allowed = causal[None] | (row_kind[micro_index] == 1)[:, None, None]
        first_normed = normed(inputs, norm_self_gain, norm_self_bias).astype(jnp.bfloat16)
        self_joint = project_rows(first_normed, self_input)
        queries = ((self_joint[..., :model_width] + self_query_bias) * query_scale).astype(
            jnp.bfloat16
        )
        own_pairs = jnp.concatenate(
            [
                self_joint[..., model_width : 2 * model_width],
                self_joint[..., 2 * model_width :] + self_value_bias,
            ],
            axis=-1,
        ).astype(jnp.bfloat16)
        gathered_self = lax.all_gather(own_pairs, "seq", axis=1, tiled=True)
        key_rows = gathered_self[..., :model_width]
        value_rows = gathered_self[..., model_width:]
        self_mixed, self_totals = attend_forward(queries, key_rows, value_rows, allowed)
        after_self = inputs + project_rows(self_mixed, self_output) + self_output_bias
        second_normed = normed(after_self, norm_cross_gain, norm_cross_bias).astype(jnp.bfloat16)
        cross_queries = (
            (project_rows(second_normed, cross_query) + cross_query_bias) * query_scale
        ).astype(jnp.bfloat16)
        joined = project_rows(lax.all_gather(memory_local, "seq", axis=1, tiled=True), cross_input)
        gathered_cross = jnp.concatenate(
            [joined[..., :model_width], joined[..., model_width:] + cross_value_bias], axis=-1
        ).astype(jnp.bfloat16)
        cross_keys = gathered_cross[..., :model_width]
        cross_values = gathered_cross[..., model_width:]
        cross_mixed, cross_totals = attend_forward(cross_queries, cross_keys, cross_values, None)
        after_cross = after_self + project_rows(cross_mixed, cross_output) + cross_output_bias
        third_normed = normed(after_cross, norm_feed_gain, norm_feed_bias).astype(jnp.bfloat16)
        activated, gelu_pullback = jax.vjp(
            gelu_exact, project_rows(third_normed, feed_in) + feed_in_bias
        )
        activated_low = activated.astype(jnp.bfloat16)
        results.append(
            (after_cross + project_rows(activated_low, feed_out) + feed_out_bias).astype(
                jnp.bfloat16
            )
        )
        pieces = [None] * 21
        grad_output = (
            cotangent[micro_index].astype(jnp.float32)
            * loss_mask[micro_index].astype(jnp.float32)[..., None]
        )
        output_low = grad_output.astype(jnp.bfloat16)
        pieces[19] = outer_sum(activated_low, output_low)
        pieces[20] = jnp.sum(grad_output, axis=(0, 1))
        grad_hidden = gelu_pullback(project_back(output_low, feed_out))[0]
        hidden_low = grad_hidden.astype(jnp.bfloat16)
        pieces[17] = outer_sum(third_normed, hidden_low)
        pieces[18] = jnp.sum(grad_hidden, axis=(0, 1))
        through_feed, pieces[15], pieces[16] = normed_back(
            after_cross, norm_feed_gain, norm_feed_bias, project_back(hidden_low, feed_in)
        )
        grad_cross = grad_output + through_feed
        cross_low = grad_cross.astype(jnp.bfloat16)
        pieces[13] = outer_sum(cross_mixed, cross_low)
        pieces[14] = jnp.sum(grad_cross, axis=(0, 1))
        cross_upstream = project_back(cross_low, cross_output).astype(jnp.bfloat16)
        cross_query_grads, cross_pair_grads = attend_backward(
            cross_queries, cross_keys, cross_values, None, cross_totals, cross_upstream
        )
        own_cross = lax.psum_scatter(
            cross_pair_grads.astype(jnp.bfloat16), "seq", scatter_dimension=1, tiled=True
        ).astype(jnp.float32)
        pieces[12] = jnp.sum(own_cross[..., model_width:], axis=(0, 1))
        own_cross_low = own_cross.astype(jnp.bfloat16)
        pieces[11] = outer_sum(memory_local, own_cross_low)
        source_grads.append(project_back(own_cross_low, cross_input))
        scaled_cross = cross_query_grads * query_scale
        pieces[10] = jnp.sum(scaled_cross, axis=(0, 1))
        scaled_cross_low = scaled_cross.astype(jnp.bfloat16)
        pieces[9] = outer_sum(second_normed, scaled_cross_low)
        through_cross, pieces[7], pieces[8] = normed_back(
            after_self,
            norm_cross_gain,
            norm_cross_bias,
            project_back(scaled_cross_low, cross_query),
        )
        grad_self = grad_cross + through_cross
        self_low = grad_self.astype(jnp.bfloat16)
        pieces[5] = outer_sum(self_mixed, self_low)
        pieces[6] = jnp.sum(grad_self, axis=(0, 1))
        self_upstream = project_back(self_low, self_output).astype(jnp.bfloat16)
        self_query_grads, self_pair_grads = attend_backward(
            queries, key_rows, value_rows, allowed, self_totals, self_upstream
        )
        own_self = lax.psum_scatter(
            self_pair_grads.astype(jnp.bfloat16), "seq", scatter_dimension=1, tiled=True
        ).astype(jnp.float32)
        scaled_self = self_query_grads * query_scale
        pieces[3] = jnp.sum(scaled_self, axis=(0, 1))
        pieces[4] = jnp.sum(own_self[..., model_width:], axis=(0, 1))
        joint_low = jnp.concatenate([scaled_self, own_self], axis=-1).astype(jnp.bfloat16)
        pieces[2] = outer_sum(first_normed, joint_low)
        through_first, pieces[0], pieces[1] = normed_back(
            inputs, norm_self_gain, norm_self_bias, project_back(joint_low, self_input)
        )
        input_grads.append(grad_self + through_first)
        totals = (
            pieces
            if totals is None
            else [running + added for running, added in zip(totals, pieces)]
        )
    def reduced(total):
        block = lax.psum_scatter(
            total.astype(jnp.bfloat16), "dp", scatter_dimension=0, tiled=True
        )
        return lax.psum(block, "seq").astype(jnp.float32)

    final = [reduced(total) for total in totals]
    return (jnp.stack(results), jnp.stack(input_grads), jnp.stack(source_grads)) + tuple(final)


def contract(first, second, first_dim, second_dim):
    return lax.dot_general(
        first, second, (((first_dim,), (second_dim,)), ((), ())), preferred_element_type=jnp.float32
    )


def head_masks(pair):
    lane = lax.broadcasted_iota(jnp.int32, (1, pair.shape[1]), 1)
    zero = jnp.zeros((), pair.dtype)
    return (jnp.where(lane < HEAD, pair, zero), jnp.where(lane < HEAD, zero, pair))


LIMIT = 62 * 2**20


def attend_kernel(info_ref, q_ref, k_ref, v_ref, *refs, use_mask, start):
    o_ref, e_ref, r_ref, mask_ref = refs[-4:]
    length = k_ref.shape[1]
    half = length // 2
    values_turned = v_ref[0].T
    ones = jnp.ones((16, length), jnp.bfloat16)

    def run(masked, shifted):
        lowest, highest = None, None
        for at in range(2):
            queries_at = slice(at * half, (at + 1) * half)
            mixed = []
            for head, queries in enumerate(head_masks(q_ref[0, queries_at, :])):
                scores = contract(k_ref[0], queries, 1, 1)
                if shifted:
                    if masked:
                        seen = mask_ref[:, queries_at].astype(jnp.float32) > 0
                        scores = jnp.where(seen, scores, blocked_score)
                    scores = scores - jnp.max(scores, axis=0, keepdims=True)
                low = jnp.exp(scores).astype(jnp.bfloat16)
                if masked:
                    low = low * mask_ref[:, queries_at]
                e_ref[0, head, :, queries_at] = low
                turned = jnp.concatenate(
                    [values_turned[head * HEAD : (head + 1) * HEAD], ones], axis=0
                )
                sums = contract(turned, low, 1, 0)
                total = sums[HEAD : HEAD + 1]
                if not shifted:
                    lowest = total if lowest is None else jnp.minimum(lowest, total)
                    highest = total if highest is None else jnp.maximum(highest, total)
                inverse = 1.0 / total
                r_ref[0, 0, head : head + 1, queries_at] = inverse
                mixed.append(sums[:HEAD] * inverse)
            o_ref[0, queries_at, :] = jnp.concatenate(mixed, axis=0).T.astype(jnp.bfloat16)
        if not shifted:
            in_range = (jnp.min(lowest) > 1e-20) & (jnp.max(highest) < 1e30)

            @pl.when(jnp.logical_not(in_range))
            def _():
                run(masked, True)

    if not use_mask:
        run(False, False)
        return
    causal = info_ref[2 + start + pl.program_id(0)] == 0

    @pl.when(causal & (pl.program_id(1) == 0))
    def _():
        later = info_ref[0] * half
        query = lax.broadcasted_iota(jnp.int32, (1, length), 1)
        query = jnp.where(query < half, query + later, query - later)

        @pl.loop(0, length, step=64)
        def _(row):
            key = lax.broadcasted_iota(jnp.int32, (64, 1), 0) + row
            key = jnp.where(key < half, key + later, key - later)
            seen = jnp.where(key <= query, 1.0, 0.0)
            mask_ref[pl.ds(pl.multiple_of(row, 64), 64), :] = seen.astype(jnp.bfloat16)

    @pl.when(causal)
    def _():
        run(True, False)

    @pl.when(jnp.logical_not(causal))
    def _():
        run(False, False)


def attend(info, start, count_now, previous, queries, keys, values, use_mask, offsets):
    count, length = queries.shape[:2]
    pairs = HEADS * HEAD // 128
    width = HEADS * HEAD

    def spec(offset):
        return pl.BlockSpec((1, length, 128), lambda s, p, info: (start + s, 0, offset * pairs + p))

    place = lambda s, p, info: (start + s, p, 0, 0)
    return pl.pallas_call(
        functools.partial(attend_kernel, use_mask=use_mask, start=start),
        grid_spec=pltpu.PrefetchScalarGridSpec(
            num_scalar_prefetch=1,
            grid=(count_now, pairs),
            in_specs=[spec(offset) for offset in offsets]
            + [pl.BlockSpec(memory_space=pl.ANY)] * len(previous),
            out_specs=[
                spec(0),
                pl.BlockSpec((1, 2, length, length), place),
                pl.BlockSpec((1, 1, 2, length), place),
            ],
            scratch_shapes=[pltpu.VMEM((length, length), jnp.bfloat16)],
        ),
        out_shape=[
            jax.ShapeDtypeStruct((count, length, width), jnp.bfloat16),
            jax.ShapeDtypeStruct((count, HEADS, length, length), jnp.bfloat16),
            jax.ShapeDtypeStruct((count, pairs, 2, length), jnp.float32),
        ],
        input_output_aliases={4: 0, 5: 1, 6: 2} if previous else {},
        compiler_params=pltpu.CompilerParams(vmem_limit_bytes=LIMIT),
        cost_estimate=pl.CostEstimate(
            flops=4 * count_now * HEADS * length * length * 256,
            bytes_accessed=count_now * HEADS * length * length * 2,
            transcendentals=count_now * HEADS * length * length,
        ),
        name="attend",
    )(info, queries, keys, values, *previous)


def attend_back_kernel(q_ref, k_ref, v_ref, o_ref, g_ref, e_ref, r_ref, dq_ref, dk_ref, dv_ref):
    length = k_ref.shape[1]
    keys_turned = k_ref[0].T
    upstream = g_ref[0].astype(jnp.float32)
    products = (o_ref[0].astype(jnp.float32) * upstream).T
    upstream = upstream.T
    parts, deltas = [], []
    for head in range(2):
        rows = slice(head * HEAD, (head + 1) * HEAD)
        inverse = r_ref[0, 0, head : head + 1, :]
        parts.append(upstream[rows] * inverse)
        deltas.append(jnp.sum(products[rows], axis=0, keepdims=True) * inverse)
    scaled = head_masks(jnp.concatenate(parts, axis=0).T.astype(jnp.bfloat16))
    queries = head_masks(q_ref[0])
    key_sum, value_sum, query_parts = 0.0, 0.0, []
    for head in range(2):
        rows = slice(head * HEAD, (head + 1) * HEAD)
        low = e_ref[0, head]
        grads = contract(v_ref[0], scaled[head], 1, 1)
        score_low = (low.astype(jnp.float32) * (grads - deltas[head])).astype(jnp.bfloat16)
        value_sum += contract(low, scaled[head], 1, 0)
        key_sum += contract(score_low, queries[head], 1, 0)
        query_parts.append(contract(keys_turned[rows], score_low, 1, 0))
    turned = jnp.concatenate(query_parts, axis=0) * (HEAD**-0.5)
    dq_ref[0] = turned.T.astype(jnp.bfloat16)
    dk_ref[0] = key_sum.astype(jnp.bfloat16)
    dv_ref[0] = value_sum.astype(jnp.bfloat16)


def attend_back(place, size, previous, queries, keys, values, offsets, *rest):
    count, length = queries.shape[:2]
    pairs = HEADS * HEAD // 128
    width = HEADS * HEAD

    start, first = place

    def spec(offset):
        return pl.BlockSpec(
            (1, length, 128), lambda s, p: (start + s, 0, offset * pairs + first + p)
        )

    kernel = attend_back_kernel
    aliases = {}
    if previous:
        kernel = lambda *refs: attend_back_kernel(*refs[3:])
        aliases = {0: 0, 1: 1, 2: 2}
    return pl.pallas_call(
        kernel,
        grid=size,
        in_specs=[pl.BlockSpec(memory_space=pl.ANY)] * len(previous)
        + [spec(offset) for offset in offsets]
        + [
            spec(0),
            spec(0),
            pl.BlockSpec((1, 2, length, length), lambda s, p: (start + s, first + p, 0, 0)),
            pl.BlockSpec((1, 1, 2, length), lambda s, p: (start + s, first + p, 0, 0)),
        ],
        out_specs=[spec(0)] * 3,
        out_shape=[jax.ShapeDtypeStruct((count, length, width), jnp.bfloat16)] * 3,
        input_output_aliases=aliases,
        compiler_params=pltpu.CompilerParams(vmem_limit_bytes=LIMIT),
        cost_estimate=pl.CostEstimate(
            flops=16 * size[0] * size[1] * length * length * 256,
            bytes_accessed=4 * size[0] * size[1] * length * length,
            transcendentals=0,
        ),
        name="attend_back",
    )(*previous, queries, keys, values, *rest)


def normal_parts(values):
    center = values - jnp.mean(values, axis=-1, keepdims=True)
    inverse = lax.rsqrt(jnp.mean(center * center, axis=-1, keepdims=True) + epsilon)
    return center * inverse, inverse


def normal_back(unit, inverse, norm_gain, upstream):
    inner = upstream * norm_gain
    shift = jnp.mean(inner, axis=-1, keepdims=True)
    tilt = jnp.mean(inner * unit, axis=-1, keepdims=True)
    return inverse * (inner - shift - unit * tilt)


def gelu_parts(values):
    size = jnp.abs(values)
    ratio = 1.0 / (1.0 + 0.2316418882663604 * size)
    series = 0.5307027145
    for weight in (-0.7265760135, 0.7107068705, -0.142248368, 0.127414796):
        series = series * ratio + weight
    bell = jnp.exp(-0.5 * values * values)
    upper = series * ratio * bell
    chance = jnp.where(values < 0, upper, 1.0 - upper)
    return values * chance, chance + values * (0.3989422804014327 * bell)


def column_sum(values):
    return jnp.sum(values, axis=0, keepdims=True)


def resident(array):
    return pl.BlockSpec(array.shape, lambda *_: (0,) * array.ndim, pipeline_mode=pl.Buffered(1))


def whole_block(array):
    return pl.BlockSpec(array.shape, lambda *_: (0,) * len(array.shape))


def like(shape, dtype=jnp.float32):
    return jax.ShapeDtypeStruct(tuple(shape), dtype)


def pick(take_first, first_ref, second_ref):
    return jnp.where(take_first, first_ref[...], second_ref[...])


ONCE = {"pipeline_mode": pl.Buffered(1)}


def own_spec(own, width, held, last, **more):
    def place(step, info):
        return (info[0] * held + jnp.minimum(step, last) // 2, 0, 0)

    return pl.BlockSpec((None, own, width), place, **more)


def got_spec(own, width, last, **more):
    return pl.BlockSpec(
        (None, own, width), lambda step, info: (jnp.minimum(step, last) // 2, 0, 0), **more
    )


def row_spec(own, width, last, **more):
    return pl.BlockSpec((own, width), lambda step, info: (jnp.minimum(step, last), 0), **more)


def kernel_call(kernel, name, info, arrays, in_specs, outs, out_specs, grid, flops, moved, **more):
    scratch = more.pop("scratch", [])
    return pl.pallas_call(
        kernel,
        grid_spec=pltpu.PrefetchScalarGridSpec(
            num_scalar_prefetch=1,
            grid=(grid,),
            in_specs=in_specs,
            out_specs=out_specs,
            scratch_shapes=scratch,
        ),
        out_shape=outs,
        compiler_params=pltpu.CompilerParams(
            vmem_limit_bytes=more.pop("limit", LIMIT)
        ),
        cost_estimate=pl.CostEstimate(flops=flops, bytes_accessed=moved, transcendentals=0),
        name=name,
        **more,
    )(info, *arrays)


def enter_kernel(info_ref, source_ref, w_ref, vec_ref, bias_ref, *refs, norm):
    x_ref, out_ref = refs[-2:]
    x = source_ref[...]
    x_ref[...] = x
    if norm:
        unit, _ = normal_parts(x.astype(jnp.float32))
        x = (unit * vec_ref[0:1, :] + vec_ref[1:2, :]).astype(jnp.bfloat16)
    width = x.shape[1]
    for start in range(0, w_ref.shape[1], width):
        part = slice(start, start + width)
        total = contract(x, w_ref[:, part], 1, 0) + bias_ref[:, part]
        if norm and start == 0:
            total = total * (HEAD**-0.5)
        out_ref[:, part] = total.astype(jnp.bfloat16)


def enter(info, first, count, previous, held, rows_in, weight, vectors, bias, norm):
    own, width = rows_in.shape[1:]
    rows = 2 * held * own
    wide = weight.shape[1]
    if first is None:
        place = lambda step, info: (info[0] * held + step, 0, 0)
        row = lambda step, info: (2 * step, 0)
    else:
        place = lambda step, info: (step, 0, 0)
        row = lambda step, info: (2 * (first + step) + 1, 0)
    return kernel_call(
        functools.partial(enter_kernel, norm=norm),
        "enter",
        info,
        (rows_in, weight, vectors, bias, *previous),
        [pl.BlockSpec((None, own, width), place)]
        + [resident(a) for a in (weight, vectors, bias)]
        + [pl.BlockSpec(memory_space=pl.ANY)] * len(previous),
        [like((rows, width), jnp.bfloat16), like((rows, wide), jnp.bfloat16)],
        [pl.BlockSpec((own, width), row), pl.BlockSpec((own, wide), row)],
        count,
        2 * count * own * width * wide,
        2 * count * own * (2 * width + wide),
        input_output_aliases={5: 0, 6: 1} if previous else {},
    )


def middle_kernel(info_ref, x_ref, mixed_ref, wo_ref, wq_ref, vec_ref, after_ref, q_ref):
    out_bias, gain, shift, query_bias = (vec_ref[i : i + 1, :] for i in range(4))
    after = (
        x_ref[...].astype(jnp.float32) + contract(mixed_ref[...], wo_ref[...], 1, 0) + out_bias
    )
    after_ref[...] = after
    unit, _ = normal_parts(after)
    normal = (unit * gain + shift).astype(jnp.bfloat16)
    queries = (contract(normal, wq_ref[...], 1, 0) + query_bias) * (HEAD**-0.5)
    q_ref[...] = queries.astype(jnp.bfloat16)


def middle(info, x, mixed, wo, wq, vectors, own):
    rows, width = x.shape
    last = rows // own - 1
    spec = row_spec(own, width, last)
    return kernel_call(
        middle_kernel,
        "middle",
        info,
        (x, mixed, wo, wq, vectors),
        [spec, spec] + [resident(a) for a in (wo, wq, vectors)],
        [like((rows, width)), like((rows, width), jnp.bfloat16)],
        [spec, spec],
        rows // own,
        4 * rows * width * width,
        10 * rows * width,
    )


def write_split(core, rows, kept_ref, sent_ref, start):
    half = rows.shape[0] // 2
    low = rows.astype(jnp.bfloat16)
    place = slice(start, start + half)

    @pl.when(core == 0)
    def _():
        kept_ref[0, place, :] = low[:half]
        sent_ref[0, place, :] = low[half:]

    @pl.when(core != 0)
    def _():
        kept_ref[0, place, :] = low[half:]
        sent_ref[0, place, :] = low[:half]


def write_wide(core, rows, kept_ref, sent_ref, start):
    half, width = rows.shape[0] // 2, kept_ref.shape[2]
    for at in range(rows.shape[1] // width):
        part = rows[:, at * width : (at + 1) * width]
        write_split(core, part, kept_ref, sent_ref, start + at * half)


def acc_rows(ref, at, rows):
    return ref[pl.ds(pl.multiple_of(at * rows, 16), rows), :]


def piece(parts, high, wide, steps, order):
    bits = parts.bit_length() - 2

    def late(step, info):
        at = jnp.maximum(step - steps, 0)
        place = 0
        for bit in order(bits):
            place = 2 * place + (at // 2**bit) % 2
        return (place, 0, 0)

    return (
        [pl.BlockSpec((1, high, wide), late)] * 2,
        [like((parts // 2, high, wide), jnp.bfloat16)] * 2,
    )


def low_first(bits):
    return list(range(bits))


def second_first(bits):
    return list(range(bits))[1:2] + [0] + list(range(2, bits))


def put_rows(step, value, own_ref, got_ref):
    @pl.when(step % 2 == 0)
    def _():
        own_ref[...] = value.astype(own_ref.dtype)

    @pl.when(step % 2 != 0)
    def _():
        got_ref[...] = value.astype(got_ref.dtype)


def feed_kernel(
    info_ref, x_ref, mixed_ref, dyo_ref, dyg_ref, wc_ref, wi_ref, wo_ref, vec_ref, bi_ref,
    own_ref, got_ref, dx_ref, do_ref, vsum_ref, bsum_ref, kept_ref, sent_ref, ai_ref, ao_ref,
    ac_ref, *, steps, chunk, parts,
):
    step = pl.program_id(0)

    @pl.when(step == 0)
    def _():
        for ref in (vsum_ref, bsum_ref, ai_ref, ao_ref, ac_ref):
            ref[...] = jnp.zeros_like(ref)

    @pl.when(step < steps)
    def _():
        cross_bias, gain, shift, out_bias = (vec_ref[i : i + 1, :] for i in range(4))
        mixed = mixed_ref[...]
        x2 = x_ref[...] + contract(mixed, wc_ref[...], 1, 0) + cross_bias
        unit, inverse = normal_parts(x2)
        normal = (unit * gain + shift).astype(jnp.bfloat16)
        normal_turned = normal.T
        dy = pick(step % 2 == 0, dyo_ref, dyg_ref)
        dy_turned = dy.T
        result, upstream = None, None
        for start in range(0, wi_ref.shape[1], chunk):
            part = slice(start, start + chunk)
            hidden = contract(normal, wi_ref[:, part], 1, 0) + bi_ref[:, part]
            active, slope = gelu_parts(hidden)
            active = active.astype(jnp.bfloat16)
            down = contract(active, wo_ref[part, :], 1, 0)
            result = down if result is None else result + down
            grads = contract(dy, wo_ref[part, :], 1, 1) * slope
            bsum_ref[:, part] += column_sum(grads)
            low = grads.astype(jnp.bfloat16)
            up = contract(low, wi_ref[:, part], 1, 1)
            upstream = up if upstream is None else upstream + up
            ao_ref[:, part] += contract(dy_turned, active, 1, 0)
            ai_ref[:, part] += contract(normal_turned, low, 1, 0)
        result = (x2 + result + out_bias).astype(jnp.bfloat16)
        wide = dy.astype(jnp.float32)
        dx = wide + normal_back(unit, inverse, gain, upstream)
        dx_ref[...] = dx
        dx_low = dx.astype(jnp.bfloat16)
        do_ref[...] = contract(dx_low, wc_ref[...], 1, 1).astype(jnp.bfloat16)
        ac_ref[...] += contract(mixed.T, dx_low, 1, 0)
        vsum_ref[0:1, :] += column_sum(dx)
        vsum_ref[1:2, :] += column_sum(upstream * unit)
        vsum_ref[2:3, :] += column_sum(upstream)
        vsum_ref[3:4, :] += column_sum(wide)
        put_rows(step, result, own_ref, got_ref)

    @pl.when(step >= steps)
    def _():
        at = step - steps
        core = info_ref[1]
        width, wide = ai_ref.shape
        rows = 2 * width // parts
        inner = 2 * wide // parts
        columns = ao_ref[:, pl.ds(pl.multiple_of(at * inner, 128), inner)]
        write_split(core, columns.astype(jnp.bfloat16).T, kept_ref, sent_ref, 0)
        write_split(core, acc_rows(ac_ref, at, rows), kept_ref, sent_ref, inner // 2)
        write_wide(core, acc_rows(ai_ref, at, rows), kept_ref, sent_ref, (inner + rows) // 2)


def feed(info, x1, mixed, dys, dy_gots, wc, wi, wo, vectors, bi, parts, chunk=768):
    rows, width = x1.shape
    held, own = dy_gots.shape[:2]
    micros = dys.shape[0]
    inner = wi.shape[1]
    steps = 2 * held
    last = steps - 1
    row = row_spec(own, width, last)
    pieces = [piece(parts, (2 * inner + width) // parts, width, steps, low_first)]
    sums = [like((8, width)), like((1, inner))]
    return kernel_call(
        functools.partial(feed_kernel, steps=steps, chunk=chunk, parts=parts),
        "feed",
        info,
        (x1, mixed, dys, dy_gots, wc, wi, wo, vectors, bi),
        [row_spec(own, width, last, **ONCE)] * 2
        + [own_spec(own, width, held, last, **ONCE), got_spec(own, width, last, **ONCE)]
        + [resident(a) for a in (wc, wi, wo, vectors, bi)],
        [
            like((micros, own, width), jnp.bfloat16),
            like((held, own, width), jnp.bfloat16),
            like((rows, width)),
            like((rows, width), jnp.bfloat16),
        ]
        + sums
        + sum([p[1] for p in pieces], []),
        [own_spec(own, width, held, last), got_spec(own, width, last), row, row]
        + [whole_block(a) for a in sums]
        + sum([p[0] for p in pieces], []),
        steps + parts // 2,
        2 * rows * width * (6 * inner + 3 * width),
        60 * 2**20,
        scratch=[
            pltpu.VMEM((width, inner), jnp.float32),
            pltpu.VMEM((width, inner), jnp.float32),
            pltpu.VMEM((width, width), jnp.float32),
        ],
        limit=LIMIT,
    )


def return_kernel(
    info_ref, dq_ref, dk_ref, dv_ref, x_ref, dx_ref, mixed_ref, src_ref, wq_ref, wi_ref, wo_ref,
    vec_ref, own_ref, got_ref, dxo_ref, do_ref, vsum_ref, kept_ref, sent_ref, aq_ref, ao_ref,
    ai_ref, *, steps, parts,
):
    step = pl.program_id(0)

    @pl.when(step == 0)
    def _():
        for ref in (vsum_ref, aq_ref, ao_ref, ai_ref):
            ref[...] = jnp.zeros_like(ref)

    @pl.when(step < steps)
    def _():
        width = x_ref.shape[1]
        gain, shift = vec_ref[0:1, :], vec_ref[1:2, :]
        dq, dk, dv = dq_ref[...], dk_ref[...], dv_ref[...]
        upstream = contract(dq, wq_ref[...], 1, 1)
        turned = src_ref[...].T
        ai_ref[:, :width] += contract(turned, dk, 1, 0)
        unit, inverse = normal_parts(x_ref[...])
        normal = (unit * gain + shift).astype(jnp.bfloat16)
        ai_ref[:, width:] += contract(turned, dv, 1, 0)
        dx = dx_ref[...] + normal_back(unit, inverse, gain, upstream)
        source = contract(dk, wi_ref[:, :width], 1, 1) + contract(dv, wi_ref[:, width:], 1, 1)
        dxo_ref[...] = dx
        low = dx.astype(jnp.bfloat16)
        aq_ref[...] += contract(normal.T, dq, 1, 0)
        do_ref[...] = contract(low, wo_ref[...], 1, 1).astype(jnp.bfloat16)
        ao_ref[...] += contract(mixed_ref[...].T, low, 1, 0)
        vsum_ref[0:1, :] += column_sum(upstream * unit)
        vsum_ref[1:2, :] += column_sum(upstream)
        vsum_ref[2:3, :] += column_sum(dx)
        vsum_ref[3:4, :] += column_sum(dq.astype(jnp.float32))
        vsum_ref[4:5, :] += column_sum(dv.astype(jnp.float32))
        put_rows(step, source, own_ref, got_ref)

    @pl.when(step >= steps)
    def _():
        at = step - steps
        core = info_ref[1]
        rows = 2 * aq_ref.shape[0] // parts
        write_split(core, acc_rows(aq_ref, at, rows), kept_ref, sent_ref, 0)
        write_split(core, acc_rows(ao_ref, at, rows), kept_ref, sent_ref, rows // 2)
        write_wide(core, acc_rows(ai_ref, at, rows), kept_ref, sent_ref, rows)


def return_rows(info, grads, x1, dx2, mixed, sources, wq, wi, wo, vectors, own, micros, parts):
    rows, width = x1.shape
    held = rows // own // 2
    steps = 2 * held
    last = steps - 1
    row = row_spec(own, width, last)
    pieces = [piece(parts, 4 * width // parts, width, steps, low_first)]
    sums = like((8, width))
    return kernel_call(
        functools.partial(return_kernel, steps=steps, parts=parts),
        "return_rows",
        info,
        (*grads, x1, dx2, mixed, sources, wq, wi, wo, vectors),
        [row] * 7 + [resident(a) for a in (wq, wi, wo, vectors)],
        [
            like((micros, own, width)),
            like((held, own, width), jnp.bfloat16),
            like((rows, width)),
            like((rows, width), jnp.bfloat16),
            sums,
        ]
        + sum([p[1] for p in pieces], []),
        [own_spec(own, width, held, last), got_spec(own, width, last), row, row, whole_block(sums)]
        + sum([p[0] for p in pieces], []),
        steps + parts // 2,
        16 * rows * width * width,
        40 * 2**20,
        scratch=[
            pltpu.VMEM((width, width), jnp.float32),
            pltpu.VMEM((width, width), jnp.float32),
            pltpu.VMEM((width, 2 * width), jnp.float32),
        ],
    )


def last_weight_kernel(
    info_ref, dq_ref, dk_ref, dv_ref, x_ref, vec_ref, ka_ref, sa_ref, kb_ref, sb_ref, acc_ref,
    *, steps,
):
    step = pl.program_id(0)

    @pl.when(step == 0)
    def _():
        acc_ref[...] = jnp.zeros_like(acc_ref)

    @pl.when(step < steps)
    def _():
        unit, _ = normal_parts(x_ref[...].astype(jnp.float32))
        turned = (unit * vec_ref[0:1, :] + vec_ref[1:2, :]).astype(jnp.bfloat16).T
        width = x_ref.shape[1]
        for at, ref in enumerate((dq_ref, dk_ref, dv_ref)):
            acc_ref[:, at * width : (at + 1) * width] += contract(turned, ref[...], 1, 0)

    @pl.when(step >= steps)
    def _():
        rows = acc_rows(acc_ref, step - steps, 2 * ka_ref.shape[1])
        half = ka_ref.shape[2]
        write_split(info_ref[1], rows[:, :half], ka_ref, sa_ref, 0)
        write_split(info_ref[1], rows[:, half:], kb_ref, sb_ref, 0)


def last_weight(info, grads, x, vectors, own, parts):
    rows, width = x.shape
    steps = rows // own
    row = row_spec(own, width, steps - 1)
    pieces = [
        piece(parts, width // parts, 3 * width // 2, steps, order)
        for order in (low_first, second_first)
    ]
    return kernel_call(
        functools.partial(last_weight_kernel, steps=steps),
        "last_weight",
        info,
        (*grads, x, vectors),
        [row] * 4 + [resident(vectors)],
        sum([p[1] for p in pieces], []),
        sum([p[0] for p in pieces], []),
        steps + parts // 2,
        24 * rows * width * width,
        20 * 2**20,
        scratch=[pltpu.VMEM((width, 3 * width), jnp.float32)],
    )


def leave_kernel(
    info_ref, dq_ref, dk_ref, dv_ref, x_ref, dx_ref, w_ref, vec_ref, *refs, halves
):
    refs = list(refs)
    up_ref, vsum_ref = refs.pop(), refs.pop()
    got_ref = refs.pop() if 1 in halves else None
    own_ref = refs.pop() if 0 in halves else None
    step = pl.program_id(0)

    @pl.when(step == 0)
    def _():
        vsum_ref[...] = jnp.zeros_like(vsum_ref)

    width = x_ref.shape[1]
    dq, dk, dv = dq_ref[...], dk_ref[...], dv_ref[...]
    upstream = (
        contract(dq, w_ref[:, :width], 1, 1)
        + contract(dk, w_ref[:, width : 2 * width], 1, 1)
        + contract(dv, w_ref[:, 2 * width :], 1, 1)
    )
    unit, inverse = normal_parts(x_ref[...].astype(jnp.float32))
    dx = dx_ref[...] + normal_back(unit, inverse, vec_ref[0:1, :], upstream)
    vsum_ref[0:1, :] += column_sum(upstream * unit)
    vsum_ref[1:2, :] += column_sum(upstream)
    vsum_ref[2:3, :] += column_sum(dq.astype(jnp.float32))
    vsum_ref[3:4, :] += column_sum(dv.astype(jnp.float32))
    if len(halves) == 2:
        put_rows(step, dx, own_ref, got_ref)
    else:
        out_ref = got_ref if own_ref is None else own_ref
        out_ref[...] = dx.astype(out_ref.dtype)


def leave(info, at, halves, previous, grads, x, dx1, weight, vectors, own, micros):
    rows, width = x.shape
    held = rows // own // 2
    row = pl.BlockSpec((own, width), lambda step, info: (2 * at + halves[0] + step, 0))
    more = {"input_output_aliases": {8: 0}} if previous else {}
    sums = like((8, width))
    outs, out_specs = [], []
    if 0 in halves:
        outs.append(like((micros, own, width)))
        out_specs.append(
            pl.BlockSpec((None, own, width), lambda step, info: (info[0] * held + at, 0, 0))
        )
    if 1 in halves:
        outs.append(like((own, width), jnp.bfloat16))
        out_specs.append(pl.BlockSpec((own, width), lambda step, info: (0, 0)))
    return kernel_call(
        functools.partial(leave_kernel, halves=halves),
        "leave",
        info,
        (*grads, x, dx1, weight, vectors, *previous),
        [row] * 5
        + [resident(a) for a in (weight, vectors)]
        + [pl.BlockSpec(memory_space=pl.ANY)] * len(previous),
        outs + [sums],
        out_specs + [whole_block(sums)],
        len(halves),
        12 * len(halves) * own * width * width,
        8 * len(halves) * 2**20,
        scratch=[pltpu.VMEM((8, 128), jnp.float32)],
        **more,
    )


SWAP = ((0, 1), (1, 0))


class Tree:
    def __init__(self, kept, sent, order):
        self.count = lax.axis_size("dp")
        bits = self.count.bit_length() - 2
        shape = (2,) * bits + kept.shape[1:]
        self.order = [2 << bit for bit in order(bits)]
        self.kept, self.sent, self.bit = kept.reshape(shape), sent.reshape(shape), 1
        self.got, self.total = None, None

    def exchange(self):
        if self.total is not None or self.got is not None:
            return
        if self.bit:
            pairs = [(i, i ^ self.bit) for i in range(self.count)]
            self.got = lax.ppermute(self.sent, "dp", pairs)
        else:
            self.got = lax.ppermute(self.kept, "seq", SWAP)

    def add(self):
        if self.got is None:
            return
        total = self.kept.astype(jnp.float32) + self.got.astype(jnp.float32)
        self.got = None
        if not self.bit:
            self.total = total
            return
        total = total.astype(jnp.bfloat16)
        if not self.order:
            self.bit, self.kept = 0, total
            return
        self.bit = self.order.pop(0)
        mine = (lax.axis_index("dp") // self.bit) % 2
        self.kept = lax.dynamic_index_in_dim(total, mine, 0, keepdims=False)
        self.sent = lax.dynamic_index_in_dim(total, 1 - mine, 0, keepdims=False)


def exchange(trees):
    for tree in trees:
        tree.exchange()


def settle(trees, values):
    trees = [tree for tree in trees if tree.got is not None]
    gots, values = lax.optimization_barrier(([tree.got for tree in trees], values))
    for tree, got in zip(trees, gots):
        tree.got = got
        tree.add()
    return values


def receive(trees, values):
    gots, values = lax.optimization_barrier(([tree.got for tree in trees], values))
    for tree, got in zip(trees, gots):
        tree.got = got
    return values


def finish(trees):
    while any(tree.total is None for tree in trees):
        exchange(trees)
        settle(trees, ())


MESH = pl.DeviceIdType.MESH


def partner(place, offset):
    bit = 1
    while bit <= offset:
        if offset & bit:
            place = place + bit * (1 - 2 * ((place // bit) % 2))
        bit *= 2
    return place


def tail_kernel(*refs, orders, groups):
    trees = len(orders)
    ins, refs = refs[: 2 * trees + 4], refs[2 * trees + 4 :]
    outs, refs = refs[: trees + 1], refs[trees + 1 :]
    send_sems, recv_sems = refs[-2:]
    scratch = list(refs[:-2])
    place = lax.axis_index("dp")
    side = lax.axis_index("seq")
    offsets = sorted({bit for order in orders for bit in order} | {o for g in groups for o in g})
    peers = [{"dp": partner(place, offset)} for offset in offsets] + [{"seq": 1 - side}]
    barrier = pltpu.get_barrier_semaphore()
    for peer in peers:
        pl.semaphore_signal(barrier, inc=1, device_id=peer, device_id_type=MESH)
    pl.semaphore_wait(barrier, len(peers))
    used = []

    def send(source, target, peer):
        at = len(used)
        copy = pltpu.make_async_remote_copy(
            src_ref=source,
            dst_ref=target,
            send_sem=send_sems.at[at],
            recv_sem=recv_sems.at[at],
            device_id=peer,
            device_id_type=MESH,
        )
        used.append(copy)
        copy.start()
        return copy

    other = {"seq": 1 - side}
    totals = []
    for at in range(trees):
        total = scratch.pop(0)
        total[...] = (
            ins[2 * at][...].astype(jnp.float32) + ins[2 * at + 1][...].astype(jnp.float32)
        ).astype(jnp.bfloat16)
        totals.append(total)
    sums = [ref[...] for ref in ins[2 * trees : 2 * trees + 3]]
    hidden, width = ins[-1][...], sums[0].shape[1]
    sums += [hidden[:, at : at + width] for at in range(0, hidden.shape[1], width)]
    spare = outs[trees].shape[0] - sum(rows.shape[0] for rows in sums)
    sums = jnp.concatenate(sums + [jnp.zeros((spare, width), jnp.float32)], axis=0)
    rounds = max(max(len(order) for order in orders) + 1, len(groups) + 1)
    for step in range(rounds):
        copies = []
        for at, order in enumerate(orders):
            if step < len(order):
                mine = (place // order[step]) % 2
                got = scratch.pop(0)
                peer = {"dp": partner(place, order[step])}
                copy = send(totals[at].at[1 - mine], got, peer)
                copies.append((copy, at, mine, got, scratch.pop(0)))
            elif step == len(order):
                got = scratch.pop(0)
                copies.append((send(totals[at], got, other), at, None, got, outs[at]))
        summed = []
        if step <= len(groups):
            low = scratch.pop(0)
            low[...] = sums.astype(jnp.bfloat16)
            goals = [other]
            if step < len(groups):
                goals = [{"dp": partner(place, offset)} for offset in groups[step]]
            for goal in goals:
                got = scratch.pop(0)
                summed.append((send(low, got, goal), got))
        for copy, at, mine, got, target in copies:
            copy.wait()
            held = totals[at][...] if mine is None else totals[at][mine]
            total = held.astype(jnp.float32) + got[...].astype(jnp.float32)
            target[...] = total.astype(target.dtype)
            totals[at] = target
        for copy, got in summed:
            copy.wait()
            sums = sums + got[...].astype(jnp.float32)
    outs[trees][...] = sums


def tail(trees, sums, parts):
    orders = [tuple(tree.order) for tree in trees]
    groups, bit = [], 1
    while bit < parts:
        groups.append(tuple(step * bit for step in (1, 2, 3) if step * bit < parts))
        bit *= 4
    arrays = []
    for tree in trees:
        arrays += [tree.kept, tree.got]
    arrays += sums
    sums = like((32, sums[0].shape[1]))
    totals = [pltpu.VMEM(tree.kept.shape, jnp.bfloat16) for tree in trees]
    scratch = totals
    shapes = [tree.kept.shape for tree in trees]
    copies = 0
    for step in range(max(max(len(order) for order in orders) + 1, len(groups) + 1)):
        for at, order in enumerate(orders):
            if step < len(order):
                shapes[at] = shapes[at][1:]
                scratch += [pltpu.VMEM(shapes[at], jnp.bfloat16)] * 2
                copies += 1
            elif step == len(order):
                scratch += [pltpu.VMEM(shapes[at], jnp.bfloat16)]
                copies += 1
        if step <= len(groups):
            each = len(groups[step]) if step < len(groups) else 1
            scratch += [pltpu.VMEM(sums.shape, jnp.bfloat16)] * (each + 1)
            copies += each
    outs = [like(shape) for shape in shapes] + [like(sums.shape)]
    vmem = pl.BlockSpec(memory_space=pltpu.VMEM)
    return pl.pallas_call(
        functools.partial(tail_kernel, orders=orders, groups=groups),
        in_specs=[vmem] * len(arrays),
        out_specs=[vmem] * len(outs),
        out_shape=outs,
        scratch_shapes=scratch + [pltpu.SemaphoreType.DMA((copies,))] * 2,
        compiler_params=pltpu.CompilerParams(
            collective_id=0, has_side_effects=True, vmem_limit_bytes=LIMIT
        ),
        cost_estimate=pl.CostEstimate(
            flops=2 * 10**10, bytes_accessed=10**7, transcendentals=0
        ),
        name="tail",
    )(*arrays)


def final_kernel(info_ref, kept_ref, got_ref, mid_ref, first_ref, second_ref, sums_ref, *outs, rows, vectors):
    place = info_ref[info_ref.shape[0] - 1]
    width = mid_ref.shape[1]
    high = kept_ref.shape[0]

    def feed_rows(start, count):
        at = slice(start, start + count)
        return kept_ref[at, :].astype(jnp.float32) + got_ref[at, :].astype(jnp.float32)

    wide = outs[17].shape[1] // width
    inner = high - (wide + 1) * rows
    outs[19][...] = feed_rows(0, inner)
    outs[13][...] = feed_rows(inner, rows)
    for at in range(wide):
        outs[17][:, at * width : (at + 1) * width] = feed_rows(inner + (at + 1) * rows, rows)
    outs[9][...] = mid_ref[:rows, :]
    outs[5][...] = mid_ref[rows : 2 * rows, :]
    for at in range(2):
        outs[11][:, at * width : (at + 1) * width] = mid_ref[(2 + at) * rows : (3 + at) * rows, :]
    half = first_ref.shape[1]
    outs[2][:, :half] = first_ref[...]
    outs[2][:, half:] = second_ref[...]
    turn = lax.rem(width - place * rows, width)
    for group in range(3):
        turned = pltpu.roll(sums_ref[8 * group : 8 * group + 8, :], turn, 1)
        for index, row in vectors:
            if row // 8 == group:
                outs[index][...] = turned[row % 8 : row % 8 + 1, :rows]
    each = width // inner
    hidden = sums_ref[24 : 24 + wide, :]
    turned = pltpu.roll(
        jnp.concatenate([hidden] * (8 // wide), axis=0),
        lax.rem(width - lax.rem(place, each) * inner, width),
        1,
    )[:, :inner]
    mine = lax.broadcasted_iota(jnp.int32, turned.shape, 0) == place // each
    outs[18][...] = jnp.sum(jnp.where(mine, turned, 0.0), axis=0, keepdims=True)


def final_outputs(info, kept, got, mid, first, second, sums, inner, rows):
    width = mid.shape[1]
    block = inner * rows // width
    vectors = tuple(
        (index, at if at < 4 else at + 4 if at < 8 else at + 8)
        for at, index in enumerate((0, 1, 3, 4, 14, 15, 16, 20, 7, 8, 6, 10, 12))
    )
    shapes = [(1, rows)] * 21
    shapes[18] = (1, block)
    shapes[2], shapes[5], shapes[9], shapes[13] = (rows, 3 * width), *[(rows, width)] * 3
    shapes[11], shapes[17], shapes[19] = (rows, 2 * width), (rows, inner), (block, width)
    arrays = (kept, got, mid, first, second, sums)
    outs = [like(shape) for shape in shapes]
    results = kernel_call(
        functools.partial(final_kernel, rows=rows, vectors=vectors),
        "final",
        info,
        arrays,
        [whole_block(a) for a in arrays],
        outs,
        [whole_block(a) for a in outs],
        1,
        10**6,
        10**7,
    )
    return [out[0] if out.shape[0] == 1 else out for out in results]


def whole_sequences(
    targets,
    memory,
    row_kind,
    loss_mask,
    cotangent,
    norm_self_gain,
    norm_self_bias,
    self_input,
    self_query_bias,
    self_value_bias,
    self_output,
    self_output_bias,
    norm_cross_gain,
    norm_cross_bias,
    cross_query,
    cross_query_bias,
    cross_input,
    cross_value_bias,
    cross_output,
    cross_output_bias,
    norm_feed_gain,
    norm_feed_bias,
    feed_in,
    feed_in_bias,
    feed_out,
    feed_out_bias,
):
    micros, _, own, width = targets.shape
    held = micros // 2
    side = lax.axis_index("seq")
    parts = lax.axis_size("dp")
    place = lax.axis_index("dp")
    length = 2 * own
    pairs = HEADS * HEAD // 128

    def swap(rows, at, count, after=()):
        sent = lax.dynamic_slice_in_dim(rows, (1 - side) * held + at, count, axis=0)
        sent, after = lax.optimization_barrier((sent, after))
        return lax.ppermute(sent, "seq", SWAP), after

    def give(owns, got, at):
        got = got.astype(owns.dtype)
        return lax.dynamic_update_slice_in_dim(owns, got, (1 - side) * held + at, axis=0)

    def pack(*rows):
        zero = jnp.zeros((8 - len(rows), width), jnp.float32)
        return jnp.concatenate([jnp.stack(rows), zero])

    def batch(rows):
        return rows.reshape(held, length, -1)

    def flat(rows):
        return rows.reshape(held * length, -1)

    targets, memory = targets[:, 0], memory[:, 0]
    upstreams = (
        cotangent[:, 0].astype(jnp.float32) * loss_mask[:, 0].astype(jnp.float32)[..., None]
    ).astype(jnp.bfloat16)
    kinds = lax.dynamic_slice_in_dim(row_kind[:, 0], side * held, held, axis=0)
    info = jnp.concatenate(
        [jnp.stack([side, place % 2]), kinds, place[None]], dtype=jnp.int32
    )

    self_vectors = pack(norm_self_gain, norm_self_bias)
    zero = jnp.zeros_like(self_query_bias)
    joint_bias = jnp.concatenate([self_query_bias, zero, self_value_bias])[None]
    pair_bias = jnp.concatenate([zero, cross_value_bias])[None]
    got, _ = swap(targets, 0, 1)
    entered = enter(
        info, None, held, (), held, targets, self_input, self_vectors, joint_bias, True
    )
    source_parts = enter(
        info, None, held, (), held, memory, cross_input, self_vectors, pair_bias, False
    )
    got, entered, source_parts = lax.optimization_barrier((got, entered, source_parts))
    attended = ()
    for at in range(held):
        if at + 1 < held:
            later, got = swap(targets, at + 1, 1, got)
        entered = enter(
            info, at, 1, entered, held, got, self_input, self_vectors, joint_bias, True
        )
        joint = batch(entered[1])
        attended = attend(info, at, 1, attended, joint, joint, joint, True, (0, 1, 2))
        if at + 1 < held:
            entered, attended, got = lax.optimization_barrier((entered, attended, later))
        if at + 2 == held:
            memory_gots, got = swap(memory, 0, held, got)
    inputs, joint = entered[0], batch(entered[1])
    self_mixed, self_raised, self_inverse = attended
    after_self, cross_queries = middle(
        info,
        inputs,
        flat(self_mixed),
        self_output,
        cross_query,
        pack(self_output_bias, norm_cross_gain, norm_cross_bias, cross_query_bias),
        own,
    )
    cross_queries, source_parts, memory_gots = lax.optimization_barrier(
        (cross_queries, source_parts, memory_gots)
    )
    upstream_gots, memory_gots = swap(upstreams, 0, held, memory_gots)
    sources, cross_pairs = enter(
        info, 0, held, source_parts, held, memory_gots, cross_input, self_vectors, pair_bias, False
    )
    cross_queries, cross_pairs = batch(cross_queries), batch(cross_pairs)
    cross_mixed, cross_raised, cross_inverse = attend(
        info, 0, held, (), cross_queries, cross_pairs, cross_pairs, False, (0, 0, 1)
    )
    results, result_gots, grad_cross, cross_upstream, feed_sums, hidden_sums, *feed_parts = feed(
        info,
        after_self,
        flat(cross_mixed),
        upstreams,
        upstream_gots,
        cross_output,
        feed_in,
        feed_out,
        pack(cross_output_bias, norm_feed_gain, norm_feed_bias, feed_out_bias),
        feed_in_bias[None],
        parts,
    )
    feed_trees = [Tree(*feed_parts, low_first)]
    first = pairs // 2
    cross_inputs = (
        cross_queries, cross_pairs, cross_pairs, (0, 0, 1), cross_mixed, batch(cross_upstream),
        cross_raised, cross_inverse,
    )
    exchange(feed_trees)
    result_gots = lax.ppermute(result_gots, "seq", SWAP)
    half_grads = settle(feed_trees, attend_back((0, 0), (held, first), (), *cross_inputs))
    exchange(feed_trees)
    cross_grads = attend_back((0, first), (held, pairs - first), half_grads, *cross_inputs)
    (source_grads, source_gots, grad_self, self_upstream, return_sums, *mid_parts), back = settle(
        feed_trees,
        (return_rows(
            info,
            [flat(rows) for rows in cross_grads],
            after_self,
            grad_cross,
            flat(self_mixed),
            sources,
            cross_query,
            cross_input,
            self_output,
            pack(norm_cross_gain, norm_cross_bias),
            own,
            micros,
            parts,
        ), result_gots),
    )
    results = give(results, back, 0)
    mid_trees = [Tree(*mid_parts, low_first)]
    exchange(feed_trees + mid_trees)
    self_inputs = (
        joint, joint, joint, (0, 1, 2), self_mixed, batch(self_upstream), self_raised, self_inverse
    )
    source_gots = lax.ppermute(source_gots, "seq", SWAP)
    grads = settle(feed_trees + mid_trees, attend_back((0, 0), (1, pairs), (), *self_inputs))
    exchange(feed_trees + mid_trees)
    kept, sums = (), 0.0
    trees = feed_trees + mid_trees

    def leave_now(at, halves, kept, grads):
        return leave(
            info, at, halves, kept, [flat(rows) for rows in grads], inputs, grad_self,
            self_input, self_vectors, own, micros,
        )

    for at in range(held - 1):
        kept, got, new_sums = leave_now(at, (0, 1), kept, grads)
        sums = sums + new_sums
        grads, kept = lax.optimization_barrier((grads, kept))
        back = lax.ppermute(got, "seq", SWAP)
        grads, back, source_gots = settle(
            trees, (attend_back((at + 1, 0), (1, pairs), grads, *self_inputs), back, source_gots)
        )
        for tree in mid_trees:
            tree.kept, tree.sent, grads = lax.optimization_barrier((tree.kept, tree.sent, grads))
        exchange(trees)
        back = back.astype(kept.dtype)[None]
        kept = (lax.dynamic_update_slice_in_dim(kept, back, (1 - side) * held + at, axis=0),)
    got, new_sums = leave_now(held - 1, (1,), (), grads)
    sums = sums + new_sums
    back = lax.ppermute(got, "seq", SWAP)
    grads, _ = lax.optimization_barrier((grads, got))
    late_parts = last_weight(info, [flat(rows) for rows in grads], inputs, self_vectors, own, parts)
    late_parts = settle(mid_trees, late_parts)
    late_trees = [Tree(*late_parts[0:2], low_first), Tree(*late_parts[2:4], second_first)]
    exchange(mid_trees + late_trees)
    (grads, _), back = lax.optimization_barrier(((grads, late_parts[0]), back))
    grads = settle(late_trees, grads)
    exchange(late_trees)
    input_grads, new_sums = leave_now(held - 1, (0,), kept, grads)
    input_grads, new_sums = receive(trees + late_trees, (input_grads, new_sums))
    sums = [sums + new_sums, feed_sums, return_sums, hidden_sums]
    mid_total, *late_totals, sums = tail(mid_trees + late_trees, sums, parts)
    input_grads = give(input_grads, back[None], held - 1)
    final = final_outputs(
        info, feed_trees[0].kept, feed_trees[0].got, mid_total, *late_totals, sums,
        feed_in.shape[1], width // parts,
    )
    source_grads = give(source_grads, source_gots, 0)
    return (results[:, None], input_grads[:, None], source_grads[:, None]) + tuple(final)


def solution(mesh):
    in_specs = (
        P(None, "dp", "seq", None),
        P(None, "dp", "seq", None),
        P(None, "dp"),
        P(None, "dp", "seq"),
        P(None, "dp", "seq", None),
        P(),
        P(),
        P(),
        P(),
        P(),
        P(),
        P(),
        P(),
        P(),
        P(),
        P(),
        P(),
        P(),
        P(),
        P(),
        P(),
        P(),
        P(),
        P(),
        P(),
        P(),
    )
    out_specs = (
        P(None, "dp", "seq", None),
        P(None, "dp", "seq", None),
        P(None, "dp", "seq", None),
        P("dp"),
        P("dp"),
        P("dp", None),
        P("dp"),
        P("dp"),
        P("dp", None),
        P("dp"),
        P("dp"),
        P("dp"),
        P("dp", None),
        P("dp"),
        P("dp", None),
        P("dp"),
        P("dp", None),
        P("dp"),
        P("dp"),
        P("dp"),
        P("dp", None),
        P("dp"),
        P("dp", None),
        P("dp"),
    )

    def on_device(*arguments):
        micros = arguments[0].shape[0]
        rows = lax.axis_size("dp")
        pairs = lax.axis_size("seq") == 2 and micros % 2 == 0
        whole = pairs and rows == 16
        return (whole_sequences if whole else split_sequences)(*arguments)

    return jax.shard_map(
        on_device, mesh=mesh, in_specs=in_specs, out_specs=out_specs, check_vma=False
    )
```
